32 devices in a mesh: lat: 8 (over y, x, core), lon: 4 (over z).
Axes of the slice: x: 2, y: 2, z: 4, core: 2. Of those that a mesh axis runs over, the one named last changes fastest.
Arguments:
- fields: bfloat16 [256, 128, 256], P('lat', 'lon'), may hold values from -6 to 6
- w_conv1: bfloat16 [3, 3, 256, 256], replicated, may hold values from -0.125 to 0.125
- b_conv1: float32 [256], replicated, may hold values from -3 to 3
- w_conv2: bfloat16 [3, 3, 256, 256], replicated, may hold values from -0.125 to 0.125
- b_conv2: float32 [256], replicated, may hold values from -3 to 3
- w_query: bfloat16 [256, 256], replicated, may hold values from -16 to 16
- w_key: bfloat16 [256, 64], replicated, may hold values from -1 to 1
- w_value: bfloat16 [256, 64], replicated, may hold values from -0.375 to 0.375
- w_out: bfloat16 [256, 256], replicated, may hold values from -0.375 to 0.375
- rotation: int32 [8, 4], replicated, may hold values from 0 to 3
- owner: int32 [8, 4], replicated, may hold values from 0 to 3, as said below
- counts: int32 [256], replicated, may hold values from 4 to 128
Outputs:
- fields_out: bfloat16 [256, 128, 256], P('lat', 'lon')
The draws below stay inside these ranges and needn't reach their ends.
Inputs may be any that keep to these rules, and one draw needn't show every extreme that they name: Each row of owner holds every number from 0 to 3 exactly once.
All inputs are finite; a program needn't handle non-finite values.
Results may differ from the reference program's by a relative error of at most 0.014.
Values may be sent and summed in bfloat16 or wider, within the bound.
No kernel may reach another device: no remote copies, remote signals or barrier semaphores. Data moves between devices by JAX's collectives and lax.ppermute only.
A program may use at most 64 MiB of HBM per device.

```python
import math
import jax
import jax.numpy as jnp
from jax import lax

C = 256
HEADS = 4
HEAD_DIM = 64
P_SIZE = 32
CYCLES = 256
LONC = 128
N_LAT = 8
N_LON = 4


def weight_pair(key):
    key_draw = jax.random.normal(jax.random.fold_in(key, 101), (C, HEAD_DIM), jnp.float32) * C ** (-0.5)
    key_draw = jnp.clip(key_draw, -1.0, 1.0)
    base = jax.random.normal(jax.random.fold_in(key, 102), (C, C), jnp.float32) * C ** (-0.5)
    query_draw = 3.0 * base
    query_draw = jnp.clip(query_draw, -16.0, 16.0)
    return (query_draw, key_draw)


def draw_w_query(key, part):
    return weight_pair(key)[0].astype(jnp.bfloat16)


def draw_w_key(key, part):
    return weight_pair(key)[1].astype(jnp.bfloat16)


def draw_owner(key, part):
    band_keys = jax.random.split(key, N_LAT)
    return jax.vmap(lambda k: jax.random.permutation(k, N_LON))(band_keys).astype(jnp.int32)


def draw_counts(key, part):
    row_ids = jnp.arange(CYCLES, dtype=jnp.int32)
    from_pole = jnp.minimum(row_ids, CYCLES - 1 - row_ids)
    extra = jax.random.randint(key, (CYCLES,), 0, 2 * P_SIZE, dtype=jnp.int32) * (from_pole > 0).astype(jnp.int32)
    return jnp.minimum(LONC, 4 * (from_pole + 1) + extra).astype(jnp.int32)


def place_ends(entries, rng, low, top_value):
    index_at = [jax.random.randint(jax.random.fold_in(rng, axis), (), 0, length) for axis, length in enumerate(entries.shape)]
    main_axis = entries.shape.index(max(entries.shape))
    next_to = index_at[:main_axis] + [(index_at[main_axis] + 1) % entries.shape[main_axis]] + index_at[main_axis + 1:]
    return entries.at[tuple(index_at)].set(low).at[tuple(next_to)].set(top_value)


def level_of(rng, shape, cuts, least, largest):
    gain = 1.0
    for dim, parts in cuts:
        steps = jax.random.uniform(jax.random.fold_in(jax.random.fold_in(rng, 6), dim), (parts,), jnp.float32, least / len(cuts), largest / len(cuts))
        gain = gain * jnp.repeat(jnp.exp(steps), shape[dim] // parts).reshape((-1,) + (1,) * (len(shape) - 1 - dim))
    return gain


def centred(rng, dims, spread, limit, pieces=(), kind=jnp.bfloat16):
    entries = jax.random.normal(rng, dims, jnp.float32) * spread
    if len(pieces) > 0:
        entries = level_of(rng, dims, pieces, -0.22, 0.18) * entries
    return jnp.clip(entries, min=-limit, max=limit).astype(kind)


def setup_inputs(seed: int = 0) -> dict:
    key_of = jax.random.split(jax.random.key(seed), 13)
    return {
        "fields": centred(key_of[0], (CYCLES, LONC, C), 1.0, 6.0, ((0, 8), (1, 4))),
        "w_conv1": centred(key_of[1], (3, 3, C, C), (9 * C) ** -0.5, 0.125),
        "b_conv1": centred(key_of[2], (C,), 0.5, 3.0, (), jnp.float32),
        "w_conv2": centred(key_of[3], (3, 3, C, C), (9 * C) ** -0.5, 0.125),
        "b_conv2": centred(key_of[4], (C,), 0.5, 3.0, (), jnp.float32),
        "w_query": draw_w_query(jax.random.fold_in(key_of[12], 71), 0),
        "w_key": draw_w_key(jax.random.fold_in(key_of[12], 71), 0),
        "w_value": centred(key_of[7], (C, HEAD_DIM), C ** -0.5, 0.375),
        "w_out": centred(key_of[8], (C, C), C ** -0.5, 0.375),
        "rotation": place_ends(jax.random.randint(key_of[9], (N_LAT, N_LON), 0, 4), jax.random.fold_in(key_of[9], 1), 0, 3).astype(jnp.int32),
        "owner": draw_owner(jax.random.fold_in(key_of[12], 71), 0),
        "counts": draw_counts(jax.random.fold_in(key_of[12], 71), 0),
    }


def inverse_owner(owner):
    shards = jnp.arange(N_LON, dtype=jnp.int32)
    matches = owner[:, None, :] == shards[None, :, None]
    return lax.optimization_barrier(jnp.sum(jnp.where(matches, shards[None, None, :], 0), axis=2)).astype(jnp.int32)

def turn_blocks(blocks, quarter_turns):
    result = blocks
    for k in (1, 2, 3):
        turned = jnp.rot90(blocks, k, axes=(2, 3))
        result = jnp.where((quarter_turns % 4 == k)[:, :, None, None, None], turned, result)
    return result

def to_true(fields, rotation, owner):
    blocks = fields.reshape(N_LAT, P_SIZE, N_LON, P_SIZE, C).transpose(0, 2, 1, 3, 4)
    upright = turn_blocks(blocks, (4 - rotation) % 4)
    placed = jnp.take_along_axis(upright, inverse_owner(owner)[:, :, None, None, None], axis=1)
    return placed.transpose(0, 2, 1, 3, 4).reshape(CYCLES, LONC, C)

def from_true(grid, rotation, owner):
    blocks = grid.reshape(N_LAT, P_SIZE, N_LON, P_SIZE, C).transpose(0, 2, 1, 3, 4)
    holder_blocks = jnp.take_along_axis(blocks, owner[:, :, None, None, None], axis=1)
    return turn_blocks(holder_blocks, rotation).transpose(0, 2, 1, 3, 4).reshape(CYCLES, LONC, C)

def convolve(field, weight, bias):
    wrapped = jnp.concatenate([field[:, -1:], field, field[:, :1]], axis=1)
    padded = jnp.pad(wrapped, ((1, 1), (0, 0), (0, 0)))
    total = jnp.zeros((CYCLES * LONC, C), jnp.float32) + bias.astype(jnp.float32)
    for i in range(3):
        for j in range(3):
            window = padded[i:i + CYCLES, j:j + LONC].reshape(CYCLES * LONC, C)
            total = total + jnp.dot(window, weight[i, j], preferred_element_type=jnp.float32)
    return total.reshape(CYCLES, LONC, C)

def attend_row(operands):
    query_row, kv_row, live_row = operands
    heads_q = query_row.reshape(LONC, HEADS, HEAD_DIM).astype(jnp.float32)
    keys_row = kv_row[:, :HEAD_DIM].astype(jnp.float32)
    values_row = kv_row[:, HEAD_DIM:].astype(jnp.float32)
    scores = jnp.einsum('chd,kd->chk', heads_q, keys_row, precision=lax.Precision.HIGHEST) / math.sqrt(HEAD_DIM)
    scores = jnp.where(live_row[None, None, :] > 0, scores, -jnp.inf)
    peak = lax.optimization_barrier(jnp.max(scores, axis=2, keepdims=True))
    expo = jnp.exp(scores - peak)
    total = lax.optimization_barrier(jnp.sum(expo, axis=2))
    weights = expo.astype(jnp.bfloat16)
    summed = jnp.einsum('chk,kd->chd', weights.astype(jnp.float32), values_row, precision=lax.Precision.HIGHEST)
    return (summed / total[:, :, None]).astype(jnp.bfloat16).reshape(LONC, C)

def reference(fields, w_conv1, b_conv1, w_conv2, b_conv2, w_query, w_key, w_value, w_out, rotation, owner, counts):
    grid = to_true(fields, rotation, owner)
    columns = jnp.arange(LONC, dtype=jnp.int32)
    live = (columns[None, :] < counts[:, None]).astype(jnp.float32)
    live_three = live[:, :, None]
    first = convolve(grid, w_conv1, b_conv1)
    act = (jax.nn.silu(first) * live_three).astype(jnp.bfloat16)
    second = convolve(act, w_conv2, b_conv2)
    mixed = ((grid.astype(jnp.float32) + second) * live_three).astype(jnp.bfloat16)
    flat = mixed.reshape(CYCLES * LONC, C).astype(jnp.float32)
    normed = (flat * lax.rsqrt(lax.optimization_barrier(jnp.mean(flat * flat, axis=1, keepdims=True)) + 1e-06)).astype(jnp.bfloat16)
    query = jnp.dot(normed, w_query, preferred_element_type=jnp.float32).astype(jnp.bfloat16)
    key_part = jnp.dot(normed, w_key, preferred_element_type=jnp.float32)
    value_part = jnp.dot(normed, w_value, preferred_element_type=jnp.float32)
    key_val = jnp.concatenate([key_part, value_part], axis=1).astype(jnp.bfloat16)
    attended = lax.map(attend_row, (query.reshape(CYCLES, LONC, C), key_val.reshape(CYCLES, LONC, 2 * HEAD_DIM), live))
    update = jnp.dot(attended.reshape(CYCLES * LONC, C), w_out, preferred_element_type=jnp.float32).reshape(CYCLES, LONC, C)
    result = (mixed.astype(jnp.float32) + update * live_three).astype(jnp.bfloat16)
    return from_true(result, rotation, owner)
```

```python
import functools

import jax
import jax.numpy as jnp
from jax import lax
from jax.experimental import pallas as pl
from jax.experimental.pallas import tpu as pltpu
from jax.sharding import PartitionSpec as P

HALO = 2
LANES = 128
VMEM_BYTES = 48 * 1024 * 1024


def turn(quarter, size, staged, spare, load_row, store_row):
    tiles = staged.shape[0]

    def column(ref, col):
        parts = [ref[t, pl.ds(col, size, stride=size), :] for t in range(tiles)]
        return jnp.concatenate(parts, axis=1)

    def keep(ref, i, row):
        for t in range(tiles):
            ref[t, pl.ds(i * size, size), :] = row[:, t * LANES : (t + 1) * LANES]

    @pl.when(quarter == 0)
    def _():
        for i in range(size):
            store_row(i, load_row(i))

    @pl.when(quarter == 1)
    def _():
        for i in range(size):
            keep(staged, i, load_row(i).astype(jnp.float32))
        for i in range(size):
            store_row(i, column(staged, size - 1 - i).astype(jnp.bfloat16))

    @pl.when(quarter == 2)
    def _():
        for i in range(size):
            keep(staged, i, load_row(i).astype(jnp.float32))
        for i in range(size):
            keep(spare, i, column(staged, size - 1 - i))
        for i in range(size):
            store_row(i, column(spare, size - 1 - i).astype(jnp.bfloat16))

    @pl.when(quarter == 3)
    def _():
        for i in range(size):
            keep(staged, size - 1 - i, load_row(i).astype(jnp.float32))
        for i in range(size):
            store_row(i, column(staged, i).astype(jnp.bfloat16))


def send_kernel(n, rows, rotation, fields, *rest):
    slabs, edges = rest[:n], rest[n : 2 * n]
    staged, spare, upright = rest[2 * n :]
    size = fields.shape[0]
    me = lax.axis_index("lon")
    quarter = rotation[lax.axis_index("lat"), me]
    blank = jnp.zeros((HALO,) + upright.shape[1:], upright.dtype)
    upright[:HALO] = blank
    upright[HALO + size :] = blank

    def store_row(i, row):
        upright[HALO + i] = row

    turn((4 - quarter) % 4, size, staged, spare, lambda i: fields[i], store_row)
    for d in range(n):
        to = lax.rem(me + d, n)
        slabs[d][...] = upright[pl.ds(to * rows, rows + 2 * HALO)]
    for k in range(n):
        edges[k][...] = upright[pl.ds(jnp.where(me == k, size, HALO), HALO)]


def row_kernel(n, rows, owner, counts, *rest):
    slabs, edges = rest[:n], rest[n : 2 * n]
    w_conv1, b_conv1, w_conv2, b_conv2, w_query, w_kv, w_out = rest[2 * n : 2 * n + 7]
    results = rest[2 * n + 7 : 3 * n + 7]
    taps1, taps2 = rest[3 * n + 7 :]
    band = lax.axis_index("lat")
    me = lax.axis_index("lon")
    bands = owner.shape[0]
    size, chans = slabs[0].shape[1:]
    cols = size * n
    centre = slice(chans, 2 * chans)

    def columns_of(segment):
        return pl.ds(pl.multiple_of(segment * size, size), size)

    for d in range(n):
        source = lax.rem(me + n - d, n)
        taps1[:, columns_of(owner[band, source]), centre] = slabs[d][...]

    @pl.when(me == 0)
    def _():
        north = jnp.maximum(band - 1, 0)
        for k in range(n):
            taps1[:HALO, columns_of(owner[north, k]), centre] = edges[k][...]

    @pl.when(me == n - 1)
    def _():
        south = jnp.minimum(band + 1, bands - 1)
        for k in range(n):
            taps1[rows + HALO :, columns_of(owner[south, (k + 1) % n]), centre] = edges[k][...]

    def spread(taps, r):
        row = taps[r, :, centre].astype(jnp.float32)
        taps[r, :, :chans] = pltpu.roll(row, 1, 0).astype(jnp.bfloat16)
        taps[r, :, 2 * chans :] = pltpu.roll(row, cols - 1, 0).astype(jnp.bfloat16)

    def convolve(taps, weight, bias, count):
        total = bias[...]
        for i in range(3):
            window = taps[i : i + count].reshape(count * cols, 3 * chans)
            total = total + jnp.dot(window, weight[i], preferred_element_type=jnp.float32)
        return total

    def live_count(row):
        inside = (row >= 0) & (row < bands * size)
        return jnp.where(inside, counts[jnp.clip(row, 0, bands * size - 1)], 0)

    cell = lax.broadcasted_iota(jnp.int32, (cols, chans), 0)
    first_row = band * size + me * rows

    for r in range(rows + 2 * HALO):
        spread(taps1, r)
    first = convolve(taps1, w_conv1, b_conv1, rows + 2)
    silu = first / (1.0 + jnp.exp(-first))
    for r in range(rows + 2):
        live = cell < live_count(first_row + r - 1)
        act = jnp.where(live, silu[r * cols : (r + 1) * cols], 0.0)
        taps2[r, :, centre] = act.astype(jnp.bfloat16)
        spread(taps2, r)
    second = convolve(taps2, w_conv2, b_conv2, rows)

    head_dim = 64
    heads = chans // head_dim
    lane_head = lax.broadcasted_iota(jnp.int32, (cols, chans), 1) // head_dim
    key_at = lax.broadcasted_iota(jnp.int32, (cols, heads * cols), 1) % cols

    def per_head(x):
        return jnp.concatenate([jnp.where(lane_head == h, x, jnp.zeros_like(x)) for h in range(heads)], axis=0)

    ones = per_head(jnp.ones((cols, chans), jnp.bfloat16))
    for r in range(rows):
        count = counts[first_row + r]
        live = cell < count
        grid = taps1[r + HALO, :, centre].astype(jnp.float32)
        mixed = jnp.where(live, grid + second[r * cols : (r + 1) * cols], 0.0).astype(jnp.bfloat16)
        flat = mixed.astype(jnp.float32)
        normed = (flat * lax.rsqrt(jnp.mean(flat * flat, axis=1, keepdims=True) + 1e-06)).astype(jnp.bfloat16)
        query = jnp.dot(normed, w_query[...], preferred_element_type=jnp.float32).astype(jnp.bfloat16)
        key_val = jnp.dot(normed, w_kv[...], preferred_element_type=jnp.float32).astype(jnp.bfloat16)
        keys = per_head(key_val[:, :chans])
        values = per_head(key_val[:, chans:])
        scores = lax.dot_general(query, keys, (((1,), (1,)), ((), ())), preferred_element_type=jnp.float32)
        scores = jnp.where(key_at < count, scores * (1.0 / head_dim**0.5), -jnp.inf)
        expo = []
        for h in range(heads):
            part = scores[:, h * cols : (h + 1) * cols]
            expo.append(jnp.exp(part - jnp.max(part, axis=1, keepdims=True)))
        weights = jnp.concatenate(expo, axis=1).astype(jnp.bfloat16)
        summed = jnp.dot(weights, values, preferred_element_type=jnp.float32)
        total = jnp.dot(weights, ones, preferred_element_type=jnp.float32)
        attended = (summed / total).astype(jnp.bfloat16)
        update = jnp.dot(attended, w_out[...], preferred_element_type=jnp.float32)
        taps2[r, :, centre] = (flat + jnp.where(live, update, 0.0)).astype(jnp.bfloat16)
    for d in range(n):
        to = lax.rem(me + d, n)
        results[d][...] = taps2[:rows, columns_of(owner[band, to]), centre]


def store_kernel(n, rows, rotation, *rest):
    slabs = rest[:n]
    out, staged, spare, upright = rest[n:]
    size = out.shape[0]
    me = lax.axis_index("lon")
    quarter = rotation[lax.axis_index("lat"), me]
    for d in range(n):
        source = lax.rem(me + n - d, n)
        upright[pl.ds(source * rows, rows)] = slabs[d][...]

    def store_row(i, row):
        out[i] = row

    turn(quarter % 4, size, staged, spare, lambda i: upright[i], store_row)


def on_device(
    bands,
    n,
    fields,
    w_conv1,
    b_conv1,
    w_conv2,
    b_conv2,
    w_query,
    w_key,
    w_value,
    w_out,
    rotation,
    owner,
    counts,
):
    size, _, chans = fields.shape
    rows = size // n
    cols = size * n
    heads = chans // w_key.shape[1]
    smem = pl.BlockSpec(memory_space=pltpu.SMEM)
    vmem = pl.BlockSpec(memory_space=pltpu.VMEM)
    params = pltpu.CompilerParams(vmem_limit_bytes=VMEM_BYTES)
    bf16 = jnp.bfloat16
    slab = jax.ShapeDtypeStruct((rows + 2 * HALO, size, chans), bf16)
    edge = jax.ShapeDtypeStruct((HALO, size, chans), bf16)
    piece = jax.ShapeDtypeStruct((rows, size, chans), bf16)
    staging = [pltpu.VMEM((chans // LANES, size * size, LANES), jnp.float32)] * 2

    sent = pl.pallas_call(
        functools.partial(send_kernel, n, rows),
        out_shape=[slab] * n + [edge] * n,
        in_specs=[smem, vmem],
        out_specs=[vmem] * (2 * n),
        scratch_shapes=staging + [pltpu.VMEM((size + 2 * HALO, size, chans), bf16)],
        compiler_params=params,
        name="send",
    )(rotation, fields)

    def around(x, d):
        return lax.ppermute(x, "lon", [(i, (i + d) % n) for i in range(n)])

    slabs = [sent[0]] + [around(sent[d], d) for d in range(1, n)]
    edges = []
    for k in range(n):
        pairs = [(a * n + k, (a + 1) * n) for a in range(bands - 1)]
        pairs += [(a * n + (k + 1) % n, a * n - 1) for a in range(1, bands)]
        edges.append(lax.ppermute(sent[n + k], ("lat", "lon"), pairs))

    w_kv = jnp.concatenate([w_key] * heads + [w_value] * heads, axis=1)
    results = pl.pallas_call(
        functools.partial(row_kernel, n, rows),
        out_shape=[piece] * n,
        in_specs=[smem] * 2 + [vmem] * (2 * n + 7),
        out_specs=[vmem] * n,
        scratch_shapes=[
            pltpu.VMEM((rows + 2 * HALO, cols, 3 * chans), bf16),
            pltpu.VMEM((rows + 2, cols, 3 * chans), bf16),
        ],
        compiler_params=params,
        name="rows",
    )(
        owner,
        counts,
        *slabs,
        *edges,
        w_conv1.reshape(3, 3 * chans, chans),
        b_conv1.reshape(1, chans),
        w_conv2.reshape(3, 3 * chans, chans),
        b_conv2.reshape(1, chans),
        w_query,
        w_kv,
        w_out,
    )
    back = [results[0]] + [around(results[d], d) for d in range(1, n)]
    return pl.pallas_call(
        functools.partial(store_kernel, n, rows),
        out_shape=jax.ShapeDtypeStruct(fields.shape, bf16),
        in_specs=[smem] + [vmem] * n,
        out_specs=vmem,
        scratch_shapes=staging + [pltpu.VMEM((size, size, chans), bf16)],
        compiler_params=params,
        name="store",
    )(rotation, *back)


def solution(mesh):
    in_specs = (P("lat", "lon", None), P(), P(), P(), P(), P(), P(), P(), P(), P(), P(), P())
    out_specs = P("lat", "lon", None)
    body = functools.partial(on_device, mesh.shape["lat"], mesh.shape["lon"])
    return jax.shard_map(body, mesh=mesh, in_specs=in_specs, out_specs=out_specs, check_vma=False)
```

```python
import functools

import jax
import jax.numpy as jnp
from jax import lax
from jax.experimental import pallas as pl
from jax.experimental.pallas import tpu as pltpu
from jax.sharding import PartitionSpec as P

HALO = 2
LANES = 128
GROUP = 256
VMEM_BYTES = 28 * 1024 * 1024


def group_of(band, shard, n):
    return jnp.where(band % 2 == 0, shard, n - 1 - shard)


def shard_of(band, group, n):
    return group if band % 2 == 0 else n - 1 - group


def first_held(group, rows):
    return group * rows - HALO * (group % 2)


def turn(quarter, staged, block, out):
    size, _, chans = out.shape
    tiles = staged.shape[0]

    def column(col):
        parts = [staged[t, pl.ds(col, size, stride=size), :] for t in range(tiles)]
        return jnp.concatenate(parts, axis=1).astype(jnp.bfloat16)

    def keep(i, row):
        for t in range(tiles):
            staged[t, pl.ds(i * size, size), :] = row[:, t * LANES : (t + 1) * LANES]

    @pl.when(quarter == 0)
    def _():
        out[...] = block[...]

    @pl.when(quarter == 1)
    def _():
        for i in range(size):
            keep(i, block[i].astype(jnp.float32))
        for i in range(size):
            out[i] = column(size - 1 - i)

    @pl.when(quarter == 2)
    def _():
        depth = GROUP // size
        i = lax.broadcasted_iota(jnp.int32, (GROUP, GROUP), 0)
        j = lax.broadcasted_iota(jnp.int32, (GROUP, GROUP), 1)
        backwards = jnp.where(i + j == GROUP - 1, 1.0, 0.0).astype(jnp.bfloat16)
        for g in range(size // depth):
            cells = block[size - (g + 1) * depth : size - g * depth].reshape(GROUP, chans)
            turned = jnp.dot(backwards, cells, preferred_element_type=jnp.float32).astype(jnp.bfloat16)
            out[g * depth : (g + 1) * depth] = turned.reshape(depth, size, chans)

    @pl.when(quarter == 3)
    def _():
        for i in range(size):
            keep(size - 1 - i, block[i].astype(jnp.float32))
        for i in range(size):
            out[i] = column(i)


def send_kernel(n, rows, rotation, fields, *rest):
    slabs = rest[:n]
    staged, upright = rest[n:]
    band = lax.axis_index("lat")
    me = lax.axis_index("lon")
    turn((4 - rotation[me, band]) % 4, staged, fields, upright)
    for d in range(n):
        group = group_of(band, lax.rem(me + d, n), n)
        slabs[d][...] = upright[pl.ds(first_held(group, rows), rows + HALO)]


def columns_of(segment, size):
    return pl.ds(pl.multiple_of(segment * size, size), size)


def gather_kernel(n, rows, owner, *rest):
    slabs = rest[:n]
    grid, edge = rest[n:]
    band = lax.axis_index("lat")
    me = lax.axis_index("lon")
    group = group_of(band, me, n)
    size = slabs[0].shape[1]
    for d in range(n):
        source = lax.rem(me + n - d, n)
        grid[:, columns_of(owner[source, band], size)] = slabs[d][...]
    edge[...] = grid[pl.ds(rows * (group % 2), HALO)]


def spread(taps, r, row):
    cols, chans = row.shape
    taps[r, :, :chans] = pltpu.roll(row, 1, 0).astype(jnp.bfloat16)
    taps[r, :, chans : 2 * chans] = row.astype(jnp.bfloat16)
    taps[r, :, 2 * chans :] = pltpu.roll(row, cols - 1, 0).astype(jnp.bfloat16)


def convolve(taps, weight, bias, count):
    cols, width = taps.shape[1:]
    total = bias[...]
    for i in range(3):
        window = taps[i : i + count].reshape(count * cols, width)
        total = total + jnp.dot(window, weight[i], preferred_element_type=jnp.float32)
    return total


def silu(x):
    return x / (1.0 + jnp.exp(-x))


def live_count(counts, row):
    inside = (row >= 0) & (row < counts.shape[0])
    return jnp.where(inside, counts[jnp.clip(row, 0, counts.shape[0] - 1)], 0)


def first_kernel(n, rows, size, counts, grid, weight, bias, acts, taps):
    band = lax.axis_index("lat")
    group = group_of(band, lax.axis_index("lon"), n)
    cols, chans = grid.shape[1:]
    cell = lax.broadcasted_iota(jnp.int32, (cols, chans), 0)
    top = band * size + first_held(group, rows) + 1
    for r in range(rows + HALO):
        spread(taps, r, grid[r].astype(jnp.float32))
    act = silu(convolve(taps, weight, bias, rows))
    for r in range(rows):
        live = cell < live_count(counts, top + r)
        spread(acts, r, jnp.where(live, act[r * cols : (r + 1) * cols], 0.0))


def rows_kernel(n, rows, size, owner, counts, *rest):
    grid, acts, sent, received = rest[:4]
    w_conv1, b_conv1, w_conv2, b_conv2, w_qv, w_key, w_out = rest[4:11]
    results = rest[11 : n + 11]
    taps1, taps2, mixed, attended = rest[n + 11 :]
    band = lax.axis_index("lat")
    me = lax.axis_index("lon")
    group = group_of(band, me, n)
    odd = group % 2
    cols, chans = grid.shape[1:]
    head_dim = w_key.shape[0]
    heads = chans // head_dim
    cell = lax.broadcasted_iota(jnp.int32, (cols, chans), 0)
    first_row = band * size + group * rows

    for r in range(HALO):
        spread(taps1, r + HALO * (1 - odd), sent[r].astype(jnp.float32))
        spread(taps1, r + HALO * odd, received[r].astype(jnp.float32))
    taps2[pl.ds(HALO * (1 - odd), rows)] = acts[...]
    act = silu(convolve(taps1, w_conv1, b_conv1, HALO))
    for r in range(HALO):
        at = r + rows * odd
        live = cell < live_count(counts, first_row + at - 1)
        spread(taps2, at, jnp.where(live, act[r * cols : (r + 1) * cols], 0.0))
    second = convolve(taps2, w_conv2, b_conv2, rows)

    for r in range(rows):
        live = cell < counts[first_row + r]
        here = grid[r + HALO * odd].astype(jnp.float32)
        part = jnp.where(live, here + second[r * cols : (r + 1) * cols], 0.0)
        mixed[r * cols : (r + 1) * cols, :] = part.astype(jnp.bfloat16)
    flat = mixed[...].astype(jnp.float32)
    normed = (flat * lax.rsqrt(jnp.mean(flat * flat, axis=1, keepdims=True) + 1e-06)).astype(jnp.bfloat16)

    def by_last(a, b):
        return lax.dot_general(a, b, (((1,), (1,)), ((), ())), preferred_element_type=jnp.float32)

    keys = by_last(normed, w_key[...]).astype(jnp.bfloat16)
    flipped = by_last(w_qv[...], normed).astype(jnp.bfloat16)
    key_at = lax.broadcasted_iota(jnp.int32, (cols, heads * cols), 0)
    scale = 1.0 / head_dim**0.5
    for r in range(rows):
        at = slice(r * cols, (r + 1) * cols)
        queries = jnp.concatenate([flipped[h * head_dim : (h + 1) * head_dim, at] for h in range(heads)], axis=1)
        scores = jnp.dot(keys[at], queries, preferred_element_type=jnp.float32)
        scores = jnp.where(key_at < counts[first_row + r], scores * scale, -jnp.inf)
        expo = jnp.exp(scores - jnp.max(scores, axis=0, keepdims=True))
        total = jnp.sum(expo, axis=0, keepdims=True)
        summed = jnp.dot(flipped[chans:, at], expo.astype(jnp.bfloat16), preferred_element_type=jnp.float32)
        share = (summed / total).astype(jnp.bfloat16)
        for h in range(heads):
            attended[h * head_dim : (h + 1) * head_dim, at] = share[:, h * cols : (h + 1) * cols]
    update = lax.dot_general(attended[...], w_out[...], (((0,), (0,)), ((), ())), preferred_element_type=jnp.float32)
    for r in range(rows):
        at = slice(r * cols, (r + 1) * cols)
        live = cell < counts[first_row + r]
        mixed[at, :] = (mixed[at, :].astype(jnp.float32) + jnp.where(live, update[at], 0.0)).astype(jnp.bfloat16)
    for d in range(n):
        segment = owner[lax.rem(me + d, n), band]
        for r in range(rows):
            results[d][r] = mixed[columns_of(segment + r * n, size), :]


def store_kernel(n, rows, rotation, *rest):
    slabs = rest[:n]
    out, staged, upright = rest[n:]
    band = lax.axis_index("lat")
    me = lax.axis_index("lon")
    for d in range(n):
        group = group_of(band, lax.rem(me + n - d, n), n)
        upright[pl.ds(group * rows, rows)] = slabs[d][...]
    turn(rotation[me, band] % 4, staged, upright, out)


def on_device(
    bands,
    n,
    fields,
    w_conv1,
    b_conv1,
    w_conv2,
    b_conv2,
    w_query,
    w_key,
    w_value,
    w_out,
    rotation,
    owner,
    counts,
):
    size, _, chans = fields.shape
    rows = size // n
    cols = size * n
    bf16 = jnp.bfloat16
    smem = pl.BlockSpec(memory_space=pltpu.SMEM)
    vmem = pl.BlockSpec(memory_space=pltpu.VMEM)
    params = pltpu.CompilerParams(vmem_limit_bytes=VMEM_BYTES)
    staging = pltpu.VMEM((chans // LANES, size * size, LANES), jnp.float32)
    block = pltpu.VMEM((size, size, chans), bf16)

    def call(kernel, name, out, scalars, arrays, scratch):
        many = isinstance(out, list)
        return pl.pallas_call(
            functools.partial(kernel, n, rows),
            out_shape=out,
            in_specs=[smem] * len(scalars) + [vmem] * len(arrays),
            out_specs=[vmem] * len(out) if many else vmem,
            scratch_shapes=scratch,
            compiler_params=params,
            name=name,
        )(*scalars, *arrays)

    def array(*shape):
        return jax.ShapeDtypeStruct(shape, bf16)

    def around(parts):
        pairs = [[(i, (i + d) % n) for i in range(n)] for d in range(n)]
        return [parts[0]] + [lax.ppermute(parts[d], "lon", pairs[d]) for d in range(1, n)]

    rotation, owner = rotation.T, owner.T
    w_first = w_conv1.reshape(3, 3 * chans, chans)
    w_second = w_conv2.reshape(3, 3 * chans, chans)
    b_first = b_conv1.reshape(1, chans)
    b_second = b_conv2.reshape(1, chans)
    w_qv = jnp.concatenate([w_query.T, w_value.T], axis=0)

    slabs = [array(rows + HALO, size, chans)] * n
    slabs = around(call(send_kernel, "send", slabs, [rotation], [fields], [staging, block]))
    held = [array(rows + HALO, cols, chans), array(HALO, cols, chans)]
    grid, sent = call(gather_kernel, "gather", held, [owner], slabs, [])
    snake = [a * n + shard_of(a, g, n) for a in range(bands) for g in range(n)]
    pairs = [(snake[i], snake[i + 1 if i % 2 else i - 1]) for i in range(1, bands * n - 1)]
    received = lax.ppermute(sent, ("lat", "lon"), pairs)
    acts = call(
        lambda n, rows, *refs: first_kernel(n, rows, size, *refs),
        "first",
        array(rows, cols, 3 * chans),
        [counts],
        [grid, w_first, b_first],
        [pltpu.VMEM((rows + HALO, cols, 3 * chans), bf16)],
    )
    results = call(
        lambda n, rows, *refs: rows_kernel(n, rows, size, *refs),
        "rows",
        [array(rows, size, chans)] * n,
        [owner, counts],
        [grid, acts, sent, received, w_first, b_first, w_second, b_second, w_qv, w_key.T, w_out],
        [
            pltpu.VMEM((2 * HALO, cols, 3 * chans), bf16),
            pltpu.VMEM((rows + HALO, cols, 3 * chans), bf16),
            pltpu.VMEM((rows * cols, chans), bf16),
            pltpu.VMEM((chans, rows * cols), bf16),
        ],
    )
    results = around(results)
    return call(store_kernel, "store", array(*fields.shape), [rotation], results, [staging, block])


def solution(mesh):
    in_specs = (P("lat", "lon", None), P(), P(), P(), P(), P(), P(), P(), P(), P(), P(), P())
    out_specs = P("lat", "lon", None)
    body = functools.partial(on_device, mesh.shape["lat"], mesh.shape["lon"])
    return jax.shard_map(body, mesh=mesh, in_specs=in_specs, out_specs=out_specs, check_vma=False)
```

```python
import functools

import jax
import jax.numpy as jnp
from jax import lax
from jax.experimental import pallas as pl
from jax.experimental.pallas import tpu as pltpu
from jax.sharding import PartitionSpec as P

HALO = 2
LANES = 128
GROUP = 256
VMEM_BYTES = 28 * 1024 * 1024


def group_of(band, shard, n):
    return jnp.where(band % 2 == 0, shard, n - 1 - shard)


def shard_of(band, group, n):
    return group if band % 2 == 0 else n - 1 - group


def first_held(group, rows):
    return group * rows - HALO * (group % 2)


def turn(quarter, staged, block, out):
    size, _, chans = out.shape
    tiles = staged.shape[0]

    def column(col):
        parts = [staged[t, pl.ds(col, size, stride=size), :] for t in range(tiles)]
        return jnp.concatenate(parts, axis=1).astype(jnp.bfloat16)

    def keep(i, row):
        for t in range(tiles):
            staged[t, pl.ds(i * size, size), :] = row[:, t * LANES : (t + 1) * LANES]

    @pl.when(quarter == 0)
    def _():
        out[...] = block[...]

    @pl.when(quarter == 1)
    def _():
        for i in range(size):
            keep(i, block[i].astype(jnp.float32))
        for i in range(size):
            out[i] = column(size - 1 - i)

    @pl.when(quarter == 2)
    def _():
        depth = GROUP // size
        i = lax.broadcasted_iota(jnp.int32, (GROUP, GROUP), 0)
        j = lax.broadcasted_iota(jnp.int32, (GROUP, GROUP), 1)
        backwards = jnp.where(i + j == GROUP - 1, 1.0, 0.0).astype(jnp.bfloat16)
        for g in range(size // depth):
            cells = block[size - (g + 1) * depth : size - g * depth].reshape(GROUP, chans)
            turned = jnp.dot(backwards, cells, preferred_element_type=jnp.float32).astype(jnp.bfloat16)
            out[g * depth : (g + 1) * depth] = turned.reshape(depth, size, chans)

    @pl.when(quarter == 3)
    def _():
        for i in range(size):
            keep(size - 1 - i, block[i].astype(jnp.float32))
        for i in range(size):
            out[i] = column(i)


def send_kernel(n, rows, rotation, fields, *rest):
    slabs, staged, upright = rest
    band = lax.axis_index("lat")
    me = lax.axis_index("lon")
    turn((4 - rotation[me, band]) % 4, staged, fields, upright)
    for s in range(n):
        group = group_of(band, s, n)
        slabs[s] = upright[pl.ds(first_held(group, rows), rows + HALO)]


def columns_of(segment, size):
    return pl.ds(pl.multiple_of(segment * size, size), size)


def gather_kernel(n, rows, owner, *rest):
    slabs, grid, edge = rest
    band = lax.axis_index("lat")
    me = lax.axis_index("lon")
    group = group_of(band, me, n)
    size = slabs.shape[2]
    for s in range(n):
        grid[:, columns_of(owner[s, band], size)] = slabs[s]
    edge[...] = grid[pl.ds(rows * (group % 2), HALO)]


def spread(taps, r, row):
    cols, chans = row.shape
    taps[r, :, :chans] = pltpu.roll(row, 1, 0).astype(jnp.bfloat16)
    taps[r, :, chans : 2 * chans] = row.astype(jnp.bfloat16)
    taps[r, :, 2 * chans :] = pltpu.roll(row, cols - 1, 0).astype(jnp.bfloat16)


def convolve(taps, weight, bias, count):
    cols, width = taps.shape[1:]
    total = bias[...]
    for i in range(3):
        window = taps[i : i + count].reshape(count * cols, width)
        total = total + jnp.dot(window, weight[i], preferred_element_type=jnp.float32)
    return total


def silu(x):
    return x / (1.0 + jnp.exp(-x))


def live_count(counts, row):
    inside = (row >= 0) & (row < counts.shape[0])
    return jnp.where(inside, counts[jnp.clip(row, 0, counts.shape[0] - 1)], 0)


def first_kernel(n, rows, size, counts, grid, weight, bias, acts, taps):
    band = lax.axis_index("lat")
    group = group_of(band, lax.axis_index("lon"), n)
    cols, chans = grid.shape[1:]
    cell = lax.broadcasted_iota(jnp.int32, (cols, chans), 0)
    top = band * size + first_held(group, rows) + 1
    for r in range(rows + HALO):
        spread(taps, r, grid[r].astype(jnp.float32))
    act = silu(convolve(taps, weight, bias, rows))
    for r in range(rows):
        live = cell < live_count(counts, top + r)
        spread(acts, r, jnp.where(live, act[r * cols : (r + 1) * cols], 0.0))


def rows_kernel(n, rows, size, owner, counts, *rest):
    grid, acts, sent, received = rest[:4]
    w_conv1, b_conv1, w_conv2, b_conv2, w_qv, w_key, w_out = rest[4:11]
    results, taps1, taps2, mixed, attended = rest[11:]
    band = lax.axis_index("lat")
    me = lax.axis_index("lon")
    group = group_of(band, me, n)
    odd = group % 2
    cols, chans = grid.shape[1:]
    head_dim = w_key.shape[0]
    heads = chans // head_dim
    cell = lax.broadcasted_iota(jnp.int32, (cols, chans), 0)
    first_row = band * size + group * rows

    for r in range(HALO):
        spread(taps1, r + HALO * (1 - odd), sent[r].astype(jnp.float32))
        spread(taps1, r + HALO * odd, received[r].astype(jnp.float32))
    taps2[pl.ds(HALO * (1 - odd), rows)] = acts[...]
    act = silu(convolve(taps1, w_conv1, b_conv1, HALO))
    for r in range(HALO):
        at = r + rows * odd
        live = cell < live_count(counts, first_row + at - 1)
        spread(taps2, at, jnp.where(live, act[r * cols : (r + 1) * cols], 0.0))
    second = convolve(taps2, w_conv2, b_conv2, rows)

    for r in range(rows):
        live = cell < counts[first_row + r]
        here = grid[r + HALO * odd].astype(jnp.float32)
        part = jnp.where(live, here + second[r * cols : (r + 1) * cols], 0.0)
        mixed[r * cols : (r + 1) * cols, :] = part.astype(jnp.bfloat16)
    flat = mixed[...].astype(jnp.float32)
    normed = (flat * lax.rsqrt(jnp.mean(flat * flat, axis=1, keepdims=True) + 1e-06)).astype(jnp.bfloat16)

    def by_last(a, b):
        return lax.dot_general(a, b, (((1,), (1,)), ((), ())), preferred_element_type=jnp.float32)

    keys = by_last(normed, w_key[...]).astype(jnp.bfloat16)
    flipped = by_last(w_qv[...], normed).astype(jnp.bfloat16)
    key_at = lax.broadcasted_iota(jnp.int32, (cols, heads * cols), 0)
    scale = 1.0 / head_dim**0.5
    for r in range(rows):
        at = slice(r * cols, (r + 1) * cols)
        queries = jnp.concatenate([flipped[h * head_dim : (h + 1) * head_dim, at] for h in range(heads)], axis=1)
        scores = jnp.dot(keys[at], queries, preferred_element_type=jnp.float32)
        scores = jnp.where(key_at < counts[first_row + r], scores * scale, -jnp.inf)
        expo = jnp.exp(scores - jnp.max(scores, axis=0, keepdims=True))
        total = jnp.sum(expo, axis=0, keepdims=True)
        summed = jnp.dot(flipped[chans:, at], expo.astype(jnp.bfloat16), preferred_element_type=jnp.float32)
        share = (summed / total).astype(jnp.bfloat16)
        for h in range(heads):
            attended[h * head_dim : (h + 1) * head_dim, at] = share[:, h * cols : (h + 1) * cols]
    update = lax.dot_general(attended[...], w_out[...], (((0,), (0,)), ((), ())), preferred_element_type=jnp.float32)
    for r in range(rows):
        at = slice(r * cols, (r + 1) * cols)
        live = cell < counts[first_row + r]
        mixed[at, :] = (mixed[at, :].astype(jnp.float32) + jnp.where(live, update[at], 0.0)).astype(jnp.bfloat16)
    for s in range(n):
        segment = owner[s, band]
        for r in range(rows):
            results[s, r] = mixed[columns_of(segment + r * n, size), :]


def store_kernel(n, rows, rotation, *rest):
    slabs, out, staged, upright = rest
    band = lax.axis_index("lat")
    me = lax.axis_index("lon")
    for s in range(n):
        group = group_of(band, s, n)
        upright[pl.ds(group * rows, rows)] = slabs[s]
    turn(rotation[me, band] % 4, staged, upright, out)


def on_device(
    bands,
    n,
    fields,
    w_conv1,
    b_conv1,
    w_conv2,
    b_conv2,
    w_query,
    w_key,
    w_value,
    w_out,
    rotation,
    owner,
    counts,
):
    size, _, chans = fields.shape
    rows = size // n
    cols = size * n
    bf16 = jnp.bfloat16
    smem = pl.BlockSpec(memory_space=pltpu.SMEM)
    vmem = pl.BlockSpec(memory_space=pltpu.VMEM)
    params = pltpu.CompilerParams(vmem_limit_bytes=VMEM_BYTES)
    staging = pltpu.VMEM((chans // LANES, size * size, LANES), jnp.float32)
    block = pltpu.VMEM((size, size, chans), bf16)

    def call(kernel, name, out, scalars, arrays, scratch):
        many = isinstance(out, list)
        return pl.pallas_call(
            functools.partial(kernel, n, rows),
            out_shape=out,
            in_specs=[smem] * len(scalars) + [vmem] * len(arrays),
            out_specs=[vmem] * len(out) if many else vmem,
            scratch_shapes=scratch,
            compiler_params=params,
            name=name,
        )(*scalars, *arrays)

    def array(*shape):
        return jax.ShapeDtypeStruct(shape, bf16)

    def around(parts):
        return lax.all_to_all(parts, "lon", 0, 0)

    rotation, owner = rotation.T, owner.T
    w_first = w_conv1.reshape(3, 3 * chans, chans)
    w_second = w_conv2.reshape(3, 3 * chans, chans)
    b_first = b_conv1.reshape(1, chans)
    b_second = b_conv2.reshape(1, chans)
    w_qv = jnp.concatenate([w_query.T, w_value.T], axis=0)

    slabs = array(n, rows + HALO, size, chans)
    slabs = around(call(send_kernel, "send", slabs, [rotation], [fields], [staging, block]))
    held = [array(rows + HALO, cols, chans), array(HALO, cols, chans)]
    grid, sent = call(gather_kernel, "gather", held, [owner], [slabs], [])
    snake = [a * n + shard_of(a, g, n) for a in range(bands) for g in range(n)]
    pairs = [(snake[i], snake[i + 1 if i % 2 else i - 1]) for i in range(1, bands * n - 1)]
    received = lax.ppermute(sent, ("lat", "lon"), pairs)
    acts = call(
        lambda n, rows, *refs: first_kernel(n, rows, size, *refs),
        "first",
        array(rows, cols, 3 * chans),
        [counts],
        [grid, w_first, b_first],
        [pltpu.VMEM((rows + HALO, cols, 3 * chans), bf16)],
    )
    results = call(
        lambda n, rows, *refs: rows_kernel(n, rows, size, *refs),
        "rows",
        array(n, rows, size, chans),
        [owner, counts],
        [grid, acts, sent, received, w_first, b_first, w_second, b_second, w_qv, w_key.T, w_out],
        [
            pltpu.VMEM((2 * HALO, cols, 3 * chans), bf16),
            pltpu.VMEM((rows + HALO, cols, 3 * chans), bf16),
            pltpu.VMEM((rows * cols, chans), bf16),
            pltpu.VMEM((chans, rows * cols), bf16),
        ],
    )
    results = around(results)
    return call(store_kernel, "store", array(*fields.shape), [rotation], [results], [staging, block])


def solution(mesh):
    in_specs = (P("lat", "lon", None), P(), P(), P(), P(), P(), P(), P(), P(), P(), P(), P())
    out_specs = P("lat", "lon", None)
    body = functools.partial(on_device, mesh.shape["lat"], mesh.shape["lon"])
    return jax.shard_map(body, mesh=mesh, in_specs=in_specs, out_specs=out_specs, check_vma=False)
```

```python
import functools
import math

import jax
import jax.numpy as jnp
from jax import lax
from jax.experimental import pallas as pl
from jax.experimental.pallas import tpu as pltpu
from jax.sharding import PartitionSpec as P

HALO = 2
LANES = 128
GROUP = 256
VMEM_BYTES = 28 * 1024 * 1024


def group_of(band, shard, n):
    return jnp.where(band % 2 == 0, shard, n - 1 - shard)


def shard_of(band, group, n):
    return group if band % 2 == 0 else n - 1 - group


def first_held(group, rows):
    return group * rows - HALO * (group % 2)


def turn(quarter, staged, block, out, ready, done):
    size, _, chans = block.shape
    tiles = staged.shape[0]
    depth = GROUP // size
    pieces = size // depth

    def column(col):
        parts = [staged[t, pl.ds(col, size, stride=size), :] for t in range(tiles)]
        return jnp.concatenate(parts, axis=1).astype(jnp.bfloat16)

    def keep(i, row):
        for t in range(tiles):
            staged[t, pl.ds(i * size, size), :] = row[:, t * LANES : (t + 1) * LANES]

    @pl.when(quarter == 0)
    def _():
        for g in range(pieces):
            ready(g)
            out[g * depth : (g + 1) * depth] = block[g * depth : (g + 1) * depth]
            done(g)

    @pl.when(quarter == 1)
    def _():
        for i in range(size):
            if i % depth == 0:
                ready(i // depth)
            keep(i, block[i].astype(jnp.float32))
        for i in range(size):
            out[i] = column(size - 1 - i)
            if i % depth == depth - 1:
                done(i // depth)

    @pl.when(quarter == 2)
    def _():
        i = lax.broadcasted_iota(jnp.int32, (GROUP, GROUP), 0)
        j = lax.broadcasted_iota(jnp.int32, (GROUP, GROUP), 1)
        backwards = jnp.where(i + j == GROUP - 1, 1.0, 0.0).astype(jnp.bfloat16)
        for g in reversed(range(pieces)):
            ready(pieces - 1 - g)
            cells = block[size - (g + 1) * depth : size - g * depth].reshape(GROUP, chans)
            turned = jnp.dot(backwards, cells, preferred_element_type=jnp.float32).astype(jnp.bfloat16)
            out[g * depth : (g + 1) * depth] = turned.reshape(depth, size, chans)
            done(g)

    @pl.when(quarter == 3)
    def _():
        for i in range(size):
            if i % depth == 0:
                ready(i // depth)
            keep(size - 1 - i, block[i].astype(jnp.float32))
        for i in range(size):
            out[i] = column(i)
            if i % depth == depth - 1:
                done(i // depth)


def send_kernel(n, rows, rotation_in, fields, *rest):
    slabs = rest[:n]
    staged, block, upright, rotation, scalar_sem, sems = rest[n:]
    band = lax.axis_index("lat")
    me = lax.axis_index("lon")
    depth = GROUP // fields.shape[0]

    def piece(g):
        at = pl.ds(g * depth, depth)
        return pltpu.make_async_copy(fields.at[at], block.at[at], sems.at[g])

    scalars = pltpu.make_async_copy(rotation_in, rotation, scalar_sem)
    scalars.start()
    for g in range(fields.shape[0] // depth):
        piece(g).start()
    scalars.wait()
    turn((4 - rotation[me, band]) % 4, staged, block, upright, lambda g: piece(g).wait(), lambda g: None)
    for d in range(n):
        group = group_of(band, lax.rem(me + d, n), n)
        slabs[d][...] = upright[pl.ds(first_held(group, rows), rows + HALO)]


def load_kernel(n, rows, after, *refs):
    del after
    count = len(refs) // 2
    copies = [pltpu.make_async_copy(refs[i], refs[count + i], refs[-1].at[i]) for i in range(count)]
    for copy in copies:
        copy.start()
    for copy in copies:
        copy.wait()


def columns_of(segment, size):
    return pl.ds(pl.multiple_of(segment * size, size), size)


def gather_kernel(n, rows, owner, *rest):
    slabs = rest[:n]
    grid, edge = rest[n:]
    band = lax.axis_index("lat")
    me = lax.axis_index("lon")
    group = group_of(band, me, n)
    size = slabs[0].shape[1]
    for d in range(n):
        source = lax.rem(me + n - d, n)
        grid[:, columns_of(owner[source, band], size)] = slabs[d][...]
    edge[...] = grid[pl.ds(rows * (group % 2), HALO)]


def spread(taps, r, row):
    cols, chans = row.shape
    taps[r, :, :chans] = pltpu.roll(row, 1, 0).astype(jnp.bfloat16)
    taps[r, :, chans : 2 * chans] = row.astype(jnp.bfloat16)
    taps[r, :, 2 * chans :] = pltpu.roll(row, cols - 1, 0).astype(jnp.bfloat16)


def convolve(taps, weight, bias, count):
    cols, width = taps.shape[1:]
    total = bias[...]
    for i in range(3):
        window = taps[i : i + count].reshape(count * cols, width)
        total = total + jnp.dot(window, weight[i], preferred_element_type=jnp.float32)
    return total


def silu(x):
    return x / (1.0 + jnp.exp(-x))


def live_count(counts, row):
    inside = (row >= 0) & (row < counts.shape[0])
    return jnp.where(inside, counts[jnp.clip(row, 0, counts.shape[0] - 1)], 0)


def finish(n, count, first_row, grid_row, second, counts, owner, w_query, w_key, w_value, w_out, results, mixed, attended):
    band = lax.axis_index("lat")
    me = lax.axis_index("lon")
    chans = mixed.shape[1]
    cols = mixed.shape[0] // count
    head_dim = w_key.shape[0]
    heads = chans // head_dim
    cell = lax.broadcasted_iota(jnp.int32, (cols, chans), 0)
    for r in range(count):
        live = cell < counts[first_row + r]
        part = jnp.where(live, grid_row(r).astype(jnp.float32) + second[r * cols : (r + 1) * cols], 0.0)
        mixed[r * cols : (r + 1) * cols, :] = part.astype(jnp.bfloat16)
    flat = mixed[...].astype(jnp.float32)
    normed = (flat * lax.rsqrt(jnp.mean(flat * flat, axis=1, keepdims=True) + 1e-06)).astype(jnp.bfloat16)

    def by_last(a, b):
        return lax.dot_general(a, b, (((1,), (1,)), ((), ())), preferred_element_type=jnp.float32)

    keys = by_last(normed, w_key[...]).astype(jnp.bfloat16)
    query = by_last(w_query[...].T, normed).astype(jnp.bfloat16)
    value = by_last(w_value[...], normed).astype(jnp.bfloat16)
    key_at = lax.broadcasted_iota(jnp.int32, (cols, cols), 0)
    scale = math.log2(math.e) / head_dim**0.5
    for r in range(count):
        at = slice(r * cols, (r + 1) * cols)
        queries = jnp.concatenate([query[h * head_dim : (h + 1) * head_dim, at] for h in range(heads)], axis=1)
        scores = jnp.dot(keys[at], queries, preferred_element_type=jnp.float32)
        live = key_at < counts[first_row + r]
        expo = []
        totals = []
        for h in range(heads):
            part = jnp.where(live, scores[:, h * cols : (h + 1) * cols], -jnp.inf)
            part = jnp.exp2((part - jnp.max(part, axis=0, keepdims=True)) * scale)
            totals.append(jnp.sum(part, axis=0, keepdims=True))
            expo.append(part.astype(jnp.bfloat16))
        summed = jnp.dot(value[:, at], jnp.concatenate(expo, axis=1), preferred_element_type=jnp.float32)
        for h in range(heads):
            share = summed[:, h * cols : (h + 1) * cols] / totals[h]
            attended[h * head_dim : (h + 1) * head_dim, at] = share.astype(jnp.bfloat16)
    update = lax.dot_general(attended[...], w_out[...], (((0,), (0,)), ((), ())), preferred_element_type=jnp.float32)
    for r in range(count):
        at = slice(r * cols, (r + 1) * cols)
        live = cell < counts[first_row + r]
        mixed[at, :] = (mixed[at, :].astype(jnp.float32) + jnp.where(live, update[at], 0.0)).astype(jnp.bfloat16)
    for d in range(n):
        segment = owner[lax.rem(me + d, n), band]
        for r in range(count):
            results[d][r] = mixed[columns_of(segment + r * n, results[d].shape[1]), :]


def inner_kernel(n, rows, owner, counts, *rest):
    grid, w_conv1, b_conv1, w_conv2, b_conv2 = rest[:5]
    weights = rest[5:9]
    inner = rows - HALO
    edge_acts, results = rest[9], rest[10 : 10 + (n if inner else 0)]
    taps, acts, mixed, attended = rest[10 + len(results) :]
    band = lax.axis_index("lat")
    group = group_of(band, lax.axis_index("lon"), n)
    cols, chans = grid.shape[1:]
    cell = lax.broadcasted_iota(jnp.int32, (cols, chans), 0)
    top = band * (rows * n) + first_held(group, rows)
    for r in range(rows + HALO):
        spread(taps, r, grid[r].astype(jnp.float32))
    act = silu(convolve(taps, w_conv1, b_conv1, rows))
    for r in range(rows):
        live = cell < live_count(counts, top + 1 + r)
        spread(acts, r, jnp.where(live, act[r * cols : (r + 1) * cols], 0.0))
    edge_acts[...] = acts[pl.ds(inner * (group % 2), HALO)]
    if inner:
        second = convolve(acts, w_conv2, b_conv2, inner)
        finish(
            n, inner, top + 2, lambda r: grid[r + 2], second, counts, owner, *weights, results, mixed, attended
        )


def edge_kernel(n, rows, owner, counts, *rest):
    sent, received, edge_acts, w_conv1, b_conv1, w_conv2, b_conv2 = rest[:7]
    weights, results = rest[7:11], rest[11 : 11 + n]
    taps, acts, mixed, attended = rest[11 + n :]
    band = lax.axis_index("lat")
    group = group_of(band, lax.axis_index("lon"), n)
    odd = group % 2
    cols, chans = sent.shape[1:]
    cell = lax.broadcasted_iota(jnp.int32, (cols, chans), 0)
    first_row = band * (rows * n) + group * rows + (rows - HALO) * odd
    near, far = HALO * (1 - odd), HALO * odd
    for r in range(HALO):
        spread(taps, near + r, sent[r].astype(jnp.float32))
        spread(taps, far + r, received[r].astype(jnp.float32))
    act = silu(convolve(taps, w_conv1, b_conv1, HALO))
    acts[pl.ds(near, HALO)] = edge_acts[...]
    for r in range(HALO):
        live = cell < live_count(counts, first_row - 1 + far + r)
        spread(acts, far + r, jnp.where(live, act[r * cols : (r + 1) * cols], 0.0))
    second = convolve(acts, w_conv2, b_conv2, HALO)
    finish(n, HALO, first_row, lambda r: sent[r], second, counts, owner, *weights, results, mixed, attended)


def store_kernel(n, rows, rotation, *rest):
    inner = rows - HALO
    slabs = rest[: n if inner else 0]
    edges = rest[len(slabs) : len(slabs) + n]
    out, staged, upright, turned, sems = rest[len(slabs) + n :]
    band = lax.axis_index("lat")
    me = lax.axis_index("lon")
    depth = GROUP // out.shape[0]
    pieces = out.shape[0] // depth
    for d in range(n):
        group = group_of(band, lax.rem(me + n - d, n), n)
        odd = group % 2
        if inner:
            upright[pl.ds(group * rows + HALO * (1 - odd), inner)] = slabs[d][...]
        upright[pl.ds(group * rows + inner * odd, HALO)] = edges[d][...]

    def piece(g):
        at = pl.ds(g * depth, depth)
        return pltpu.make_async_copy(turned.at[at], out.at[at], sems.at[g])

    turn(rotation[me, band] % 4, staged, upright, turned, lambda g: None, lambda g: piece(g).start())
    for g in range(pieces):
        piece(g).wait()


def on_device(
    bands,
    n,
    fields,
    w_conv1,
    b_conv1,
    w_conv2,
    b_conv2,
    w_query,
    w_key,
    w_value,
    w_out,
    rotation,
    owner,
    counts,
):
    size, _, chans = fields.shape
    rows = size // n
    inner = rows - HALO
    cols = size * n
    bf16 = jnp.bfloat16
    smem = pl.BlockSpec(memory_space=pltpu.SMEM)
    vmem = pl.BlockSpec(memory_space=pltpu.VMEM)
    hbm = pl.BlockSpec(memory_space=pltpu.HBM)
    params = pltpu.CompilerParams(vmem_limit_bytes=VMEM_BYTES)
    pieces = size * size // GROUP

    def call(kernel, name, out, scalars, arrays, scratch, array_spec=vmem, scalar_spec=smem, out_spec=vmem):
        many = isinstance(out, list)
        return pl.pallas_call(
            functools.partial(kernel, n, rows),
            out_shape=out,
            in_specs=[scalar_spec] * len(scalars) + [array_spec] * len(arrays),
            out_specs=[out_spec] * len(out) if many else out_spec,
            scratch_shapes=scratch,
            compiler_params=params,
            name=name,
        )(*scalars, *arrays)

    def array(*shape):
        return jax.ShapeDtypeStruct(shape, bf16)

    def around(parts):
        pairs = [[(i, (i + d) % n) for i in range(n)] for d in range(n)]
        return [parts[0]] + [lax.ppermute(parts[d], "lon", pairs[d]) for d in range(1, n)]

    def in_hbm(x):
        return pltpu.with_memory_space_constraint(x, pltpu.HBM)

    loaded = [rotation.T, owner.T, counts]
    loaded += [w_conv1.reshape(3, 3 * chans, chans), b_conv1.reshape(1, chans)]
    loaded += [w_conv2.reshape(3, 3 * chans, chans), b_conv2.reshape(1, chans)]
    loaded = [in_hbm(x) for x in loaded + [w_query, w_key.T, w_value.T, w_out]]
    staging = pltpu.VMEM((chans // LANES, size * size, LANES), jnp.float32)
    block = pltpu.VMEM((size, size, chans), bf16)

    slabs = [array(rows + HALO, size, chans)] * n
    scratch = [staging, block, block, pltpu.SMEM(rotation.T.shape, rotation.dtype)]
    scratch += [pltpu.SemaphoreType.DMA, pltpu.SemaphoreType.DMA((pieces,))]
    slabs = call(send_kernel, "send", slabs, loaded[:1], [in_hbm(fields)], scratch, hbm, hbm)
    held = [pltpu.VMEM(x.shape, x.dtype) for x in loaded]
    scratch = [pltpu.SemaphoreType.DMA((len(loaded),))]
    rotation, owner, counts, *weights = call(load_kernel, "load", held, slabs[:1], loaded, scratch, hbm, hbm)
    slabs = around(slabs)

    held = [array(rows + HALO, cols, chans), array(HALO, cols, chans)]
    grid, sent = call(gather_kernel, "gather", held, [owner], slabs, [])
    snake = [a * n + shard_of(a, g, n) for a in range(bands) for g in range(n)]
    pairs = [(snake[i], snake[i + 1 if i % 2 else i - 1]) for i in range(1, bands * n - 1)]
    received = lax.ppermute(sent, ("lat", "lon"), pairs)

    def taps(count):
        return pltpu.VMEM((count, cols, 3 * chans), bf16)

    def flat(count):
        return [pltpu.VMEM((max(count, 1) * cols, chans), bf16), pltpu.VMEM((chans, max(count, 1) * cols), bf16)]

    edge_acts, *results = call(
        inner_kernel,
        "inner",
        [array(HALO, cols, 3 * chans)] + [array(inner, size, chans)] * (n if inner else 0),
        [owner, counts],
        [grid] + weights,
        [taps(rows + HALO), taps(rows)] + flat(inner),
    )
    results = around(results) if inner else []
    edges = call(
        edge_kernel,
        "edge",
        [array(HALO, size, chans)] * n,
        [owner, counts],
        [sent, received, edge_acts] + weights,
        [taps(2 * HALO), taps(2 * HALO)] + flat(HALO),
    )
    edges = around(edges)
    scratch = [staging, block, block, pltpu.SemaphoreType.DMA((pieces,))]
    return call(store_kernel, "store", array(*fields.shape), [rotation], results + edges, scratch, out_spec=hbm)


def solution(mesh):
    in_specs = (P("lat", "lon", None), P(), P(), P(), P(), P(), P(), P(), P(), P(), P(), P())
    out_specs = P("lat", "lon", None)
    body = functools.partial(on_device, mesh.shape["lat"], mesh.shape["lon"])
    return jax.shard_map(body, mesh=mesh, in_specs=in_specs, out_specs=out_specs, check_vma=False)
```

```python
import functools
import math

import jax
import jax.numpy as jnp
from jax import lax
from jax.experimental import pallas as pl
from jax.experimental.pallas import tpu as pltpu
from jax.sharding import PartitionSpec as P

HALO = 2
LANES = 128
GROUP = 256
VMEM_BYTES = 28 * 1024 * 1024


def group_of(band, shard, n):
    return jnp.where(band % 2 == 0, shard, n - 1 - shard)


def shard_of(band, group, n):
    return group if band % 2 == 0 else n - 1 - group


def first_held(group, rows):
    return group * rows - HALO * (group % 2)


def turn(quarter, staged, block, out, ready, done):
    size, _, chans = block.shape
    tiles = staged.shape[0]
    depth = GROUP // size
    pieces = size // depth

    def column(col):
        parts = [staged[t, pl.ds(col, size, stride=size), :] for t in range(tiles)]
        return jnp.concatenate(parts, axis=1).astype(jnp.bfloat16)

    def keep(i, row):
        for t in range(tiles):
            staged[t, pl.ds(i * size, size), :] = row[:, t * LANES : (t + 1) * LANES]

    @pl.when(quarter == 0)
    def _():
        for g in range(pieces):
            ready(g)
            out[g * depth : (g + 1) * depth] = block[g * depth : (g + 1) * depth]
            done(g)

    @pl.when(quarter == 1)
    def _():
        for i in range(size):
            if i % depth == 0:
                ready(i // depth)
            keep(i, block[i].astype(jnp.float32))
        for i in range(size):
            out[i] = column(size - 1 - i)
            if i % depth == depth - 1:
                done(i // depth)

    @pl.when(quarter == 2)
    def _():
        i = lax.broadcasted_iota(jnp.int32, (GROUP, GROUP), 0)
        j = lax.broadcasted_iota(jnp.int32, (GROUP, GROUP), 1)
        backwards = jnp.where(i + j == GROUP - 1, 1.0, 0.0).astype(jnp.bfloat16)
        for g in reversed(range(pieces)):
            ready(pieces - 1 - g)
            cells = block[size - (g + 1) * depth : size - g * depth].reshape(GROUP, chans)
            turned = jnp.dot(backwards, cells, preferred_element_type=jnp.float32).astype(jnp.bfloat16)
            out[g * depth : (g + 1) * depth] = turned.reshape(depth, size, chans)
            done(g)

    @pl.when(quarter == 3)
    def _():
        for i in range(size):
            if i % depth == 0:
                ready(i // depth)
            keep(size - 1 - i, block[i].astype(jnp.float32))
        for i in range(size):
            out[i] = column(i)
            if i % depth == depth - 1:
                done(i // depth)


def send_kernel(n, rows, rotation_in, fields, *rest):
    slabs = rest[:n]
    staged, block, upright, rotation, scalar_sem, sems = rest[n:]
    band = lax.axis_index("lat")
    me = lax.axis_index("lon")
    depth = GROUP // fields.shape[0]

    def piece(g):
        at = pl.ds(g * depth, depth)
        return pltpu.make_async_copy(fields.at[at], block.at[at], sems.at[g])

    scalars = pltpu.make_async_copy(rotation_in, rotation, scalar_sem)
    scalars.start()
    for g in range(fields.shape[0] // depth):
        piece(g).start()
    scalars.wait()
    turn((4 - rotation[me, band]) % 4, staged, block, upright, lambda g: piece(g).wait(), lambda g: None)
    for d in range(n):
        group = group_of(band, me ^ d, n)
        slabs[d][...] = upright[pl.ds(first_held(group, rows), rows + HALO)]


def load_kernel(n, rows, after, *refs):
    del after
    count = (len(refs) - 9) // 2
    direct, (query, key, value) = refs[:count], refs[count : count + 3]
    loaded, (w_key, w_qv) = refs[count + 3 : 2 * count + 3], refs[2 * count + 3 : 2 * count + 5]
    query_in, key_in, value_in, sems = refs[2 * count + 5 :]
    chans = query.shape[0]
    pairs = list(zip(direct, loaded)) + [(query, query_in), (key, key_in), (value, value_in)]
    copies = [pltpu.make_async_copy(*pair, sems.at[i]) for i, pair in enumerate(pairs)]
    for copy in copies:
        copy.start()
    for copy in copies:
        copy.wait()
    w_key[...] = key_in[...].T
    w_qv[:chans] = query_in[...].T
    w_qv[chans:] = value_in[...]


def columns_of(segment, size):
    return pl.ds(pl.multiple_of(segment * size, size), size)


def spread(taps, r, row):
    cols, chans = row.shape
    taps[r, :, :chans] = pltpu.roll(row, 1, 0).astype(jnp.bfloat16)
    taps[r, :, chans : 2 * chans] = row.astype(jnp.bfloat16)
    taps[r, :, 2 * chans :] = pltpu.roll(row, cols - 1, 0).astype(jnp.bfloat16)


def convolve(taps, weight, bias, count):
    cols, width = taps.shape[1:]
    total = bias[...]
    for i in range(3):
        window = taps[i : i + count].reshape(count * cols, width)
        total = total + jnp.dot(window, weight[i], preferred_element_type=jnp.float32)
    return total


def silu(x):
    return x / (1.0 + jnp.exp(-x))


def live_count(counts, row):
    inside = (row >= 0) & (row < counts.shape[0])
    return jnp.where(inside, counts[jnp.clip(row, 0, counts.shape[0] - 1)], 0)


def finish(n, count, first_row, grid_row, second, counts, owner, w_key, w_qv, w_out, results, *scratch):
    mixed, attended, scores, expo = scratch
    band = lax.axis_index("lat")
    me = lax.axis_index("lon")
    chans = mixed.shape[1]
    cols = mixed.shape[0] // count
    head_dim = w_key.shape[1]
    heads = chans // head_dim
    scale = math.log2(math.e) / head_dim**0.5
    cell = lax.broadcasted_iota(jnp.int32, (cols, chans), 0)
    spans = [slice(r * cols, (r + 1) * cols) for r in range(count)]
    lanes = [slice(h * cols, (h + 1) * cols) for h in range(heads)]
    limits = [counts[first_row + r] for r in range(count)]
    for r, at in enumerate(spans):
        part = jnp.where(cell < limits[r], grid_row(r).astype(jnp.float32) + second[at], 0.0)
        mixed[at, :] = part.astype(jnp.bfloat16)
    flat = mixed[...].astype(jnp.float32)
    normed = (flat * lax.rsqrt(jnp.mean(flat * flat, axis=1, keepdims=True) + 1e-06)).astype(jnp.bfloat16)

    keys = jnp.dot(normed, w_key[...], preferred_element_type=jnp.float32).astype(jnp.bfloat16)
    flipped = jnp.dot(w_qv[...], normed.T, preferred_element_type=jnp.float32).astype(jnp.bfloat16)
    for r, at in enumerate(spans):
        queries = jnp.concatenate([flipped[h * head_dim : (h + 1) * head_dim, at] for h in range(heads)], axis=1)
        scores[r] = jnp.dot(keys[at], queries, preferred_element_type=jnp.float32)
    key_at = lax.broadcasted_iota(jnp.int32, (cols, cols), 0)
    shares = []
    for r in range(count):
        live = key_at < limits[r]
        for h in range(heads):
            part = jnp.where(live, scores[r, :, lanes[h]], -jnp.inf)
            part = jnp.exp2((part - jnp.max(part, axis=0, keepdims=True)) * scale)
            shares.append(1.0 / jnp.sum(part, axis=0, keepdims=True))
            expo[r, :, lanes[h]] = part.astype(jnp.bfloat16)
    for r, at in enumerate(spans):
        summed = jnp.dot(flipped[chans:, at], expo[r], preferred_element_type=jnp.float32)
        for h in range(heads):
            part = summed[:, lanes[h]] * shares[r * heads + h]
            attended[h * head_dim : (h + 1) * head_dim, at] = part.astype(jnp.bfloat16)
    update = lax.dot_general(attended[...], w_out[...], (((0,), (0,)), ((), ())), preferred_element_type=jnp.float32)
    for r, at in enumerate(spans):
        mixed[at, :] = (flat[at] + jnp.where(cell < limits[r], update[at], 0.0)).astype(jnp.bfloat16)
    for d in range(n):
        segment = owner[me ^ d, band]
        for r in range(count):
            results[d][r] = mixed[columns_of(segment + r * n, cols // n), :]


def inner_kernel(n, rows, owner, counts, *rest):
    slabs, (w_conv1, b_conv1, w_conv2, b_conv2), weights = rest[:n], rest[n : n + 4], rest[n + 4 : n + 7]
    inner = rows - HALO
    edge, edge_acts, *rest = rest[n + 7 :]
    results = rest[: n if inner else 0]
    grid, taps, acts, *scratch = rest[len(results) :]
    band = lax.axis_index("lat")
    me = lax.axis_index("lon")
    group = group_of(band, me, n)
    cols, chans = grid.shape[1:]
    cell = lax.broadcasted_iota(jnp.int32, (cols, chans), 0)
    top = band * (rows * n) + first_held(group, rows)
    for d in range(n):
        grid[:, columns_of(owner[me ^ d, band], cols // n)] = slabs[d][...]
    edge[...] = grid[pl.ds(rows * (group % 2), HALO)]
    for r in range(rows + HALO):
        spread(taps, r, grid[r].astype(jnp.float32))
    act = silu(convolve(taps, w_conv1, b_conv1, rows))
    for r in range(rows):
        live = cell < live_count(counts, top + 1 + r)
        spread(acts, r, jnp.where(live, act[r * cols : (r + 1) * cols], 0.0))
    edge_acts[...] = acts[pl.ds(inner * (group % 2), HALO)]
    if inner:
        second = convolve(acts, w_conv2, b_conv2, inner)
        finish(n, inner, top + 2, lambda r: grid[r + 2], second, counts, owner, *weights, results, *scratch)


def edge_kernel(n, rows, owner, counts, *rest):
    sent, received, edge_acts, w_conv1, b_conv1, w_conv2, b_conv2 = rest[:7]
    weights, results = rest[7:10], rest[10 : 10 + n]
    taps, acts, *scratch = rest[10 + n :]
    band = lax.axis_index("lat")
    group = group_of(band, lax.axis_index("lon"), n)
    odd = group % 2
    cols, chans = sent.shape[1:]
    cell = lax.broadcasted_iota(jnp.int32, (cols, chans), 0)
    first_row = band * (rows * n) + group * rows + (rows - HALO) * odd
    near, far = HALO * (1 - odd), HALO * odd
    for r in range(HALO):
        spread(taps, near + r, sent[r].astype(jnp.float32))
        spread(taps, far + r, received[r].astype(jnp.float32))
    act = silu(convolve(taps, w_conv1, b_conv1, HALO))
    acts[pl.ds(near, HALO)] = edge_acts[...]
    for r in range(HALO):
        live = cell < live_count(counts, first_row - 1 + far + r)
        spread(acts, far + r, jnp.where(live, act[r * cols : (r + 1) * cols], 0.0))
    second = convolve(acts, w_conv2, b_conv2, HALO)
    finish(n, HALO, first_row, lambda r: sent[r], second, counts, owner, *weights, results, *scratch)


def store_kernel(n, rows, rotation, *rest):
    inner = rows - HALO
    slabs = rest[: n if inner else 0]
    edges = rest[len(slabs) : len(slabs) + n]
    out, staged, upright, turned, sems = rest[len(slabs) + n :]
    band = lax.axis_index("lat")
    me = lax.axis_index("lon")
    depth = GROUP // out.shape[0]
    pieces = out.shape[0] // depth
    for d in range(n):
        group = group_of(band, me ^ d, n)
        odd = group % 2
        if inner:
            upright[pl.ds(group * rows + HALO * (1 - odd), inner)] = slabs[d][...]
        upright[pl.ds(group * rows + inner * odd, HALO)] = edges[d][...]

    def piece(g):
        at = pl.ds(g * depth, depth)
        return pltpu.make_async_copy(turned.at[at], out.at[at], sems.at[g])

    turn(rotation[me, band] % 4, staged, upright, turned, lambda g: None, lambda g: piece(g).start())
    for g in range(pieces):
        piece(g).wait()


def on_device(
    bands,
    n,
    fields,
    w_conv1,
    b_conv1,
    w_conv2,
    b_conv2,
    w_query,
    w_key,
    w_value,
    w_out,
    rotation,
    owner,
    counts,
):
    size, _, chans = fields.shape
    rows = size // n
    inner = rows - HALO
    cols = size * n
    bf16 = jnp.bfloat16
    smem = pl.BlockSpec(memory_space=pltpu.SMEM)
    vmem = pl.BlockSpec(memory_space=pltpu.VMEM)
    hbm = pl.BlockSpec(memory_space=pltpu.HBM)
    params = pltpu.CompilerParams(vmem_limit_bytes=VMEM_BYTES)
    pieces = size * size // GROUP

    def call(kernel, name, out, scalars, arrays, scratch, array_spec=vmem, scalar_spec=smem, out_spec=vmem):
        many = isinstance(out, list)
        return pl.pallas_call(
            functools.partial(kernel, n, rows),
            out_shape=out,
            in_specs=[scalar_spec] * len(scalars) + [array_spec] * len(arrays),
            out_specs=[out_spec] * len(out) if many else out_spec,
            scratch_shapes=scratch,
            compiler_params=params,
            name=name,
        )(*scalars, *arrays)

    def array(*shape):
        return jax.ShapeDtypeStruct(shape, bf16)

    def around(parts):
        far_first = reversed(range(1, n))
        moved = {d: lax.ppermute(parts[d], "lon", [(i, i ^ d) for i in range(n)]) for d in far_first}
        return [parts[0]] + [moved[d] for d in range(1, n)]

    def in_hbm(x):
        return pltpu.with_memory_space_constraint(x, pltpu.HBM)

    loaded = [rotation.T, owner.T, counts]
    loaded += [w_conv1.reshape(3, 3 * chans, chans), b_conv1.reshape(1, chans)]
    loaded += [w_conv2.reshape(3, 3 * chans, chans), b_conv2.reshape(1, chans), w_out]
    loaded = [in_hbm(x) for x in loaded]
    turned = [in_hbm(x) for x in (w_query, w_key.T, w_value.T)]
    staging = pltpu.VMEM((chans // LANES, size * size, LANES), jnp.float32)
    block = pltpu.VMEM((size, size, chans), bf16)

    slabs = [array(rows + HALO, size, chans)] * n
    scratch = [staging, block, block, pltpu.SMEM(rotation.T.shape, rotation.dtype)]
    scratch += [pltpu.SemaphoreType.DMA, pltpu.SemaphoreType.DMA((pieces,))]
    slabs = call(send_kernel, "send", slabs, loaded[:1], [in_hbm(fields)], scratch, hbm, hbm)
    held = [pltpu.VMEM(x.shape, x.dtype) for x in loaded]
    held += [pltpu.VMEM(w_key.shape, bf16), pltpu.VMEM((chans + w_key.shape[1], chans), bf16)]
    scratch = [pltpu.VMEM(x.shape, bf16) for x in turned] + [pltpu.SemaphoreType.DMA((len(loaded) + 3,))]
    loaded = call(load_kernel, "load", held, slabs[:1], loaded + turned, scratch, hbm, hbm)
    rotation, owner, counts, *convs, w_out, w_key, w_qv = loaded
    weights = [*convs, w_key, w_qv, w_out]
    slabs = around(slabs)

    snake = [a * n + shard_of(a, g, n) for a in range(bands) for g in range(n)]
    pairs = [(snake[i], snake[i + 1 if i % 2 else i - 1]) for i in range(1, bands * n - 1)]

    def taps(count):
        return pltpu.VMEM((count, cols, 3 * chans), bf16)

    def working(count):
        count, heads = max(count, 1), chans // w_key.shape[1]
        return [
            pltpu.VMEM((count * cols, chans), bf16),
            pltpu.VMEM((chans, count * cols), bf16),
            pltpu.VMEM((count, cols, heads * cols), jnp.float32),
            pltpu.VMEM((count, cols, heads * cols), bf16),
        ]

    held = [array(HALO, cols, chans), array(HALO, cols, 3 * chans)]
    sent, edge_acts, *results = call(
        inner_kernel,
        "inner",
        held + [array(inner, size, chans)] * (n if inner else 0),
        [owner, counts],
        slabs + weights,
        [pltpu.VMEM((rows + HALO, cols, chans), bf16), taps(rows + HALO), taps(rows)] + working(inner),
    )
    received = lax.ppermute(sent, ("lat", "lon"), pairs)
    results = around(results) if inner else []
    edges = call(
        edge_kernel,
        "edge",
        [array(HALO, size, chans)] * n,
        [owner, counts],
        [sent, received, edge_acts] + weights,
        [taps(2 * HALO), taps(2 * HALO)] + working(HALO),
    )
    edges = around(edges)
    scratch = [staging, block, block, pltpu.SemaphoreType.DMA((pieces,))]
    return call(store_kernel, "store", array(*fields.shape), [rotation], results + edges, scratch, out_spec=hbm)


def solution(mesh):
    in_specs = (P("lat", "lon", None), P(), P(), P(), P(), P(), P(), P(), P(), P(), P(), P())
    out_specs = P("lat", "lon", None)
    body = functools.partial(on_device, mesh.shape["lat"], mesh.shape["lon"])
    return jax.shard_map(body, mesh=mesh, in_specs=in_specs, out_specs=out_specs, check_vma=False)
```

```python
import functools
import math

import jax
import jax.numpy as jnp
from jax import lax
from jax.experimental import pallas as pl
from jax.experimental.pallas import tpu as pltpu
from jax.sharding import PartitionSpec as P

HALO = 2
LANES = 128
GROUP = 256
VMEM_BYTES = 28 * 1024 * 1024


def group_of(band, shard, n):
    return jnp.where(band % 2 == 0, shard, n - 1 - shard)


def shard_of(band, group, n):
    return group if band % 2 == 0 else n - 1 - group


def first_held(group, rows):
    return group * rows - HALO * (group % 2)


def turn(quarter, staged, block, out, ready, done):
    size, _, chans = block.shape
    tiles = staged.shape[0]
    depth = GROUP // size
    pieces = size // depth

    def column(col):
        parts = [staged[t, pl.ds(col, size, stride=size), :] for t in range(tiles)]
        return jnp.concatenate(parts, axis=1).astype(jnp.bfloat16)

    def keep(i, row):
        for t in range(tiles):
            staged[t, pl.ds(i * size, size), :] = row[:, t * LANES : (t + 1) * LANES]

    @pl.when(quarter == 0)
    def _():
        for g in range(pieces):
            ready(g)
            out[g * depth : (g + 1) * depth] = block[g * depth : (g + 1) * depth]
            done(g)

    @pl.when(quarter == 1)
    def _():
        for i in range(size):
            if i % depth == 0:
                ready(i // depth)
            keep(i, block[i].astype(jnp.float32))
        for i in range(size):
            out[i] = column(size - 1 - i)
            if i % depth == depth - 1:
                done(i // depth)

    @pl.when(quarter == 2)
    def _():
        i = lax.broadcasted_iota(jnp.int32, (GROUP, GROUP), 0)
        j = lax.broadcasted_iota(jnp.int32, (GROUP, GROUP), 1)
        backwards = jnp.where(i + j == GROUP - 1, 1.0, 0.0).astype(jnp.bfloat16)
        for g in reversed(range(pieces)):
            ready(pieces - 1 - g)
            cells = block[size - (g + 1) * depth : size - g * depth].reshape(GROUP, chans)
            turned = jnp.dot(backwards, cells, preferred_element_type=jnp.float32).astype(jnp.bfloat16)
            out[g * depth : (g + 1) * depth] = turned.reshape(depth, size, chans)
            done(g)

    @pl.when(quarter == 3)
    def _():
        for i in range(size):
            if i % depth == 0:
                ready(i // depth)
            keep(size - 1 - i, block[i].astype(jnp.float32))
        for i in range(size):
            out[i] = column(i)
            if i % depth == depth - 1:
                done(i // depth)


def moves(n):
    return [(d, way) for d in range(1, n) for way in ((1, -1) if 2 * d < n else (0,))]


def partner(me, distance, way, n):
    if way == 0:
        return jnp.where(me + distance < n, me + distance, me - distance)
    return me + way * distance


def send_kernel(n, rows, rotation_in, fields, *rest):
    slabs = rest[:-6]
    staged, block, upright, rotation, scalar_sem, sems = rest[-6:]
    band = lax.axis_index("lat")
    me = lax.axis_index("lon")
    depth = GROUP // fields.shape[0]

    def piece(g):
        at = pl.ds(g * depth, depth)
        return pltpu.make_async_copy(fields.at[at], block.at[at], sems.at[g])

    scalars = pltpu.make_async_copy(rotation_in, rotation, scalar_sem)
    scalars.start()
    for g in range(fields.shape[0] // depth):
        piece(g).start()
    scalars.wait()
    turn((4 - rotation[me, band]) % 4, staged, block, upright, lambda g: piece(g).wait(), lambda g: None)
    for slab, (d, way) in zip(slabs, [(0, 1)] + moves(n)):
        group = group_of(band, jnp.clip(partner(me, d, way, n), 0, n - 1), n)
        slab[...] = upright[pl.ds(first_held(group, rows), rows + HALO)]


def load_kernel(n, rows, after, *refs):
    del after
    count = (len(refs) - 9) // 2
    direct, (query, key, value) = refs[:count], refs[count : count + 3]
    loaded, (w_key, w_qv) = refs[count + 3 : 2 * count + 3], refs[2 * count + 3 : 2 * count + 5]
    query_in, key_in, value_in, sems = refs[2 * count + 5 :]
    chans = query.shape[0]
    pairs = list(zip(direct, loaded)) + [(query, query_in), (key, key_in), (value, value_in)]
    copies = [pltpu.make_async_copy(*pair, sems.at[i]) for i, pair in enumerate(pairs)]
    for copy in copies:
        copy.start()
    for copy in copies:
        copy.wait()
    w_key[...] = key_in[...].T
    w_qv[:chans] = query_in[...].T
    w_qv[chans:] = value_in[...]


def columns_of(segment, size):
    return pl.ds(pl.multiple_of(segment * size, size), size)


def gather_kernel(n, rows, owner, *rest):
    slabs, (grid, edge) = rest[:-2], rest[-2:]
    band = lax.axis_index("lat")
    me = lax.axis_index("lon")
    size = grid.shape[1] // n
    for slab, (d, way) in zip(slabs, [(0, 1)] + moves(n)):
        source = partner(me, d, -way, n)

        @pl.when((source >= 0) & (source < n))
        def _(slab=slab, source=source):
            grid[:, columns_of(owner[jnp.clip(source, 0, n - 1), band], size)] = slab[...]

    edge[...] = grid[pl.ds(rows * (group_of(band, me, n) % 2), HALO)]


def spread(taps, r, row):
    cols, chans = row.shape
    taps[r, :, :chans] = pltpu.roll(row, 1, 0).astype(jnp.bfloat16)
    taps[r, :, chans : 2 * chans] = row.astype(jnp.bfloat16)
    taps[r, :, 2 * chans :] = pltpu.roll(row, cols - 1, 0).astype(jnp.bfloat16)


def convolve(taps, weight, bias, count):
    cols, width = taps.shape[1:]
    total = bias[...]
    for i in range(3):
        window = taps[i : i + count].reshape(count * cols, width)
        total = total + jnp.dot(window, weight[i], preferred_element_type=jnp.float32)
    return total


def silu(x):
    return x / (1.0 + jnp.exp(-x))


def live_count(counts, row):
    inside = (row >= 0) & (row < counts.shape[0])
    return jnp.where(inside, counts[jnp.clip(row, 0, counts.shape[0] - 1)], 0)


def finish(n, count, first_row, grid_row, second, counts, owner, w_key, w_qv, w_out, results, *scratch):
    mixed, attended, scores, expo = scratch
    band = lax.axis_index("lat")
    me = lax.axis_index("lon")
    chans = mixed.shape[1]
    cols = mixed.shape[0] // count
    head_dim = w_key.shape[1]
    heads = chans // head_dim
    scale = math.log2(math.e) / head_dim**0.5
    cell = lax.broadcasted_iota(jnp.int32, (cols, chans), 0)
    spans = [slice(r * cols, (r + 1) * cols) for r in range(count)]
    lanes = [slice(h * cols, (h + 1) * cols) for h in range(heads)]
    limits = [counts[first_row + r] for r in range(count)]
    for r, at in enumerate(spans):
        part = jnp.where(cell < limits[r], grid_row(r).astype(jnp.float32) + second[at], 0.0)
        mixed[at, :] = part.astype(jnp.bfloat16)
    flat = mixed[...].astype(jnp.float32)
    normed = (flat * lax.rsqrt(jnp.mean(flat * flat, axis=1, keepdims=True) + 1e-06)).astype(jnp.bfloat16)

    def by_last(a, b):
        return lax.dot_general(a, b, (((1,), (1,)), ((), ())), preferred_element_type=jnp.float32)

    keys = jnp.dot(normed, w_key[...], preferred_element_type=jnp.float32).astype(jnp.bfloat16)
    flipped = by_last(w_qv[...], normed).astype(jnp.bfloat16)
    for r, at in enumerate(spans):
        queries = jnp.concatenate([flipped[h * head_dim : (h + 1) * head_dim, at] for h in range(heads)], axis=1)
        scores[r] = jnp.dot(keys[at], queries, preferred_element_type=jnp.float32)
    key_at = lax.broadcasted_iota(jnp.int32, (cols, cols), 0)
    shares = []
    same = key_at == lax.broadcasted_iota(jnp.int32, (cols, cols), 1)
    same = jnp.where(same, 1.0, 0.0).astype(jnp.bfloat16)
    for r in range(count):
        live = key_at < limits[r]
        for h in range(heads):
            part = jnp.where(live, scores[r, :, lanes[h]], -jnp.inf)
            part = jnp.exp2((part - jnp.max(part, axis=0, keepdims=True)) * scale)
            shares.append(1.0 / jnp.sum(part, axis=0, keepdims=True))
            expo[r, :, lanes[h]] = part.astype(jnp.bfloat16)
    for r, at in enumerate(spans):
        summed = jnp.dot(flipped[chans:, at], expo[r], preferred_element_type=jnp.float32)
        parts = [(summed[:, lanes[h]] * shares[r * heads + h]).astype(jnp.bfloat16) for h in range(heads)]
        attended[at, :] = by_last(same, jnp.concatenate(parts, axis=0)).astype(jnp.bfloat16)
    update = jnp.dot(attended[...], w_out[...], preferred_element_type=jnp.float32)
    for r, at in enumerate(spans):
        mixed[at, :] = (flat[at] + jnp.where(cell < limits[r], update[at], 0.0)).astype(jnp.bfloat16)
    for d in range(n):
        segment = owner[lax.rem(me + d, n), band]
        for r in range(count):
            results[d][r] = mixed[columns_of(segment + r * n, cols // n), :]


def inner_kernel(n, rows, owner, counts, *rest):
    grid, w_conv1, b_conv1, w_conv2, b_conv2 = rest[:5]
    weights = rest[5:8]
    inner = rows - HALO
    edge_acts, results = rest[8], rest[9 : 9 + (n if inner else 0)]
    taps, acts, *scratch = rest[9 + len(results) :]
    band = lax.axis_index("lat")
    group = group_of(band, lax.axis_index("lon"), n)
    cols, chans = grid.shape[1:]
    cell = lax.broadcasted_iota(jnp.int32, (cols, chans), 0)
    top = band * (rows * n) + first_held(group, rows)
    for r in range(rows + HALO):
        spread(taps, r, grid[r].astype(jnp.float32))
    act = silu(convolve(taps, w_conv1, b_conv1, rows))
    for r in range(rows):
        live = cell < live_count(counts, top + 1 + r)
        spread(acts, r, jnp.where(live, act[r * cols : (r + 1) * cols], 0.0))
    edge_acts[...] = acts[pl.ds(inner * (group % 2), HALO)]
    if inner:
        second = convolve(acts, w_conv2, b_conv2, inner)
        finish(n, inner, top + 2, lambda r: grid[r + 2], second, counts, owner, *weights, results, *scratch)


def edge_kernel(n, rows, owner, counts, *rest):
    sent, received, edge_acts, w_conv1, b_conv1, w_conv2, b_conv2 = rest[:7]
    weights, results = rest[7:10], rest[10 : 10 + n]
    taps, acts, *scratch = rest[10 + n :]
    band = lax.axis_index("lat")
    group = group_of(band, lax.axis_index("lon"), n)
    odd = group % 2
    cols, chans = sent.shape[1:]
    cell = lax.broadcasted_iota(jnp.int32, (cols, chans), 0)
    first_row = band * (rows * n) + group * rows + (rows - HALO) * odd
    near, far = HALO * (1 - odd), HALO * odd
    for r in range(HALO):
        spread(taps, near + r, sent[r].astype(jnp.float32))
        spread(taps, far + r, received[r].astype(jnp.float32))
    act = silu(convolve(taps, w_conv1, b_conv1, HALO))
    acts[pl.ds(near, HALO)] = edge_acts[...]
    for r in range(HALO):
        live = cell < live_count(counts, first_row - 1 + far + r)
        spread(acts, far + r, jnp.where(live, act[r * cols : (r + 1) * cols], 0.0))
    second = convolve(acts, w_conv2, b_conv2, HALO)
    finish(n, HALO, first_row, lambda r: sent[r], second, counts, owner, *weights, results, *scratch)


def store_kernel(n, rows, rotation, *rest):
    inner = rows - HALO
    slabs = rest[: n if inner else 0]
    edges = rest[len(slabs) : len(slabs) + n]
    out, staged, upright, turned, sems = rest[len(slabs) + n :]
    band = lax.axis_index("lat")
    me = lax.axis_index("lon")
    depth = GROUP // out.shape[0]
    pieces = out.shape[0] // depth
    for d in range(n):
        group = group_of(band, lax.rem(me + n - d, n), n)
        odd = group % 2
        if inner:
            upright[pl.ds(group * rows + HALO * (1 - odd), inner)] = slabs[d][...]
        upright[pl.ds(group * rows + inner * odd, HALO)] = edges[d][...]

    def piece(g):
        at = pl.ds(g * depth, depth)
        return pltpu.make_async_copy(turned.at[at], out.at[at], sems.at[g])

    turn(rotation[me, band] % 4, staged, upright, turned, lambda g: None, lambda g: piece(g).start())
    for g in range(pieces):
        piece(g).wait()


def on_device(
    bands,
    n,
    fields,
    w_conv1,
    b_conv1,
    w_conv2,
    b_conv2,
    w_query,
    w_key,
    w_value,
    w_out,
    rotation,
    owner,
    counts,
):
    size, _, chans = fields.shape
    rows = size // n
    inner = rows - HALO
    cols = size * n
    bf16 = jnp.bfloat16
    smem = pl.BlockSpec(memory_space=pltpu.SMEM)
    vmem = pl.BlockSpec(memory_space=pltpu.VMEM)
    hbm = pl.BlockSpec(memory_space=pltpu.HBM)
    params = pltpu.CompilerParams(vmem_limit_bytes=VMEM_BYTES)
    pieces = size * size // GROUP

    def call(kernel, name, out, scalars, arrays, scratch, array_spec=vmem, scalar_spec=smem, out_spec=vmem):
        many = isinstance(out, list)
        return pl.pallas_call(
            functools.partial(kernel, n, rows),
            out_shape=out,
            in_specs=[scalar_spec] * len(scalars) + [array_spec] * len(arrays),
            out_specs=[out_spec] * len(out) if many else out_spec,
            scratch_shapes=scratch,
            compiler_params=params,
            name=name,
        )(*scalars, *arrays)

    def array(*shape):
        return jax.ShapeDtypeStruct(shape, bf16)

    def around(parts):
        pairs = [[(i, (i + d) % n) for i in range(n)] for d in range(n)]
        return [parts[0]] + [lax.ppermute(parts[d], "lon", pairs[d]) for d in range(1, n)]

    def outwards(parts):
        pairs = [[(i, i + d) for i in range(n) if way >= 0 and i + d < n] for d, way in moves(n)]
        backs = [[(i, i - d) for i in range(n) if way <= 0 and i >= d] for d, way in moves(n)]
        return [parts[0]] + [lax.ppermute(part, "lon", there + back) for part, there, back in zip(parts[1:], pairs, backs)]

    def in_hbm(x):
        return pltpu.with_memory_space_constraint(x, pltpu.HBM)

    loaded = [rotation.T, owner.T, counts]
    loaded += [w_conv1.reshape(3, 3 * chans, chans), b_conv1.reshape(1, chans)]
    loaded += [w_conv2.reshape(3, 3 * chans, chans), b_conv2.reshape(1, chans), w_out]
    loaded = [in_hbm(x) for x in loaded]
    turned = [in_hbm(x) for x in (w_query, w_key.T, w_value.T)]
    staging = pltpu.VMEM((chans // LANES, size * size, LANES), jnp.float32)
    block = pltpu.VMEM((size, size, chans), bf16)

    slabs = [array(rows + HALO, size, chans)] * (1 + len(moves(n)))
    scratch = [staging, block, block, pltpu.SMEM(rotation.T.shape, rotation.dtype)]
    scratch += [pltpu.SemaphoreType.DMA, pltpu.SemaphoreType.DMA((pieces,))]
    slabs = call(send_kernel, "send", slabs, loaded[:1], [in_hbm(fields)], scratch, hbm, hbm)
    held = [pltpu.VMEM(x.shape, x.dtype) for x in loaded]
    held += [pltpu.VMEM(w_key.shape, bf16), pltpu.VMEM((chans + w_key.shape[1], chans), bf16)]
    scratch = [pltpu.VMEM(x.shape, bf16) for x in turned] + [pltpu.SemaphoreType.DMA((len(loaded) + 3,))]
    loaded = call(load_kernel, "load", held, slabs[:1], loaded + turned, scratch, hbm, hbm)
    rotation, owner, counts, *convs, w_out, w_key, w_qv = loaded
    weights = [*convs, w_key, w_qv, w_out]
    slabs = outwards(slabs)

    held = [array(rows + HALO, cols, chans), array(HALO, cols, chans)]
    grid, sent = call(gather_kernel, "gather", held, [owner], slabs, [])
    snake = [a * n + shard_of(a, g, n) for a in range(bands) for g in range(n)]
    pairs = [(snake[i], snake[i + 1 if i % 2 else i - 1]) for i in range(1, bands * n - 1)]
    received = lax.ppermute(sent, ("lat", "lon"), pairs)

    def taps(count):
        return pltpu.VMEM((count, cols, 3 * chans), bf16)

    def working(count):
        count, heads = max(count, 1), chans // w_key.shape[1]
        return [
            pltpu.VMEM((count * cols, chans), bf16),
            pltpu.VMEM((count * cols, chans), bf16),
            pltpu.VMEM((count, cols, heads * cols), jnp.float32),
            pltpu.VMEM((count, cols, heads * cols), bf16),
        ]

    edge_acts, *results = call(
        inner_kernel,
        "inner",
        [array(HALO, cols, 3 * chans)] + [array(inner, size, chans)] * (n if inner else 0),
        [owner, counts],
        [grid] + weights,
        [taps(rows + HALO), taps(rows)] + working(inner),
    )
    results = around(results) if inner else []
    edges = call(
        edge_kernel,
        "edge",
        [array(HALO, size, chans)] * n,
        [owner, counts],
        [sent, received, edge_acts] + weights,
        [taps(2 * HALO), taps(2 * HALO)] + working(HALO),
    )
    edges = around(edges)
    scratch = [staging, block, block, pltpu.SemaphoreType.DMA((pieces,))]
    return call(store_kernel, "store", array(*fields.shape), [rotation], results + edges, scratch, out_spec=hbm)


def solution(mesh):
    in_specs = (P("lat", "lon", None), P(), P(), P(), P(), P(), P(), P(), P(), P(), P(), P())
    out_specs = P("lat", "lon", None)
    body = functools.partial(on_device, mesh.shape["lat"], mesh.shape["lon"])
    return jax.shard_map(body, mesh=mesh, in_specs=in_specs, out_specs=out_specs, check_vma=False)
```

```python
import functools
import math

import jax
import jax.numpy as jnp
from jax import lax
from jax.experimental import pallas as pl
from jax.experimental.pallas import tpu as pltpu
from jax.sharding import PartitionSpec as P

HALO = 2
LANES = 128
GROUP = 256
VMEM_BYTES = 28 * 1024 * 1024


def group_of(band, shard, n):
    outer = jnp.where((shard == n - 2) == (band % 2 == 0), 0, n - 1)
    return jnp.where(shard < n - 2, shard + 1, outer)


def shard_of(band, group, n):
    if 0 < group < n - 1:
        return group - 1
    return n - 2 if (group == 0) == (band % 2 == 0) else n - 1


def first_held(group, rows):
    return group * rows - HALO * (group % 2)


def turn(quarter, staged, block, out, ready, done):
    size, _, chans = block.shape
    tiles = staged.shape[0]
    depth = GROUP // size
    pieces = size // depth

    def column(col):
        parts = [staged[t, pl.ds(col, size, stride=size), :] for t in range(tiles)]
        return jnp.concatenate(parts, axis=1).astype(jnp.bfloat16)

    def keep(i, row):
        for t in range(tiles):
            staged[t, pl.ds(i * size, size), :] = row[:, t * LANES : (t + 1) * LANES]

    @pl.when(quarter == 0)
    def _():
        for g in range(pieces):
            ready(g)
            out[g * depth : (g + 1) * depth] = block[g * depth : (g + 1) * depth]
            done(g)

    @pl.when(quarter == 1)
    def _():
        for i in range(size):
            if i % depth == 0:
                ready(i // depth)
            keep(i, block[i].astype(jnp.float32))
        for i in range(size):
            out[i] = column(size - 1 - i)
            if i % depth == depth - 1:
                done(i // depth)

    @pl.when(quarter == 2)
    def _():
        i = lax.broadcasted_iota(jnp.int32, (GROUP, GROUP), 0)
        j = lax.broadcasted_iota(jnp.int32, (GROUP, GROUP), 1)
        backwards = jnp.where(i + j == GROUP - 1, 1.0, 0.0).astype(jnp.bfloat16)
        for g in reversed(range(pieces)):
            ready(pieces - 1 - g)
            cells = block[size - (g + 1) * depth : size - g * depth].reshape(GROUP, chans)
            turned = jnp.dot(backwards, cells, preferred_element_type=jnp.float32).astype(jnp.bfloat16)
            out[g * depth : (g + 1) * depth] = turned.reshape(depth, size, chans)
            done(g)

    @pl.when(quarter == 3)
    def _():
        for i in range(size):
            if i % depth == 0:
                ready(i // depth)
            keep(size - 1 - i, block[i].astype(jnp.float32))
        for i in range(size):
            out[i] = column(i)
            if i % depth == depth - 1:
                done(i // depth)


def send_kernel(n, rows, rotation_in, fields, *rest):
    edges, slabs = rest[:n], rest[n : 2 * n]
    staged, block, upright, rotation, scalar_sem, sems = rest[2 * n :]
    band = lax.axis_index("lat")
    me = lax.axis_index("lon")
    depth = GROUP // fields.shape[0]

    def piece(g):
        at = pl.ds(g * depth, depth)
        return pltpu.make_async_copy(fields.at[at], block.at[at], sems.at[g])

    scalars = pltpu.make_async_copy(rotation_in, rotation, scalar_sem)
    scalars.start()
    for g in range(fields.shape[0] // depth):
        piece(g).start()
    scalars.wait()
    turn((4 - rotation[me, band]) % 4, staged, block, upright, lambda g: piece(g).wait(), lambda g: None)
    for d in range(n):
        group = group_of(band, lax.rem(me + d, n), n)
        top, odd = first_held(group, rows), group % 2
        edges[d][...] = upright[pl.ds(top + rows * odd, HALO)]
        slabs[d][...] = upright[pl.ds(top + HALO * (1 - odd), rows)]


def load_kernel(n, rows, after, *refs):
    del after
    count = (len(refs) - 9) // 2
    direct, (query, key, value) = refs[:count], refs[count : count + 3]
    loaded, (w_key, w_qv) = refs[count + 3 : 2 * count + 3], refs[2 * count + 3 : 2 * count + 5]
    query_in, key_in, value_in, sems = refs[2 * count + 5 :]
    chans = query.shape[0]
    pairs = list(zip(direct, loaded)) + [(query, query_in), (key, key_in), (value, value_in)]
    copies = [pltpu.make_async_copy(*pair, sems.at[i]) for i, pair in enumerate(pairs)]
    for copy in copies:
        copy.start()
    for copy in copies:
        copy.wait()
    w_key[...] = key_in[...].T
    w_qv[:chans] = query_in[...].T
    w_qv[chans:] = value_in[...]


def columns_of(segment, size):
    return pl.ds(pl.multiple_of(segment * size, size), size)


def whole_rows(n, owner, slabs, out, first):
    band = lax.axis_index("lat")
    me = lax.axis_index("lon")
    count, size = slabs[0].shape[:2]
    for d in range(n):
        segment = owner[lax.rem(me + n - d, n), band]
        out[pl.ds(first, count), columns_of(segment, size)] = slabs[d][...]


def edge_kernel(n, rows, owner, *rest):
    del rows
    whole_rows(n, owner, rest[:n], rest[n], 0)


def spread(taps, r, row):
    cols, chans = row.shape
    taps[r, :, :chans] = pltpu.roll(row, 1, 0).astype(jnp.bfloat16)
    taps[r, :, chans : 2 * chans] = row.astype(jnp.bfloat16)
    taps[r, :, 2 * chans :] = pltpu.roll(row, cols - 1, 0).astype(jnp.bfloat16)


def convolve(taps, weight, bias, count):
    cols, width = taps.shape[1:]
    total = bias[...]
    for i in range(3):
        window = taps[i : i + count].reshape(count * cols, width)
        total = total + jnp.dot(window, weight[i], preferred_element_type=jnp.float32)
    return total


def silu(x):
    return x / (1.0 + jnp.exp(-x))


def live_count(counts, row):
    inside = (row >= 0) & (row < counts.shape[0])
    return jnp.where(inside, counts[jnp.clip(row, 0, counts.shape[0] - 1)], 0)


def finish(n, count, first_row, grid_row, second, counts, owner, w_key, w_qv, w_out, results, *scratch):
    mixed, attended, scores, expo = scratch
    band = lax.axis_index("lat")
    me = lax.axis_index("lon")
    chans = mixed.shape[1]
    cols = mixed.shape[0] // count
    head_dim = w_key.shape[1]
    heads = chans // head_dim
    scale = math.log2(math.e) / head_dim**0.5
    cell = lax.broadcasted_iota(jnp.int32, (cols, chans), 0)
    spans = [slice(r * cols, (r + 1) * cols) for r in range(count)]
    lanes = [slice(h * cols, (h + 1) * cols) for h in range(heads)]
    limits = [counts[first_row + r] for r in range(count)]
    for r, at in enumerate(spans):
        part = jnp.where(cell < limits[r], grid_row(r).astype(jnp.float32) + second[at], 0.0)
        mixed[at, :] = part.astype(jnp.bfloat16)
    flat = mixed[...].astype(jnp.float32)
    normed = (flat * lax.rsqrt(jnp.mean(flat * flat, axis=1, keepdims=True) + 1e-06)).astype(jnp.bfloat16)

    keys = jnp.dot(normed, w_key[...], preferred_element_type=jnp.float32).astype(jnp.bfloat16)
    flipped = jnp.dot(w_qv[...], normed.T, preferred_element_type=jnp.float32).astype(jnp.bfloat16)
    for r, at in enumerate(spans):
        queries = jnp.concatenate([flipped[h * head_dim : (h + 1) * head_dim, at] for h in range(heads)], axis=1)
        scores[r] = jnp.dot(keys[at], queries, preferred_element_type=jnp.float32)
    key_at = lax.broadcasted_iota(jnp.int32, (cols, cols), 0)
    shares = []
    for r in range(count):
        live = key_at < limits[r]
        for h in range(heads):
            part = jnp.where(live, scores[r, :, lanes[h]], -jnp.inf)
            part = jnp.exp2((part - jnp.max(part, axis=0, keepdims=True)) * scale)
            shares.append(1.0 / jnp.sum(part, axis=0, keepdims=True))
            expo[r, :, lanes[h]] = part.astype(jnp.bfloat16)
    for r, at in enumerate(spans):
        summed = jnp.dot(flipped[chans:, at], expo[r], preferred_element_type=jnp.float32)
        for h in range(heads):
            part = summed[:, lanes[h]] * shares[r * heads + h]
            attended[h * head_dim : (h + 1) * head_dim, at] = part.astype(jnp.bfloat16)
    update = lax.dot_general(attended[...], w_out[...], (((0,), (0,)), ((), ())), preferred_element_type=jnp.float32)
    for r, at in enumerate(spans):
        mixed[at, :] = (flat[at] + jnp.where(cell < limits[r], update[at], 0.0)).astype(jnp.bfloat16)
    for d in range(n):
        segment = owner[lax.rem(me + d, n), band]
        for r in range(count):
            results[d][r] = mixed[columns_of(segment + r * n, cols // n), :]


def main_kernel(n, rows, owner, counts, *rest):
    slabs, sent, received = rest[:n], rest[n], rest[n + 1]
    w_conv1, b_conv1, w_conv2, b_conv2 = rest[n + 2 : n + 6]
    weights = rest[n + 6 : n + 9]
    inner = rows - HALO
    last_grid, last_acts, *rest = rest[n + 9 :]
    results = rest[: n if inner else 0]
    grid, taps, acts, *scratch = rest[len(results) :]
    band = lax.axis_index("lat")
    group = group_of(band, lax.axis_index("lon"), n)
    odd = group % 2
    cols, chans = sent.shape[1:]
    cell = lax.broadcasted_iota(jnp.int32, (cols, chans), 0)
    first_row = band * (rows * n) + group * rows
    whole_rows(n, owner, slabs, grid, 2 * HALO * (1 - odd))
    grid[pl.ds(HALO + (rows - HALO) * odd, HALO)] = sent[...]
    grid[pl.ds((rows + HALO) * odd, HALO)] = received[...]
    for r in range(rows + 2 * HALO):
        spread(taps, r, grid[r].astype(jnp.float32))
    act = silu(convolve(taps, w_conv1, b_conv1, rows + HALO))
    for r in range(rows + HALO):
        live = cell < live_count(counts, first_row - 1 + r)
        spread(acts, r, jnp.where(live, act[r * cols : (r + 1) * cols], 0.0))
    last_grid[...] = grid[rows : rows + HALO]
    last_acts[...] = acts[inner:]
    if inner:
        second = convolve(acts, w_conv2, b_conv2, inner)
        finish(n, inner, first_row, lambda r: grid[r + HALO], second, counts, owner, *weights, results, *scratch)


def last_kernel(n, rows, owner, counts, *rest):
    grid, acts, w_conv2, b_conv2 = rest[:4]
    weights, results, scratch = rest[4:7], rest[7 : 7 + n], rest[7 + n :]
    band = lax.axis_index("lat")
    group = group_of(band, lax.axis_index("lon"), n)
    first_row = band * (rows * n) + group * rows + rows - HALO
    second = convolve(acts, w_conv2, b_conv2, HALO)
    finish(n, HALO, first_row, lambda r: grid[r], second, counts, owner, *weights, results, *scratch)


def store_kernel(n, rows, rotation, *rest):
    inner = rows - HALO
    slabs = rest[: n if inner else 0]
    lasts = rest[len(slabs) : len(slabs) + n]
    out, staged, upright, turned, sems = rest[len(slabs) + n :]
    band = lax.axis_index("lat")
    me = lax.axis_index("lon")
    depth = GROUP // out.shape[0]
    pieces = out.shape[0] // depth
    for d in range(n):
        group = group_of(band, lax.rem(me + n - d, n), n)
        if inner:
            upright[pl.ds(group * rows, inner)] = slabs[d][...]
        upright[pl.ds(group * rows + inner, HALO)] = lasts[d][...]

    def piece(g):
        at = pl.ds(g * depth, depth)
        return pltpu.make_async_copy(turned.at[at], out.at[at], sems.at[g])

    turn(rotation[me, band] % 4, staged, upright, turned, lambda g: None, lambda g: piece(g).start())
    for g in range(pieces):
        piece(g).wait()


def on_device(
    bands,
    n,
    fields,
    w_conv1,
    b_conv1,
    w_conv2,
    b_conv2,
    w_query,
    w_key,
    w_value,
    w_out,
    rotation,
    owner,
    counts,
):
    size, _, chans = fields.shape
    rows = size // n
    inner = rows - HALO
    cols = size * n
    bf16 = jnp.bfloat16
    smem = pl.BlockSpec(memory_space=pltpu.SMEM)
    vmem = pl.BlockSpec(memory_space=pltpu.VMEM)
    hbm = pl.BlockSpec(memory_space=pltpu.HBM)
    params = pltpu.CompilerParams(vmem_limit_bytes=VMEM_BYTES)
    pieces = size * size // GROUP

    def call(kernel, name, out, scalars, arrays, scratch, array_spec=vmem, scalar_spec=smem, out_spec=vmem):
        many = isinstance(out, list)
        return pl.pallas_call(
            functools.partial(kernel, n, rows),
            out_shape=out,
            in_specs=[scalar_spec] * len(scalars) + [array_spec] * len(arrays),
            out_specs=[out_spec] * len(out) if many else out_spec,
            scratch_shapes=scratch,
            compiler_params=params,
            name=name,
        )(*scalars, *arrays)

    def array(*shape):
        return jax.ShapeDtypeStruct(shape, bf16)

    def around(parts):
        order = sorted(range(1, n), key=lambda d: -min(d, n - d))
        moved = {d: lax.ppermute(parts[d], "lon", [(i, (i + d) % n) for i in range(n)]) for d in order}
        return [parts[0]] + [moved[d] for d in range(1, n)]

    def in_hbm(x):
        return pltpu.with_memory_space_constraint(x, pltpu.HBM)

    loaded = [rotation.T, owner.T, counts]
    loaded += [w_conv1.reshape(3, 3 * chans, chans), b_conv1.reshape(1, chans)]
    loaded += [w_conv2.reshape(3, 3 * chans, chans), b_conv2.reshape(1, chans), w_out]
    loaded = [in_hbm(x) for x in loaded]
    turned = [in_hbm(x) for x in (w_query, w_key.T, w_value.T)]
    staging = pltpu.VMEM((chans // LANES, size * size, LANES), jnp.float32)
    block = pltpu.VMEM((size, size, chans), bf16)

    slabs = [array(HALO, size, chans)] * n + [array(rows, size, chans)] * n
    scratch = [staging, block, block, pltpu.SMEM(rotation.T.shape, rotation.dtype)]
    scratch += [pltpu.SemaphoreType.DMA, pltpu.SemaphoreType.DMA((pieces,))]
    slabs = call(send_kernel, "send", slabs, loaded[:1], [in_hbm(fields)], scratch, hbm, hbm)
    held = [pltpu.VMEM(x.shape, x.dtype) for x in loaded]
    held += [pltpu.VMEM(w_key.shape, bf16), pltpu.VMEM((chans + w_key.shape[1], chans), bf16)]
    scratch = [pltpu.VMEM(x.shape, bf16) for x in turned] + [pltpu.SemaphoreType.DMA((len(loaded) + 3,))]
    loaded = call(load_kernel, "load", held, slabs[:1], loaded + turned, scratch, hbm, hbm)
    rotation, owner, counts, *convs, w_out, w_key, w_qv = loaded
    weights = [*convs, w_key, w_qv, w_out]
    edges = around(slabs[:n])
    slabs = around(slabs[n:])

    snake = [a * n + shard_of(a, g, n) for a in range(bands) for g in range(n)]
    pairs = [(snake[i], snake[i + 1 if i % 2 else i - 1]) for i in range(1, bands * n - 1)]
    sent = call(edge_kernel, "edge", array(HALO, cols, chans), [owner], edges, [])
    received = lax.ppermute(sent, ("lat", "lon"), pairs)

    def taps(count):
        return pltpu.VMEM((count, cols, 3 * chans), bf16)

    def working(count):
        count, heads = max(count, 1), chans // w_key.shape[1]
        return [
            pltpu.VMEM((count * cols, chans), bf16),
            pltpu.VMEM((chans, count * cols), bf16),
            pltpu.VMEM((count, cols, heads * cols), jnp.float32),
            pltpu.VMEM((count, cols, heads * cols), bf16),
        ]

    held = [array(HALO, cols, chans), array(2 * HALO, cols, 3 * chans)]
    last_grid, last_acts, *results = call(
        main_kernel,
        "main",
        held + [array(inner, size, chans)] * (n if inner else 0),
        [owner, counts],
        slabs + [sent, received] + weights,
        [pltpu.VMEM((rows + 2 * HALO, cols, chans), bf16), taps(rows + 2 * HALO), taps(rows + HALO)] + working(inner),
    )
    results = around(results) if inner else []
    lasts = call(
        last_kernel,
        "last",
        [array(HALO, size, chans)] * n,
        [owner, counts],
        [last_grid, last_acts] + weights[2:],
        working(HALO),
    )
    lasts = around(lasts)
    scratch = [staging, block, block, pltpu.SemaphoreType.DMA((pieces,))]
    return call(store_kernel, "store", array(*fields.shape), [rotation], results + lasts, scratch, out_spec=hbm)


def solution(mesh):
    in_specs = (P("lat", "lon", None), P(), P(), P(), P(), P(), P(), P(), P(), P(), P(), P())
    out_specs = P("lat", "lon", None)
    body = functools.partial(on_device, mesh.shape["lat"], mesh.shape["lon"])
    return jax.shard_map(body, mesh=mesh, in_specs=in_specs, out_specs=out_specs, check_vma=False)
```

```python
import functools
import math

import jax
import jax.numpy as jnp
from jax import lax
from jax.experimental import pallas as pl
from jax.experimental.pallas import tpu as pltpu
from jax.sharding import PartitionSpec as P

HALO = 2
LANES = 128
GROUP = 256
AHEAD = 16
VMEM_BYTES = 28 * 1024 * 1024


def group_of(band, shard, n):
    outer = jnp.where((shard == n - 2) == (band % 2 == 0), 0, n - 1)
    return jnp.where(shard < n - 2, shard + 1, outer)


def shard_of(band, group, n):
    if 0 < group < n - 1:
        return group - 1
    return n - 2 if (group == 0) == (band % 2 == 0) else n - 1


def first_held(group, rows):
    return group * rows - HALO * (group % 2)


def turn(quarter, staged, block, out, ready, done):
    size, _, chans = block.shape
    tiles = staged.shape[0]
    depth = GROUP // size
    pieces = size // depth

    def column(col):
        parts = [staged[t, pl.ds(col, size, stride=size), :] for t in range(tiles)]
        return jnp.concatenate(parts, axis=1).astype(jnp.bfloat16)

    def keep(i, row):
        for t in range(tiles):
            staged[t, pl.ds(i * size, size), :] = row[:, t * LANES : (t + 1) * LANES]

    @pl.when(quarter == 0)
    def _():
        for g in range(pieces):
            ready(g)
            out[g * depth : (g + 1) * depth] = block[g * depth : (g + 1) * depth]
            done(g)

    @pl.when(quarter == 1)
    def _():
        for i in range(size):
            if i % depth == 0:
                ready(i // depth)
            keep(i, block[i].astype(jnp.float32))
        for i in range(size):
            out[i] = column(size - 1 - i)
            if i % depth == depth - 1:
                done(i // depth)

    @pl.when(quarter == 2)
    def _():
        i = lax.broadcasted_iota(jnp.int32, (GROUP, GROUP), 0)
        j = lax.broadcasted_iota(jnp.int32, (GROUP, GROUP), 1)
        backwards = jnp.where(i + j == GROUP - 1, 1.0, 0.0).astype(jnp.bfloat16)
        for g in reversed(range(pieces)):
            ready(pieces - 1 - g)
            cells = block[size - (g + 1) * depth : size - g * depth].reshape(GROUP, chans)
            turned = jnp.dot(backwards, cells, preferred_element_type=jnp.float32).astype(jnp.bfloat16)
            out[g * depth : (g + 1) * depth] = turned.reshape(depth, size, chans)
            done(g)

    @pl.when(quarter == 3)
    def _():
        for i in range(size):
            if i % depth == 0:
                ready(i // depth)
            keep(size - 1 - i, block[i].astype(jnp.float32))
        for i in range(size):
            out[i] = column(i)
            if i % depth == depth - 1:
                done(i // depth)


def send_kernel(n, rows, rotation_in, owner_in, fields, *rest):
    edges, slabs, (rotation_out, owner_out) = rest[:n], rest[n : 2 * n], rest[2 * n : 2 * n + 2]
    staged, block, upright, rotation, scalar_sems, sems = rest[2 * n + 2 :]
    band = lax.axis_index("lat")
    me = lax.axis_index("lon")
    depth = GROUP // fields.shape[0]

    def piece(g):
        at = pl.ds(g * depth, depth)
        return pltpu.make_async_copy(fields.at[at], block.at[at], sems.at[g])

    scalars = [
        pltpu.make_async_copy(rotation_in, rotation, scalar_sems.at[0]),
        pltpu.make_async_copy(rotation_in, rotation_out, scalar_sems.at[1]),
        pltpu.make_async_copy(owner_in, owner_out, scalar_sems.at[2]),
    ]
    for copy in scalars:
        copy.start()
    for g in range(fields.shape[0] // depth):
        piece(g).start()
    scalars[0].wait()
    turn((4 - rotation[me, band]) % 4, staged, block, upright, lambda g: piece(g).wait(), lambda g: None)
    for d in range(n):
        group = group_of(band, lax.rem(me + d, n), n)
        top, odd = first_held(group, rows), group % 2
        edges[d][...] = upright[pl.ds(top + rows * odd, HALO)]
        slabs[d][...] = upright[pl.ds(top + HALO * (1 - odd), rows)]
    scalars[1].wait()
    scalars[2].wait()


def load_kernel(n, rows, after, *refs):
    del after
    count = (len(refs) - 7) // 2
    direct, (query, key) = refs[:count], refs[count : count + 2]
    loaded, (w_query, w_key) = refs[count + 2 : 2 * count + 2], refs[2 * count + 2 : 2 * count + 4]
    query_in, key_in, sems = refs[2 * count + 4 :]
    heads, _, head_dim = w_query.shape
    pairs = list(zip(direct, loaded)) + [(query, query_in), (key, key_in)]
    copies = [pltpu.make_async_copy(*pair, sems.at[i]) for i, pair in enumerate(pairs)]
    for copy in copies:
        copy.start()
    for copy in copies:
        copy.wait()
    w_key[...] = key_in[...].T
    for h in range(heads):
        w_query[h] = query_in[:, h * head_dim : (h + 1) * head_dim]


def columns_of(segment, size):
    return pl.ds(pl.multiple_of(segment * size, size), size)


def whole_rows(n, owner, slabs, out, first):
    band = lax.axis_index("lat")
    me = lax.axis_index("lon")
    count, size = slabs[0].shape[:2]
    for d in range(n):
        segment = owner[lax.rem(me + n - d, n), band]
        out[pl.ds(first, count), columns_of(segment, size)] = slabs[d][...]


def edge_kernel(n, rows, owner, *rest):
    del rows
    whole_rows(n, owner, rest[:n], rest[n], 0)


def spread(taps, r, row):
    cols, chans = row.shape
    taps[r, :, :chans] = pltpu.roll(row, 1, 0).astype(jnp.bfloat16)
    taps[r, :, chans : 2 * chans] = row.astype(jnp.bfloat16)
    taps[r, :, 2 * chans :] = pltpu.roll(row, cols - 1, 0).astype(jnp.bfloat16)


def convolve(taps, weight, bias, count):
    cols, width = taps.shape[1:]
    total = bias[...]
    for i in range(3):
        window = taps[i : i + count].reshape(count * cols, width)
        total = total + jnp.dot(window, weight[i], preferred_element_type=jnp.float32)
    return total


def silu(x):
    return x / (1.0 + jnp.exp(-x))


def live_count(counts, row):
    inside = (row >= 0) & (row < counts.shape[0])
    return jnp.where(inside, counts[jnp.clip(row, 0, counts.shape[0] - 1)], 0)


def by_last(a, b):
    return lax.dot_general(a, b, (((1,), (1,)), ((), ())), preferred_element_type=jnp.float32)


def attend(segments, limits, mixed, normed, keys, values, w_query, w_out, results, here, scores, expo, turned):
    rows, chans = len(limits), mixed.shape[1]
    size = here.shape[0] // (rows * len(segments))
    heads, _, head_dim = w_query.shape
    cols = mixed.shape[0] // rows
    width = heads * size
    blocks = [(s, r) for s in range(len(segments)) for r in range(rows)]

    def cells(s, r):
        return columns_of(segments[s] + r * (cols // size), size)

    for b, (s, r) in enumerate(blocks):
        here[b * size : (b + 1) * size, :] = normed[cells(s, r), :]
    queries = [jnp.dot(here[...], w_query[h], preferred_element_type=jnp.float32) for h in range(heads)]
    queries = [query.astype(jnp.bfloat16) for query in queries]
    for b, (s, r) in enumerate(blocks):
        own = jnp.concatenate([query[b * size : (b + 1) * size] for query in queries], axis=0)
        scores[b] = by_last(keys[r * cols : (r + 1) * cols, :], own)
    key_at = lax.broadcasted_iota(jnp.int32, (cols, width), 0)
    scale = math.log2(math.e) / head_dim**0.5
    shares = []
    for b, (s, r) in enumerate(blocks):
        part = jnp.where(key_at < limits[r], scores[b], -jnp.inf)
        part = jnp.exp2((part - jnp.max(part, axis=0, keepdims=True)) * scale)
        shares.append(1.0 / jnp.sum(part, axis=0, keepdims=True))
        expo[b] = part.astype(jnp.bfloat16)
    for b, (s, r) in enumerate(blocks):
        summed = jnp.dot(values[:, r * cols : (r + 1) * cols], expo[b], preferred_element_type=jnp.float32)
        turned[:, b * width : (b + 1) * width] = (summed * shares[b]).astype(jnp.bfloat16)
    attended = turned[...].T
    update = jnp.zeros(here.shape, jnp.float32)
    for h in range(heads):
        starts = [b * width + h * size for b in range(len(blocks))]
        part = jnp.concatenate([attended[start : start + size] for start in starts], axis=0)
        weight = w_out[h * head_dim : (h + 1) * head_dim, :]
        update = update + jnp.dot(part, weight, preferred_element_type=jnp.float32)
    for b, (s, r) in enumerate(blocks):
        cell = segments[s] * size + lax.broadcasted_iota(jnp.int32, (size, chans), 0)
        part = jnp.where(cell < limits[r], update[b * size : (b + 1) * size], 0.0)
        results[s][r * size : (r + 1) * size, :] = (mixed[cells(s, r), :].astype(jnp.float32) + part).astype(jnp.bfloat16)


def main_kernel(first, n, rows, owner, counts, *rest):
    slabs, sent, received = rest[:n], rest[n], rest[n + 1]
    w_conv1, b_conv1, w_conv2, b_conv2, w_key, w_value, w_query, w_out = rest[n + 2 : n + 10]
    result, mixed, normed, keys, values = rest[n + 10 : n + 15]
    grid, taps, acts, *scratch = rest[n + 15 :]
    band = lax.axis_index("lat")
    me = lax.axis_index("lon")
    group = group_of(band, me, n)
    odd = group % 2
    cols, chans = sent.shape[1:]
    cell = lax.broadcasted_iota(jnp.int32, (cols, chans), 0)
    first_row = band * (rows * n) + group * rows
    whole_rows(n, owner, slabs, grid, 2 * HALO * (1 - odd))
    grid[pl.ds(HALO + (rows - HALO) * odd, HALO)] = sent[...]
    grid[pl.ds((rows + HALO) * odd, HALO)] = received[...]
    for r in range(rows + 2 * HALO):
        spread(taps, r, grid[r].astype(jnp.float32))
    act = silu(convolve(taps, w_conv1, b_conv1, rows + HALO))
    limits = [live_count(counts, first_row - 1 + r) for r in range(rows + HALO)]
    for r in range(rows + HALO):
        spread(acts, r, jnp.where(cell < limits[r], act[r * cols : (r + 1) * cols], 0.0))
    limits = limits[1 : rows + 1]
    second = convolve(acts, w_conv2, b_conv2, rows)
    for r in range(rows):
        at = slice(r * cols, (r + 1) * cols)
        part = jnp.where(cell < limits[r], grid[r + HALO].astype(jnp.float32) + second[at], 0.0)
        mixed[at, :] = part.astype(jnp.bfloat16)
    flat = mixed[...].astype(jnp.float32)
    scaled = (flat * lax.rsqrt(jnp.mean(flat * flat, axis=1, keepdims=True) + 1e-06)).astype(jnp.bfloat16)
    normed[...] = scaled
    keys[...] = jnp.dot(scaled, w_key[...], preferred_element_type=jnp.float32).astype(jnp.bfloat16)
    values[...] = by_last(w_value[...], scaled).astype(jnp.bfloat16)
    result[rows * (cols // n) :, :] = jnp.zeros((AHEAD, chans), result.dtype)
    segments = [owner[lax.rem(me + first, n), band]]
    attend(segments, limits, mixed, normed, keys, values, w_query, w_out, [result], *scratch)


def rest_kernel(moves, n, rows, owner, counts, *rest):
    mixed, normed, keys, values, w_query, w_out = rest[:6]
    results, scratch = rest[6 : 6 + len(moves)], rest[6 + len(moves) :]
    band = lax.axis_index("lat")
    me = lax.axis_index("lon")
    first_row = band * (rows * n) + group_of(band, me, n) * rows
    limits = [counts[first_row + r] for r in range(rows)]
    segments = [owner[lax.rem(me + d, n), band] for d in moves]
    attend(segments, limits, mixed, normed, keys, values, w_query, w_out, results, *scratch)


def store_kernel(n, rows, rotation, *rest):
    slabs, (out, staged, upright, turned, sems) = rest[:n], rest[n:]
    band = lax.axis_index("lat")
    me = lax.axis_index("lon")
    depth = GROUP // out.shape[0]
    pieces = out.shape[0] // depth
    for d in range(n):
        top = group_of(band, lax.rem(me + n - d, n), n) * rows
        upright[pl.ds(top, rows)] = slabs[d][: rows * out.shape[0], :].reshape(rows, *out.shape[1:])

    def piece(g):
        at = pl.ds(g * depth, depth)
        return pltpu.make_async_copy(turned.at[at], out.at[at], sems.at[g])

    turn(rotation[me, band] % 4, staged, upright, turned, lambda g: None, lambda g: piece(g).start())
    for g in range(pieces):
        piece(g).wait()


def on_device(
    bands,
    n,
    fields,
    w_conv1,
    b_conv1,
    w_conv2,
    b_conv2,
    w_query,
    w_key,
    w_value,
    w_out,
    rotation,
    owner,
    counts,
):
    size, _, chans = fields.shape
    rows = size // n
    inner = rows - HALO
    cols = size * n
    bf16 = jnp.bfloat16
    smem = pl.BlockSpec(memory_space=pltpu.SMEM)
    vmem = pl.BlockSpec(memory_space=pltpu.VMEM)
    hbm = pl.BlockSpec(memory_space=pltpu.HBM)
    params = pltpu.CompilerParams(vmem_limit_bytes=VMEM_BYTES)
    pieces = size * size // GROUP

    def call(kernel, name, out, scalars, arrays, scratch, array_spec=vmem, scalar_spec=smem, out_spec=vmem):
        many = isinstance(out, list)
        return pl.pallas_call(
            functools.partial(kernel, n, rows),
            out_shape=out,
            in_specs=[scalar_spec] * len(scalars) + [array_spec] * len(arrays),
            out_specs=[out_spec] * len(out) if many else out_spec,
            scratch_shapes=scratch,
            compiler_params=params,
            name=name,
        )(*scalars, *arrays)

    def array(*shape):
        return jax.ShapeDtypeStruct(shape, bf16)

    order = sorted(range(1, n), key=lambda d: -min(d, n - d))

    def around_by(x, d):
        return lax.ppermute(x, "lon", [(i, (i + d) % n) for i in range(n)])

    def around(parts):
        moved = {d: around_by(parts[d], d) for d in order}
        return [parts[0]] + [moved[d] for d in range(1, n)]

    def in_hbm(x):
        return pltpu.with_memory_space_constraint(x, pltpu.HBM)

    rotation, owner = in_hbm(rotation.T), in_hbm(owner.T)
    loaded = [counts]
    loaded += [w_conv1.reshape(3, 3 * chans, chans), b_conv1.reshape(1, chans)]
    loaded += [w_conv2.reshape(3, 3 * chans, chans), b_conv2.reshape(1, chans), w_value.T, w_out]
    loaded = [in_hbm(x) for x in loaded]
    turned = [in_hbm(x) for x in (w_query, w_key.T)]
    staging = pltpu.VMEM((chans // LANES, size * size, LANES), jnp.float32)
    block = pltpu.VMEM((size, size, chans), bf16)

    slabs = [array(HALO, size, chans)] * n + [array(rows, size, chans)] * n
    scratch = [staging, block, block, pltpu.SMEM(rotation.shape, rotation.dtype)]
    scratch += [pltpu.SemaphoreType.DMA((3,)), pltpu.SemaphoreType.DMA((pieces,))]
    held = slabs + [pltpu.VMEM(x.shape, x.dtype) for x in (rotation, owner)]
    *slabs, rotation, owner = call(send_kernel, "send", held, [rotation, owner], [in_hbm(fields)], scratch, hbm, hbm)
    edges = around(slabs[:n])
    slabs = around(slabs[n:])

    snake = [a * n + shard_of(a, g, n) for a in range(bands) for g in range(n)]
    pairs = [(snake[i], snake[i + 1 if i % 2 else i - 1]) for i in range(1, bands * n - 1)]
    sent = call(edge_kernel, "edge", array(HALO, cols, chans), [owner], edges, [])
    received = lax.ppermute(sent, ("lat", "lon"), pairs)

    head_dim = w_key.shape[1]
    heads = chans // head_dim
    held = [pltpu.VMEM(x.shape, x.dtype) for x in loaded]
    held += [pltpu.VMEM((heads, chans, head_dim), bf16), pltpu.VMEM(w_key.shape, bf16)]
    scratch = [pltpu.VMEM(x.shape, bf16) for x in turned] + [pltpu.SemaphoreType.DMA((len(loaded) + 2,))]
    loaded = call(load_kernel, "load", held, [sent], loaded + turned, scratch, hbm, hbm)
    counts, *convs, w_value, w_out, w_query, w_key = loaded

    def taps(count):
        return pltpu.VMEM((count, cols, 3 * chans), bf16)

    def working(segments):
        blocks, width = segments * rows, heads * size
        return [
            pltpu.VMEM((blocks * size, chans), bf16),
            pltpu.VMEM((blocks, cols, width), jnp.float32),
            pltpu.VMEM((blocks, cols, width), bf16),
            pltpu.VMEM((head_dim, blocks * width), bf16),
        ]

    cells = rows * cols
    result = array(rows * size, chans)
    first, *others = [*order, 0]
    results = {}
    results[first], *held = call(
        functools.partial(main_kernel, first),
        "main",
        [array(rows * size + AHEAD, chans), array(cells, chans), array(cells, chans), array(cells, head_dim), array(head_dim, cells)],
        [owner, counts],
        slabs + [sent, received, *convs, w_key, w_value, w_query, w_out],
        [pltpu.VMEM((rows + 2 * HALO, cols, chans), bf16), taps(rows + 2 * HALO), taps(rows + HALO)] + working(1),
    )
    moved = {first: around_by(results[first], first)}
    rest = call(
        functools.partial(rest_kernel, others),
        "rest",
        [result] * len(others),
        [owner, counts],
        held + [w_query, w_out],
        working(len(others)),
    )
    for d, x in zip(others, rest):
        moved[d] = around_by(x, d) if d else x
    slabs = [moved[d] for d in range(n)]
    scratch = [staging, block, block, pltpu.SemaphoreType.DMA((pieces,))]
    return call(store_kernel, "store", array(*fields.shape), [rotation], slabs, scratch, out_spec=hbm)


def solution(mesh):
    in_specs = (P("lat", "lon", None), P(), P(), P(), P(), P(), P(), P(), P(), P(), P(), P())
    out_specs = P("lat", "lon", None)
    body = functools.partial(on_device, mesh.shape["lat"], mesh.shape["lon"])
    return jax.shard_map(body, mesh=mesh, in_specs=in_specs, out_specs=out_specs, check_vma=False)
```

```python
import functools
import math

import jax
import jax.numpy as jnp
from jax import lax
from jax.experimental import pallas as pl
from jax.experimental.pallas import tpu as pltpu
from jax.sharding import PartitionSpec as P

HALO = 2
LANES = 128
GROUP = 256
AHEAD = 16
VMEM_BYTES = 28 * 1024 * 1024


def group_of(band, shard, n):
    outer = jnp.where((shard == n - 2) == (band % 2 == 0), 0, n - 1)
    return jnp.where(shard < n - 2, shard + 1, outer)


def shard_of(band, group, n):
    if 0 < group < n - 1:
        return group - 1
    return n - 2 if (group == 0) == (band % 2 == 0) else n - 1


def first_held(group, rows):
    return group * rows - HALO * (group % 2)


def turn(quarter, staged, block, out, ready, done):
    size, _, chans = block.shape
    tiles = staged.shape[0]
    depth = GROUP // size
    pieces = size // depth

    def column(col):
        parts = [staged[t, pl.ds(col, size, stride=size), :] for t in range(tiles)]
        return jnp.concatenate(parts, axis=1).astype(jnp.bfloat16)

    def keep(i, row):
        for t in range(tiles):
            staged[t, pl.ds(i * size, size), :] = row[:, t * LANES : (t + 1) * LANES]

    @pl.when(quarter == 0)
    def _():
        for g in range(pieces):
            ready(g)
            out[g * depth : (g + 1) * depth] = block[g * depth : (g + 1) * depth]
            done(g)

    @pl.when(quarter == 1)
    def _():
        for i in range(size):
            if i % depth == 0:
                ready(i // depth)
            keep(i, block[i].astype(jnp.float32))
        for i in range(size):
            out[i] = column(size - 1 - i)
            if i % depth == depth - 1:
                done(i // depth)

    @pl.when(quarter == 2)
    def _():
        i = lax.broadcasted_iota(jnp.int32, (GROUP, GROUP), 0)
        j = lax.broadcasted_iota(jnp.int32, (GROUP, GROUP), 1)
        backwards = jnp.where(i + j == GROUP - 1, 1.0, 0.0).astype(jnp.bfloat16)
        for g in reversed(range(pieces)):
            ready(pieces - 1 - g)
            cells = block[size - (g + 1) * depth : size - g * depth].reshape(GROUP, chans)
            turned = jnp.dot(backwards, cells, preferred_element_type=jnp.float32).astype(jnp.bfloat16)
            out[g * depth : (g + 1) * depth] = turned.reshape(depth, size, chans)
            done(g)

    @pl.when(quarter == 3)
    def _():
        for i in range(size):
            if i % depth == 0:
                ready(i // depth)
            keep(size - 1 - i, block[i].astype(jnp.float32))
        for i in range(size):
            out[i] = column(i)
            if i % depth == depth - 1:
                done(i // depth)


def send_kernel(n, rows, rotation_in, owner_in, fields, *rest):
    edges, slabs, (rotation_out, owner_out) = rest[:n], rest[n : 2 * n], rest[2 * n : 2 * n + 2]
    staged, block, upright, rotation, scalar_sems, sems = rest[2 * n + 2 :]
    band = lax.axis_index("lat")
    me = lax.axis_index("lon")
    depth = GROUP // fields.shape[0]

    def piece(g):
        at = pl.ds(g * depth, depth)
        return pltpu.make_async_copy(fields.at[at], block.at[at], sems.at[g])

    scalars = [
        pltpu.make_async_copy(rotation_in, rotation, scalar_sems.at[0]),
        pltpu.make_async_copy(rotation_in, rotation_out, scalar_sems.at[1]),
        pltpu.make_async_copy(owner_in, owner_out, scalar_sems.at[2]),
    ]
    for copy in scalars:
        copy.start()
    for g in range(fields.shape[0] // depth):
        piece(g).start()
    scalars[0].wait()
    turn((4 - rotation[me, band]) % 4, staged, block, upright, lambda g: piece(g).wait(), lambda g: None)
    for d in range(n):
        group = group_of(band, lax.rem(me + d, n), n)
        top, odd = first_held(group, rows), group % 2
        edges[d][...] = upright[pl.ds(top + rows * odd, HALO)]
        slabs[d][...] = upright[pl.ds(top + HALO * (1 - odd), rows)]
    scalars[1].wait()
    scalars[2].wait()


def load_kernel(n, rows, after, *refs):
    del after
    count = (len(refs) - 7) // 2
    direct, (query, key) = refs[:count], refs[count : count + 2]
    loaded, (w_query, w_key) = refs[count + 2 : 2 * count + 2], refs[2 * count + 2 : 2 * count + 4]
    query_in, key_in, sems = refs[2 * count + 4 :]
    heads, _, head_dim = w_query.shape
    pairs = list(zip(direct, loaded)) + [(query, query_in), (key, key_in)]
    copies = [pltpu.make_async_copy(*pair, sems.at[i]) for i, pair in enumerate(pairs)]
    for copy in copies:
        copy.start()
    for copy in copies:
        copy.wait()
    w_key[...] = key_in[...].T
    for h in range(heads):
        w_query[h] = query_in[:, h * head_dim : (h + 1) * head_dim]


def columns_of(segment, size):
    return pl.ds(pl.multiple_of(segment * size, size), size)


def whole_rows(n, owner, slabs, out, first):
    band = lax.axis_index("lat")
    me = lax.axis_index("lon")
    count, size = slabs[0].shape[:2]
    for d in range(n):
        segment = owner[lax.rem(me + n - d, n), band]
        out[pl.ds(first, count), columns_of(segment, size)] = slabs[d][...]


def edge_kernel(n, rows, owner, *rest):
    del rows
    whole_rows(n, owner, rest[:n], rest[n], 0)


def spread(taps, r, row):
    cols, chans = row.shape
    taps[r, :, :chans] = pltpu.roll(row, 1, 0).astype(jnp.bfloat16)
    taps[r, :, chans : 2 * chans] = row.astype(jnp.bfloat16)
    taps[r, :, 2 * chans :] = pltpu.roll(row, cols - 1, 0).astype(jnp.bfloat16)


def convolve(taps, weight, bias, first, count):
    cols, width = taps.shape[1:]
    windows = [taps[first + i : first + i + count].reshape(count * cols, width) for i in range(3)]
    depth = weight.shape[0] * width
    product = jnp.dot(
        jnp.concatenate(windows, axis=1),
        weight[...].reshape(depth, weight.shape[2]),
        preferred_element_type=jnp.float32,
    )
    return product + bias[...]


def silu(x):
    return x / (1.0 + jnp.exp(-x))


def live_count(counts, row):
    inside = (row >= 0) & (row < counts.shape[0])
    return jnp.where(inside, counts[jnp.clip(row, 0, counts.shape[0] - 1)], 0)


def by_last(a, b):
    return lax.dot_general(a, b, (((1,), (1,)), ((), ())), preferred_element_type=jnp.float32)


def attend(segments, limits, mixed, normed, keys, values, w_query, w_out, results, here, scores, expo, turned):
    rows, chans = len(limits), mixed.shape[1]
    size = here.shape[0] // (rows * len(segments))
    heads, _, head_dim = w_query.shape
    cols = mixed.shape[0] // rows
    width = heads * size
    blocks = [(s, r) for s in range(len(segments)) for r in range(rows)]

    def cells(s, r):
        return columns_of(segments[s] + r * (cols // size), size)

    for b, (s, r) in enumerate(blocks):
        here[b * size : (b + 1) * size, :] = normed[cells(s, r), :]
    queries = [jnp.dot(here[...], w_query[h], preferred_element_type=jnp.float32) for h in range(heads)]
    queries = [query.astype(jnp.bfloat16) for query in queries]
    for b, (s, r) in enumerate(blocks):
        own = jnp.concatenate([query[b * size : (b + 1) * size] for query in queries], axis=0)
        scores[b] = by_last(keys[r * cols : (r + 1) * cols, :], own)
    key_at = lax.broadcasted_iota(jnp.int32, (cols, width), 0)
    scale = math.log2(math.e) / head_dim**0.5
    shares = []
    for b, (s, r) in enumerate(blocks):
        part = jnp.where(key_at < limits[r], scores[b], -jnp.inf)
        part = jnp.exp2((part - jnp.max(part, axis=0, keepdims=True)) * scale)
        shares.append(1.0 / jnp.sum(part, axis=0, keepdims=True))
        expo[b] = part.astype(jnp.bfloat16)
    for b, (s, r) in enumerate(blocks):
        summed = jnp.dot(values[:, r * cols : (r + 1) * cols], expo[b], preferred_element_type=jnp.float32)
        turned[:, b * width : (b + 1) * width] = (summed * shares[b]).astype(jnp.bfloat16)
    attended = turned[...].T
    update = jnp.zeros(here.shape, jnp.float32)
    for h in range(heads):
        starts = [b * width + h * size for b in range(len(blocks))]
        part = jnp.concatenate([attended[start : start + size] for start in starts], axis=0)
        weight = w_out[h * head_dim : (h + 1) * head_dim, :]
        update = update + jnp.dot(part, weight, preferred_element_type=jnp.float32)
    for b, (s, r) in enumerate(blocks):
        cell = segments[s] * size + lax.broadcasted_iota(jnp.int32, (size, chans), 0)
        part = jnp.where(cell < limits[r], update[b * size : (b + 1) * size], 0.0)
        results[s][r * size : (r + 1) * size, :] = (mixed[cells(s, r), :].astype(jnp.float32) + part).astype(jnp.bfloat16)


def main_kernel(first, n, rows, owner, counts, *rest):
    slabs, sent, received = rest[:n], rest[n], rest[n + 1]
    w_conv1, b_conv1, w_conv2, b_conv2, w_key, w_value, w_query, w_out = rest[n + 2 : n + 10]
    result, mixed, normed, keys, values = rest[n + 10 : n + 15]
    grid, taps, acts, *scratch = rest[n + 15 :]
    band = lax.axis_index("lat")
    me = lax.axis_index("lon")
    group = group_of(band, me, n)
    odd = group % 2
    cols, chans = sent.shape[1:]
    cell = lax.broadcasted_iota(jnp.int32, (cols, chans), 0)
    first_row = band * (rows * n) + group * rows
    whole_rows(n, owner, slabs, grid, 2 * HALO * (1 - odd))
    grid[pl.ds(HALO + (rows - HALO) * odd, HALO)] = sent[...]
    grid[pl.ds((rows + HALO) * odd, HALO)] = received[...]
    limits = [live_count(counts, first_row - 1 + r) for r in range(rows + HALO)]
    half = (rows + HALO) // 2
    spans = [(0, half), (half, rows + HALO)]
    done = 0
    convolved = []
    for low, high in spans:
        for r in range(done, high + HALO):
            spread(taps, r, grid[r].astype(jnp.float32))
        done = high + HALO
        convolved.append(convolve(taps, w_conv1, b_conv1, low, high - low))
    low = 0
    for (start, stop), first_conv in zip(spans, convolved):
        act = silu(first_conv)
        for r in range(start, stop):
            at = slice((r - start) * cols, (r - start + 1) * cols)
            spread(acts, r, jnp.where(cell < limits[r], act[at], 0.0))
        high = stop - HALO
        if high <= low:
            continue
        second = convolve(acts, w_conv2, b_conv2, low, high - low)
        for r in range(low, high):
            here = grid[r + HALO].astype(jnp.float32) + second[(r - low) * cols : (r - low + 1) * cols]
            here = jnp.where(cell < limits[r + 1], here, 0.0)
            mixed[r * cols : (r + 1) * cols, :] = here.astype(jnp.bfloat16)
        low = high
    limits = limits[1 : rows + 1]
    flat = mixed[...].astype(jnp.float32)
    scaled = (flat * lax.rsqrt(jnp.mean(flat * flat, axis=1, keepdims=True) + 1e-06)).astype(jnp.bfloat16)
    normed[...] = scaled
    keys[...] = jnp.dot(scaled, w_key[...], preferred_element_type=jnp.float32).astype(jnp.bfloat16)
    values[...] = by_last(w_value[...], scaled).astype(jnp.bfloat16)
    result[rows * (cols // n) :, :] = jnp.zeros((AHEAD, chans), result.dtype)
    segments = [owner[lax.rem(me + first, n), band]]
    attend(segments, limits, mixed, normed, keys, values, w_query, w_out, [result], *scratch)


def rest_kernel(moves, n, rows, owner, counts, *rest):
    mixed, normed, keys, values, w_query, w_out = rest[:6]
    results, scratch = rest[6 : 6 + len(moves)], rest[6 + len(moves) :]
    band = lax.axis_index("lat")
    me = lax.axis_index("lon")
    first_row = band * (rows * n) + group_of(band, me, n) * rows
    limits = [counts[first_row + r] for r in range(rows)]
    segments = [owner[lax.rem(me + d, n), band] for d in moves]
    attend(segments, limits, mixed, normed, keys, values, w_query, w_out, results, *scratch)


def store_kernel(n, rows, rotation, *rest):
    slabs, (out, staged, upright, turned, sems) = rest[:n], rest[n:]
    band = lax.axis_index("lat")
    me = lax.axis_index("lon")
    depth = GROUP // out.shape[0]
    pieces = out.shape[0] // depth
    for d in range(n):
        top = group_of(band, lax.rem(me + n - d, n), n) * rows
        upright[pl.ds(top, rows)] = slabs[d][: rows * out.shape[0], :].reshape(rows, *out.shape[1:])

    def piece(g):
        at = pl.ds(g * depth, depth)
        return pltpu.make_async_copy(turned.at[at], out.at[at], sems.at[g])

    turn(rotation[me, band] % 4, staged, upright, turned, lambda g: None, lambda g: piece(g).start())
    for g in range(pieces):
        piece(g).wait()


def on_device(
    bands,
    n,
    fields,
    w_conv1,
    b_conv1,
    w_conv2,
    b_conv2,
    w_query,
    w_key,
    w_value,
    w_out,
    rotation,
    owner,
    counts,
):
    size, _, chans = fields.shape
    rows = size // n
    inner = rows - HALO
    cols = size * n
    bf16 = jnp.bfloat16
    smem = pl.BlockSpec(memory_space=pltpu.SMEM)
    vmem = pl.BlockSpec(memory_space=pltpu.VMEM)
    hbm = pl.BlockSpec(memory_space=pltpu.HBM)
    params = pltpu.CompilerParams(vmem_limit_bytes=VMEM_BYTES)
    pieces = size * size // GROUP

    def call(kernel, name, out, scalars, arrays, scratch, array_spec=vmem, scalar_spec=smem, out_spec=vmem):
        many = isinstance(out, list)
        return pl.pallas_call(
            functools.partial(kernel, n, rows),
            out_shape=out,
            in_specs=[scalar_spec] * len(scalars) + [array_spec] * len(arrays),
            out_specs=[out_spec] * len(out) if many else out_spec,
            scratch_shapes=scratch,
            compiler_params=params,
            name=name,
        )(*scalars, *arrays)

    def array(*shape):
        return jax.ShapeDtypeStruct(shape, bf16)

    order = sorted(range(1, n), key=lambda d: -min(d, n - d))

    def around_by(x, d):
        return lax.ppermute(x, "lon", [(i, (i + d) % n) for i in range(n)])

    def around(parts):
        moved = {d: around_by(parts[d], d) for d in order}
        return [parts[0]] + [moved[d] for d in range(1, n)]

    def in_hbm(x):
        return pltpu.with_memory_space_constraint(x, pltpu.HBM)

    rotation, owner = in_hbm(rotation.T), in_hbm(owner.T)
    loaded = [counts]
    loaded += [w_conv1.reshape(3, 3 * chans, chans), b_conv1.reshape(1, chans)]
    loaded += [w_conv2.reshape(3, 3 * chans, chans), b_conv2.reshape(1, chans), w_value.T, w_out]
    loaded = [in_hbm(x) for x in loaded]
    turned = [in_hbm(x) for x in (w_query, w_key.T)]
    staging = pltpu.VMEM((chans // LANES, size * size, LANES), jnp.float32)
    block = pltpu.VMEM((size, size, chans), bf16)

    slabs = [array(HALO, size, chans)] * n + [array(rows, size, chans)] * n
    scratch = [staging, block, block, pltpu.SMEM(rotation.shape, rotation.dtype)]
    scratch += [pltpu.SemaphoreType.DMA((3,)), pltpu.SemaphoreType.DMA((pieces,))]
    held = slabs + [pltpu.VMEM(x.shape, x.dtype) for x in (rotation, owner)]
    *slabs, rotation, owner = call(send_kernel, "send", held, [rotation, owner], [in_hbm(fields)], scratch, hbm, hbm)
    edges = around(slabs[:n])
    slabs = around(slabs[n:])

    snake = [a * n + shard_of(a, g, n) for a in range(bands) for g in range(n)]
    pairs = [(snake[i], snake[i + 1 if i % 2 else i - 1]) for i in range(1, bands * n - 1)]
    sent = call(edge_kernel, "edge", array(HALO, cols, chans), [owner], edges, [])
    received = lax.ppermute(sent, ("lat", "lon"), pairs)

    head_dim = w_key.shape[1]
    heads = chans // head_dim
    held = [pltpu.VMEM(x.shape, x.dtype) for x in loaded]
    held += [pltpu.VMEM((heads, chans, head_dim), bf16), pltpu.VMEM(w_key.shape, bf16)]
    scratch = [pltpu.VMEM(x.shape, bf16) for x in turned] + [pltpu.SemaphoreType.DMA((len(loaded) + 2,))]
    loaded = call(load_kernel, "load", held, [sent], loaded + turned, scratch, hbm, hbm)
    counts, *convs, w_value, w_out, w_query, w_key = loaded

    def taps(count):
        return pltpu.VMEM((count, cols, 3 * chans), bf16)

    def working(segments):
        blocks, width = segments * rows, heads * size
        return [
            pltpu.VMEM((blocks * size, chans), bf16),
            pltpu.VMEM((blocks, cols, width), jnp.float32),
            pltpu.VMEM((blocks, cols, width), bf16),
            pltpu.VMEM((head_dim, blocks * width), bf16),
        ]

    cells = rows * cols
    result = array(rows * size, chans)
    first, *others = [*order, 0]
    results = {}
    results[first], *held = call(
        functools.partial(main_kernel, first),
        "main",
        [array(rows * size + AHEAD, chans), array(cells, chans), array(cells, chans), array(cells, head_dim), array(head_dim, cells)],
        [owner, counts],
        slabs + [sent, received, *convs, w_key, w_value, w_query, w_out],
        [pltpu.VMEM((rows + 2 * HALO, cols, chans), bf16), taps(rows + 2 * HALO), taps(rows + HALO)] + working(1),
    )
    moved = {first: around_by(results[first], first)}
    rest = call(
        functools.partial(rest_kernel, others),
        "rest",
        [result] * len(others),
        [owner, counts],
        held + [w_query, w_out],
        working(len(others)),
    )
    for d, x in zip(others, rest):
        moved[d] = around_by(x, d) if d else x
    slabs = [moved[d] for d in range(n)]
    scratch = [staging, block, block, pltpu.SemaphoreType.DMA((pieces,))]
    return call(store_kernel, "store", array(*fields.shape), [rotation], slabs, scratch, out_spec=hbm)


def solution(mesh):
    in_specs = (P("lat", "lon", None), P(), P(), P(), P(), P(), P(), P(), P(), P(), P(), P())
    out_specs = P("lat", "lon", None)
    body = functools.partial(on_device, mesh.shape["lat"], mesh.shape["lon"])
    return jax.shard_map(body, mesh=mesh, in_specs=in_specs, out_specs=out_specs, check_vma=False)
```

```python
import functools
import math

import jax
import jax.numpy as jnp
from jax import lax
from jax.experimental import pallas as pl
from jax.experimental.pallas import tpu as pltpu
from jax.sharding import PartitionSpec as P

HALO = 2
LANES = 128
GROUP = 256
AHEAD = 16
VMEM_BYTES = 28 * 1024 * 1024


def group_of(band, shard, n):
    outer = jnp.where((shard == n - 2) == (band % 2 == 0), 0, n - 1)
    return jnp.where(shard < n - 2, shard + 1, outer)


def shard_of(band, group, n):
    if 0 < group < n - 1:
        return group - 1
    return n - 2 if (group == 0) == (band % 2 == 0) else n - 1


def first_held(group, rows):
    return group * rows - HALO * (group % 2)


def turn(quarter, staged, block, out, ready, done):
    size, _, chans = block.shape
    tiles = staged.shape[0]
    pitch = staged.shape[1] // size
    depth = GROUP // size
    pieces = size // depth

    def column(col):
        parts = [staged[t, pl.ds(col, size, stride=pitch), :] for t in range(tiles)]
        return jnp.concatenate(parts, axis=1).astype(jnp.bfloat16)

    def keep(i, row):
        for t in range(tiles):
            staged[t, pl.ds(i * pitch, size), :] = row[:, t * LANES : (t + 1) * LANES]

    @pl.when(quarter == 0)
    def _():
        for g in range(pieces):
            ready(g)
            out[g * depth : (g + 1) * depth] = block[g * depth : (g + 1) * depth]
            done(g)

    @pl.when(quarter == 1)
    def _():
        for i in range(size):
            if i % depth == 0:
                ready(i // depth)
            keep(i, block[i].astype(jnp.float32))
        for i in range(size):
            out[i] = column(size - 1 - i)
            if i % depth == depth - 1:
                done(i // depth)

    @pl.when(quarter == 2)
    def _():
        i = lax.broadcasted_iota(jnp.int32, (GROUP, GROUP), 0)
        j = lax.broadcasted_iota(jnp.int32, (GROUP, GROUP), 1)
        backwards = jnp.where(i + j == GROUP - 1, 1.0, 0.0).astype(jnp.bfloat16)
        for g in reversed(range(pieces)):
            ready(pieces - 1 - g)
            cells = block[size - (g + 1) * depth : size - g * depth].reshape(GROUP, chans)
            turned = jnp.dot(backwards, cells, preferred_element_type=jnp.float32).astype(jnp.bfloat16)
            out[g * depth : (g + 1) * depth] = turned.reshape(depth, size, chans)
            done(g)

    @pl.when(quarter == 3)
    def _():
        for i in range(size):
            if i % depth == 0:
                ready(i // depth)
            keep(size - 1 - i, block[i].astype(jnp.float32))
        for i in range(size):
            out[i] = column(i)
            if i % depth == depth - 1:
                done(i // depth)


def send_kernel(n, rows, rotation_in, owner_in, fields, *rest):
    edges, slabs, (rotation_out, owner_out) = rest[:n], rest[n : 2 * n], rest[2 * n : 2 * n + 2]
    staged, block, upright, rotation, scalar_sems, sems = rest[2 * n + 2 :]
    band = lax.axis_index("lat")
    me = lax.axis_index("lon")
    depth = GROUP // fields.shape[0]

    def piece(g):
        at = pl.ds(g * depth, depth)
        return pltpu.make_async_copy(fields.at[at], block.at[at], sems.at[g])

    scalars = [
        pltpu.make_async_copy(rotation_in, rotation, scalar_sems.at[0]),
        pltpu.make_async_copy(rotation_in, rotation_out, scalar_sems.at[1]),
        pltpu.make_async_copy(owner_in, owner_out, scalar_sems.at[2]),
    ]
    for copy in scalars:
        copy.start()
    for g in range(fields.shape[0] // depth):
        piece(g).start()
    scalars[0].wait()
    turn((4 - rotation[me, band]) % 4, staged, block, upright, lambda g: piece(g).wait(), lambda g: None)
    for d in range(n):
        group = group_of(band, lax.rem(me + d, n), n)
        top, odd = first_held(group, rows), group % 2
        edges[d][...] = upright[pl.ds(top + rows * odd, HALO)]
        slabs[d][...] = upright[pl.ds(top + HALO * (1 - odd), rows)]
    scalars[1].wait()
    scalars[2].wait()


def load_kernel(n, rows, after, *refs):
    del after
    count = (len(refs) - 7) // 2
    direct, (query, key) = refs[:count], refs[count : count + 2]
    loaded, (w_query, w_key) = refs[count + 2 : 2 * count + 2], refs[2 * count + 2 : 2 * count + 4]
    query_in, key_in, sems = refs[2 * count + 4 :]
    heads, _, head_dim = w_query.shape
    pairs = list(zip(direct, loaded)) + [(query, query_in), (key, key_in)]
    copies = [pltpu.make_async_copy(*pair, sems.at[i]) for i, pair in enumerate(pairs)]
    for copy in copies:
        copy.start()
    for copy in copies:
        copy.wait()
    w_key[...] = key_in[...].T
    for h in range(heads):
        w_query[h] = query_in[:, h * head_dim : (h + 1) * head_dim]


def columns_of(segment, size):
    return pl.ds(pl.multiple_of(segment * size, size), size)


def whole_rows(n, owner, slabs, out, first):
    band = lax.axis_index("lat")
    me = lax.axis_index("lon")
    count, size = slabs[0].shape[:2]
    for d in range(n):
        segment = owner[lax.rem(me + n - d, n), band]
        out[pl.ds(first, count), columns_of(segment, size)] = slabs[d][...]


def edge_kernel(n, rows, owner, *rest):
    del rows
    held, (out, *passed, rows_out) = rest[: 2 * n - 2], rest[2 * n - 2 :]
    _, cols, chans = rows_out.shape
    whole_rows(n, owner, held[:n], rows_out, 0)
    out[: HALO * cols, :] = rows_out[...].reshape(HALO * cols, chans)
    out[HALO * cols :, :] = jnp.zeros((AHEAD, chans), out.dtype)
    for slab, copy in zip(held[n:], passed):
        copy[...] = slab[...]


def spread(taps, r, row):
    cols, chans = row.shape
    taps[r, :, :chans] = pltpu.roll(row, 1, 0).astype(jnp.bfloat16)
    taps[r, :, chans : 2 * chans] = row.astype(jnp.bfloat16)
    taps[r, :, 2 * chans :] = pltpu.roll(row, cols - 1, 0).astype(jnp.bfloat16)


def convolve(taps, weight, bias, first, count):
    cols, width = taps.shape[1:]
    windows = [taps[first + i : first + i + count].reshape(count * cols, width) for i in range(3)]
    depth = weight.shape[0] * width
    product = jnp.dot(
        jnp.concatenate(windows, axis=1),
        weight[...].reshape(depth, weight.shape[2]),
        preferred_element_type=jnp.float32,
    )
    return product + bias[...]


def silu(x):
    return x / (1.0 + jnp.exp(-x))


def live_count(counts, row):
    inside = (row >= 0) & (row < counts.shape[0])
    return jnp.where(inside, counts[jnp.clip(row, 0, counts.shape[0] - 1)], 0)


def by_last(a, b):
    return lax.dot_general(a, b, (((1,), (1,)), ((), ())), preferred_element_type=jnp.float32)


def attend(segments, limits, mixed, normed, keys, values, w_query, w_out, results, here, scores, expo, turned):
    rows, chans = len(limits), mixed.shape[1]
    size = here.shape[0] // (rows * len(segments))
    heads, _, head_dim = w_query.shape
    cols = mixed.shape[0] // rows
    width = heads * size
    blocks = [(s, r) for s in range(len(segments)) for r in range(rows)]

    def cells(s, r):
        return columns_of(segments[s] + r * (cols // size), size)

    for b, (s, r) in enumerate(blocks):
        here[b * size : (b + 1) * size, :] = normed[cells(s, r), :]
    queries = [jnp.dot(here[...], w_query[h], preferred_element_type=jnp.float32) for h in range(heads)]
    queries = [query.astype(jnp.bfloat16) for query in queries]
    for b, (s, r) in enumerate(blocks):
        own = jnp.concatenate([query[b * size : (b + 1) * size] for query in queries], axis=0)
        scores[b] = by_last(keys[r * cols : (r + 1) * cols, :], own)
    key_at = lax.broadcasted_iota(jnp.int32, (cols, width), 0)
    scale = math.log2(math.e) / head_dim**0.5
    shares = []
    for b, (s, r) in enumerate(blocks):
        part = jnp.where(key_at < limits[r], scores[b], -jnp.inf)
        part = jnp.exp2((part - jnp.max(part, axis=0, keepdims=True)) * scale)
        shares.append(1.0 / jnp.sum(part, axis=0, keepdims=True))
        expo[b] = part.astype(jnp.bfloat16)
    for b, (s, r) in enumerate(blocks):
        summed = jnp.dot(values[:, r * cols : (r + 1) * cols], expo[b], preferred_element_type=jnp.float32)
        turned[:, b * width : (b + 1) * width] = (summed * shares[b]).astype(jnp.bfloat16)
    attended = turned[...].T
    update = jnp.zeros(here.shape, jnp.float32)
    for h in range(heads):
        starts = [b * width + h * size for b in range(len(blocks))]
        part = jnp.concatenate([attended[start : start + size] for start in starts], axis=0)
        weight = w_out[h * head_dim : (h + 1) * head_dim, :]
        update = update + jnp.dot(part, weight, preferred_element_type=jnp.float32)
    for b, (s, r) in enumerate(blocks):
        cell = segments[s] * size + lax.broadcasted_iota(jnp.int32, (size, chans), 0)
        part = jnp.where(cell < limits[r], update[b * size : (b + 1) * size], 0.0)
        results[s][r * size : (r + 1) * size, :] = (mixed[cells(s, r), :].astype(jnp.float32) + part).astype(jnp.bfloat16)


def main_kernel(first, n, rows, owner, counts, *rest):
    slabs, sent, received = rest[:n], rest[n], rest[n + 1]
    w_conv1, b_conv1, w_conv2, b_conv2, w_key, w_value, w_query, w_out = rest[n + 2 : n + 10]
    result, mixed, normed, keys, values = rest[n + 10 : n + 15]
    grid, taps, acts, *scratch = rest[n + 15 :]
    band = lax.axis_index("lat")
    me = lax.axis_index("lon")
    group = group_of(band, me, n)
    odd = group % 2
    cols, chans = grid.shape[1:]
    edge = (HALO, cols, chans)
    cell = lax.broadcasted_iota(jnp.int32, (cols, chans), 0)
    first_row = band * (rows * n) + group * rows
    whole_rows(n, owner, slabs, grid, 2 * HALO * (1 - odd))
    grid[pl.ds(HALO + (rows - HALO) * odd, HALO)] = sent[: HALO * cols, :].reshape(edge)
    grid[pl.ds((rows + HALO) * odd, HALO)] = received[: HALO * cols, :].reshape(edge)
    limits = [live_count(counts, first_row - 1 + r) for r in range(rows + HALO)]
    half = (rows + HALO) // 2
    spans = [(0, half), (half, rows + HALO)]
    done = 0
    convolved = []
    for low, high in spans:
        for r in range(done, high + HALO):
            spread(taps, r, grid[r].astype(jnp.float32))
        done = high + HALO
        convolved.append(convolve(taps, w_conv1, b_conv1, low, high - low))
    low = 0
    for (start, stop), first_conv in zip(spans, convolved):
        act = silu(first_conv)
        for r in range(start, stop):
            at = slice((r - start) * cols, (r - start + 1) * cols)
            spread(acts, r, jnp.where(cell < limits[r], act[at], 0.0))
        high = stop - HALO
        if high <= low:
            continue
        second = convolve(acts, w_conv2, b_conv2, low, high - low)
        for r in range(low, high):
            here = grid[r + HALO].astype(jnp.float32) + second[(r - low) * cols : (r - low + 1) * cols]
            here = jnp.where(cell < limits[r + 1], here, 0.0)
            mixed[r * cols : (r + 1) * cols, :] = here.astype(jnp.bfloat16)
        low = high
    limits = limits[1 : rows + 1]
    flat = mixed[...].astype(jnp.float32)
    scaled = (flat * lax.rsqrt(jnp.mean(flat * flat, axis=1, keepdims=True) + 1e-06)).astype(jnp.bfloat16)
    normed[...] = scaled
    keys[...] = jnp.dot(scaled, w_key[...], preferred_element_type=jnp.float32).astype(jnp.bfloat16)
    values[...] = by_last(w_value[...], scaled).astype(jnp.bfloat16)
    result[rows * (cols // n) :, :] = jnp.zeros((AHEAD, chans), result.dtype)
    segments = [owner[lax.rem(me + first, n), band]]
    attend(segments, limits, mixed, normed, keys, values, w_query, w_out, [result], *scratch)


def rest_kernel(moves, n, rows, owner, counts, *rest):
    mixed, normed, keys, values, w_query, w_out = rest[:6]
    results, scratch = rest[6 : 6 + len(moves)], rest[6 + len(moves) :]
    band = lax.axis_index("lat")
    me = lax.axis_index("lon")
    first_row = band * (rows * n) + group_of(band, me, n) * rows
    limits = [counts[first_row + r] for r in range(rows)]
    segments = [owner[lax.rem(me + d, n), band] for d in moves]
    attend(segments, limits, mixed, normed, keys, values, w_query, w_out, results, *scratch)


def store_kernel(n, rows, rotation, *rest):
    slabs, (out, staged, upright, turned, sems) = rest[:n], rest[n:]
    band = lax.axis_index("lat")
    me = lax.axis_index("lon")
    depth = GROUP // out.shape[0]
    pieces = out.shape[0] // depth
    for d in range(n):
        top = group_of(band, lax.rem(me + n - d, n), n) * rows
        upright[pl.ds(top, rows)] = slabs[d][: rows * out.shape[0], :].reshape(rows, *out.shape[1:])

    def piece(g):
        at = pl.ds(g * depth, depth)
        return pltpu.make_async_copy(turned.at[at], out.at[at], sems.at[g])

    turn(rotation[me, band] % 4, staged, upright, turned, lambda g: None, lambda g: piece(g).start())
    for g in range(pieces):
        piece(g).wait()


def on_device(
    bands,
    n,
    fields,
    w_conv1,
    b_conv1,
    w_conv2,
    b_conv2,
    w_query,
    w_key,
    w_value,
    w_out,
    rotation,
    owner,
    counts,
):
    size, _, chans = fields.shape
    rows = size // n
    inner = rows - HALO
    cols = size * n
    bf16 = jnp.bfloat16
    smem = pl.BlockSpec(memory_space=pltpu.SMEM)
    vmem = pl.BlockSpec(memory_space=pltpu.VMEM)
    hbm = pl.BlockSpec(memory_space=pltpu.HBM)
    params = pltpu.CompilerParams(vmem_limit_bytes=VMEM_BYTES)
    pieces = size * size // GROUP

    def call(kernel, name, out, scalars, arrays, scratch, array_spec=vmem, scalar_spec=smem, out_spec=vmem):
        many = isinstance(out, list)
        return pl.pallas_call(
            functools.partial(kernel, n, rows),
            out_shape=out,
            in_specs=[scalar_spec] * len(scalars) + [array_spec] * len(arrays),
            out_specs=[out_spec] * len(out) if many else out_spec,
            scratch_shapes=scratch,
            compiler_params=params,
            name=name,
        )(*scalars, *arrays)

    def array(*shape):
        return jax.ShapeDtypeStruct(shape, bf16)

    order = sorted(range(1, n), key=lambda d: -min(d, n - d))

    def around_by(x, d):
        return lax.ppermute(x, "lon", [(i, (i + d) % n) for i in range(n)])

    def around(parts):
        moved = {d: around_by(parts[d], d) for d in order}
        return [parts[0]] + [moved[d] for d in range(1, n)]

    def in_hbm(x):
        return pltpu.with_memory_space_constraint(x, pltpu.HBM)

    rotation, owner = in_hbm(rotation.T), in_hbm(owner.T)
    loaded = [counts]
    loaded += [w_conv1.reshape(3, 3 * chans, chans), b_conv1.reshape(1, chans)]
    loaded += [w_conv2.reshape(3, 3 * chans, chans), b_conv2.reshape(1, chans), w_value.T, w_out]
    loaded = [in_hbm(x) for x in loaded]
    turned = [in_hbm(x) for x in (w_query, w_key.T)]
    staging = pltpu.VMEM((chans // LANES, size * (size + 8), LANES), jnp.float32)
    block = pltpu.VMEM((size, size, chans), bf16)

    slabs = [array(HALO, size, chans)] * n + [array(rows, size, chans)] * n
    scratch = [staging, block, block, pltpu.SMEM(rotation.shape, rotation.dtype)]
    scratch += [pltpu.SemaphoreType.DMA((3,)), pltpu.SemaphoreType.DMA((pieces,))]
    held = slabs + [pltpu.VMEM(x.shape, x.dtype) for x in (rotation, owner)]
    *slabs, rotation, owner = call(send_kernel, "send", held, [rotation, owner], [in_hbm(fields)], scratch, hbm, hbm)
    edges = around(slabs[:n])
    slabs = slabs[n:]
    first, *others = order

    snake = [a * n + shard_of(a, g, n) for a in range(bands) for g in range(n)]
    pairs = [(snake[i], snake[i + 1 if i % 2 else i - 1]) for i in range(1, bands * n - 1)]
    moved = {first: around_by(slabs[first], first)}
    held = [array(HALO * cols + AHEAD, chans)] + [array(*slabs[0].shape)] * len(others)
    scratch = [pltpu.VMEM((HALO, cols, chans), bf16)]
    sent, *passed = call(edge_kernel, "edge", held, [owner], edges + [slabs[d] for d in others], scratch)
    received = lax.ppermute(sent, ("lat", "lon"), pairs)
    moved |= {d: around_by(x, d) for d, x in zip(others, passed)}
    slabs = [slabs[0]] + [moved[d] for d in range(1, n)]

    head_dim = w_key.shape[1]
    heads = chans // head_dim
    held = [pltpu.VMEM(x.shape, x.dtype) for x in loaded]
    held += [pltpu.VMEM((heads, chans, head_dim), bf16), pltpu.VMEM(w_key.shape, bf16)]
    scratch = [pltpu.VMEM(x.shape, bf16) for x in turned] + [pltpu.SemaphoreType.DMA((len(loaded) + 2,))]
    loaded = call(load_kernel, "load", held, [sent], loaded + turned, scratch, hbm, hbm)
    counts, *convs, w_value, w_out, w_query, w_key = loaded

    def taps(count):
        return pltpu.VMEM((count, cols, 3 * chans), bf16)

    def working(segments):
        blocks, width = segments * rows, heads * size
        return [
            pltpu.VMEM((blocks * size, chans), bf16),
            pltpu.VMEM((blocks, cols, width), jnp.float32),
            pltpu.VMEM((blocks, cols, width), bf16),
            pltpu.VMEM((head_dim, blocks * width), bf16),
        ]

    cells = rows * cols
    result = array(rows * size, chans)
    others = [*others, 0]
    results = {}
    results[first], *held = call(
        functools.partial(main_kernel, first),
        "main",
        [array(rows * size + AHEAD, chans), array(cells, chans), array(cells, chans), array(cells, head_dim), array(head_dim, cells)],
        [owner, counts],
        slabs + [sent, received, *convs, w_key, w_value, w_query, w_out],
        [pltpu.VMEM((rows + 2 * HALO, cols, chans), bf16), taps(rows + 2 * HALO), taps(rows + HALO)] + working(1),
    )
    moved = {first: around_by(results[first], first)}
    rest = call(
        functools.partial(rest_kernel, others),
        "rest",
        [result] * len(others),
        [owner, counts],
        held + [w_query, w_out],
        working(len(others)),
    )
    for d, x in zip(others, rest):
        moved[d] = around_by(x, d) if d else x
    slabs = [moved[d] for d in range(n)]
    scratch = [staging, block, block, pltpu.SemaphoreType.DMA((pieces,))]
    return call(store_kernel, "store", array(*fields.shape), [rotation], slabs, scratch, out_spec=hbm)


def solution(mesh):
    in_specs = (P("lat", "lon", None), P(), P(), P(), P(), P(), P(), P(), P(), P(), P(), P())
    out_specs = P("lat", "lon", None)
    body = functools.partial(on_device, mesh.shape["lat"], mesh.shape["lon"])
    return jax.shard_map(body, mesh=mesh, in_specs=in_specs, out_specs=out_specs, check_vma=False)
```

```python
import functools
import math

import jax
import jax.numpy as jnp
from jax import lax
from jax.experimental import pallas as pl
from jax.experimental.pallas import tpu as pltpu
from jax.sharding import PartitionSpec as P

HALO = 2
LANES = 128
GROUP = 256
AHEAD = 16
VMEM_BYTES = 28 * 1024 * 1024


def group_of(band, shard, n):
    outer = jnp.where((shard == n - 2) == (band % 2 == 0), 0, n - 1)
    return jnp.where(shard < n - 2, shard + 1, outer)


def shard_of(band, group, n):
    if 0 < group < n - 1:
        return group - 1
    return n - 2 if (group == 0) == (band % 2 == 0) else n - 1


def first_held(group, rows):
    return group * rows - HALO * (group % 2)


def turn(quarter, staged, block, out, ready, done):
    size, _, chans = block.shape
    tiles = staged.shape[0]
    pitch = staged.shape[1] // size
    depth = GROUP // size
    pieces = size // depth

    def column(col):
        parts = [staged[t, pl.ds(col, size, stride=pitch), :] for t in range(tiles)]
        return jnp.concatenate(parts, axis=1).astype(jnp.bfloat16)

    def keep(i, row):
        for t in range(tiles):
            staged[t, pl.ds(i * pitch, size), :] = row[:, t * LANES : (t + 1) * LANES]

    @pl.when(quarter == 0)
    def _():
        for g in range(pieces):
            ready(g)
            out[g * depth : (g + 1) * depth] = block[g * depth : (g + 1) * depth]
            done(g)

    @pl.when(quarter == 1)
    def _():
        for i in range(size):
            if i % depth == 0:
                ready(i // depth)
            keep(i, block[i].astype(jnp.float32))
        for i in range(size):
            out[i] = column(size - 1 - i)
            if i % depth == depth - 1:
                done(i // depth)

    @pl.when(quarter == 2)
    def _():
        i = lax.broadcasted_iota(jnp.int32, (GROUP, GROUP), 0)
        j = lax.broadcasted_iota(jnp.int32, (GROUP, GROUP), 1)
        backwards = jnp.where(i + j == GROUP - 1, 1.0, 0.0).astype(jnp.bfloat16)
        for g in reversed(range(pieces)):
            ready(pieces - 1 - g)
            cells = block[size - (g + 1) * depth : size - g * depth].reshape(GROUP, chans)
            turned = jnp.dot(backwards, cells, preferred_element_type=jnp.float32).astype(jnp.bfloat16)
            out[g * depth : (g + 1) * depth] = turned.reshape(depth, size, chans)
            done(g)

    @pl.when(quarter == 3)
    def _():
        for i in range(size):
            if i % depth == 0:
                ready(i // depth)
            keep(size - 1 - i, block[i].astype(jnp.float32))
        for i in range(size):
            out[i] = column(i)
            if i % depth == depth - 1:
                done(i // depth)


def send_kernel(n, rows, rotation_in, owner_in, fields, *rest):
    edges, slabs, (rotation_out, owner_out) = rest[:n], rest[n : 2 * n], rest[2 * n : 2 * n + 2]
    staged, block, upright, rotation, scalar_sems, sems = rest[2 * n + 2 :]
    band = lax.axis_index("lat")
    me = lax.axis_index("lon")
    size, _, chans = fields.shape
    depth = GROUP // size

    def piece(g):
        at = pl.ds(g * depth, depth)
        return pltpu.make_async_copy(fields.at[at], block.at[at], sems.at[g])

    scalars = [
        pltpu.make_async_copy(rotation_in, rotation, scalar_sems.at[0]),
        pltpu.make_async_copy(rotation_in, rotation_out, scalar_sems.at[1]),
        pltpu.make_async_copy(owner_in, owner_out, scalar_sems.at[2]),
    ]
    for copy in scalars:
        copy.start()
    for g in range(size // depth):
        piece(g).start()
    scalars[0].wait()
    turn((4 - rotation[me, band]) % 4, staged, block, upright, lambda g: piece(g).wait(), lambda g: None)
    for d in range(n):
        group = group_of(band, lax.rem(me + d, n), n)
        top, odd = first_held(group, rows), group % 2
        edges[d][...] = upright[pl.ds(top + rows * odd, HALO)].reshape(HALO * size, chans)
        slab = upright[pl.ds(top + HALO * (1 - odd), rows)]
        slabs[d][: rows * size, :] = slab.reshape(rows * size, chans)
        if slabs[d].shape[0] > rows * size:
            slabs[d][rows * size :, :] = jnp.zeros((slabs[d].shape[0] - rows * size, chans), slab.dtype)
    scalars[1].wait()
    scalars[2].wait()


def load_kernel(n, rows, after, *refs):
    del after
    count = (len(refs) - 7) // 2
    direct, (query, key) = refs[:count], refs[count : count + 2]
    loaded, (w_query, w_key) = refs[count + 2 : 2 * count + 2], refs[2 * count + 2 : 2 * count + 4]
    query_in, key_in, sems = refs[2 * count + 4 :]
    heads, _, head_dim = w_query.shape
    pairs = list(zip(direct, loaded)) + [(query, query_in), (key, key_in)]
    copies = [pltpu.make_async_copy(*pair, sems.at[i]) for i, pair in enumerate(pairs)]
    for copy in copies:
        copy.start()
    for copy in copies:
        copy.wait()
    w_key[...] = key_in[...].T
    for h in range(heads):
        w_query[h] = query_in[:, h * head_dim : (h + 1) * head_dim]


def columns_of(segment, size):
    return pl.ds(pl.multiple_of(segment * size, size), size)


def whole_rows(n, count, owner, slabs, out, first):
    band = lax.axis_index("lat")
    me = lax.axis_index("lon")
    size, chans = out.shape[1] // n, out.shape[2]
    for d in range(n):
        segment = owner[lax.rem(me + n - d, n), band]
        piece = slabs[d][: count * size, :].reshape(count, size, chans)
        out[pl.ds(first, count), columns_of(segment, size)] = piece


def edge_kernel(n, rows, owner, *rest):
    del rows
    held, (out, *passed, rows_out) = rest[: 2 * n - 2], rest[2 * n - 2 :]
    _, cols, chans = rows_out.shape
    whole_rows(n, HALO, owner, held[:n], rows_out, 0)
    out[: HALO * cols, :] = rows_out[...].reshape(HALO * cols, chans)
    out[HALO * cols :, :] = jnp.zeros((AHEAD, chans), out.dtype)
    for slab, copy in zip(held[n:], passed):
        copy[...] = slab[...]


def spread(taps, r, row):
    cols, chans = row.shape
    taps[r, :, :chans] = pltpu.roll(row, 1, 0).astype(jnp.bfloat16)
    taps[r, :, chans : 2 * chans] = row.astype(jnp.bfloat16)
    taps[r, :, 2 * chans :] = pltpu.roll(row, cols - 1, 0).astype(jnp.bfloat16)


def convolve(taps, weight, bias, first, count):
    cols, width = taps.shape[1:]
    windows = [taps[first + i : first + i + count].reshape(count * cols, width) for i in range(3)]
    depth = weight.shape[0] * width
    product = jnp.dot(
        jnp.concatenate(windows, axis=1),
        weight[...].reshape(depth, weight.shape[2]),
        preferred_element_type=jnp.float32,
    )
    return product + bias[...]


def silu(x):
    return x / (1.0 + jnp.exp(-x))


def live_count(counts, row):
    inside = (row >= 0) & (row < counts.shape[0])
    return jnp.where(inside, counts[jnp.clip(row, 0, counts.shape[0] - 1)], 0)


def by_last(a, b):
    return lax.dot_general(a, b, (((1,), (1,)), ((), ())), preferred_element_type=jnp.float32)


def attend(segments, limits, mixed, normed, keys, values, w_query, w_out, results, here, scores, expo, turned):
    rows, chans = len(limits), mixed.shape[1]
    size = here.shape[0] // (rows * len(segments))
    heads, _, head_dim = w_query.shape
    cols = mixed.shape[0] // rows
    width = heads * size
    blocks = [(s, r) for s in range(len(segments)) for r in range(rows)]

    def cells(s, r):
        return columns_of(segments[s] + r * (cols // size), size)

    for b, (s, r) in enumerate(blocks):
        here[b * size : (b + 1) * size, :] = normed[cells(s, r), :]
    queries = [jnp.dot(here[...], w_query[h], preferred_element_type=jnp.float32) for h in range(heads)]
    queries = [query.astype(jnp.bfloat16) for query in queries]
    for b, (s, r) in enumerate(blocks):
        own = jnp.concatenate([query[b * size : (b + 1) * size] for query in queries], axis=0)
        scores[b] = by_last(keys[r * cols : (r + 1) * cols, :], own)
    key_at = lax.broadcasted_iota(jnp.int32, (cols, width), 0)
    scale = math.log2(math.e) / head_dim**0.5
    shares = []
    for b, (s, r) in enumerate(blocks):
        part = jnp.where(key_at < limits[r], scores[b], -jnp.inf)
        part = jnp.exp2((part - jnp.max(part, axis=0, keepdims=True)) * scale)
        shares.append(1.0 / jnp.sum(part, axis=0, keepdims=True))
        expo[b] = part.astype(jnp.bfloat16)
    for b, (s, r) in enumerate(blocks):
        summed = jnp.dot(values[:, r * cols : (r + 1) * cols], expo[b], preferred_element_type=jnp.float32)
        turned[:, b * width : (b + 1) * width] = (summed * shares[b]).astype(jnp.bfloat16)
    attended = turned[...].T
    update = jnp.zeros(here.shape, jnp.float32)
    for h in range(heads):
        starts = [b * width + h * size for b in range(len(blocks))]
        part = jnp.concatenate([attended[start : start + size] for start in starts], axis=0)
        weight = w_out[h * head_dim : (h + 1) * head_dim, :]
        update = update + jnp.dot(part, weight, preferred_element_type=jnp.float32)
    for b, (s, r) in enumerate(blocks):
        cell = segments[s] * size + lax.broadcasted_iota(jnp.int32, (size, chans), 0)
        part = jnp.where(cell < limits[r], update[b * size : (b + 1) * size], 0.0)
        results[s][r * size : (r + 1) * size, :] = (mixed[cells(s, r), :].astype(jnp.float32) + part).astype(jnp.bfloat16)


def main_kernel(first, n, rows, owner, counts, *rest):
    slabs, sent, received = rest[:n], rest[n], rest[n + 1]
    w_conv1, b_conv1, w_conv2, b_conv2, w_key, w_value, w_query, w_out = rest[n + 2 : n + 10]
    result, mixed, normed, keys, values = rest[n + 10 : n + 15]
    grid, taps, acts, *scratch = rest[n + 15 :]
    band = lax.axis_index("lat")
    me = lax.axis_index("lon")
    group = group_of(band, me, n)
    odd = group % 2
    cols, chans = grid.shape[1:]
    edge = (HALO, cols, chans)
    cell = lax.broadcasted_iota(jnp.int32, (cols, chans), 0)
    first_row = band * (rows * n) + group * rows
    whole_rows(n, rows, owner, slabs, grid, 2 * HALO * (1 - odd))
    grid[pl.ds(HALO + (rows - HALO) * odd, HALO)] = sent[: HALO * cols, :].reshape(edge)
    grid[pl.ds((rows + HALO) * odd, HALO)] = received[: HALO * cols, :].reshape(edge)
    limits = [live_count(counts, first_row - 1 + r) for r in range(rows + HALO)]
    half = (rows + HALO) // 2
    spans = [(0, half), (half, rows + HALO)]
    done = 0
    convolved = []
    for low, high in spans:
        for r in range(done, high + HALO):
            spread(taps, r, grid[r].astype(jnp.float32))
        done = high + HALO
        convolved.append(convolve(taps, w_conv1, b_conv1, low, high - low))
    low = 0
    for (start, stop), first_conv in zip(spans, convolved):
        act = silu(first_conv)
        for r in range(start, stop):
            at = slice((r - start) * cols, (r - start + 1) * cols)
            spread(acts, r, jnp.where(cell < limits[r], act[at], 0.0))
        high = stop - HALO
        if high <= low:
            continue
        second = convolve(acts, w_conv2, b_conv2, low, high - low)
        for r in range(low, high):
            here = grid[r + HALO].astype(jnp.float32) + second[(r - low) * cols : (r - low + 1) * cols]
            here = jnp.where(cell < limits[r + 1], here, 0.0)
            mixed[r * cols : (r + 1) * cols, :] = here.astype(jnp.bfloat16)
        low = high
    limits = limits[1 : rows + 1]
    flat = mixed[...].astype(jnp.float32)
    scaled = (flat * lax.rsqrt(jnp.mean(flat * flat, axis=1, keepdims=True) + 1e-06)).astype(jnp.bfloat16)
    normed[...] = scaled
    keys[...] = jnp.dot(scaled, w_key[...], preferred_element_type=jnp.float32).astype(jnp.bfloat16)
    values[...] = by_last(w_value[...], scaled).astype(jnp.bfloat16)
    result[rows * (cols // n) :, :] = jnp.zeros((AHEAD, chans), result.dtype)
    segments = [owner[lax.rem(me + first, n), band]]
    attend(segments, limits, mixed, normed, keys, values, w_query, w_out, [result], *scratch)


def rest_kernel(moves, n, rows, owner, counts, *rest):
    mixed, normed, keys, values, w_query, w_out = rest[:6]
    results, scratch = rest[6 : 6 + len(moves)], rest[6 + len(moves) :]
    band = lax.axis_index("lat")
    me = lax.axis_index("lon")
    first_row = band * (rows * n) + group_of(band, me, n) * rows
    limits = [counts[first_row + r] for r in range(rows)]
    segments = [owner[lax.rem(me + d, n), band] for d in moves]
    attend(segments, limits, mixed, normed, keys, values, w_query, w_out, results, *scratch)


def store_kernel(n, rows, rotation, *rest):
    slabs, (out, staged, upright, turned, sems) = rest[:n], rest[n:]
    band = lax.axis_index("lat")
    me = lax.axis_index("lon")
    depth = GROUP // out.shape[0]
    pieces = out.shape[0] // depth
    for d in range(n):
        top = group_of(band, lax.rem(me + n - d, n), n) * rows
        upright[pl.ds(top, rows)] = slabs[d][: rows * out.shape[0], :].reshape(rows, *out.shape[1:])

    def piece(g):
        at = pl.ds(g * depth, depth)
        return pltpu.make_async_copy(turned.at[at], out.at[at], sems.at[g])

    turn(rotation[me, band] % 4, staged, upright, turned, lambda g: None, lambda g: piece(g).start())
    for g in range(pieces):
        piece(g).wait()


def on_device(
    bands,
    n,
    fields,
    w_conv1,
    b_conv1,
    w_conv2,
    b_conv2,
    w_query,
    w_key,
    w_value,
    w_out,
    rotation,
    owner,
    counts,
):
    size, _, chans = fields.shape
    rows = size // n
    inner = rows - HALO
    cols = size * n
    bf16 = jnp.bfloat16
    smem = pl.BlockSpec(memory_space=pltpu.SMEM)
    vmem = pl.BlockSpec(memory_space=pltpu.VMEM)
    hbm = pl.BlockSpec(memory_space=pltpu.HBM)
    params = pltpu.CompilerParams(vmem_limit_bytes=VMEM_BYTES)
    pieces = size * size // GROUP

    def call(kernel, name, out, scalars, arrays, scratch, array_spec=vmem, scalar_spec=smem, out_spec=vmem):
        many = isinstance(out, list)
        return pl.pallas_call(
            functools.partial(kernel, n, rows),
            out_shape=out,
            in_specs=[scalar_spec] * len(scalars) + [array_spec] * len(arrays),
            out_specs=[out_spec] * len(out) if many else out_spec,
            scratch_shapes=scratch,
            compiler_params=params,
            name=name,
        )(*scalars, *arrays)

    def array(*shape):
        return jax.ShapeDtypeStruct(shape, bf16)

    order = sorted(range(1, n), key=lambda d: -min(d, n - d))

    def around_by(x, d):
        return lax.ppermute(x, "lon", [(i, (i + d) % n) for i in range(n)])

    def around(parts):
        moved = {d: around_by(parts[d], d) for d in order}
        return [parts[0]] + [moved[d] for d in range(1, n)]

    def in_hbm(x):
        return pltpu.with_memory_space_constraint(x, pltpu.HBM)

    rotation, owner = in_hbm(rotation.T), in_hbm(owner.T)
    loaded = [counts]
    loaded += [w_conv1.reshape(3, 3 * chans, chans), b_conv1.reshape(1, chans)]
    loaded += [w_conv2.reshape(3, 3 * chans, chans), b_conv2.reshape(1, chans), w_value.T, w_out]
    loaded = [in_hbm(x) for x in loaded]
    turned = [in_hbm(x) for x in (w_query, w_key.T)]
    staging = pltpu.VMEM((chans // LANES, size * (size + 8), LANES), jnp.float32)
    block = pltpu.VMEM((size, size, chans), bf16)

    first, *others = order
    slabs = [array(HALO * size, chans)] * n
    slabs += [array(rows * size + (2 * AHEAD if d == first else 0), chans) for d in range(n)]
    scratch = [staging, block, block, pltpu.SMEM(rotation.shape, rotation.dtype)]
    scratch += [pltpu.SemaphoreType.DMA((3,)), pltpu.SemaphoreType.DMA((pieces,))]
    held = slabs + [pltpu.VMEM(x.shape, x.dtype) for x in (rotation, owner)]
    *slabs, rotation, owner = call(send_kernel, "send", held, [rotation, owner], [in_hbm(fields)], scratch, hbm, hbm)
    edges = around(slabs[:n])
    slabs = slabs[n:]

    snake = [a * n + shard_of(a, g, n) for a in range(bands) for g in range(n)]
    pairs = [(snake[i], snake[i + 1 if i % 2 else i - 1]) for i in range(1, bands * n - 1)]
    moved = {first: around_by(slabs[first], first)}
    held = [array(HALO * cols + AHEAD, chans)] + [array(*slabs[0].shape)] * len(others)
    scratch = [pltpu.VMEM((HALO, cols, chans), bf16)]
    sent, *passed = call(edge_kernel, "edge", held, [owner], edges + [slabs[d] for d in others], scratch)
    received = lax.ppermute(sent, ("lat", "lon"), pairs)
    moved |= {d: around_by(x, d) for d, x in zip(others, passed)}
    slabs = [slabs[0]] + [moved[d] for d in range(1, n)]

    head_dim = w_key.shape[1]
    heads = chans // head_dim
    held = [pltpu.VMEM(x.shape, x.dtype) for x in loaded]
    held += [pltpu.VMEM((heads, chans, head_dim), bf16), pltpu.VMEM(w_key.shape, bf16)]
    scratch = [pltpu.VMEM(x.shape, bf16) for x in turned] + [pltpu.SemaphoreType.DMA((len(loaded) + 2,))]
    loaded = call(load_kernel, "load", held, [sent], loaded + turned, scratch, hbm, hbm)
    counts, *convs, w_value, w_out, w_query, w_key = loaded

    def taps(count):
        return pltpu.VMEM((count, cols, 3 * chans), bf16)

    def working(segments):
        blocks, width = segments * rows, heads * size
        return [
            pltpu.VMEM((blocks * size, chans), bf16),
            pltpu.VMEM((blocks, cols, width), jnp.float32),
            pltpu.VMEM((blocks, cols, width), bf16),
            pltpu.VMEM((head_dim, blocks * width), bf16),
        ]

    cells = rows * cols
    result = array(rows * size, chans)
    others = [*others, 0]
    results = {}
    results[first], *held = call(
        functools.partial(main_kernel, first),
        "main",
        [array(rows * size + AHEAD, chans), array(cells, chans), array(cells, chans), array(cells, head_dim), array(head_dim, cells)],
        [owner, counts],
        slabs + [sent, received, *convs, w_key, w_value, w_query, w_out],
        [pltpu.VMEM((rows + 2 * HALO, cols, chans), bf16), taps(rows + 2 * HALO), taps(rows + HALO)] + working(1),
    )
    moved = {first: around_by(results[first], first)}
    rest = call(
        functools.partial(rest_kernel, others),
        "rest",
        [result] * len(others),
        [owner, counts],
        held + [w_query, w_out],
        working(len(others)),
    )
    for d, x in zip(others, rest):
        moved[d] = around_by(x, d) if d else x
    slabs = [moved[d] for d in range(n)]
    scratch = [staging, block, block, pltpu.SemaphoreType.DMA((pieces,))]
    return call(store_kernel, "store", array(*fields.shape), [rotation], slabs, scratch, out_spec=hbm)


def solution(mesh):
    in_specs = (P("lat", "lon", None), P(), P(), P(), P(), P(), P(), P(), P(), P(), P(), P())
    out_specs = P("lat", "lon", None)
    body = functools.partial(on_device, mesh.shape["lat"], mesh.shape["lon"])
    return jax.shard_map(body, mesh=mesh, in_specs=in_specs, out_specs=out_specs, check_vma=False)
```

```python
import functools
import math

import jax
import jax.numpy as jnp
from jax import lax
from jax.experimental import pallas as pl
from jax.experimental.pallas import tpu as pltpu
from jax.sharding import PartitionSpec as P

HALO = 2
LANES = 128
GROUP = 256
CHUNKS = 3
AHEAD = 16
VMEM_BYTES = 28 * 1024 * 1024


def group_of(band, shard, n):
    outer = jnp.where((shard == n - 2) == (band % 2 == 0), 0, n - 1)
    return jnp.where(shard < n - 2, shard + 1, outer)


def shard_of(band, group, n):
    if 0 < group < n - 1:
        return group - 1
    return n - 2 if (group == 0) == (band % 2 == 0) else n - 1


def first_held(group, rows):
    return group * rows - HALO * (group % 2)


def turn(quarter, staged, block, out, ready, done):
    size, _, chans = block.shape
    tiles = staged.shape[0]
    pitch = staged.shape[1] // size
    depth = GROUP // size
    pieces = size // depth

    def column(col):
        parts = [staged[t, pl.ds(col, size, stride=pitch), :] for t in range(tiles)]
        return jnp.concatenate(parts, axis=1).astype(jnp.bfloat16)

    def keep(i, row):
        for t in range(tiles):
            staged[t, pl.ds(i * pitch, size), :] = row[:, t * LANES : (t + 1) * LANES]

    @pl.when(quarter == 0)
    def _():
        for g in range(pieces):
            ready(g)
            out[g * depth : (g + 1) * depth] = block[g * depth : (g + 1) * depth]
            done(g)

    @pl.when(quarter == 1)
    def _():
        for i in range(size):
            if i % depth == 0:
                ready(i // depth)
            keep(i, block[i].astype(jnp.float32))
        for i in range(size):
            out[i] = column(size - 1 - i)
            if i % depth == depth - 1:
                done(i // depth)

    @pl.when(quarter == 2)
    def _():
        i = lax.broadcasted_iota(jnp.int32, (GROUP, GROUP), 0)
        j = lax.broadcasted_iota(jnp.int32, (GROUP, GROUP), 1)
        backwards = jnp.where(i + j == GROUP - 1, 1.0, 0.0).astype(jnp.bfloat16)
        for g in reversed(range(pieces)):
            ready(pieces - 1 - g)
            cells = block[size - (g + 1) * depth : size - g * depth].reshape(GROUP, chans)
            turned = jnp.dot(backwards, cells, preferred_element_type=jnp.float32).astype(jnp.bfloat16)
            out[g * depth : (g + 1) * depth] = turned.reshape(depth, size, chans)
            done(g)

    @pl.when(quarter == 3)
    def _():
        for i in range(size):
            if i % depth == 0:
                ready(i // depth)
            keep(size - 1 - i, block[i].astype(jnp.float32))
        for i in range(size):
            out[i] = column(i)
            if i % depth == depth - 1:
                done(i // depth)


def send_kernel(n, rows, rotation_in, owner_in, fields, *rest):
    edges, slabs, (rotation_out, owner_out) = rest[:n], rest[n : 2 * n], rest[2 * n : 2 * n + 2]
    staged, block, upright, rotation, scalar_sems, sems = rest[2 * n + 2 :]
    band = lax.axis_index("lat")
    me = lax.axis_index("lon")
    depth = GROUP // fields.shape[0]

    def piece(g):
        at = pl.ds(g * depth, depth)
        return pltpu.make_async_copy(fields.at[at], block.at[at], sems.at[g])

    scalars = [
        pltpu.make_async_copy(rotation_in, rotation, scalar_sems.at[0]),
        pltpu.make_async_copy(rotation_in, rotation_out, scalar_sems.at[1]),
        pltpu.make_async_copy(owner_in, owner_out, scalar_sems.at[2]),
    ]
    for copy in scalars:
        copy.start()
    for g in range(fields.shape[0] // depth):
        piece(g).start()
    scalars[0].wait()
    turn((4 - rotation[me, band]) % 4, staged, block, upright, lambda g: piece(g).wait(), lambda g: None)
    for d in range(n):
        group = group_of(band, lax.rem(me + d, n), n)
        top, odd = first_held(group, rows), group % 2
        edges[d][...] = upright[pl.ds(top + rows * odd, HALO)]
        slabs[d][...] = upright[pl.ds(top + HALO * (1 - odd), rows)]
    scalars[1].wait()
    scalars[2].wait()


def load_kernel(n, rows, after, *refs):
    del after
    count = (len(refs) - 7) // 2
    direct, (query, key) = refs[:count], refs[count : count + 2]
    loaded, (w_query, w_key) = refs[count + 2 : 2 * count + 2], refs[2 * count + 2 : 2 * count + 4]
    query_in, key_in, sems = refs[2 * count + 4 :]
    heads, _, head_dim = w_query.shape
    pairs = list(zip(direct, loaded)) + [(query, query_in), (key, key_in)]
    copies = [pltpu.make_async_copy(*pair, sems.at[i]) for i, pair in enumerate(pairs)]
    for copy in copies:
        copy.start()
    for copy in copies:
        copy.wait()
    w_key[...] = key_in[...].T
    for h in range(heads):
        w_query[h] = query_in[:, h * head_dim : (h + 1) * head_dim]


def columns_of(segment, size):
    return pl.ds(pl.multiple_of(segment * size, size), size)


def whole_rows(n, owner, slabs, out, first):
    band = lax.axis_index("lat")
    me = lax.axis_index("lon")
    count, size = slabs[0].shape[:2]
    for d in range(n):
        segment = owner[lax.rem(me + n - d, n), band]
        out[pl.ds(first, count), columns_of(segment, size)] = slabs[d][...]


def edge_kernel(n, rows, owner, *rest):
    del rows
    whole_rows(n, owner, rest[:n], rest[n], 0)


def spread(taps, r, row):
    cols, chans = row.shape
    taps[r, :, :chans] = pltpu.roll(row, 1, 0).astype(jnp.bfloat16)
    taps[r, :, chans : 2 * chans] = row.astype(jnp.bfloat16)
    taps[r, :, 2 * chans :] = pltpu.roll(row, cols - 1, 0).astype(jnp.bfloat16)


def convolve(taps, weight, bias, first, count):
    cols, width = taps.shape[1:]
    windows = [taps[first + i : first + i + count].reshape(count * cols, width) for i in range(3)]
    depth = weight.shape[0] * width
    product = jnp.dot(
        jnp.concatenate(windows, axis=1),
        weight[...].reshape(depth, weight.shape[2]),
        preferred_element_type=jnp.float32,
    )
    return product + bias[...]


def silu(x):
    return x / (1.0 + jnp.exp(-x))


def live_count(counts, row):
    inside = (row >= 0) & (row < counts.shape[0])
    return jnp.where(inside, counts[jnp.clip(row, 0, counts.shape[0] - 1)], 0)


def by_last(a, b):
    return lax.dot_general(a, b, (((1,), (1,)), ((), ())), preferred_element_type=jnp.float32)


def attend(segments, limits, mixed, normed, keys, values, w_query, w_out, results, here, scores, expo, turned):
    rows, chans = len(limits), mixed.shape[1]
    size = here.shape[0] // (rows * len(segments))
    heads, _, head_dim = w_query.shape
    cols = mixed.shape[0] // rows
    width = heads * size
    blocks = [(s, r) for s in range(len(segments)) for r in range(rows)]

    def cells(s, r):
        return columns_of(segments[s] + r * (cols // size), size)

    for b, (s, r) in enumerate(blocks):
        here[b * size : (b + 1) * size, :] = normed[cells(s, r), :]
    queries = [jnp.dot(here[...], w_query[h], preferred_element_type=jnp.float32) for h in range(heads)]
    queries = [query.astype(jnp.bfloat16) for query in queries]
    for b, (s, r) in enumerate(blocks):
        own = jnp.concatenate([query[b * size : (b + 1) * size] for query in queries], axis=0)
        scores[b] = by_last(keys[r * cols : (r + 1) * cols, :], own)
    key_at = lax.broadcasted_iota(jnp.int32, (cols, width), 0)
    scale = math.log2(math.e) / head_dim**0.5
    shares = []
    for b, (s, r) in enumerate(blocks):
        part = jnp.where(key_at < limits[r], scores[b], -jnp.inf)
        part = jnp.exp2((part - jnp.max(part, axis=0, keepdims=True)) * scale)
        shares.append(1.0 / jnp.sum(part, axis=0, keepdims=True))
        expo[b] = part.astype(jnp.bfloat16)
    for b, (s, r) in enumerate(blocks):
        summed = jnp.dot(values[:, r * cols : (r + 1) * cols], expo[b], preferred_element_type=jnp.float32)
        turned[:, b * width : (b + 1) * width] = (summed * shares[b]).astype(jnp.bfloat16)
    attended = turned[...].T
    update = jnp.zeros(here.shape, jnp.float32)
    for h in range(heads):
        starts = [b * width + h * size for b in range(len(blocks))]
        part = jnp.concatenate([attended[start : start + size] for start in starts], axis=0)
        weight = w_out[h * head_dim : (h + 1) * head_dim, :]
        update = update + jnp.dot(part, weight, preferred_element_type=jnp.float32)
    for b, (s, r) in enumerate(blocks):
        cell = segments[s] * size + lax.broadcasted_iota(jnp.int32, (size, chans), 0)
        part = jnp.where(cell < limits[r], update[b * size : (b + 1) * size], 0.0)
        results[s][r * size : (r + 1) * size, :] = (mixed[cells(s, r), :].astype(jnp.float32) + part).astype(jnp.bfloat16)


def main_kernel(first, n, rows, owner, counts, *rest):
    slabs, sent, received = rest[:n], rest[n], rest[n + 1]
    w_conv1, b_conv1, w_conv2, b_conv2, w_key, w_value, w_query, w_out = rest[n + 2 : n + 10]
    result, mixed, normed, keys, values = rest[n + 10 : n + 15]
    grid, taps, acts, *scratch = rest[n + 15 :]
    band = lax.axis_index("lat")
    me = lax.axis_index("lon")
    group = group_of(band, me, n)
    odd = group % 2
    cols, chans = sent.shape[1:]
    cell = lax.broadcasted_iota(jnp.int32, (cols, chans), 0)
    first_row = band * (rows * n) + group * rows
    whole_rows(n, owner, slabs, grid, 2 * HALO * (1 - odd))
    grid[pl.ds(HALO + (rows - HALO) * odd, HALO)] = sent[...]
    grid[pl.ds((rows + HALO) * odd, HALO)] = received[...]
    limits = [live_count(counts, first_row - 1 + r) for r in range(rows + HALO)]
    total = rows + HALO
    chunks = min(CHUNKS, total // HALO)
    cuts = [-(-total * i // chunks) for i in range(chunks + 1)]
    done = low = 0
    for start, stop in zip(cuts, cuts[1:]):
        for r in range(done, stop + HALO):
            spread(taps, r, grid[r].astype(jnp.float32))
        done = stop + HALO
        act = silu(convolve(taps, w_conv1, b_conv1, start, stop - start))
        for r in range(start, stop):
            at = slice((r - start) * cols, (r - start + 1) * cols)
            spread(acts, r, jnp.where(cell < limits[r], act[at], 0.0))
        high = stop - HALO
        if high <= low:
            continue
        second = convolve(acts, w_conv2, b_conv2, low, high - low)
        for r in range(low, high):
            here = grid[r + HALO].astype(jnp.float32) + second[(r - low) * cols : (r - low + 1) * cols]
            here = jnp.where(cell < limits[r + 1], here, 0.0)
            mixed[r * cols : (r + 1) * cols, :] = here.astype(jnp.bfloat16)
        at = slice(low * cols, high * cols)
        flat = mixed[at, :].astype(jnp.float32)
        scaled = (flat * lax.rsqrt(jnp.mean(flat * flat, axis=1, keepdims=True) + 1e-06)).astype(jnp.bfloat16)
        normed[at, :] = scaled
        keys[at, :] = jnp.dot(scaled, w_key[...], preferred_element_type=jnp.float32).astype(jnp.bfloat16)
        values[:, at] = by_last(w_value[...], scaled).astype(jnp.bfloat16)
        low = high
    limits = limits[1 : rows + 1]
    result[rows * (cols // n) :, :] = jnp.zeros((AHEAD, chans), result.dtype)
    segments = [owner[lax.rem(me + first, n), band]]
    attend(segments, limits, mixed, normed, keys, values, w_query, w_out, [result], *scratch)


def rest_kernel(moves, n, rows, owner, counts, *rest):
    mixed, normed, keys, values, w_query, w_out = rest[:6]
    results, scratch = rest[6 : 6 + len(moves)], rest[6 + len(moves) :]
    band = lax.axis_index("lat")
    me = lax.axis_index("lon")
    first_row = band * (rows * n) + group_of(band, me, n) * rows
    limits = [counts[first_row + r] for r in range(rows)]
    segments = [owner[lax.rem(me + d, n), band] for d in moves]
    attend(segments, limits, mixed, normed, keys, values, w_query, w_out, results, *scratch)


def store_kernel(n, rows, rotation, *rest):
    slabs, (out, staged, upright, turned, sems) = rest[:n], rest[n:]
    band = lax.axis_index("lat")
    me = lax.axis_index("lon")
    depth = GROUP // out.shape[0]
    pieces = out.shape[0] // depth
    for d in range(n):
        top = group_of(band, lax.rem(me + n - d, n), n) * rows
        upright[pl.ds(top, rows)] = slabs[d][: rows * out.shape[0], :].reshape(rows, *out.shape[1:])

    def piece(g):
        at = pl.ds(g * depth, depth)
        return pltpu.make_async_copy(turned.at[at], out.at[at], sems.at[g])

    turn(rotation[me, band] % 4, staged, upright, turned, lambda g: None, lambda g: piece(g).start())
    for g in range(pieces):
        piece(g).wait()


def on_device(
    bands,
    n,
    fields,
    w_conv1,
    b_conv1,
    w_conv2,
    b_conv2,
    w_query,
    w_key,
    w_value,
    w_out,
    rotation,
    owner,
    counts,
):
    size, _, chans = fields.shape
    rows = size // n
    inner = rows - HALO
    cols = size * n
    bf16 = jnp.bfloat16
    smem = pl.BlockSpec(memory_space=pltpu.SMEM)
    vmem = pl.BlockSpec(memory_space=pltpu.VMEM)
    hbm = pl.BlockSpec(memory_space=pltpu.HBM)
    params = pltpu.CompilerParams(vmem_limit_bytes=VMEM_BYTES)
    pieces = size * size // GROUP

    def call(kernel, name, out, scalars, arrays, scratch, array_spec=vmem, scalar_spec=smem, out_spec=vmem):
        many = isinstance(out, list)
        return pl.pallas_call(
            functools.partial(kernel, n, rows),
            out_shape=out,
            in_specs=[scalar_spec] * len(scalars) + [array_spec] * len(arrays),
            out_specs=[out_spec] * len(out) if many else out_spec,
            scratch_shapes=scratch,
            compiler_params=params,
            name=name,
        )(*scalars, *arrays)

    def array(*shape):
        return jax.ShapeDtypeStruct(shape, bf16)

    order = sorted(range(1, n), key=lambda d: -min(d, n - d))

    def around_by(x, d):
        return lax.ppermute(x, "lon", [(i, (i + d) % n) for i in range(n)])

    def around(parts):
        moved = {d: around_by(parts[d], d) for d in order}
        return [parts[0]] + [moved[d] for d in range(1, n)]

    def in_hbm(x):
        return pltpu.with_memory_space_constraint(x, pltpu.HBM)

    rotation, owner = in_hbm(rotation.T), in_hbm(owner.T)
    loaded = [counts]
    loaded += [w_conv1.reshape(3, 3 * chans, chans), b_conv1.reshape(1, chans)]
    loaded += [w_conv2.reshape(3, 3 * chans, chans), b_conv2.reshape(1, chans), w_value.T, w_out]
    loaded = [in_hbm(x) for x in loaded]
    turned = [in_hbm(x) for x in (w_query, w_key.T)]
    staging = pltpu.VMEM((chans // LANES, size * (size + 8), LANES), jnp.float32)
    block = pltpu.VMEM((size, size, chans), bf16)

    slabs = [array(HALO, size, chans)] * n + [array(rows, size, chans)] * n
    scratch = [staging, block, block, pltpu.SMEM(rotation.shape, rotation.dtype)]
    scratch += [pltpu.SemaphoreType.DMA((3,)), pltpu.SemaphoreType.DMA((pieces,))]
    held = slabs + [pltpu.VMEM(x.shape, x.dtype) for x in (rotation, owner)]
    *slabs, rotation, owner = call(send_kernel, "send", held, [rotation, owner], [in_hbm(fields)], scratch, hbm, hbm)
    edges = around(slabs[:n])
    slabs = around(slabs[n:])

    snake = [a * n + shard_of(a, g, n) for a in range(bands) for g in range(n)]
    pairs = [(snake[i], snake[i + 1 if i % 2 else i - 1]) for i in range(1, bands * n - 1)]
    sent = call(edge_kernel, "edge", array(HALO, cols, chans), [owner], edges, [])
    received = lax.ppermute(sent, ("lat", "lon"), pairs)

    head_dim = w_key.shape[1]
    heads = chans // head_dim
    held = [pltpu.VMEM(x.shape, x.dtype) for x in loaded]
    held += [pltpu.VMEM((heads, chans, head_dim), bf16), pltpu.VMEM(w_key.shape, bf16)]
    scratch = [pltpu.VMEM(x.shape, bf16) for x in turned] + [pltpu.SemaphoreType.DMA((len(loaded) + 2,))]
    loaded = call(load_kernel, "load", held, [sent], loaded + turned, scratch, hbm, hbm)
    counts, *convs, w_value, w_out, w_query, w_key = loaded

    def taps(count):
        return pltpu.VMEM((count, cols, 3 * chans), bf16)

    def working(segments):
        blocks, width = segments * rows, heads * size
        return [
            pltpu.VMEM((blocks * size, chans), bf16),
            pltpu.VMEM((blocks, cols, width), jnp.float32),
            pltpu.VMEM((blocks, cols, width), bf16),
            pltpu.VMEM((head_dim, blocks * width), bf16),
        ]

    cells = rows * cols
    result = array(rows * size, chans)
    first, *others = [*order, 0]
    results = {}
    results[first], *held = call(
        functools.partial(main_kernel, first),
        "main",
        [array(rows * size + AHEAD, chans), array(cells, chans), array(cells, chans), array(cells, head_dim), array(head_dim, cells)],
        [owner, counts],
        slabs + [sent, received, *convs, w_key, w_value, w_query, w_out],
        [pltpu.VMEM((rows + 2 * HALO, cols, chans), bf16), taps(rows + 2 * HALO), taps(rows + HALO)] + working(1),
    )
    moved = {first: around_by(results[first], first)}
    rest = call(
        functools.partial(rest_kernel, others),
        "rest",
        [result] * len(others),
        [owner, counts],
        held + [w_query, w_out],
        working(len(others)),
    )
    for d, x in zip(others, rest):
        moved[d] = around_by(x, d) if d else x
    slabs = [moved[d] for d in range(n)]
    scratch = [staging, block, block, pltpu.SemaphoreType.DMA((pieces,))]
    return call(store_kernel, "store", array(*fields.shape), [rotation], slabs, scratch, out_spec=hbm)


def solution(mesh):
    in_specs = (P("lat", "lon", None), P(), P(), P(), P(), P(), P(), P(), P(), P(), P(), P())
    out_specs = P("lat", "lon", None)
    body = functools.partial(on_device, mesh.shape["lat"], mesh.shape["lon"])
    return jax.shard_map(body, mesh=mesh, in_specs=in_specs, out_specs=out_specs, check_vma=False)
```

```python
import functools
import math

import jax
import jax.numpy as jnp
from jax import lax
from jax.experimental import pallas as pl
from jax.experimental.pallas import tpu as pltpu
from jax.sharding import PartitionSpec as P

HALO = 2
LANES = 128
GROUP = 256
AHEAD = 16
VMEM_BYTES = 28 * 1024 * 1024


def group_of(band, shard, n):
    outer = jnp.where((shard == n - 2) == (band % 2 == 0), 0, n - 1)
    return jnp.where(shard < n - 2, shard + 1, outer)


def shard_of(band, group, n):
    if 0 < group < n - 1:
        return group - 1
    return n - 2 if (group == 0) == (band % 2 == 0) else n - 1


def first_held(group, rows):
    return group * rows - HALO * (group % 2)


def turn(quarter, staged, block, out, ready, done):
    size, _, chans = block.shape
    tiles = staged.shape[0]
    pitch = staged.shape[1] // size
    depth = GROUP // size
    pieces = size // depth

    def column(col):
        parts = [staged[t, pl.ds(col, size, stride=pitch), :] for t in range(tiles)]
        return jnp.concatenate(parts, axis=1).astype(jnp.bfloat16)

    def keep(i, row):
        for t in range(tiles):
            staged[t, pl.ds(i * pitch, size), :] = row[:, t * LANES : (t + 1) * LANES]

    @pl.when(quarter == 0)
    def _():
        for g in range(pieces):
            ready(g)
            out[g * depth : (g + 1) * depth] = block[g * depth : (g + 1) * depth]
            done(g)

    @pl.when(quarter == 1)
    def _():
        for i in range(size):
            if i % depth == 0:
                ready(i // depth)
            keep(i, block[i].astype(jnp.float32))
        for i in range(size):
            out[i] = column(size - 1 - i)
            if i % depth == depth - 1:
                done(i // depth)

    @pl.when(quarter == 2)
    def _():
        i = lax.broadcasted_iota(jnp.int32, (GROUP, GROUP), 0)
        j = lax.broadcasted_iota(jnp.int32, (GROUP, GROUP), 1)
        backwards = jnp.where(i + j == GROUP - 1, 1.0, 0.0).astype(jnp.bfloat16)
        for g in reversed(range(pieces)):
            ready(pieces - 1 - g)
            cells = block[size - (g + 1) * depth : size - g * depth].reshape(GROUP, chans)
            turned = jnp.dot(backwards, cells, preferred_element_type=jnp.float32).astype(jnp.bfloat16)
            out[g * depth : (g + 1) * depth] = turned.reshape(depth, size, chans)
            done(g)

    @pl.when(quarter == 3)
    def _():
        for i in range(size):
            if i % depth == 0:
                ready(i // depth)
            keep(size - 1 - i, block[i].astype(jnp.float32))
        for i in range(size):
            out[i] = column(i)
            if i % depth == depth - 1:
                done(i // depth)


def send_kernel(n, rows, rotation_in, owner_in, fields, *rest):
    edges, slabs, (rotation_out, owner_out) = rest[:n], rest[n : 2 * n], rest[2 * n : 2 * n + 2]
    staged, block, upright, rotation, scalar_sems, sems = rest[2 * n + 2 :]
    band = lax.axis_index("lat")
    me = lax.axis_index("lon")
    depth = GROUP // fields.shape[0]

    def piece(g):
        at = pl.ds(g * depth, depth)
        return pltpu.make_async_copy(fields.at[at], block.at[at], sems.at[g])

    scalars = [
        pltpu.make_async_copy(rotation_in, rotation, scalar_sems.at[0]),
        pltpu.make_async_copy(rotation_in, rotation_out, scalar_sems.at[1]),
        pltpu.make_async_copy(owner_in, owner_out, scalar_sems.at[2]),
    ]
    for copy in scalars:
        copy.start()
    for g in range(fields.shape[0] // depth):
        piece(g).start()
    scalars[0].wait()
    turn((4 - rotation[me, band]) % 4, staged, block, upright, lambda g: piece(g).wait(), lambda g: None)
    for d in range(n):
        group = group_of(band, lax.rem(me + d, n), n)
        top, odd = first_held(group, rows), group % 2
        edges[d][...] = upright[pl.ds(top + rows * odd, HALO)]
        slabs[d][...] = upright[pl.ds(top + HALO * (1 - odd), rows)]
    scalars[1].wait()
    scalars[2].wait()


def load_kernel(n, rows, after, *refs):
    del after
    count = (len(refs) - 7) // 2
    direct, (query, key) = refs[:count], refs[count : count + 2]
    loaded, (w_query, w_key) = refs[count + 2 : 2 * count + 2], refs[2 * count + 2 : 2 * count + 4]
    query_in, key_in, sems = refs[2 * count + 4 :]
    heads, _, head_dim = w_query.shape
    pairs = list(zip(direct, loaded)) + [(query, query_in), (key, key_in)]
    copies = [pltpu.make_async_copy(*pair, sems.at[i]) for i, pair in enumerate(pairs)]
    for copy in copies:
        copy.start()
    for copy in copies:
        copy.wait()
    w_key[...] = key_in[...].T
    for h in range(heads):
        w_query[h] = query_in[:, h * head_dim : (h + 1) * head_dim]


def columns_of(segment, size):
    return pl.ds(pl.multiple_of(segment * size, size), size)


def whole_rows(n, owner, slabs, out, first):
    band = lax.axis_index("lat")
    me = lax.axis_index("lon")
    count, size = slabs[0].shape[:2]
    for d in range(n):
        segment = owner[lax.rem(me + n - d, n), band]
        out[pl.ds(first, count), columns_of(segment, size)] = slabs[d][...]


def edge_kernel(n, rows, owner, *rest):
    del rows
    whole_rows(n, owner, rest[:n], rest[n], 0)


def spread(taps, r, row):
    cols, chans = row.shape
    taps[r, :, :chans] = pltpu.roll(row, 1, 0).astype(jnp.bfloat16)
    taps[r, :, chans : 2 * chans] = row.astype(jnp.bfloat16)
    taps[r, :, 2 * chans :] = pltpu.roll(row, cols - 1, 0).astype(jnp.bfloat16)


def convolve(taps, weight, bias, first, count):
    cols, width = taps.shape[1:]
    windows = [taps[first + i : first + i + count].reshape(count * cols, width) for i in range(3)]
    depth = weight.shape[0] * width
    product = jnp.dot(
        jnp.concatenate(windows, axis=1),
        weight[...].reshape(depth, weight.shape[2]),
        preferred_element_type=jnp.float32,
    )
    return product + bias[...]


def silu(x):
    return x / (1.0 + jnp.exp(-x))


def live_count(counts, row):
    inside = (row >= 0) & (row < counts.shape[0])
    return jnp.where(inside, counts[jnp.clip(row, 0, counts.shape[0] - 1)], 0)


def by_last(a, b):
    return lax.dot_general(a, b, (((1,), (1,)), ((), ())), preferred_element_type=jnp.float32)


def attend(segments, limits, mixed, normed, keys, values, w_query, w_out, results, here, scores, expo, turned):
    rows, chans = len(limits), mixed.shape[1]
    size = here.shape[0] // (rows * len(segments))
    heads, _, head_dim = w_query.shape
    cols = mixed.shape[0] // rows
    width = heads * size
    blocks = [(s, r) for s in range(len(segments)) for r in range(rows)]

    def cells(s, r):
        return columns_of(segments[s] + r * (cols // size), size)

    for b, (s, r) in enumerate(blocks):
        here[b * size : (b + 1) * size, :] = normed[cells(s, r), :]
    queries = [jnp.dot(here[...], w_query[h], preferred_element_type=jnp.float32) for h in range(heads)]
    queries = [query.astype(jnp.bfloat16) for query in queries]
    key_at = lax.broadcasted_iota(jnp.int32, (cols, width), 0)
    scale = math.log2(math.e) / head_dim**0.5
    shares = {}

    def score(b, r):
        own = jnp.concatenate([query[b * size : (b + 1) * size] for query in queries], axis=0)
        scores[b] = by_last(keys[r * cols : (r + 1) * cols, :], own)

    def weigh(b, r):
        part = jnp.where(key_at < limits[r], scores[b], -jnp.inf)
        part = jnp.exp2((part - jnp.max(part, axis=0, keepdims=True)) * scale)
        shares[b] = 1.0 / jnp.sum(part, axis=0, keepdims=True)
        expo[b] = part.astype(jnp.bfloat16)

    def add_up(b, r):
        summed = jnp.dot(values[:, r * cols : (r + 1) * cols], expo[b], preferred_element_type=jnp.float32)
        turned[:, b * width : (b + 1) * width] = (summed * shares[b]).astype(jnp.bfloat16)

    for turn_at in range(len(blocks) + 4):
        for lag, step in ((0, score), (2, weigh), (4, add_up)):
            if 0 <= turn_at - lag < len(blocks):
                step(turn_at - lag, blocks[turn_at - lag][1])
    attended = turned[...].T
    update = jnp.zeros(here.shape, jnp.float32)
    for h in range(heads):
        starts = [b * width + h * size for b in range(len(blocks))]
        part = jnp.concatenate([attended[start : start + size] for start in starts], axis=0)
        weight = w_out[h * head_dim : (h + 1) * head_dim, :]
        update = update + jnp.dot(part, weight, preferred_element_type=jnp.float32)
    for b, (s, r) in enumerate(blocks):
        cell = segments[s] * size + lax.broadcasted_iota(jnp.int32, (size, chans), 0)
        part = jnp.where(cell < limits[r], update[b * size : (b + 1) * size], 0.0)
        results[s][r * size : (r + 1) * size, :] = (mixed[cells(s, r), :].astype(jnp.float32) + part).astype(jnp.bfloat16)


def main_kernel(first, n, rows, owner, counts, *rest):
    slabs, sent, received = rest[:n], rest[n], rest[n + 1]
    w_conv1, b_conv1, w_conv2, b_conv2, w_key, w_value, w_query, w_out = rest[n + 2 : n + 10]
    result, mixed, normed, keys, values = rest[n + 10 : n + 15]
    grid, taps, acts, *scratch = rest[n + 15 :]
    band = lax.axis_index("lat")
    me = lax.axis_index("lon")
    group = group_of(band, me, n)
    odd = group % 2
    cols, chans = sent.shape[1:]
    cell = lax.broadcasted_iota(jnp.int32, (cols, chans), 0)
    first_row = band * (rows * n) + group * rows
    whole_rows(n, owner, slabs, grid, 2 * HALO * (1 - odd))
    grid[pl.ds(HALO + (rows - HALO) * odd, HALO)] = sent[...]
    grid[pl.ds((rows + HALO) * odd, HALO)] = received[...]
    limits = [live_count(counts, first_row - 1 + r) for r in range(rows + HALO)]

    def spread_inputs(start, stop):
        for r in range(start, stop):
            spread(taps, r, grid[r].astype(jnp.float32))

    def spread_acts(start, stop, product):
        act = silu(product)
        for r in range(start, stop):
            at = slice((r - start) * cols, (r - start + 1) * cols)
            spread(acts, r, jnp.where(cell < limits[r], act[at], 0.0))

    def mix(start, stop, product):
        for r in range(start, stop):
            here = grid[r + HALO].astype(jnp.float32) + product[(r - start) * cols : (r - start + 1) * cols]
            here = jnp.where(cell < limits[r + 1], here, 0.0)
            mixed[r * cols : (r + 1) * cols, :] = here.astype(jnp.bfloat16)
        at = slice(start * cols, stop * cols)
        flat = mixed[at, :].astype(jnp.float32)
        scaled = (flat * lax.rsqrt(jnp.mean(flat * flat, axis=1, keepdims=True) + 1e-06)).astype(jnp.bfloat16)
        normed[at, :] = scaled
        keys[at, :] = jnp.dot(scaled, w_key[...], preferred_element_type=jnp.float32).astype(jnp.bfloat16)
        values[:, at] = by_last(w_value[...], scaled).astype(jnp.bfloat16)

    total = rows + HALO
    half = total // 2
    low = half - HALO
    spread_inputs(0, half + HALO)
    first_low = convolve(taps, w_conv1, b_conv1, 0, half)
    spread_inputs(half + HALO, total + HALO)
    first_high = convolve(taps, w_conv1, b_conv1, half, total - half)
    spread_acts(0, half, first_low)
    if low:
        second_low = convolve(acts, w_conv2, b_conv2, 0, low)
    spread_acts(half, total, first_high)
    second_high = convolve(acts, w_conv2, b_conv2, low, rows - low)
    if low:
        mix(0, low, second_low)
    mix(low, rows, second_high)
    limits = limits[1 : rows + 1]
    result[rows * (cols // n) :, :] = jnp.zeros((AHEAD, chans), result.dtype)
    segments = [owner[lax.rem(me + first, n), band]]
    attend(segments, limits, mixed, normed, keys, values, w_query, w_out, [result], *scratch)


def rest_kernel(moves, n, rows, owner, counts, *rest):
    mixed, normed, keys, values, w_query, w_out = rest[:6]
    results, scratch = rest[6 : 6 + len(moves)], rest[6 + len(moves) :]
    band = lax.axis_index("lat")
    me = lax.axis_index("lon")
    first_row = band * (rows * n) + group_of(band, me, n) * rows
    limits = [counts[first_row + r] for r in range(rows)]
    segments = [owner[lax.rem(me + d, n), band] for d in moves]
    attend(segments, limits, mixed, normed, keys, values, w_query, w_out, results, *scratch)


def store_kernel(n, rows, rotation, *rest):
    slabs, (out, staged, upright, turned, sems) = rest[:n], rest[n:]
    band = lax.axis_index("lat")
    me = lax.axis_index("lon")
    depth = GROUP // out.shape[0]
    pieces = out.shape[0] // depth
    for d in range(n):
        top = group_of(band, lax.rem(me + n - d, n), n) * rows
        upright[pl.ds(top, rows)] = slabs[d][: rows * out.shape[0], :].reshape(rows, *out.shape[1:])

    def piece(g):
        at = pl.ds(g * depth, depth)
        return pltpu.make_async_copy(turned.at[at], out.at[at], sems.at[g])

    turn(rotation[me, band] % 4, staged, upright, turned, lambda g: None, lambda g: piece(g).start())
    for g in range(pieces):
        piece(g).wait()


def on_device(
    bands,
    n,
    fields,
    w_conv1,
    b_conv1,
    w_conv2,
    b_conv2,
    w_query,
    w_key,
    w_value,
    w_out,
    rotation,
    owner,
    counts,
):
    size, _, chans = fields.shape
    rows = size // n
    inner = rows - HALO
    cols = size * n
    bf16 = jnp.bfloat16
    smem = pl.BlockSpec(memory_space=pltpu.SMEM)
    vmem = pl.BlockSpec(memory_space=pltpu.VMEM)
    hbm = pl.BlockSpec(memory_space=pltpu.HBM)
    params = pltpu.CompilerParams(vmem_limit_bytes=VMEM_BYTES)
    pieces = size * size // GROUP

    def call(kernel, name, out, scalars, arrays, scratch, array_spec=vmem, scalar_spec=smem, out_spec=vmem):
        many = isinstance(out, list)
        return pl.pallas_call(
            functools.partial(kernel, n, rows),
            out_shape=out,
            in_specs=[scalar_spec] * len(scalars) + [array_spec] * len(arrays),
            out_specs=[out_spec] * len(out) if many else out_spec,
            scratch_shapes=scratch,
            compiler_params=params,
            name=name,
        )(*scalars, *arrays)

    def array(*shape):
        return jax.ShapeDtypeStruct(shape, bf16)

    order = sorted(range(1, n), key=lambda d: -min(d, n - d))

    def around_by(x, d):
        return lax.ppermute(x, "lon", [(i, (i + d) % n) for i in range(n)])

    def around(parts):
        moved = {d: around_by(parts[d], d) for d in order}
        return [parts[0]] + [moved[d] for d in range(1, n)]

    def in_hbm(x):
        return pltpu.with_memory_space_constraint(x, pltpu.HBM)

    rotation, owner = in_hbm(rotation.T), in_hbm(owner.T)
    loaded = [counts]
    loaded += [w_conv1.reshape(3, 3 * chans, chans), b_conv1.reshape(1, chans)]
    loaded += [w_conv2.reshape(3, 3 * chans, chans), b_conv2.reshape(1, chans), w_value.T, w_out]
    loaded = [in_hbm(x) for x in loaded]
    turned = [in_hbm(x) for x in (w_query, w_key.T)]
    staging = pltpu.VMEM((chans // LANES, size * (size + 8), LANES), jnp.float32)
    block = pltpu.VMEM((size, size, chans), bf16)

    slabs = [array(HALO, size, chans)] * n + [array(rows, size, chans)] * n
    scratch = [staging, block, block, pltpu.SMEM(rotation.shape, rotation.dtype)]
    scratch += [pltpu.SemaphoreType.DMA((3,)), pltpu.SemaphoreType.DMA((pieces,))]
    held = slabs + [pltpu.VMEM(x.shape, x.dtype) for x in (rotation, owner)]
    *slabs, rotation, owner = call(send_kernel, "send", held, [rotation, owner], [in_hbm(fields)], scratch, hbm, hbm)
    edges = around(slabs[:n])
    slabs = around(slabs[n:])

    snake = [a * n + shard_of(a, g, n) for a in range(bands) for g in range(n)]
    pairs = [(snake[i], snake[i + 1 if i % 2 else i - 1]) for i in range(1, bands * n - 1)]
    sent = call(edge_kernel, "edge", array(HALO, cols, chans), [owner], edges, [])
    received = lax.ppermute(sent, ("lat", "lon"), pairs)

    head_dim = w_key.shape[1]
    heads = chans // head_dim
    held = [pltpu.VMEM(x.shape, x.dtype) for x in loaded]
    held += [pltpu.VMEM((heads, chans, head_dim), bf16), pltpu.VMEM(w_key.shape, bf16)]
    scratch = [pltpu.VMEM(x.shape, bf16) for x in turned] + [pltpu.SemaphoreType.DMA((len(loaded) + 2,))]
    loaded = call(load_kernel, "load", held, [sent], loaded + turned, scratch, hbm, hbm)
    counts, *convs, w_value, w_out, w_query, w_key = loaded

    def taps(count):
        return pltpu.VMEM((count, cols, 3 * chans), bf16)

    def working(segments):
        blocks, width = segments * rows, heads * size
        return [
            pltpu.VMEM((blocks * size, chans), bf16),
            pltpu.VMEM((blocks, cols, width), jnp.float32),
            pltpu.VMEM((blocks, cols, width), bf16),
            pltpu.VMEM((head_dim, blocks * width), bf16),
        ]

    cells = rows * cols
    result = array(rows * size, chans)
    first, *others = [*order, 0]
    results = {}
    results[first], *held = call(
        functools.partial(main_kernel, first),
        "main",
        [array(rows * size + AHEAD, chans), array(cells, chans), array(cells, chans), array(cells, head_dim), array(head_dim, cells)],
        [owner, counts],
        slabs + [sent, received, *convs, w_key, w_value, w_query, w_out],
        [pltpu.VMEM((rows + 2 * HALO, cols, chans), bf16), taps(rows + 2 * HALO), taps(rows + HALO)] + working(1),
    )
    moved = {first: around_by(results[first], first)}
    rest = call(
        functools.partial(rest_kernel, others),
        "rest",
        [result] * len(others),
        [owner, counts],
        held + [w_query, w_out],
        working(len(others)),
    )
    for d, x in zip(others, rest):
        moved[d] = around_by(x, d) if d else x
    slabs = [moved[d] for d in range(n)]
    scratch = [staging, block, block, pltpu.SemaphoreType.DMA((pieces,))]
    return call(store_kernel, "store", array(*fields.shape), [rotation], slabs, scratch, out_spec=hbm)


def solution(mesh):
    in_specs = (P("lat", "lon", None), P(), P(), P(), P(), P(), P(), P(), P(), P(), P(), P())
    out_specs = P("lat", "lon", None)
    body = functools.partial(on_device, mesh.shape["lat"], mesh.shape["lon"])
    return jax.shard_map(body, mesh=mesh, in_specs=in_specs, out_specs=out_specs, check_vma=False)
```

```python
import functools
import math

import jax
import jax.numpy as jnp
from jax import lax
from jax.experimental import pallas as pl
from jax.experimental.pallas import tpu as pltpu
from jax.sharding import PartitionSpec as P

HALO = 2
LANES = 128
GROUP = 256
AHEAD = 16
VMEM_BYTES = 28 * 1024 * 1024


def group_of(band, shard, n):
    outer = jnp.where((shard == n - 2) == (band % 2 == 0), 0, n - 1)
    return jnp.where(shard < n - 2, shard + 1, outer)


def shard_of(band, group, n):
    if 0 < group < n - 1:
        return group - 1
    return n - 2 if (group == 0) == (band % 2 == 0) else n - 1


def first_held(group, rows):
    return group * rows - HALO * (group % 2)


def turn(quarter, staged, block, out, ready, done):
    size, _, chans = block.shape
    tiles = staged.shape[0]
    pitch = staged.shape[1] // size
    depth = GROUP // size
    pieces = size // depth

    def column(col):
        parts = [staged[t, pl.ds(col, size, stride=pitch), :] for t in range(tiles)]
        return jnp.concatenate(parts, axis=1).astype(jnp.bfloat16)

    def keep(i, row):
        for t in range(tiles):
            staged[t, pl.ds(i * pitch, size), :] = row[:, t * LANES : (t + 1) * LANES]

    @pl.when(quarter == 0)
    def _():
        for g in range(pieces):
            ready(g)
            out[g * depth : (g + 1) * depth] = block[g * depth : (g + 1) * depth]
            done(g)

    @pl.when(quarter == 1)
    def _():
        for i in range(size):
            if i % depth == 0:
                ready(i // depth)
            keep(i, block[i].astype(jnp.float32))
        for i in range(size):
            out[i] = column(size - 1 - i)
            if i % depth == depth - 1:
                done(i // depth)

    @pl.when(quarter == 2)
    def _():
        i = lax.broadcasted_iota(jnp.int32, (GROUP, GROUP), 0)
        j = lax.broadcasted_iota(jnp.int32, (GROUP, GROUP), 1)
        backwards = jnp.where(i + j == GROUP - 1, 1.0, 0.0).astype(jnp.bfloat16)
        for g in reversed(range(pieces)):
            ready(pieces - 1 - g)
            cells = block[size - (g + 1) * depth : size - g * depth].reshape(GROUP, chans)
            turned = jnp.dot(backwards, cells, preferred_element_type=jnp.float32).astype(jnp.bfloat16)
            out[g * depth : (g + 1) * depth] = turned.reshape(depth, size, chans)
            done(g)

    @pl.when(quarter == 3)
    def _():
        for i in range(size):
            if i % depth == 0:
                ready(i // depth)
            keep(size - 1 - i, block[i].astype(jnp.float32))
        for i in range(size):
            out[i] = column(i)
            if i % depth == depth - 1:
                done(i // depth)


def parts(rows):
    if rows > 2 * HALO:
        return [(0, rows, HALO), (HALO, HALO, rows - HALO), (rows, 0, HALO)]
    return [(0, rows, HALO), (HALO, 0, rows)]


def send_kernel(n, rows, rotation_in, owner_in, fields, *rest):
    pieces, (rotation_out, owner_out) = rest[:-8], rest[-8:-6]
    staged, block, upright, rotation, scalar_sems, sems = rest[-6:]
    band = lax.axis_index("lat")
    me = lax.axis_index("lon")
    depth = GROUP // fields.shape[0]

    def piece(g):
        at = pl.ds(g * depth, depth)
        return pltpu.make_async_copy(fields.at[at], block.at[at], sems.at[g])

    scalars = [
        pltpu.make_async_copy(rotation_in, rotation, scalar_sems.at[0]),
        pltpu.make_async_copy(rotation_in, rotation_out, scalar_sems.at[1]),
        pltpu.make_async_copy(owner_in, owner_out, scalar_sems.at[2]),
    ]
    for copy in scalars:
        copy.start()
    for g in range(fields.shape[0] // depth):
        piece(g).start()
    scalars[0].wait()
    turn((4 - rotation[me, band]) % 4, staged, block, upright, lambda g: piece(g).wait(), lambda g: None)
    for d in range(n):
        group = group_of(band, lax.rem(me + d, n), n)
        top, odd = first_held(group, rows), group % 2
        for slab, (even_at, odd_at, count) in zip(pieces[d::n], parts(rows)):
            slab[...] = upright[pl.ds(top + jnp.where(odd == 0, even_at, odd_at), count)]
    scalars[1].wait()
    scalars[2].wait()


def load_kernel(n, rows, after, *refs):
    del after
    passed = n - 1 if rows > 2 * HALO else 0
    for i in range(passed):
        refs[len(refs) - 3 - passed + i][...] = refs[i][...]
    refs = refs[passed : len(refs) - 3 - passed] + refs[-3:]
    count = (len(refs) - 7) // 2
    direct, (query, key) = refs[:count], refs[count : count + 2]
    loaded, (w_query, w_key) = refs[count + 2 : 2 * count + 2], refs[2 * count + 2 : 2 * count + 4]
    query_in, key_in, sems = refs[2 * count + 4 :]
    heads, _, head_dim = w_query.shape
    pairs = list(zip(direct, loaded)) + [(query, query_in), (key, key_in)]
    copies = [pltpu.make_async_copy(*pair, sems.at[i]) for i, pair in enumerate(pairs)]
    for copy in copies:
        copy.start()
    for copy in copies:
        copy.wait()
    w_key[...] = key_in[...].T
    for h in range(heads):
        w_query[h] = query_in[:, h * head_dim : (h + 1) * head_dim]


def columns_of(segment, size):
    return pl.ds(pl.multiple_of(segment * size, size), size)


def whole_rows(n, owner, slabs, out, first):
    band = lax.axis_index("lat")
    me = lax.axis_index("lon")
    count, size = slabs[0].shape[:2]
    for d in range(n):
        segment = owner[lax.rem(me + n - d, n), band]
        out[pl.ds(first, count), columns_of(segment, size)] = slabs[d][...]


def edge_kernel(n, rows, owner, *rest):
    del rows
    whole_rows(n, owner, rest[:n], rest[n], 0)


def spread(taps, r, row):
    cols, chans = row.shape
    taps[r, :, :chans] = pltpu.roll(row, 1, 0).astype(jnp.bfloat16)
    taps[r, :, chans : 2 * chans] = row.astype(jnp.bfloat16)
    taps[r, :, 2 * chans :] = pltpu.roll(row, cols - 1, 0).astype(jnp.bfloat16)


def convolve(taps, weight, bias, first, count):
    cols, width = taps.shape[1:]
    windows = [taps[first + i : first + i + count].reshape(count * cols, width) for i in range(3)]
    depth = weight.shape[0] * width
    product = jnp.dot(
        jnp.concatenate(windows, axis=1),
        weight[...].reshape(depth, weight.shape[2]),
        preferred_element_type=jnp.float32,
    )
    return product + bias[...]


def silu(x):
    return x / (1.0 + jnp.exp(-x))


def live_count(counts, row):
    inside = (row >= 0) & (row < counts.shape[0])
    return jnp.where(inside, counts[jnp.clip(row, 0, counts.shape[0] - 1)], 0)


def by_last(a, b):
    return lax.dot_general(a, b, (((1,), (1,)), ((), ())), preferred_element_type=jnp.float32)


def attend(segments, limits, mixed, normed, keys, values, w_query, w_out, results, here, scores, expo, turned):
    rows, chans = len(limits), mixed.shape[1]
    size = here.shape[0] // (rows * len(segments))
    heads, _, head_dim = w_query.shape
    cols = mixed.shape[0] // rows
    width = heads * size
    blocks = [(s, r) for s in range(len(segments)) for r in range(rows)]

    def cells(s, r):
        return columns_of(segments[s] + r * (cols // size), size)

    for b, (s, r) in enumerate(blocks):
        here[b * size : (b + 1) * size, :] = normed[cells(s, r), :]
    queries = [jnp.dot(here[...], w_query[h], preferred_element_type=jnp.float32) for h in range(heads)]
    queries = [query.astype(jnp.bfloat16) for query in queries]
    for b, (s, r) in enumerate(blocks):
        own = jnp.concatenate([query[b * size : (b + 1) * size] for query in queries], axis=0)
        scores[b] = by_last(keys[r * cols : (r + 1) * cols, :], own)
    key_at = lax.broadcasted_iota(jnp.int32, (cols, width), 0)
    scale = math.log2(math.e) / head_dim**0.5
    shares = []
    for b, (s, r) in enumerate(blocks):
        part = jnp.where(key_at < limits[r], scores[b], -jnp.inf)
        part = jnp.exp2((part - jnp.max(part, axis=0, keepdims=True)) * scale)
        shares.append(1.0 / jnp.sum(part, axis=0, keepdims=True))
        expo[b] = part.astype(jnp.bfloat16)
    for b, (s, r) in enumerate(blocks):
        summed = jnp.dot(values[:, r * cols : (r + 1) * cols], expo[b], preferred_element_type=jnp.float32)
        turned[:, b * width : (b + 1) * width] = (summed * shares[b]).astype(jnp.bfloat16)
    attended = turned[...].T
    update = jnp.zeros(here.shape, jnp.float32)
    for h in range(heads):
        starts = [b * width + h * size for b in range(len(blocks))]
        part = jnp.concatenate([attended[start : start + size] for start in starts], axis=0)
        weight = w_out[h * head_dim : (h + 1) * head_dim, :]
        update = update + jnp.dot(part, weight, preferred_element_type=jnp.float32)
    for b, (s, r) in enumerate(blocks):
        cell = segments[s] * size + lax.broadcasted_iota(jnp.int32, (size, chans), 0)
        part = jnp.where(cell < limits[r], update[b * size : (b + 1) * size], 0.0)
        results[s][r * size : (r + 1) * size, :] = (mixed[cells(s, r), :].astype(jnp.float32) + part).astype(jnp.bfloat16)


def main_kernel(first, n, rows, owner, counts, *rest):
    slabs, sent, received = rest[:n], rest[n], rest[n + 1]
    w_conv1, b_conv1, w_conv2, b_conv2, w_key, w_value, w_query, w_out = rest[n + 2 : n + 10]
    result, mixed, normed, keys, values = rest[n + 10 : n + 15]
    grid, taps, acts, *scratch = rest[n + 15 :]
    band = lax.axis_index("lat")
    me = lax.axis_index("lon")
    group = group_of(band, me, n)
    odd = group % 2
    cols, chans = sent.shape[1:]
    cell = lax.broadcasted_iota(jnp.int32, (cols, chans), 0)
    first_row = band * (rows * n) + group * rows
    whole_rows(n, owner, slabs, grid, 2 * HALO * (1 - odd))
    grid[pl.ds(HALO + (rows - HALO) * odd, HALO)] = sent[...]
    grid[pl.ds((rows + HALO) * odd, HALO)] = received[...]
    limits = [live_count(counts, first_row - 1 + r) for r in range(rows + HALO)]

    def spread_inputs(start, stop):
        for r in range(start, stop):
            spread(taps, r, grid[r].astype(jnp.float32))

    def spread_acts(start, stop, product):
        act = silu(product)
        for r in range(start, stop):
            at = slice((r - start) * cols, (r - start + 1) * cols)
            spread(acts, r, jnp.where(cell < limits[r], act[at], 0.0))

    def mix(start, stop, product):
        for r in range(start, stop):
            here = grid[r + HALO].astype(jnp.float32) + product[(r - start) * cols : (r - start + 1) * cols]
            here = jnp.where(cell < limits[r + 1], here, 0.0)
            mixed[r * cols : (r + 1) * cols, :] = here.astype(jnp.bfloat16)
        at = slice(start * cols, stop * cols)
        flat = mixed[at, :].astype(jnp.float32)
        scaled = (flat * lax.rsqrt(jnp.mean(flat * flat, axis=1, keepdims=True) + 1e-06)).astype(jnp.bfloat16)
        normed[at, :] = scaled
        keys[at, :] = jnp.dot(scaled, w_key[...], preferred_element_type=jnp.float32).astype(jnp.bfloat16)
        values[:, at] = by_last(w_value[...], scaled).astype(jnp.bfloat16)

    total = rows + HALO
    half = total // 2
    low = half - HALO
    spread_inputs(0, half + HALO)
    first_low = convolve(taps, w_conv1, b_conv1, 0, half)
    spread_inputs(half + HALO, total + HALO)
    first_high = convolve(taps, w_conv1, b_conv1, half, total - half)
    spread_acts(0, half, first_low)
    if low:
        second_low = convolve(acts, w_conv2, b_conv2, 0, low)
    spread_acts(half, total, first_high)
    second_high = convolve(acts, w_conv2, b_conv2, low, rows - low)
    if low:
        mix(0, low, second_low)
    mix(low, rows, second_high)
    limits = limits[1 : rows + 1]
    result[rows * (cols // n) :, :] = jnp.zeros((AHEAD, chans), result.dtype)
    segments = [owner[lax.rem(me + first, n), band]]
    attend(segments, limits, mixed, normed, keys, values, w_query, w_out, [result], *scratch)


def mix(start, stop, product, grid_row, limits, mixed, normed, keys, values, w_key, w_value):
    cols = product.shape[0] // (stop - start)
    cell = lax.broadcasted_iota(jnp.int32, (cols, product.shape[1]), 0)
    for r in range(start, stop):
        here = grid_row(r).astype(jnp.float32) + product[(r - start) * cols : (r - start + 1) * cols]
        here = jnp.where(cell < limits[r], here, 0.0)
        mixed[r * cols : (r + 1) * cols, :] = here.astype(jnp.bfloat16)
    at = slice(start * cols, stop * cols)
    flat = mixed[at, :].astype(jnp.float32)
    scaled = (flat * lax.rsqrt(jnp.mean(flat * flat, axis=1, keepdims=True) + 1e-06)).astype(jnp.bfloat16)
    normed[at, :] = scaled
    keys[at, :] = jnp.dot(scaled, w_key[...], preferred_element_type=jnp.float32).astype(jnp.bfloat16)
    values[:, at] = by_last(w_value[...], scaled).astype(jnp.bfloat16)


def activate(start, stop, product, limits, acts, at):
    cols = product.shape[0] // (stop - start)
    cell = lax.broadcasted_iota(jnp.int32, (cols, product.shape[1]), 0)
    act = silu(product)
    for r in range(start, stop):
        here = act[(r - start) * cols : (r - start + 1) * cols]
        spread(acts, r - start + at, jnp.where(cell < limits[r], here, 0.0))


def inner_kernel(n, rows, owner, counts, *rest):
    slabs, (sent, w_conv1, b_conv1, w_conv2, b_conv2, w_key, w_value) = rest[:n], rest[n : n + 7]
    edge_taps, edge_acts, mixed, normed, keys, values = rest[n + 7 : n + 13]
    grid, taps, acts = rest[n + 13 :]
    band = lax.axis_index("lat")
    group = group_of(band, lax.axis_index("lon"), n)
    odd = group % 2
    first_row = band * (rows * n) + group * rows
    whole_rows(n, owner, slabs, grid, HALO * (1 - odd))
    grid[pl.ds((rows - HALO) * odd, HALO)] = sent[...]
    limits = [counts[first_row + 1 + r] for r in range(rows - HALO)]
    half = rows // 2 - 1
    last = rows - HALO

    def spread_inputs(start, stop):
        for r in range(start, stop):
            spread(taps, r, grid[r].astype(jnp.float32))

    def mix_rows(start, stop, product):
        row = lambda r: grid[r + HALO]
        mix(start, stop, product, row, limits[1:], mixed, normed, keys, values, w_key, w_value)

    spread_inputs(0, half + HALO)
    first_low = convolve(taps, w_conv1, b_conv1, 0, half)
    spread_inputs(half + HALO, rows)
    first_high = convolve(taps, w_conv1, b_conv1, half, last - half)
    activate(0, half, first_low, limits, acts, 0)
    edge_taps[:HALO] = taps[:HALO]
    edge_taps[HALO:] = taps[rows - HALO :]
    activate(half, last, first_high, limits, acts, half)
    second = convolve(acts, w_conv2, b_conv2, 0, last - HALO)
    edge_acts[:HALO] = acts[:HALO]
    edge_acts[HALO:] = acts[last - HALO :]
    mix_rows(0, last - HALO, second)


def outer_kernel(first, n, rows, owner, counts, *rest):
    slabs, (received, edge_taps, edge_acts, *inner), rest = rest[:n], rest[n : n + 7], rest[n + 7 :]
    w_conv1, b_conv1, w_conv2, b_conv2, w_key, w_value, w_query, w_out = rest[:8]
    result, mixed, normed, keys, values, ends, taps, acts, *scratch = rest[8:]
    band = lax.axis_index("lat")
    me = lax.axis_index("lon")
    group = group_of(band, me, n)
    odd = group % 2
    cols, chans = ends.shape[1:]
    first_row = band * (rows * n) + group * rows
    limits = [live_count(counts, first_row - 1 + r) for r in range(rows + HALO)]
    low, high = HALO * cols, (rows - HALO) * cols
    whole_rows(n, owner, slabs, ends, HALO * (1 - odd))
    ends[pl.ds(HALO * odd, HALO)] = received[...]
    tops = [0, 1, 6, 7]
    taps[HALO : 3 * HALO] = edge_taps[...]
    acts[HALO : 3 * HALO] = edge_acts[...]

    def mix_rows(start, product, at):
        row = lambda r: taps[r - start + at, :, chans : 2 * chans]
        mix(start, start + HALO, product, row, limits[1:], mixed, normed, keys, values, w_key, w_value)

    for r in range(HALO):
        spread(taps, tops[r], ends[r].astype(jnp.float32))
    first_top = convolve(taps, w_conv1, b_conv1, 0, HALO)
    for r in range(HALO, 2 * HALO):
        spread(taps, tops[r], ends[r].astype(jnp.float32))
    first_end = convolve(taps, w_conv1, b_conv1, 2 * HALO, HALO)
    activate(0, HALO, first_top, limits, acts, 0)
    second_top = convolve(acts, w_conv2, b_conv2, 0, HALO)
    activate(rows, rows + HALO, first_end, limits, acts, 3 * HALO)
    second_end = convolve(acts, w_conv2, b_conv2, 2 * HALO, HALO)
    for whole, part in zip((mixed, normed, keys), inner):
        whole[low:high, :] = part[...]
    values[:, low:high] = inner[3][...]
    mix_rows(0, second_top, HALO)
    mix_rows(rows - HALO, second_end, 2 * HALO)
    result[rows * (cols // n) :, :] = jnp.zeros((AHEAD, chans), result.dtype)
    segments = [owner[lax.rem(me + first, n), band]]
    attend(segments, limits[1 : rows + 1], mixed, normed, keys, values, w_query, w_out, [result], *scratch)


def rest_kernel(moves, n, rows, owner, counts, *rest):
    mixed, normed, keys, values, w_query, w_out = rest[:6]
    results, scratch = rest[6 : 6 + len(moves)], rest[6 + len(moves) :]
    band = lax.axis_index("lat")
    me = lax.axis_index("lon")
    first_row = band * (rows * n) + group_of(band, me, n) * rows
    limits = [counts[first_row + r] for r in range(rows)]
    segments = [owner[lax.rem(me + d, n), band] for d in moves]
    attend(segments, limits, mixed, normed, keys, values, w_query, w_out, results, *scratch)


def store_kernel(n, rows, rotation, *rest):
    slabs, (out, staged, upright, turned, sems) = rest[:n], rest[n:]
    band = lax.axis_index("lat")
    me = lax.axis_index("lon")
    depth = GROUP // out.shape[0]
    pieces = out.shape[0] // depth
    for d in range(n):
        top = group_of(band, lax.rem(me + n - d, n), n) * rows
        upright[pl.ds(top, rows)] = slabs[d][: rows * out.shape[0], :].reshape(rows, *out.shape[1:])

    def piece(g):
        at = pl.ds(g * depth, depth)
        return pltpu.make_async_copy(turned.at[at], out.at[at], sems.at[g])

    turn(rotation[me, band] % 4, staged, upright, turned, lambda g: None, lambda g: piece(g).start())
    for g in range(pieces):
        piece(g).wait()


def on_device(
    bands,
    n,
    fields,
    w_conv1,
    b_conv1,
    w_conv2,
    b_conv2,
    w_query,
    w_key,
    w_value,
    w_out,
    rotation,
    owner,
    counts,
):
    size, _, chans = fields.shape
    rows = size // n
    inner = rows - HALO
    cols = size * n
    bf16 = jnp.bfloat16
    smem = pl.BlockSpec(memory_space=pltpu.SMEM)
    vmem = pl.BlockSpec(memory_space=pltpu.VMEM)
    hbm = pl.BlockSpec(memory_space=pltpu.HBM)
    params = pltpu.CompilerParams(vmem_limit_bytes=VMEM_BYTES)
    pieces = size * size // GROUP

    def call(kernel, name, out, scalars, arrays, scratch, array_spec=vmem, scalar_spec=smem, out_spec=vmem, in_place=None):
        many = isinstance(out, list)
        specs = [array_spec if in_place is None or i >= in_place else vmem for i in range(len(arrays))]
        return pl.pallas_call(
            functools.partial(kernel, n, rows),
            out_shape=out,
            in_specs=[scalar_spec] * len(scalars) + specs,
            out_specs=[out_spec] * len(out) if many else out_spec,
            scratch_shapes=scratch,
            compiler_params=params,
            name=name,
        )(*scalars, *arrays)

    def array(*shape):
        return jax.ShapeDtypeStruct(shape, bf16)

    order = sorted(range(1, n), key=lambda d: -min(d, n - d))

    def around_by(x, d):
        return lax.ppermute(x, "lon", [(i, (i + d) % n) for i in range(n)])

    def around(parts):
        moved = {d: around_by(parts[d], d) for d in order}
        return [parts[0]] + [moved[d] for d in range(1, n)]

    def in_hbm(x):
        return pltpu.with_memory_space_constraint(x, pltpu.HBM)

    rotation, owner = in_hbm(rotation.T), in_hbm(owner.T)
    loaded = [counts]
    loaded += [w_conv1.reshape(3, 3 * chans, chans), b_conv1.reshape(1, chans)]
    loaded += [w_conv2.reshape(3, 3 * chans, chans), b_conv2.reshape(1, chans), w_value.T, w_out]
    loaded = [in_hbm(x) for x in loaded]
    turned = [in_hbm(x) for x in (w_query, w_key.T)]
    staging = pltpu.VMEM((chans // LANES, size * (size + 8), LANES), jnp.float32)
    block = pltpu.VMEM((size, size, chans), bf16)

    slabs = [array(count, size, chans) for *_, count in parts(rows) for _ in range(n)]
    scratch = [staging, block, block, pltpu.SMEM(rotation.shape, rotation.dtype)]
    scratch += [pltpu.SemaphoreType.DMA((3,)), pltpu.SemaphoreType.DMA((pieces,))]
    held = slabs + [pltpu.VMEM(x.shape, x.dtype) for x in (rotation, owner)]
    *slabs, rotation, owner = call(send_kernel, "send", held, [rotation, owner], [in_hbm(fields)], scratch, hbm, hbm)
    edges, *slabs = [slabs[i : i + n] for i in range(0, len(slabs), n)]
    edges = around(edges)
    slabs[0] = around(slabs[0])

    snake = [a * n + shard_of(a, g, n) for a in range(bands) for g in range(n)]
    pairs = [(snake[i], snake[i + 1 if i % 2 else i - 1]) for i in range(1, bands * n - 1)]
    sent = call(edge_kernel, "edge", array(HALO, cols, chans), [owner], edges, [])
    received = lax.ppermute(sent, ("lat", "lon"), pairs)

    head_dim = w_key.shape[1]
    heads = chans // head_dim
    held = [pltpu.VMEM(x.shape, x.dtype) for x in loaded]
    held += [pltpu.VMEM((heads, chans, head_dim), bf16), pltpu.VMEM(w_key.shape, bf16)]
    scratch = [pltpu.VMEM(x.shape, bf16) for x in turned] + [pltpu.SemaphoreType.DMA((len(loaded) + 2,))]
    passed = [x for late in slabs[1:] for x in late[1:]]
    held += [array(*x.shape) for x in passed]
    loaded = call(load_kernel, "load", held, [sent], passed + loaded + turned, scratch, hbm, hbm, in_place=len(passed))
    loaded, passed = loaded[: len(loaded) - len(passed)], loaded[len(loaded) - len(passed) :]
    counts, *convs, w_value, w_out, w_query, w_key = loaded
    if passed:
        slabs[1] = around([slabs[1][0], *passed])

    def taps(count):
        return pltpu.VMEM((count, cols, 3 * chans), bf16)

    def working(segments):
        blocks, width = segments * rows, heads * size
        return [
            pltpu.VMEM((blocks * size, chans), bf16),
            pltpu.VMEM((blocks, cols, width), jnp.float32),
            pltpu.VMEM((blocks, cols, width), bf16),
            pltpu.VMEM((head_dim, blocks * width), bf16),
        ]

    result = array(rows * size, chans)
    first, *others = [*order, 0]
    results = {}
    message = array(rows * size + AHEAD, chans)

    def kept(count):
        cells = count * cols
        return [array(cells, chans), array(cells, chans), array(cells, head_dim), array(head_dim, cells)]

    def window(count):
        return pltpu.VMEM((count, cols, chans), bf16)

    attention = [w_key, w_value, w_query, w_out]
    if len(slabs) == 1:
        results[first], *held = call(
            functools.partial(main_kernel, first),
            "main",
            [message] + kept(rows),
            [owner, counts],
            slabs[0] + [sent, received, *convs, *attention],
            [window(rows + 2 * HALO), taps(rows + 2 * HALO), taps(rows + HALO)] + working(1),
        )
    else:
        ends = array(2 * HALO, cols, 3 * chans)
        inner = call(
            inner_kernel,
            "inner",
            [ends, ends] + kept(rows - 2 * HALO),
            [owner, counts],
            slabs[0] + [sent, *convs, w_key, w_value],
            [window(rows), taps(rows), taps(rows - HALO)],
        )
        results[first], *held = call(
            functools.partial(outer_kernel, first),
            "outer",
            [message] + kept(rows),
            [owner, counts],
            slabs[1] + [received, *inner, *convs, *attention],
            [window(2 * HALO), taps(4 * HALO), taps(4 * HALO)] + working(1),
        )
    moved = {first: around_by(results[first], first)}
    rest = call(
        functools.partial(rest_kernel, others),
        "rest",
        [result] * len(others),
        [owner, counts],
        held + [w_query, w_out],
        working(len(others)),
    )
    for d, x in zip(others, rest):
        moved[d] = around_by(x, d) if d else x
    slabs = [moved[d] for d in range(n)]
    scratch = [staging, block, block, pltpu.SemaphoreType.DMA((pieces,))]
    return call(store_kernel, "store", array(*fields.shape), [rotation], slabs, scratch, out_spec=hbm)


def solution(mesh):
    in_specs = (P("lat", "lon", None), P(), P(), P(), P(), P(), P(), P(), P(), P(), P(), P())
    out_specs = P("lat", "lon", None)
    body = functools.partial(on_device, mesh.shape["lat"], mesh.shape["lon"])
    return jax.shard_map(body, mesh=mesh, in_specs=in_specs, out_specs=out_specs, check_vma=False)
```

```python
import functools
import math

import jax
import jax.numpy as jnp
from jax import lax
from jax.experimental import pallas as pl
from jax.experimental.pallas import tpu as pltpu
from jax.sharding import PartitionSpec as P

HALO = 2
LANES = 128
GROUP = 256
AHEAD = 16
VMEM_BYTES = 28 * 1024 * 1024


def group_of(band, shard, n):
    outer = jnp.where((shard == n - 2) == (band % 2 == 0), 0, n - 1)
    return jnp.where(shard < n - 2, shard + 1, outer)


def shard_of(band, group, n):
    if 0 < group < n - 1:
        return group - 1
    return n - 2 if (group == 0) == (band % 2 == 0) else n - 1


def first_held(group, rows):
    return group * rows - HALO * (group % 2)


def turn(quarter, staged, block, out, ready, done):
    size, _, chans = block.shape
    tiles = staged.shape[0]
    pitch = staged.shape[1] // size
    depth = GROUP // size
    pieces = size // depth

    def column(col):
        parts = [staged[t, pl.ds(col, size, stride=pitch), :] for t in range(tiles)]
        return jnp.concatenate(parts, axis=1).astype(jnp.bfloat16)

    def keep(i, row):
        for t in range(tiles):
            staged[t, pl.ds(i * pitch, size), :] = row[:, t * LANES : (t + 1) * LANES]

    @pl.when(quarter == 0)
    def _():
        for g in range(pieces):
            ready(g)
            out[g * depth : (g + 1) * depth] = block[g * depth : (g + 1) * depth]
            done(g)

    @pl.when(quarter == 1)
    def _():
        for i in range(size):
            if i % depth == 0:
                ready(i // depth)
            keep(i, block[i].astype(jnp.float32))
        for i in range(size):
            out[i] = column(size - 1 - i)
            if i % depth == depth - 1:
                done(i // depth)

    @pl.when(quarter == 2)
    def _():
        i = lax.broadcasted_iota(jnp.int32, (GROUP, GROUP), 0)
        j = lax.broadcasted_iota(jnp.int32, (GROUP, GROUP), 1)
        backwards = jnp.where(i + j == GROUP - 1, 1.0, 0.0).astype(jnp.bfloat16)
        for g in reversed(range(pieces)):
            ready(pieces - 1 - g)
            cells = block[size - (g + 1) * depth : size - g * depth].reshape(GROUP, chans)
            turned = jnp.dot(backwards, cells, preferred_element_type=jnp.float32).astype(jnp.bfloat16)
            out[g * depth : (g + 1) * depth] = turned.reshape(depth, size, chans)
            done(g)

    @pl.when(quarter == 3)
    def _():
        for i in range(size):
            if i % depth == 0:
                ready(i // depth)
            keep(size - 1 - i, block[i].astype(jnp.float32))
        for i in range(size):
            out[i] = column(i)
            if i % depth == depth - 1:
                done(i // depth)


def send_kernel(n, rows, rotation_in, owner_in, fields, *rest):
    edges, slabs, (rotation_out, owner_out) = rest[:n], rest[n : 2 * n], rest[2 * n : 2 * n + 2]
    staged, block, upright, rotation, scalar_sems, sems = rest[2 * n + 2 :]
    band = lax.axis_index("lat")
    me = lax.axis_index("lon")
    depth = GROUP // fields.shape[0]

    def piece(g):
        at = pl.ds(g * depth, depth)
        return pltpu.make_async_copy(fields.at[at], block.at[at], sems.at[g])

    scalars = [
        pltpu.make_async_copy(rotation_in, rotation, scalar_sems.at[0]),
        pltpu.make_async_copy(rotation_in, rotation_out, scalar_sems.at[1]),
        pltpu.make_async_copy(owner_in, owner_out, scalar_sems.at[2]),
    ]
    for copy in scalars:
        copy.start()
    for g in range(fields.shape[0] // depth):
        piece(g).start()
    scalars[0].wait()
    turn((4 - rotation[me, band]) % 4, staged, block, upright, lambda g: piece(g).wait(), lambda g: None)
    for d in range(n):
        group = group_of(band, lax.rem(me + d, n), n)
        top, odd = first_held(group, rows), group % 2
        edges[d][...] = upright[pl.ds(top + rows * odd, HALO)]
        slabs[d][...] = upright[pl.ds(top + HALO * (1 - odd), rows)]
    scalars[1].wait()
    scalars[2].wait()


def load_kernel(n, rows, after, *refs):
    del after
    count = (len(refs) - 7) // 2
    direct, (query, key) = refs[:count], refs[count : count + 2]
    loaded, (w_query, w_key) = refs[count + 2 : 2 * count + 2], refs[2 * count + 2 : 2 * count + 4]
    query_in, key_in, sems = refs[2 * count + 4 :]
    heads, _, head_dim = w_query.shape
    pairs = list(zip(direct, loaded)) + [(query, query_in), (key, key_in)]
    copies = [pltpu.make_async_copy(*pair, sems.at[i]) for i, pair in enumerate(pairs)]
    for copy in copies:
        copy.start()
    for copy in copies:
        copy.wait()
    w_key[...] = key_in[...].T
    for h in range(heads):
        w_query[h] = query_in[:, h * head_dim : (h + 1) * head_dim]


def columns_of(segment, size):
    return pl.ds(pl.multiple_of(segment * size, size), size)


def whole_rows(n, owner, slabs, out, first):
    band = lax.axis_index("lat")
    me = lax.axis_index("lon")
    count, size = slabs[0].shape[:2]
    for d in range(n):
        segment = owner[lax.rem(me + n - d, n), band]
        out[pl.ds(first, count), columns_of(segment, size)] = slabs[d][...]


def edge_kernel(n, rows, owner, *rest):
    del rows
    whole_rows(n, owner, rest[:n], rest[n], 0)


def spread(taps, r, row):
    cols, chans = row.shape
    taps[r, :, :chans] = pltpu.roll(row, 1, 0).astype(jnp.bfloat16)
    taps[r, :, chans : 2 * chans] = row.astype(jnp.bfloat16)
    taps[r, :, 2 * chans :] = pltpu.roll(row, cols - 1, 0).astype(jnp.bfloat16)


def convolve(taps, weight, bias, first, count):
    cols, width = taps.shape[1:]
    windows = [taps[first + i : first + i + count].reshape(count * cols, width) for i in range(3)]
    depth = weight.shape[0] * width
    product = jnp.dot(
        jnp.concatenate(windows, axis=1),
        weight[...].reshape(depth, weight.shape[2]),
        preferred_element_type=jnp.float32,
    )
    return product + bias[...]


def silu(x):
    return x / (1.0 + jnp.exp(-x))


def live_count(counts, row):
    inside = (row >= 0) & (row < counts.shape[0])
    return jnp.where(inside, counts[jnp.clip(row, 0, counts.shape[0] - 1)], 0)


def by_last(a, b):
    return lax.dot_general(a, b, (((1,), (1,)), ((), ())), preferred_element_type=jnp.float32)


def attend(segments, span, limits, mixed, normed, keys, values, w_query, w_out, results, here, scores, expo, turned):
    rows, chans = len(limits), mixed.shape[1]
    size = here.shape[0] // (rows * len(segments))
    heads, _, head_dim = w_query.shape
    cols = mixed.shape[0] // rows
    width = heads * size
    blocks = [(s * rows + r, s, r) for s in range(len(segments)) for r in range(*span)]
    low, high = blocks[0][0], blocks[-1][0] + 1

    def cells(s, r):
        return columns_of(segments[s] + r * (cols // size), size)

    for b, s, r in blocks:
        here[b * size : (b + 1) * size, :] = normed[cells(s, r), :]
    own = here[low * size : high * size, :]
    queries = [jnp.dot(own, w_query[h], preferred_element_type=jnp.float32) for h in range(heads)]
    queries = [query.astype(jnp.bfloat16) for query in queries]
    for b, s, r in blocks:
        part = [query[(b - low) * size : (b - low + 1) * size] for query in queries]
        scores[b] = by_last(keys[r * cols : (r + 1) * cols, :], jnp.concatenate(part, axis=0))
    key_at = lax.broadcasted_iota(jnp.int32, (cols, width), 0)
    scale = math.log2(math.e) / head_dim**0.5
    shares = {}
    for b, s, r in blocks:
        part = jnp.where(key_at < limits[r], scores[b], -jnp.inf)
        part = jnp.exp2((part - jnp.max(part, axis=0, keepdims=True)) * scale)
        shares[b] = 1.0 / jnp.sum(part, axis=0, keepdims=True)
        expo[b] = part.astype(jnp.bfloat16)
    for b, s, r in blocks:
        summed = jnp.dot(values[:, r * cols : (r + 1) * cols], expo[b], preferred_element_type=jnp.float32)
        turned[:, b * width : (b + 1) * width] = (summed * shares[b]).astype(jnp.bfloat16)
    attended = turned[:, low * width : high * width].T
    update = jnp.zeros(own.shape, jnp.float32)
    for h in range(heads):
        starts = [(b - low) * width + h * size for b, *_ in blocks]
        part = jnp.concatenate([attended[start : start + size] for start in starts], axis=0)
        weight = w_out[h * head_dim : (h + 1) * head_dim, :]
        update = update + jnp.dot(part, weight, preferred_element_type=jnp.float32)
    for b, s, r in blocks:
        cell = segments[s] * size + lax.broadcasted_iota(jnp.int32, (size, chans), 0)
        part = jnp.where(cell < limits[r], update[(b - low) * size : (b - low + 1) * size], 0.0)
        results[s][r * size : (r + 1) * size, :] = (mixed[cells(s, r), :].astype(jnp.float32) + part).astype(jnp.bfloat16)


def main_kernel(first, n, rows, owner, counts, *rest):
    slabs, sent, received = rest[:n], rest[n], rest[n + 1]
    w_conv1, b_conv1, w_conv2, b_conv2, w_key, w_value, w_query, w_out = rest[n + 2 : n + 10]
    result, mixed, normed, keys, values = rest[n + 10 : n + 15]
    grid, taps, acts, *scratch = rest[n + 15 :]
    band = lax.axis_index("lat")
    me = lax.axis_index("lon")
    group = group_of(band, me, n)
    odd = group % 2
    cols, chans = sent.shape[1:]
    cell = lax.broadcasted_iota(jnp.int32, (cols, chans), 0)
    first_row = band * (rows * n) + group * rows
    whole_rows(n, owner, slabs, grid, 2 * HALO * (1 - odd))
    grid[pl.ds(HALO + (rows - HALO) * odd, HALO)] = sent[...]
    grid[pl.ds((rows + HALO) * odd, HALO)] = received[...]
    limits = [live_count(counts, first_row - 1 + r) for r in range(rows + HALO)]

    def spread_inputs(start, stop):
        for r in range(start, stop):
            spread(taps, r, grid[r].astype(jnp.float32))

    def spread_acts(start, stop, product):
        act = silu(product)
        for r in range(start, stop):
            at = slice((r - start) * cols, (r - start + 1) * cols)
            spread(acts, r, jnp.where(cell < limits[r], act[at], 0.0))

    def mix(start, stop, product):
        for r in range(start, stop):
            here = grid[r + HALO].astype(jnp.float32) + product[(r - start) * cols : (r - start + 1) * cols]
            here = jnp.where(cell < limits[r + 1], here, 0.0)
            mixed[r * cols : (r + 1) * cols, :] = here.astype(jnp.bfloat16)
        at = slice(start * cols, stop * cols)
        flat = mixed[at, :].astype(jnp.float32)
        scaled = (flat * lax.rsqrt(jnp.mean(flat * flat, axis=1, keepdims=True) + 1e-06)).astype(jnp.bfloat16)
        normed[at, :] = scaled
        keys[at, :] = jnp.dot(scaled, w_key[...], preferred_element_type=jnp.float32).astype(jnp.bfloat16)
        values[:, at] = by_last(w_value[...], scaled).astype(jnp.bfloat16)

    total = rows + HALO
    half = total // 2 + total // 8
    low = half - HALO
    spread_inputs(0, half + HALO)
    first_low = convolve(taps, w_conv1, b_conv1, 0, half)
    spread_inputs(half + HALO, total + HALO)
    first_high = convolve(taps, w_conv1, b_conv1, half, total - half)
    spread_acts(0, half, first_low)
    if low:
        second_low = convolve(acts, w_conv2, b_conv2, 0, low)
    spread_acts(half, total, first_high)
    second_high = convolve(acts, w_conv2, b_conv2, low, rows - low)
    result[rows * (cols // n) :, :] = jnp.zeros((AHEAD, chans), result.dtype)
    segments = [owner[lax.rem(me + first, n), band]]

    def attend_rows(*span):
        shared = limits[1 : rows + 1], mixed, normed, keys, values, w_query, w_out
        attend(segments, span, *shared, [result], *scratch)

    if low:
        mix(0, low, second_low)
        attend_rows(0, low)
    mix(low, rows, second_high)
    attend_rows(low, rows)


def rest_kernel(moves, n, rows, owner, counts, *rest):
    mixed, normed, keys, values, w_query, w_out = rest[:6]
    results, scratch = rest[6 : 6 + len(moves)], rest[6 + len(moves) :]
    band = lax.axis_index("lat")
    me = lax.axis_index("lon")
    first_row = band * (rows * n) + group_of(band, me, n) * rows
    limits = [counts[first_row + r] for r in range(rows)]
    segments = [owner[lax.rem(me + d, n), band] for d in moves]
    attend(segments, (0, rows), limits, mixed, normed, keys, values, w_query, w_out, results, *scratch)


def store_kernel(n, rows, rotation, *rest):
    slabs, (out, staged, upright, turned, sems) = rest[:n], rest[n:]
    band = lax.axis_index("lat")
    me = lax.axis_index("lon")
    depth = GROUP // out.shape[0]
    pieces = out.shape[0] // depth
    for d in range(n):
        top = group_of(band, lax.rem(me + n - d, n), n) * rows
        upright[pl.ds(top, rows)] = slabs[d][: rows * out.shape[0], :].reshape(rows, *out.shape[1:])

    def piece(g):
        at = pl.ds(g * depth, depth)
        return pltpu.make_async_copy(turned.at[at], out.at[at], sems.at[g])

    turn(rotation[me, band] % 4, staged, upright, turned, lambda g: None, lambda g: piece(g).start())
    for g in range(pieces):
        piece(g).wait()


def on_device(
    bands,
    n,
    fields,
    w_conv1,
    b_conv1,
    w_conv2,
    b_conv2,
    w_query,
    w_key,
    w_value,
    w_out,
    rotation,
    owner,
    counts,
):
    size, _, chans = fields.shape
    rows = size // n
    inner = rows - HALO
    cols = size * n
    bf16 = jnp.bfloat16
    smem = pl.BlockSpec(memory_space=pltpu.SMEM)
    vmem = pl.BlockSpec(memory_space=pltpu.VMEM)
    hbm = pl.BlockSpec(memory_space=pltpu.HBM)
    params = pltpu.CompilerParams(vmem_limit_bytes=VMEM_BYTES)
    pieces = size * size // GROUP

    def call(kernel, name, out, scalars, arrays, scratch, array_spec=vmem, scalar_spec=smem, out_spec=vmem):
        many = isinstance(out, list)
        return pl.pallas_call(
            functools.partial(kernel, n, rows),
            out_shape=out,
            in_specs=[scalar_spec] * len(scalars) + [array_spec] * len(arrays),
            out_specs=[out_spec] * len(out) if many else out_spec,
            scratch_shapes=scratch,
            compiler_params=params,
            name=name,
        )(*scalars, *arrays)

    def array(*shape):
        return jax.ShapeDtypeStruct(shape, bf16)

    order = sorted(range(1, n), key=lambda d: -min(d, n - d))

    def around_by(x, d):
        return lax.ppermute(x, "lon", [(i, (i + d) % n) for i in range(n)])

    def around(parts):
        moved = {d: around_by(parts[d], d) for d in order}
        return [parts[0]] + [moved[d] for d in range(1, n)]

    def in_hbm(x):
        return pltpu.with_memory_space_constraint(x, pltpu.HBM)

    rotation, owner = in_hbm(rotation.T), in_hbm(owner.T)
    loaded = [counts]
    loaded += [w_conv1.reshape(3, 3 * chans, chans), b_conv1.reshape(1, chans)]
    loaded += [w_conv2.reshape(3, 3 * chans, chans), b_conv2.reshape(1, chans), w_value.T, w_out]
    loaded = [in_hbm(x) for x in loaded]
    turned = [in_hbm(x) for x in (w_query, w_key.T)]
    staging = pltpu.VMEM((chans // LANES, size * (size + 8), LANES), jnp.float32)
    block = pltpu.VMEM((size, size, chans), bf16)

    slabs = [array(HALO, size, chans)] * n + [array(rows, size, chans)] * n
    scratch = [staging, block, block, pltpu.SMEM(rotation.shape, rotation.dtype)]
    scratch += [pltpu.SemaphoreType.DMA((3,)), pltpu.SemaphoreType.DMA((pieces,))]
    held = slabs + [pltpu.VMEM(x.shape, x.dtype) for x in (rotation, owner)]
    *slabs, rotation, owner = call(send_kernel, "send", held, [rotation, owner], [in_hbm(fields)], scratch, hbm, hbm)
    edges = around(slabs[:n])
    slabs = around(slabs[n:])

    snake = [a * n + shard_of(a, g, n) for a in range(bands) for g in range(n)]
    pairs = [(snake[i], snake[i + 1 if i % 2 else i - 1]) for i in range(1, bands * n - 1)]
    sent = call(edge_kernel, "edge", array(HALO, cols, chans), [owner], edges, [])
    received = lax.ppermute(sent, ("lat", "lon"), pairs)

    head_dim = w_key.shape[1]
    heads = chans // head_dim
    held = [pltpu.VMEM(x.shape, x.dtype) for x in loaded]
    held += [pltpu.VMEM((heads, chans, head_dim), bf16), pltpu.VMEM(w_key.shape, bf16)]
    scratch = [pltpu.VMEM(x.shape, bf16) for x in turned] + [pltpu.SemaphoreType.DMA((len(loaded) + 2,))]
    loaded = call(load_kernel, "load", held, [sent], loaded + turned, scratch, hbm, hbm)
    counts, *convs, w_value, w_out, w_query, w_key = loaded

    def taps(count):
        return pltpu.VMEM((count, cols, 3 * chans), bf16)

    def working(segments):
        blocks, width = segments * rows, heads * size
        return [
            pltpu.VMEM((blocks * size, chans), bf16),
            pltpu.VMEM((blocks, cols, width), jnp.float32),
            pltpu.VMEM((blocks, cols, width), bf16),
            pltpu.VMEM((head_dim, blocks * width), bf16),
        ]

    cells = rows * cols
    result = array(rows * size, chans)
    first, *others = [*order, 0]
    results = {}
    results[first], *held = call(
        functools.partial(main_kernel, first),
        "main",
        [array(rows * size + AHEAD, chans), array(cells, chans), array(cells, chans), array(cells, head_dim), array(head_dim, cells)],
        [owner, counts],
        slabs + [sent, received, *convs, w_key, w_value, w_query, w_out],
        [pltpu.VMEM((rows + 2 * HALO, cols, chans), bf16), taps(rows + 2 * HALO), taps(rows + HALO)] + working(1),
    )
    moved = {first: around_by(results[first], first)}
    rest = call(
        functools.partial(rest_kernel, others),
        "rest",
        [result] * len(others),
        [owner, counts],
        held + [w_query, w_out],
        working(len(others)),
    )
    for d, x in zip(others, rest):
        moved[d] = around_by(x, d) if d else x
    slabs = [moved[d] for d in range(n)]
    scratch = [staging, block, block, pltpu.SemaphoreType.DMA((pieces,))]
    return call(store_kernel, "store", array(*fields.shape), [rotation], slabs, scratch, out_spec=hbm)


def solution(mesh):
    in_specs = (P("lat", "lon", None), P(), P(), P(), P(), P(), P(), P(), P(), P(), P(), P())
    out_specs = P("lat", "lon", None)
    body = functools.partial(on_device, mesh.shape["lat"], mesh.shape["lon"])
    return jax.shard_map(body, mesh=mesh, in_specs=in_specs, out_specs=out_specs, check_vma=False)
```

```python
import functools
import math

import jax
import jax.numpy as jnp
from jax import lax
from jax.experimental import pallas as pl
from jax.experimental.pallas import tpu as pltpu
from jax.sharding import PartitionSpec as P

HALO = 2
LANES = 128
GROUP = 256
AHEAD = 16
VMEM_BYTES = 28 * 1024 * 1024


def group_of(band, shard, n):
    outer = jnp.where((shard == n - 2) == (band % 2 == 0), 0, n - 1)
    return jnp.where(shard < n - 2, shard + 1, outer)


def shard_of(band, group, n):
    if 0 < group < n - 1:
        return group - 1
    return n - 2 if (group == 0) == (band % 2 == 0) else n - 1


def first_held(group, rows):
    return group * rows - HALO * (group % 2)


def turn(quarter, staged, block, out, ready, done):
    size, _, chans = block.shape
    tiles = staged.shape[0]
    pitch = staged.shape[1] // size
    depth = GROUP // size
    pieces = size // depth

    def column(col):
        parts = [staged[t, pl.ds(col, size, stride=pitch), :] for t in range(tiles)]
        return jnp.concatenate(parts, axis=1).astype(jnp.bfloat16)

    def keep(i, row):
        for t in range(tiles):
            staged[t, pl.ds(i * pitch, size), :] = row[:, t * LANES : (t + 1) * LANES]

    @pl.when(quarter == 0)
    def _():
        for g in range(pieces):
            ready(g)
            out[g * depth : (g + 1) * depth] = block[g * depth : (g + 1) * depth]
            done(g)

    @pl.when(quarter == 1)
    def _():
        for i in range(size):
            if i % depth == 0:
                ready(i // depth)
            keep(i, block[i].astype(jnp.float32))
        for i in range(size):
            out[i] = column(size - 1 - i)
            if i % depth == depth - 1:
                done(i // depth)

    @pl.when(quarter == 2)
    def _():
        i = lax.broadcasted_iota(jnp.int32, (GROUP, GROUP), 0)
        j = lax.broadcasted_iota(jnp.int32, (GROUP, GROUP), 1)
        backwards = jnp.where(i + j == GROUP - 1, 1.0, 0.0).astype(jnp.bfloat16)
        for g in reversed(range(pieces)):
            ready(pieces - 1 - g)
            cells = block[size - (g + 1) * depth : size - g * depth].reshape(GROUP, chans)
            turned = jnp.dot(backwards, cells, preferred_element_type=jnp.float32).astype(jnp.bfloat16)
            out[g * depth : (g + 1) * depth] = turned.reshape(depth, size, chans)
            done(g)

    @pl.when(quarter == 3)
    def _():
        for i in range(size):
            if i % depth == 0:
                ready(i // depth)
            keep(size - 1 - i, block[i].astype(jnp.float32))
        for i in range(size):
            out[i] = column(i)
            if i % depth == depth - 1:
                done(i // depth)


def send_kernel(first, n, rows, rotation_in, owner_in, fields, *rest):
    edges = [*rest[:first], None, *rest[first : n - 1]]
    slabs, (rotation_out, owner_out) = rest[n - 1 : 2 * n - 1], rest[2 * n - 1 : 2 * n + 1]
    staged, block, upright, rotation, scalar_sems, sems = rest[2 * n + 1 :]
    band = lax.axis_index("lat")
    me = lax.axis_index("lon")
    depth = GROUP // fields.shape[0]

    def piece(g):
        at = pl.ds(g * depth, depth)
        return pltpu.make_async_copy(fields.at[at], block.at[at], sems.at[g])

    scalars = [
        pltpu.make_async_copy(rotation_in, rotation, scalar_sems.at[0]),
        pltpu.make_async_copy(rotation_in, rotation_out, scalar_sems.at[1]),
        pltpu.make_async_copy(owner_in, owner_out, scalar_sems.at[2]),
    ]
    for copy in scalars:
        copy.start()
    for g in range(fields.shape[0] // depth):
        piece(g).start()
    scalars[0].wait()
    turn((4 - rotation[me, band]) % 4, staged, block, upright, lambda g: piece(g).wait(), lambda g: None)
    for d in range(n):
        group = group_of(band, lax.rem(me + d, n), n)
        top, odd = first_held(group, rows), group % 2
        if d == first:
            slabs[d][...] = upright[pl.ds(top, rows + HALO)]
            continue
        edges[d][...] = upright[pl.ds(top + rows * odd, HALO)]
        slabs[d][...] = upright[pl.ds(top + HALO * (1 - odd), rows)]
    scalars[1].wait()
    scalars[2].wait()


def load_kernel(n, rows, after, *refs):
    del after
    count = (len(refs) - 7) // 2
    direct, (query, key) = refs[:count], refs[count : count + 2]
    loaded, (w_query, w_key) = refs[count + 2 : 2 * count + 2], refs[2 * count + 2 : 2 * count + 4]
    query_in, key_in, sems = refs[2 * count + 4 :]
    heads, _, head_dim = w_query.shape
    pairs = list(zip(direct, loaded)) + [(query, query_in), (key, key_in)]
    copies = [pltpu.make_async_copy(*pair, sems.at[i]) for i, pair in enumerate(pairs)]
    for copy in copies:
        copy.start()
    for copy in copies:
        copy.wait()
    w_key[...] = key_in[...].T
    for h in range(heads):
        w_query[h] = query_in[:, h * head_dim : (h + 1) * head_dim]


def columns_of(segment, size):
    return pl.ds(pl.multiple_of(segment * size, size), size)


def whole_rows(n, count, start, owner, slabs, out, first):
    band = lax.axis_index("lat")
    me = lax.axis_index("lon")
    size = slabs[0].shape[1]
    for d, slab in enumerate(slabs):
        segment = owner[lax.rem(me + n - d, n), band]
        piece = slab[...] if slab.shape[0] == count else slab[pl.ds(start, count)]
        out[pl.ds(first, count), columns_of(segment, size)] = piece


def edge_kernel(n, rows, owner, *rest):
    odd = group_of(lax.axis_index("lat"), lax.axis_index("lon"), n) % 2
    whole_rows(n, HALO, rows * odd, owner, rest[:n], rest[n], 0)


def spread(taps, r, row):
    cols, chans = row.shape
    taps[r, :, :chans] = pltpu.roll(row, 1, 0).astype(jnp.bfloat16)
    taps[r, :, chans : 2 * chans] = row.astype(jnp.bfloat16)
    taps[r, :, 2 * chans :] = pltpu.roll(row, cols - 1, 0).astype(jnp.bfloat16)


def convolve(taps, weight, bias, first, count):
    cols, width = taps.shape[1:]
    windows = [taps[first + i : first + i + count].reshape(count * cols, width) for i in range(3)]
    depth = weight.shape[0] * width
    product = jnp.dot(
        jnp.concatenate(windows, axis=1),
        weight[...].reshape(depth, weight.shape[2]),
        preferred_element_type=jnp.float32,
    )
    return product + bias[...]


def silu(x):
    return x / (1.0 + jnp.exp(-x))


def live_count(counts, row):
    inside = (row >= 0) & (row < counts.shape[0])
    return jnp.where(inside, counts[jnp.clip(row, 0, counts.shape[0] - 1)], 0)


def by_last(a, b):
    return lax.dot_general(a, b, (((1,), (1,)), ((), ())), preferred_element_type=jnp.float32)


def attend(segments, span, limits, mixed, normed, keys, values, w_query, w_out, results, here, scores, expo, turned):
    rows, chans = len(limits), mixed.shape[1]
    size = here.shape[0] // (rows * len(segments))
    heads, _, head_dim = w_query.shape
    cols = mixed.shape[0] // rows
    width = heads * size
    blocks = [(s * rows + r, s, r) for s in range(len(segments)) for r in range(*span)]
    low, high = blocks[0][0], blocks[-1][0] + 1

    def cells(s, r):
        return columns_of(segments[s] + r * (cols // size), size)

    for b, s, r in blocks:
        here[b * size : (b + 1) * size, :] = normed[cells(s, r), :]
    own = here[low * size : high * size, :]
    queries = [jnp.dot(own, w_query[h], preferred_element_type=jnp.float32) for h in range(heads)]
    queries = [query.astype(jnp.bfloat16) for query in queries]
    for b, s, r in blocks:
        part = [query[(b - low) * size : (b - low + 1) * size] for query in queries]
        scores[b] = by_last(keys[r * cols : (r + 1) * cols, :], jnp.concatenate(part, axis=0))
    key_at = lax.broadcasted_iota(jnp.int32, (cols, width), 0)
    scale = math.log2(math.e) / head_dim**0.5
    shares = {}
    for b, s, r in blocks:
        part = jnp.where(key_at < limits[r], scores[b], -jnp.inf)
        part = jnp.exp2((part - jnp.max(part, axis=0, keepdims=True)) * scale)
        shares[b] = 1.0 / jnp.sum(part, axis=0, keepdims=True)
        expo[b] = part.astype(jnp.bfloat16)
    for b, s, r in blocks:
        summed = jnp.dot(values[:, r * cols : (r + 1) * cols], expo[b], preferred_element_type=jnp.float32)
        turned[:, b * width : (b + 1) * width] = (summed * shares[b]).astype(jnp.bfloat16)
    attended = turned[:, low * width : high * width].T
    update = jnp.zeros(own.shape, jnp.float32)
    for h in range(heads):
        starts = [(b - low) * width + h * size for b, *_ in blocks]
        part = jnp.concatenate([attended[start : start + size] for start in starts], axis=0)
        weight = w_out[h * head_dim : (h + 1) * head_dim, :]
        update = update + jnp.dot(part, weight, preferred_element_type=jnp.float32)
    for b, s, r in blocks:
        cell = segments[s] * size + lax.broadcasted_iota(jnp.int32, (size, chans), 0)
        part = jnp.where(cell < limits[r], update[(b - low) * size : (b - low + 1) * size], 0.0)
        results[s][r * size : (r + 1) * size, :] = (mixed[cells(s, r), :].astype(jnp.float32) + part).astype(jnp.bfloat16)


def main_kernel(first, n, rows, owner, counts, *rest):
    slabs, sent, received = rest[:n], rest[n], rest[n + 1]
    w_conv1, b_conv1, w_conv2, b_conv2, w_key, w_value, w_query, w_out = rest[n + 2 : n + 10]
    result, mixed, normed, keys, values = rest[n + 10 : n + 15]
    grid, taps, acts, *scratch = rest[n + 15 :]
    band = lax.axis_index("lat")
    me = lax.axis_index("lon")
    group = group_of(band, me, n)
    odd = group % 2
    cols, chans = sent.shape[1:]
    cell = lax.broadcasted_iota(jnp.int32, (cols, chans), 0)
    first_row = band * (rows * n) + group * rows
    whole_rows(n, rows, HALO * (1 - odd), owner, slabs, grid, 2 * HALO * (1 - odd))
    grid[pl.ds(HALO + (rows - HALO) * odd, HALO)] = sent[...]
    grid[pl.ds((rows + HALO) * odd, HALO)] = received[...]
    limits = [live_count(counts, first_row - 1 + r) for r in range(rows + HALO)]

    def spread_inputs(start, stop):
        for r in range(start, stop):
            spread(taps, r, grid[r].astype(jnp.float32))

    def spread_acts(start, stop, product):
        act = silu(product)
        for r in range(start, stop):
            at = slice((r - start) * cols, (r - start + 1) * cols)
            spread(acts, r, jnp.where(cell < limits[r], act[at], 0.0))

    def mix(start, stop, product):
        for r in range(start, stop):
            here = grid[r + HALO].astype(jnp.float32) + product[(r - start) * cols : (r - start + 1) * cols]
            here = jnp.where(cell < limits[r + 1], here, 0.0)
            mixed[r * cols : (r + 1) * cols, :] = here.astype(jnp.bfloat16)
        at = slice(start * cols, stop * cols)
        flat = mixed[at, :].astype(jnp.float32)
        scaled = (flat * lax.rsqrt(jnp.mean(flat * flat, axis=1, keepdims=True) + 1e-06)).astype(jnp.bfloat16)
        normed[at, :] = scaled
        keys[at, :] = jnp.dot(scaled, w_key[...], preferred_element_type=jnp.float32).astype(jnp.bfloat16)
        values[:, at] = by_last(w_value[...], scaled).astype(jnp.bfloat16)

    total = rows + HALO
    half = total // 2
    low = half - HALO
    spread_inputs(0, half + HALO)
    first_low = convolve(taps, w_conv1, b_conv1, 0, half)
    spread_inputs(half + HALO, total + HALO)
    first_high = convolve(taps, w_conv1, b_conv1, half, total - half)
    spread_acts(0, half, first_low)
    if low:
        second_low = convolve(acts, w_conv2, b_conv2, 0, low)
    spread_acts(half, total, first_high)
    second_high = convolve(acts, w_conv2, b_conv2, low, rows - low)
    result[rows * (cols // n) :, :] = jnp.zeros((AHEAD, chans), result.dtype)
    segments = [owner[lax.rem(me + first, n), band]]
    if low:
        mix(0, low, second_low)
    mix(low, rows, second_high)
    shared = limits[1 : rows + 1], mixed, normed, keys, values, w_query, w_out
    attend(segments, (0, rows), *shared, [result], *scratch)


def rest_kernel(moves, n, rows, owner, counts, *rest):
    mixed, normed, keys, values, w_query, w_out = rest[:6]
    results, scratch = rest[6 : 6 + len(moves)], rest[6 + len(moves) :]
    band = lax.axis_index("lat")
    me = lax.axis_index("lon")
    first_row = band * (rows * n) + group_of(band, me, n) * rows
    limits = [counts[first_row + r] for r in range(rows)]
    segments = [owner[lax.rem(me + d, n), band] for d in moves]
    attend(segments, (0, rows), limits, mixed, normed, keys, values, w_query, w_out, results, *scratch)


def store_kernel(n, rows, rotation, *rest):
    slabs, (out, staged, upright, turned, sems) = rest[:n], rest[n:]
    band = lax.axis_index("lat")
    me = lax.axis_index("lon")
    depth = GROUP // out.shape[0]
    pieces = out.shape[0] // depth
    for d in range(n):
        top = group_of(band, lax.rem(me + n - d, n), n) * rows
        upright[pl.ds(top, rows)] = slabs[d][: rows * out.shape[0], :].reshape(rows, *out.shape[1:])

    def piece(g):
        at = pl.ds(g * depth, depth)
        return pltpu.make_async_copy(turned.at[at], out.at[at], sems.at[g])

    turn(rotation[me, band] % 4, staged, upright, turned, lambda g: None, lambda g: piece(g).start())
    for g in range(pieces):
        piece(g).wait()


def on_device(
    bands,
    n,
    fields,
    w_conv1,
    b_conv1,
    w_conv2,
    b_conv2,
    w_query,
    w_key,
    w_value,
    w_out,
    rotation,
    owner,
    counts,
):
    size, _, chans = fields.shape
    rows = size // n
    inner = rows - HALO
    cols = size * n
    bf16 = jnp.bfloat16
    smem = pl.BlockSpec(memory_space=pltpu.SMEM)
    vmem = pl.BlockSpec(memory_space=pltpu.VMEM)
    hbm = pl.BlockSpec(memory_space=pltpu.HBM)
    params = pltpu.CompilerParams(vmem_limit_bytes=VMEM_BYTES)
    pieces = size * size // GROUP

    def call(kernel, name, out, scalars, arrays, scratch, array_spec=vmem, scalar_spec=smem, out_spec=vmem):
        many = isinstance(out, list)
        return pl.pallas_call(
            functools.partial(kernel, n, rows),
            out_shape=out,
            in_specs=[scalar_spec] * len(scalars) + [array_spec] * len(arrays),
            out_specs=[out_spec] * len(out) if many else out_spec,
            scratch_shapes=scratch,
            compiler_params=params,
            name=name,
        )(*scalars, *arrays)

    def array(*shape):
        return jax.ShapeDtypeStruct(shape, bf16)

    order = sorted(range(1, n), key=lambda d: -min(d, n - d))

    def around_by(x, d):
        return lax.ppermute(x, "lon", [(i, (i + d) % n) for i in range(n)])

    def around(parts):
        moved = {d: around_by(parts[d], d) for d in order}
        return [parts[0]] + [moved[d] for d in range(1, n)]

    def in_hbm(x):
        return pltpu.with_memory_space_constraint(x, pltpu.HBM)

    rotation, owner = in_hbm(rotation.T), in_hbm(owner.T)
    loaded = [counts]
    loaded += [w_conv1.reshape(3, 3 * chans, chans), b_conv1.reshape(1, chans)]
    loaded += [w_conv2.reshape(3, 3 * chans, chans), b_conv2.reshape(1, chans), w_value.T, w_out]
    loaded = [in_hbm(x) for x in loaded]
    turned = [in_hbm(x) for x in (w_query, w_key.T)]
    staging = pltpu.VMEM((chans // LANES, size * (size + 8), LANES), jnp.float32)
    block = pltpu.VMEM((size, size, chans), bf16)

    first = order[0]
    slabs = [array(HALO, size, chans)] * (n - 1)
    slabs += [array(rows + (HALO if d == first else 0), size, chans) for d in range(n)]
    scratch = [staging, block, block, pltpu.SMEM(rotation.shape, rotation.dtype)]
    scratch += [pltpu.SemaphoreType.DMA((3,)), pltpu.SemaphoreType.DMA((pieces,))]
    held = slabs + [pltpu.VMEM(x.shape, x.dtype) for x in (rotation, owner)]
    *slabs, rotation, owner = call(functools.partial(send_kernel, first), "send", held, [rotation, owner], [in_hbm(fields)], scratch, hbm, hbm)
    edges, slabs = slabs[: n - 1], around(slabs[n - 1 :])
    edges.insert(first, slabs[first])
    edges = [x if d in (0, first) else around_by(x, d) for d, x in enumerate(edges)]

    snake = [a * n + shard_of(a, g, n) for a in range(bands) for g in range(n)]
    pairs = [(snake[i], snake[i + 1 if i % 2 else i - 1]) for i in range(1, bands * n - 1)]
    sent = call(edge_kernel, "edge", array(HALO, cols, chans), [owner], edges, [])
    received = lax.ppermute(sent, ("lat", "lon"), pairs)

    head_dim = w_key.shape[1]
    heads = chans // head_dim
    held = [pltpu.VMEM(x.shape, x.dtype) for x in loaded]
    held += [pltpu.VMEM((heads, chans, head_dim), bf16), pltpu.VMEM(w_key.shape, bf16)]
    scratch = [pltpu.VMEM(x.shape, bf16) for x in turned] + [pltpu.SemaphoreType.DMA((len(loaded) + 2,))]
    loaded = call(load_kernel, "load", held, [sent], loaded + turned, scratch, hbm, hbm)
    counts, *convs, w_value, w_out, w_query, w_key = loaded

    def taps(count):
        return pltpu.VMEM((count, cols, 3 * chans), bf16)

    def working(segments):
        blocks, width = segments * rows, heads * size
        return [
            pltpu.VMEM((blocks * size, chans), bf16),
            pltpu.VMEM((blocks, cols, width), jnp.float32),
            pltpu.VMEM((blocks, cols, width), bf16),
            pltpu.VMEM((head_dim, blocks * width), bf16),
        ]

    cells = rows * cols
    result = array(rows * size, chans)
    first, *others = [*order, 0]
    results = {}
    results[first], *held = call(
        functools.partial(main_kernel, first),
        "main",
        [array(rows * size + AHEAD, chans), array(cells, chans), array(cells, chans), array(cells, head_dim), array(head_dim, cells)],
        [owner, counts],
        slabs + [sent, received, *convs, w_key, w_value, w_query, w_out],
        [pltpu.VMEM((rows + 2 * HALO, cols, chans), bf16), taps(rows + 2 * HALO), taps(rows + HALO)] + working(1),
    )
    moved = {first: around_by(results[first], first)}
    rest = call(
        functools.partial(rest_kernel, others),
        "rest",
        [result] * len(others),
        [owner, counts],
        held + [w_query, w_out],
        working(len(others)),
    )
    for d, x in zip(others, rest):
        moved[d] = around_by(x, d) if d else x
    slabs = [moved[d] for d in range(n)]
    scratch = [staging, block, block, pltpu.SemaphoreType.DMA((pieces,))]
    return call(store_kernel, "store", array(*fields.shape), [rotation], slabs, scratch, out_spec=hbm)


def solution(mesh):
    in_specs = (P("lat", "lon", None), P(), P(), P(), P(), P(), P(), P(), P(), P(), P(), P())
    out_specs = P("lat", "lon", None)
    body = functools.partial(on_device, mesh.shape["lat"], mesh.shape["lon"])
    return jax.shard_map(body, mesh=mesh, in_specs=in_specs, out_specs=out_specs, check_vma=False)
```

```python
import functools
import math

import jax
import jax.numpy as jnp
from jax import lax
from jax.experimental import pallas as pl
from jax.experimental.pallas import tpu as pltpu
from jax.sharding import PartitionSpec as P

HALO = 2
LANES = 128
GROUP = 256
AHEAD = 16
VMEM_BYTES = 28 * 1024 * 1024


def group_of(band, shard, n):
    outer = jnp.where((shard == n - 2) == (band % 2 == 0), 0, n - 1)
    return jnp.where(shard < n - 2, shard + 1, outer)


def shard_of(band, group, n):
    if 0 < group < n - 1:
        return group - 1
    return n - 2 if (group == 0) == (band % 2 == 0) else n - 1


def first_held(group, rows):
    return group * rows - HALO * (group % 2)


def turn(quarter, staged, block, out, ready, done):
    size, _, chans = block.shape
    tiles = staged.shape[0]
    pitch = staged.shape[1] // size
    depth = GROUP // size
    pieces = size // depth

    def column(col):
        parts = [staged[t, pl.ds(col, size, stride=pitch), :] for t in range(tiles)]
        return jnp.concatenate(parts, axis=1).astype(jnp.bfloat16)

    def keep(i, row):
        for t in range(tiles):
            staged[t, pl.ds(i * pitch, size), :] = row[:, t * LANES : (t + 1) * LANES]

    @pl.when(quarter == 0)
    def _():
        for g in range(pieces):
            ready(g)
            out[g * depth : (g + 1) * depth] = block[g * depth : (g + 1) * depth]
            done(g)

    @pl.when(quarter == 1)
    def _():
        for i in range(size):
            if i % depth == 0:
                ready(i // depth)
            keep(i, block[i].astype(jnp.float32))
        for i in range(size):
            out[i] = column(size - 1 - i)
            if i % depth == depth - 1:
                done(i // depth)

    @pl.when(quarter == 2)
    def _():
        i = lax.broadcasted_iota(jnp.int32, (GROUP, GROUP), 0)
        j = lax.broadcasted_iota(jnp.int32, (GROUP, GROUP), 1)
        backwards = jnp.where(i + j == GROUP - 1, 1.0, 0.0).astype(jnp.bfloat16)
        for g in reversed(range(pieces)):
            ready(pieces - 1 - g)
            cells = block[size - (g + 1) * depth : size - g * depth].reshape(GROUP, chans)
            turned = jnp.dot(backwards, cells, preferred_element_type=jnp.float32).astype(jnp.bfloat16)
            out[g * depth : (g + 1) * depth] = turned.reshape(depth, size, chans)
            done(g)

    @pl.when(quarter == 3)
    def _():
        for i in range(size):
            if i % depth == 0:
                ready(i // depth)
            keep(size - 1 - i, block[i].astype(jnp.float32))
        for i in range(size):
            out[i] = column(i)
            if i % depth == depth - 1:
                done(i // depth)


def send_kernel(n, rows, rotation_in, owner_in, fields, *rest):
    edges, slabs, (rotation_out, owner_out) = rest[:n], rest[n : 2 * n], rest[2 * n : 2 * n + 2]
    staged, block, upright, rotation, scalar_sems, sems = rest[2 * n + 2 :]
    band = lax.axis_index("lat")
    me = lax.axis_index("lon")
    depth = GROUP // fields.shape[0]

    def piece(g):
        at = pl.ds(g * depth, depth)
        return pltpu.make_async_copy(fields.at[at], block.at[at], sems.at[g])

    scalars = [
        pltpu.make_async_copy(rotation_in, rotation, scalar_sems.at[0]),
        pltpu.make_async_copy(rotation_in, rotation_out, scalar_sems.at[1]),
        pltpu.make_async_copy(owner_in, owner_out, scalar_sems.at[2]),
    ]
    for copy in scalars:
        copy.start()
    for g in range(fields.shape[0] // depth):
        piece(g).start()
    scalars[0].wait()
    turn((4 - rotation[me, band]) % 4, staged, block, upright, lambda g: piece(g).wait(), lambda g: None)
    for d in range(n):
        group = group_of(band, lax.rem(me + d, n), n)
        top, odd = first_held(group, rows), group % 2
        edges[d][...] = upright[pl.ds(top + rows * odd, HALO)]
        slabs[d][...] = upright[pl.ds(top + HALO * (1 - odd), rows)]
    scalars[1].wait()
    scalars[2].wait()


def load_kernel(n, rows, after, *refs):
    del after
    count = (len(refs) - 7) // 2
    direct, (query, key) = refs[:count], refs[count : count + 2]
    loaded, (w_query, w_key) = refs[count + 2 : 2 * count + 2], refs[2 * count + 2 : 2 * count + 4]
    query_in, key_in, sems = refs[2 * count + 4 :]
    heads, _, head_dim = w_query.shape
    pairs = list(zip(direct, loaded)) + [(query, query_in), (key, key_in)]
    copies = [pltpu.make_async_copy(*pair, sems.at[i]) for i, pair in enumerate(pairs)]
    for copy in copies:
        copy.start()
    for copy in copies:
        copy.wait()
    w_key[...] = key_in[...].T
    for h in range(heads):
        w_query[h] = query_in[:, h * head_dim : (h + 1) * head_dim]


def columns_of(segment, size):
    return pl.ds(pl.multiple_of(segment * size, size), size)


def whole_rows(n, owner, slabs, out, first):
    band = lax.axis_index("lat")
    me = lax.axis_index("lon")
    count, size = slabs[0].shape[:2]
    for d in range(n):
        segment = owner[lax.rem(me + n - d, n), band]
        out[pl.ds(first, count), columns_of(segment, size)] = slabs[d][...]


def edge_kernel(n, rows, owner, *rest):
    del rows
    whole_rows(n, owner, rest[:n], rest[n], 0)


def spread(taps, r, row):
    cols, chans = row.shape
    taps[r, :, :chans] = pltpu.roll(row, 1, 0).astype(jnp.bfloat16)
    taps[r, :, chans : 2 * chans] = row.astype(jnp.bfloat16)
    taps[r, :, 2 * chans :] = pltpu.roll(row, cols - 1, 0).astype(jnp.bfloat16)


def convolve(taps, weight, bias, first, count):
    cols, width = taps.shape[1:]
    windows = [taps[first + i : first + i + count].reshape(count * cols, width) for i in range(3)]
    depth = weight.shape[0] * width
    product = jnp.dot(
        jnp.concatenate(windows, axis=1),
        weight[...].reshape(depth, weight.shape[2]),
        preferred_element_type=jnp.float32,
    )
    return product + bias[...]


def silu(x):
    half = 0.5 * x
    return half + half * jnp.tanh(half)


def live_count(counts, row):
    inside = (row >= 0) & (row < counts.shape[0])
    return jnp.where(inside, counts[jnp.clip(row, 0, counts.shape[0] - 1)], 0)


def by_last(a, b):
    return lax.dot_general(a, b, (((1,), (1,)), ((), ())), preferred_element_type=jnp.float32)


def attend(segments, span, limits, mixed, normed, keys, values, w_query, w_out, results, here, scores, expo, turned):
    rows, chans = len(limits), mixed.shape[1]
    size = here.shape[0] // (rows * len(segments))
    heads, _, head_dim = w_query.shape
    cols = mixed.shape[0] // rows
    width = heads * size
    blocks = [(s * rows + r, s, r) for s in range(len(segments)) for r in range(*span)]
    low, high = blocks[0][0], blocks[-1][0] + 1

    def cells(s, r):
        return columns_of(segments[s] + r * (cols // size), size)

    for b, s, r in blocks:
        here[b * size : (b + 1) * size, :] = normed[cells(s, r), :]
    own = here[low * size : high * size, :]
    queries = [jnp.dot(own, w_query[h], preferred_element_type=jnp.float32) for h in range(heads)]
    queries = [query.astype(jnp.bfloat16) for query in queries]
    for b, s, r in blocks:
        part = [query[(b - low) * size : (b - low + 1) * size] for query in queries]
        scores[b] = by_last(keys[r * cols : (r + 1) * cols, :], jnp.concatenate(part, axis=0))
    key_at = lax.broadcasted_iota(jnp.int32, (cols, width), 0)
    scale = math.log2(math.e) / head_dim**0.5
    shares = {}
    for b, s, r in blocks:
        part = jnp.where(key_at < limits[r], scores[b], -jnp.inf)
        part = jnp.exp2((part - jnp.max(part, axis=0, keepdims=True)) * scale)
        shares[b] = 1.0 / jnp.sum(part, axis=0, keepdims=True)
        expo[b] = part.astype(jnp.bfloat16)
    for b, s, r in blocks:
        summed = jnp.dot(values[:, r * cols : (r + 1) * cols], expo[b], preferred_element_type=jnp.float32)
        turned[:, b * width : (b + 1) * width] = (summed * shares[b]).astype(jnp.bfloat16)
    attended = turned[:, low * width : high * width].T
    update = jnp.zeros(own.shape, jnp.float32)
    for h in range(heads):
        starts = [(b - low) * width + h * size for b, *_ in blocks]
        part = jnp.concatenate([attended[start : start + size] for start in starts], axis=0)
        weight = w_out[h * head_dim : (h + 1) * head_dim, :]
        update = update + jnp.dot(part, weight, preferred_element_type=jnp.float32)
    for b, s, r in blocks:
        cell = segments[s] * size + lax.broadcasted_iota(jnp.int32, (size, chans), 0)
        part = jnp.where(cell < limits[r], update[(b - low) * size : (b - low + 1) * size], 0.0)
        results[s][r * size : (r + 1) * size, :] = (mixed[cells(s, r), :].astype(jnp.float32) + part).astype(jnp.bfloat16)


def main_kernel(first, n, rows, owner, counts, *rest):
    slabs, sent, received = rest[:n], rest[n], rest[n + 1]
    w_conv1, b_conv1, w_conv2, b_conv2, w_key, w_value, w_query, w_out = rest[n + 2 : n + 10]
    result, mixed, normed, keys, values = rest[n + 10 : n + 15]
    grid, taps, acts, *scratch = rest[n + 15 :]
    band = lax.axis_index("lat")
    me = lax.axis_index("lon")
    group = group_of(band, me, n)
    odd = group % 2
    cols, chans = sent.shape[1:]
    cell = lax.broadcasted_iota(jnp.int32, (cols, chans), 0)
    first_row = band * (rows * n) + group * rows
    whole_rows(n, owner, slabs, grid, 2 * HALO * (1 - odd))
    grid[pl.ds(HALO + (rows - HALO) * odd, HALO)] = sent[...]
    grid[pl.ds((rows + HALO) * odd, HALO)] = received[...]
    limits = [live_count(counts, first_row - 1 + r) for r in range(rows + HALO)]

    def spread_inputs(start, stop):
        for r in range(start, stop):
            spread(taps, r, grid[r].astype(jnp.float32))

    def spread_acts(start, stop, product):
        act = silu(product)
        for r in range(start, stop):
            at = slice((r - start) * cols, (r - start + 1) * cols)
            spread(acts, r, jnp.where(cell < limits[r], act[at], 0.0))

    def mix(start, stop, product):
        for r in range(start, stop):
            here = grid[r + HALO].astype(jnp.float32) + product[(r - start) * cols : (r - start + 1) * cols]
            here = jnp.where(cell < limits[r + 1], here, 0.0)
            mixed[r * cols : (r + 1) * cols, :] = here.astype(jnp.bfloat16)
        at = slice(start * cols, stop * cols)
        flat = mixed[at, :].astype(jnp.float32)
        scaled = (flat * lax.rsqrt(jnp.mean(flat * flat, axis=1, keepdims=True) + 1e-06)).astype(jnp.bfloat16)
        normed[at, :] = scaled
        keys[at, :] = jnp.dot(scaled, w_key[...], preferred_element_type=jnp.float32).astype(jnp.bfloat16)
        values[:, at] = by_last(w_value[...], scaled).astype(jnp.bfloat16)

    total = rows + HALO
    half = total // 2
    low = half - HALO
    spread_inputs(0, half + HALO)
    first_low = convolve(taps, w_conv1, b_conv1, 0, half)
    spread_inputs(half + HALO, total + HALO)
    first_high = convolve(taps, w_conv1, b_conv1, half, total - half)
    spread_acts(0, half, first_low)
    if low:
        second_low = convolve(acts, w_conv2, b_conv2, 0, low)
    spread_acts(half, total, first_high)
    second_high = convolve(acts, w_conv2, b_conv2, low, rows - low)
    result[rows * (cols // n) :, :] = jnp.zeros((AHEAD, chans), result.dtype)
    segments = [owner[lax.rem(me + first, n), band]]
    if low:
        mix(0, low, second_low)
    mix(low, rows, second_high)
    shared = limits[1 : rows + 1], mixed, normed, keys, values, w_query, w_out
    attend(segments, (0, rows), *shared, [result], *scratch)


def rest_kernel(moves, n, rows, owner, counts, *rest):
    mixed, normed, keys, values, w_query, w_out = rest[:6]
    results, scratch = rest[6 : 6 + len(moves)], rest[6 + len(moves) :]
    band = lax.axis_index("lat")
    me = lax.axis_index("lon")
    first_row = band * (rows * n) + group_of(band, me, n) * rows
    limits = [counts[first_row + r] for r in range(rows)]
    segments = [owner[lax.rem(me + d, n), band] for d in moves]
    attend(segments, (0, rows), limits, mixed, normed, keys, values, w_query, w_out, results, *scratch)


def store_kernel(n, rows, rotation, *rest):
    slabs, (out, staged, upright, turned, sems) = rest[:n], rest[n:]
    band = lax.axis_index("lat")
    me = lax.axis_index("lon")
    depth = GROUP // out.shape[0]
    pieces = out.shape[0] // depth
    for d in range(n):
        top = group_of(band, lax.rem(me + n - d, n), n) * rows
        upright[pl.ds(top, rows)] = slabs[d][: rows * out.shape[0], :].reshape(rows, *out.shape[1:])

    def piece(g):
        at = pl.ds(g * depth, depth)
        return pltpu.make_async_copy(turned.at[at], out.at[at], sems.at[g])

    turn(rotation[me, band] % 4, staged, upright, turned, lambda g: None, lambda g: piece(g).start())
    for g in range(pieces):
        piece(g).wait()


def on_device(
    bands,
    n,
    fields,
    w_conv1,
    b_conv1,
    w_conv2,
    b_conv2,
    w_query,
    w_key,
    w_value,
    w_out,
    rotation,
    owner,
    counts,
):
    size, _, chans = fields.shape
    rows = size // n
    inner = rows - HALO
    cols = size * n
    bf16 = jnp.bfloat16
    smem = pl.BlockSpec(memory_space=pltpu.SMEM)
    vmem = pl.BlockSpec(memory_space=pltpu.VMEM)
    hbm = pl.BlockSpec(memory_space=pltpu.HBM)
    params = pltpu.CompilerParams(vmem_limit_bytes=VMEM_BYTES)
    pieces = size * size // GROUP

    def call(kernel, name, out, scalars, arrays, scratch, array_spec=vmem, scalar_spec=smem, out_spec=vmem):
        many = isinstance(out, list)
        return pl.pallas_call(
            functools.partial(kernel, n, rows),
            out_shape=out,
            in_specs=[scalar_spec] * len(scalars) + [array_spec] * len(arrays),
            out_specs=[out_spec] * len(out) if many else out_spec,
            scratch_shapes=scratch,
            compiler_params=params,
            name=name,
        )(*scalars, *arrays)

    def array(*shape):
        return jax.ShapeDtypeStruct(shape, bf16)

    order = sorted(range(1, n), key=lambda d: -min(d, n - d))

    def around_by(x, d):
        return lax.ppermute(x, "lon", [(i, (i + d) % n) for i in range(n)])

    def around(parts):
        moved = {d: around_by(parts[d], d) for d in order}
        return [parts[0]] + [moved[d] for d in range(1, n)]

    def in_hbm(x):
        return pltpu.with_memory_space_constraint(x, pltpu.HBM)

    rotation, owner = in_hbm(rotation.T), in_hbm(owner.T)
    loaded = [counts]
    loaded += [w_conv1.reshape(3, 3 * chans, chans), b_conv1.reshape(1, chans)]
    loaded += [w_conv2.reshape(3, 3 * chans, chans), b_conv2.reshape(1, chans), w_value.T, w_out]
    loaded = [in_hbm(x) for x in loaded]
    turned = [in_hbm(x) for x in (w_query, w_key.T)]
    staging = pltpu.VMEM((chans // LANES, size * (size + 8), LANES), jnp.float32)
    block = pltpu.VMEM((size, size, chans), bf16)

    slabs = [array(HALO, size, chans)] * n + [array(rows, size, chans)] * n
    scratch = [staging, block, block, pltpu.SMEM(rotation.shape, rotation.dtype)]
    scratch += [pltpu.SemaphoreType.DMA((3,)), pltpu.SemaphoreType.DMA((pieces,))]
    held = slabs + [pltpu.VMEM(x.shape, x.dtype) for x in (rotation, owner)]
    *slabs, rotation, owner = call(send_kernel, "send", held, [rotation, owner], [in_hbm(fields)], scratch, hbm, hbm)
    edges = around(slabs[:n])
    slabs = around(slabs[n:])

    snake = [a * n + shard_of(a, g, n) for a in range(bands) for g in range(n)]
    pairs = [(snake[i], snake[i + 1 if i % 2 else i - 1]) for i in range(1, bands * n - 1)]
    sent = call(edge_kernel, "edge", array(HALO, cols, chans), [owner], edges, [])
    received = lax.ppermute(sent, ("lat", "lon"), pairs)

    head_dim = w_key.shape[1]
    heads = chans // head_dim
    held = [pltpu.VMEM(x.shape, x.dtype) for x in loaded]
    held += [pltpu.VMEM((heads, chans, head_dim), bf16), pltpu.VMEM(w_key.shape, bf16)]
    scratch = [pltpu.VMEM(x.shape, bf16) for x in turned] + [pltpu.SemaphoreType.DMA((len(loaded) + 2,))]
    loaded = call(load_kernel, "load", held, [sent], loaded + turned, scratch, hbm, hbm)
    counts, *convs, w_value, w_out, w_query, w_key = loaded

    def taps(count):
        return pltpu.VMEM((count, cols, 3 * chans), bf16)

    def working(segments):
        blocks, width = segments * rows, heads * size
        return [
            pltpu.VMEM((blocks * size, chans), bf16),
            pltpu.VMEM((blocks, cols, width), jnp.float32),
            pltpu.VMEM((blocks, cols, width), bf16),
            pltpu.VMEM((head_dim, blocks * width), bf16),
        ]

    cells = rows * cols
    result = array(rows * size, chans)
    first, *others = [*order, 0]
    results = {}
    results[first], *held = call(
        functools.partial(main_kernel, first),
        "main",
        [array(rows * size + AHEAD, chans), array(cells, chans), array(cells, chans), array(cells, head_dim), array(head_dim, cells)],
        [owner, counts],
        slabs + [sent, received, *convs, w_key, w_value, w_query, w_out],
        [pltpu.VMEM((rows + 2 * HALO, cols, chans), bf16), taps(rows + 2 * HALO), taps(rows + HALO)] + working(1),
    )
    moved = {first: around_by(results[first], first)}
    rest = call(
        functools.partial(rest_kernel, others),
        "rest",
        [result] * len(others),
        [owner, counts],
        held + [w_query, w_out],
        working(len(others)),
    )
    for d, x in zip(others, rest):
        moved[d] = around_by(x, d) if d else x
    slabs = [moved[d] for d in range(n)]
    scratch = [staging, block, block, pltpu.SemaphoreType.DMA((pieces,))]
    return call(store_kernel, "store", array(*fields.shape), [rotation], slabs, scratch, out_spec=hbm)


def solution(mesh):
    in_specs = (P("lat", "lon", None), P(), P(), P(), P(), P(), P(), P(), P(), P(), P(), P())
    out_specs = P("lat", "lon", None)
    body = functools.partial(on_device, mesh.shape["lat"], mesh.shape["lon"])
    return jax.shard_map(body, mesh=mesh, in_specs=in_specs, out_specs=out_specs, check_vma=False)
```

```python
import functools
import math

import jax
import jax.numpy as jnp
from jax import lax
from jax.experimental import pallas as pl
from jax.experimental.pallas import tpu as pltpu
from jax.sharding import PartitionSpec as P

HALO = 2
LANES = 128
GROUP = 256
AHEAD = 16
VMEM_BYTES = 28 * 1024 * 1024


def group_of(band, shard, n):
    outer = jnp.where((shard == n - 2) == (band % 2 == 0), 0, n - 1)
    return jnp.where(shard < n - 2, shard + 1, outer)


def shard_of(band, group, n):
    if 0 < group < n - 1:
        return group - 1
    return n - 2 if (group == 0) == (band % 2 == 0) else n - 1


def first_held(group, rows):
    return group * rows - HALO * (group % 2)


def turn(quarter, staged, block, out, ready, done):
    size, _, chans = block.shape
    tiles = staged.shape[0]
    pitch = staged.shape[1] // size
    depth = GROUP // size
    pieces = size // depth

    def column(col):
        parts = [staged[t, pl.ds(col, size, stride=pitch), :] for t in range(tiles)]
        return jnp.concatenate(parts, axis=1).astype(jnp.bfloat16)

    def keep(i, row):
        for t in range(tiles):
            staged[t, pl.ds(i * pitch, size), :] = row[:, t * LANES : (t + 1) * LANES]

    @pl.when(quarter == 0)
    def _():
        for g in range(pieces):
            ready(g)
            out[g * depth : (g + 1) * depth] = block[g * depth : (g + 1) * depth]
            done(g)

    @pl.when(quarter == 1)
    def _():
        for i in range(size):
            if i % depth == 0:
                ready(i // depth)
            keep(i, block[i].astype(jnp.float32))
        for i in range(size):
            out[i] = column(size - 1 - i)
            if i % depth == depth - 1:
                done(i // depth)

    @pl.when(quarter == 2)
    def _():
        i = lax.broadcasted_iota(jnp.int32, (GROUP, GROUP), 0)
        j = lax.broadcasted_iota(jnp.int32, (GROUP, GROUP), 1)
        backwards = jnp.where(i + j == GROUP - 1, 1.0, 0.0).astype(jnp.bfloat16)
        for g in reversed(range(pieces)):
            ready(pieces - 1 - g)
            cells = block[size - (g + 1) * depth : size - g * depth].reshape(GROUP, chans)
            turned = jnp.dot(backwards, cells, preferred_element_type=jnp.float32).astype(jnp.bfloat16)
            out[g * depth : (g + 1) * depth] = turned.reshape(depth, size, chans)
            done(g)

    @pl.when(quarter == 3)
    def _():
        for i in range(size):
            if i % depth == 0:
                ready(i // depth)
            keep(size - 1 - i, block[i].astype(jnp.float32))
        for i in range(size):
            out[i] = column(i)
            if i % depth == depth - 1:
                done(i // depth)


def send_kernel(n, rows, rotation_in, owner_in, fields, *rest):
    edges, slabs, (rotation_out, owner_out) = rest[:n], rest[n : 2 * n], rest[2 * n : 2 * n + 2]
    staged, block, upright, rotation, scalar_sems, sems = rest[2 * n + 2 :]
    band = lax.axis_index("lat")
    me = lax.axis_index("lon")
    depth = GROUP // fields.shape[0]

    def piece(g):
        at = pl.ds(g * depth, depth)
        return pltpu.make_async_copy(fields.at[at], block.at[at], sems.at[g])

    scalars = [
        pltpu.make_async_copy(rotation_in, rotation, scalar_sems.at[0]),
        pltpu.make_async_copy(rotation_in, rotation_out, scalar_sems.at[1]),
        pltpu.make_async_copy(owner_in, owner_out, scalar_sems.at[2]),
    ]
    for copy in scalars:
        copy.start()
    for g in range(fields.shape[0] // depth):
        piece(g).start()
    scalars[0].wait()
    turn((4 - rotation[me, band]) % 4, staged, block, upright, lambda g: piece(g).wait(), lambda g: None)
    for d in range(n):
        group = group_of(band, lax.rem(me + d, n), n)
        top, odd = first_held(group, rows), group % 2
        edges[d][...] = upright[pl.ds(top + rows * odd, HALO)]
        slabs[d][...] = upright[pl.ds(top + HALO * (1 - odd), rows)]
    scalars[1].wait()
    scalars[2].wait()


def load_kernel(n, rows, after, *refs):
    del after
    count = (len(refs) - 7) // 2
    direct, (query, key) = refs[:count], refs[count : count + 2]
    loaded, (w_query, w_key) = refs[count + 2 : 2 * count + 2], refs[2 * count + 2 : 2 * count + 4]
    query_in, key_in, sems = refs[2 * count + 4 :]
    heads, _, head_dim = w_query.shape
    pairs = list(zip(direct, loaded)) + [(query, query_in), (key, key_in)]
    copies = [pltpu.make_async_copy(*pair, sems.at[i]) for i, pair in enumerate(pairs)]
    for copy in copies:
        copy.start()
    for copy in copies:
        copy.wait()
    w_key[...] = key_in[...].T
    for h in range(heads):
        w_query[h] = query_in[:, h * head_dim : (h + 1) * head_dim]


def columns_of(segment, size):
    return pl.ds(pl.multiple_of(segment * size, size), size)


def whole_rows(n, owner, slabs, out, first):
    band = lax.axis_index("lat")
    me = lax.axis_index("lon")
    count, size = slabs[0].shape[:2]
    for d in range(n):
        segment = owner[lax.rem(me + n - d, n), band]
        out[pl.ds(first, count), columns_of(segment, size)] = slabs[d][...]


def edge_kernel(n, rows, owner, *rest):
    del rows
    whole_rows(n, owner, rest[:n], rest[n], 0)


def spread(taps, r, row):
    cols, chans = row.shape
    taps[r, :, :chans] = pltpu.roll(row, 1, 0).astype(jnp.bfloat16)
    taps[r, :, chans : 2 * chans] = row.astype(jnp.bfloat16)
    taps[r, :, 2 * chans :] = pltpu.roll(row, cols - 1, 0).astype(jnp.bfloat16)


def convolve(taps, weight, bias, first, count):
    cols, width = taps.shape[1:]
    windows = [taps[first + i : first + i + count].reshape(count * cols, width) for i in range(3)]
    depth = weight.shape[0] * width
    product = jnp.dot(
        jnp.concatenate(windows, axis=1),
        weight[...].reshape(depth, weight.shape[2]),
        preferred_element_type=jnp.float32,
    )
    return product + bias[...]


def silu(x):
    half = 0.5 * x
    return half + half * jnp.tanh(half)


def live_count(counts, row):
    inside = (row >= 0) & (row < counts.shape[0])
    return jnp.where(inside, counts[jnp.clip(row, 0, counts.shape[0] - 1)], 0)


def by_last(a, b):
    return lax.dot_general(a, b, (((1,), (1,)), ((), ())), preferred_element_type=jnp.float32)


def attend(segments, span, limits, mixed, normed, keys, values, w_query, w_out, results, here, scores, expo, turned):
    rows, chans = len(limits), mixed.shape[1]
    size = here.shape[0] // (rows * len(segments))
    heads, _, head_dim = w_query.shape
    cols = mixed.shape[0] // rows
    width = heads * size
    blocks = [(s * rows + r, s, r) for s in range(len(segments)) for r in range(*span)]
    low, high = blocks[0][0], blocks[-1][0] + 1

    def cells(s, r):
        return columns_of(segments[s] + r * (cols // size), size)

    for b, s, r in blocks:
        here[b * size : (b + 1) * size, :] = normed[cells(s, r), :]
    own = here[low * size : high * size, :]
    queries = [jnp.dot(own, w_query[h], preferred_element_type=jnp.float32) for h in range(heads)]
    queries = [query.astype(jnp.bfloat16) for query in queries]
    for b, s, r in blocks:
        part = [query[(b - low) * size : (b - low + 1) * size] for query in queries]
        scores[b] = by_last(keys[r * cols : (r + 1) * cols, :], jnp.concatenate(part, axis=0))
    key_at = lax.broadcasted_iota(jnp.int32, (cols, width), 0)
    scale = math.log2(math.e) / head_dim**0.5
    shares = {}
    for b, s, r in blocks:
        part = jnp.where(key_at < limits[r], scores[b], -jnp.inf)
        part = jnp.exp2((part - jnp.max(part, axis=0, keepdims=True)) * scale)
        shares[b] = 1.0 / jnp.sum(part, axis=0, keepdims=True)
        expo[b] = part.astype(jnp.bfloat16)
    for b, s, r in blocks:
        summed = jnp.dot(values[:, r * cols : (r + 1) * cols], expo[b], preferred_element_type=jnp.float32)
        turned[:, b * width : (b + 1) * width] = (summed * shares[b]).astype(jnp.bfloat16)
    attended = turned[:, low * width : high * width].T
    update = jnp.zeros(own.shape, jnp.float32)
    for h in range(heads):
        starts = [(b - low) * width + h * size for b, *_ in blocks]
        part = jnp.concatenate([attended[start : start + size] for start in starts], axis=0)
        weight = w_out[h * head_dim : (h + 1) * head_dim, :]
        update = update + jnp.dot(part, weight, preferred_element_type=jnp.float32)
    for b, s, r in blocks:
        cell = segments[s] * size + lax.broadcasted_iota(jnp.int32, (size, chans), 0)
        part = jnp.where(cell < limits[r], update[(b - low) * size : (b - low + 1) * size], 0.0)
        results[s][r * size : (r + 1) * size, :] = (mixed[cells(s, r), :].astype(jnp.float32) + part).astype(jnp.bfloat16)


def main_kernel(first, n, rows, owner, counts, *rest):
    slabs, sent, received = rest[:n], rest[n], rest[n + 1]
    w_conv1, b_conv1, w_conv2, b_conv2, w_key, w_value, w_query, w_out = rest[n + 2 : n + 10]
    result, mixed, normed, keys, values = rest[n + 10 : n + 15]
    grid, taps, acts, *scratch = rest[n + 15 :]
    band = lax.axis_index("lat")
    me = lax.axis_index("lon")
    group = group_of(band, me, n)
    odd = group % 2
    cols, chans = sent.shape[1:]
    cell = lax.broadcasted_iota(jnp.int32, (cols, chans), 0)
    first_row = band * (rows * n) + group * rows
    whole_rows(n, owner, slabs, grid, 2 * HALO * (1 - odd))
    grid[pl.ds(HALO + (rows - HALO) * odd, HALO)] = sent[...]
    grid[pl.ds((rows + HALO) * odd, HALO)] = received[...]
    limits = [live_count(counts, first_row - 1 + r) for r in range(rows + HALO)]

    def spread_inputs(start, stop):
        for r in range(start, stop):
            spread(taps, r, grid[r].astype(jnp.float32))

    def spread_acts(start, stop, product):
        act = silu(product)
        for r in range(start, stop):
            at = slice((r - start) * cols, (r - start + 1) * cols)
            spread(acts, r, jnp.where(cell < limits[r], act[at], 0.0))

    def mix(start, stop, product):
        for r in range(start, stop):
            here = grid[r + HALO].astype(jnp.float32) + product[(r - start) * cols : (r - start + 1) * cols]
            here = jnp.where(cell < limits[r + 1], here, 0.0)
            mixed[r * cols : (r + 1) * cols, :] = here.astype(jnp.bfloat16)
        at = slice(start * cols, stop * cols)
        flat = mixed[at, :].astype(jnp.float32)
        scaled = (flat * lax.rsqrt(jnp.mean(flat * flat, axis=1, keepdims=True) + 1e-06)).astype(jnp.bfloat16)
        normed[at, :] = scaled
        keys[at, :] = jnp.dot(scaled, w_key[...], preferred_element_type=jnp.float32).astype(jnp.bfloat16)
        values[:, at] = by_last(w_value[...], scaled).astype(jnp.bfloat16)

    total = rows + HALO
    spread_inputs(0, total + HALO)
    spread_acts(0, total, convolve(taps, w_conv1, b_conv1, 0, total))
    mix(0, rows, convolve(acts, w_conv2, b_conv2, 0, rows))
    result[rows * (cols // n) :, :] = jnp.zeros((AHEAD, chans), result.dtype)
    segments = [owner[lax.rem(me + first, n), band]]
    shared = limits[1 : rows + 1], mixed, normed, keys, values, w_query, w_out
    attend(segments, (0, rows), *shared, [result], *scratch)


def rest_kernel(moves, n, rows, owner, counts, *rest):
    mixed, normed, keys, values, w_query, w_out = rest[:6]
    results, scratch = rest[6 : 6 + len(moves)], rest[6 + len(moves) :]
    band = lax.axis_index("lat")
    me = lax.axis_index("lon")
    first_row = band * (rows * n) + group_of(band, me, n) * rows
    limits = [counts[first_row + r] for r in range(rows)]
    segments = [owner[lax.rem(me + d, n), band] for d in moves]
    attend(segments, (0, rows), limits, mixed, normed, keys, values, w_query, w_out, results, *scratch)


def store_kernel(n, rows, rotation, *rest):
    slabs, (out, staged, upright, turned, sems) = rest[:n], rest[n:]
    band = lax.axis_index("lat")
    me = lax.axis_index("lon")
    depth = GROUP // out.shape[0]
    pieces = out.shape[0] // depth
    for d in range(n):
        top = group_of(band, lax.rem(me + n - d, n), n) * rows
        upright[pl.ds(top, rows)] = slabs[d][: rows * out.shape[0], :].reshape(rows, *out.shape[1:])

    def piece(g):
        at = pl.ds(g * depth, depth)
        return pltpu.make_async_copy(turned.at[at], out.at[at], sems.at[g])

    turn(rotation[me, band] % 4, staged, upright, turned, lambda g: None, lambda g: piece(g).start())
    for g in range(pieces):
        piece(g).wait()


def on_device(
    bands,
    n,
    fields,
    w_conv1,
    b_conv1,
    w_conv2,
    b_conv2,
    w_query,
    w_key,
    w_value,
    w_out,
    rotation,
    owner,
    counts,
):
    size, _, chans = fields.shape
    rows = size // n
    inner = rows - HALO
    cols = size * n
    bf16 = jnp.bfloat16
    smem = pl.BlockSpec(memory_space=pltpu.SMEM)
    vmem = pl.BlockSpec(memory_space=pltpu.VMEM)
    hbm = pl.BlockSpec(memory_space=pltpu.HBM)
    params = pltpu.CompilerParams(vmem_limit_bytes=VMEM_BYTES)
    pieces = size * size // GROUP

    def call(kernel, name, out, scalars, arrays, scratch, array_spec=vmem, scalar_spec=smem, out_spec=vmem):
        many = isinstance(out, list)
        return pl.pallas_call(
            functools.partial(kernel, n, rows),
            out_shape=out,
            in_specs=[scalar_spec] * len(scalars) + [array_spec] * len(arrays),
            out_specs=[out_spec] * len(out) if many else out_spec,
            scratch_shapes=scratch,
            compiler_params=params,
            name=name,
        )(*scalars, *arrays)

    def array(*shape):
        return jax.ShapeDtypeStruct(shape, bf16)

    order = sorted(range(1, n), key=lambda d: -min(d, n - d))

    def around_by(x, d):
        return lax.ppermute(x, "lon", [(i, (i + d) % n) for i in range(n)])

    def around(parts):
        moved = {d: around_by(parts[d], d) for d in order}
        return [parts[0]] + [moved[d] for d in range(1, n)]

    def in_hbm(x):
        return pltpu.with_memory_space_constraint(x, pltpu.HBM)

    rotation, owner = in_hbm(rotation.T), in_hbm(owner.T)
    loaded = [counts]
    loaded += [w_conv1.reshape(3, 3 * chans, chans), b_conv1.reshape(1, chans)]
    loaded += [w_conv2.reshape(3, 3 * chans, chans), b_conv2.reshape(1, chans), w_value.T, w_out]
    loaded = [in_hbm(x) for x in loaded]
    turned = [in_hbm(x) for x in (w_query, w_key.T)]
    staging = pltpu.VMEM((chans // LANES, size * (size + 8), LANES), jnp.float32)
    block = pltpu.VMEM((size, size, chans), bf16)

    slabs = [array(HALO, size, chans)] * n + [array(rows, size, chans)] * n
    scratch = [staging, block, block, pltpu.SMEM(rotation.shape, rotation.dtype)]
    scratch += [pltpu.SemaphoreType.DMA((3,)), pltpu.SemaphoreType.DMA((pieces,))]
    held = slabs + [pltpu.VMEM(x.shape, x.dtype) for x in (rotation, owner)]
    *slabs, rotation, owner = call(send_kernel, "send", held, [rotation, owner], [in_hbm(fields)], scratch, hbm, hbm)
    edges = around(slabs[:n])
    slabs = around(slabs[n:])

    snake = [a * n + shard_of(a, g, n) for a in range(bands) for g in range(n)]
    pairs = [(snake[i], snake[i + 1 if i % 2 else i - 1]) for i in range(1, bands * n - 1)]
    sent = call(edge_kernel, "edge", array(HALO, cols, chans), [owner], edges, [])
    received = lax.ppermute(sent, ("lat", "lon"), pairs)

    head_dim = w_key.shape[1]
    heads = chans // head_dim
    held = [pltpu.VMEM(x.shape, x.dtype) for x in loaded]
    held += [pltpu.VMEM((heads, chans, head_dim), bf16), pltpu.VMEM(w_key.shape, bf16)]
    scratch = [pltpu.VMEM(x.shape, bf16) for x in turned] + [pltpu.SemaphoreType.DMA((len(loaded) + 2,))]
    loaded = call(load_kernel, "load", held, [sent], loaded + turned, scratch, hbm, hbm)
    counts, *convs, w_value, w_out, w_query, w_key = loaded

    def taps(count):
        return pltpu.VMEM((count, cols, 3 * chans), bf16)

    def working(segments):
        blocks, width = segments * rows, heads * size
        return [
            pltpu.VMEM((blocks * size, chans), bf16),
            pltpu.VMEM((blocks, cols, width), jnp.float32),
            pltpu.VMEM((blocks, cols, width), bf16),
            pltpu.VMEM((head_dim, blocks * width), bf16),
        ]

    cells = rows * cols
    result = array(rows * size, chans)
    first, *others = [*order, 0]
    results = {}
    results[first], *held = call(
        functools.partial(main_kernel, first),
        "main",
        [array(rows * size + AHEAD, chans), array(cells, chans), array(cells, chans), array(cells, head_dim), array(head_dim, cells)],
        [owner, counts],
        slabs + [sent, received, *convs, w_key, w_value, w_query, w_out],
        [pltpu.VMEM((rows + 2 * HALO, cols, chans), bf16), taps(rows + 2 * HALO), taps(rows + HALO)] + working(1),
    )
    moved = {first: around_by(results[first], first)}
    rest = call(
        functools.partial(rest_kernel, others),
        "rest",
        [result] * len(others),
        [owner, counts],
        held + [w_query, w_out],
        working(len(others)),
    )
    for d, x in zip(others, rest):
        moved[d] = around_by(x, d) if d else x
    slabs = [moved[d] for d in range(n)]
    scratch = [staging, block, block, pltpu.SemaphoreType.DMA((pieces,))]
    return call(store_kernel, "store", array(*fields.shape), [rotation], slabs, scratch, out_spec=hbm)


def solution(mesh):
    in_specs = (P("lat", "lon", None), P(), P(), P(), P(), P(), P(), P(), P(), P(), P(), P())
    out_specs = P("lat", "lon", None)
    body = functools.partial(on_device, mesh.shape["lat"], mesh.shape["lon"])
    return jax.shard_map(body, mesh=mesh, in_specs=in_specs, out_specs=out_specs, check_vma=False)
```

```python
import functools
import math

import jax
import jax.numpy as jnp
from jax import lax
from jax.experimental import pallas as pl
from jax.experimental.pallas import tpu as pltpu
from jax.sharding import PartitionSpec as P

HALO = 2
LANES = 128
GROUP = 256
CHUNKS = 3
AHEAD = 16
VMEM_BYTES = 28 * 1024 * 1024


def group_of(band, shard, n):
    outer = jnp.where((shard == n - 2) == (band % 2 == 0), 0, n - 1)
    return jnp.where(shard < n - 2, shard + 1, outer)


def shard_of(band, group, n):
    if 0 < group < n - 1:
        return group - 1
    return n - 2 if (group == 0) == (band % 2 == 0) else n - 1


def first_held(group, rows):
    return group * rows - HALO * (group % 2)


def turn(quarter, staged, block, out, ready, done):
    size, _, chans = block.shape
    tiles = staged.shape[0]
    pitch = staged.shape[1] // size
    depth = GROUP // size
    pieces = size // depth

    def column(col):
        parts = [staged[t, pl.ds(col, size, stride=pitch), :] for t in range(tiles)]
        return jnp.concatenate(parts, axis=1).astype(jnp.bfloat16)

    def keep(i, row):
        for t in range(tiles):
            staged[t, pl.ds(i * pitch, size), :] = row[:, t * LANES : (t + 1) * LANES]

    @pl.when(quarter == 0)
    def _():
        for g in range(pieces):
            ready(g)
            out[g * depth : (g + 1) * depth] = block[g * depth : (g + 1) * depth]
            done(g)

    @pl.when(quarter == 1)
    def _():
        for i in range(size):
            if i % depth == 0:
                ready(i // depth)
            keep(i, block[i].astype(jnp.float32))
        for i in range(size):
            out[i] = column(size - 1 - i)
            if i % depth == depth - 1:
                done(i // depth)

    @pl.when(quarter == 2)
    def _():
        i = lax.broadcasted_iota(jnp.int32, (GROUP, GROUP), 0)
        j = lax.broadcasted_iota(jnp.int32, (GROUP, GROUP), 1)
        backwards = jnp.where(i + j == GROUP - 1, 1.0, 0.0).astype(jnp.bfloat16)
        for g in reversed(range(pieces)):
            ready(pieces - 1 - g)
            cells = block[size - (g + 1) * depth : size - g * depth].reshape(GROUP, chans)
            turned = jnp.dot(backwards, cells, preferred_element_type=jnp.float32).astype(jnp.bfloat16)
            out[g * depth : (g + 1) * depth] = turned.reshape(depth, size, chans)
            done(g)

    @pl.when(quarter == 3)
    def _():
        for i in range(size):
            if i % depth == 0:
                ready(i // depth)
            keep(size - 1 - i, block[i].astype(jnp.float32))
        for i in range(size):
            out[i] = column(i)
            if i % depth == depth - 1:
                done(i // depth)


def send_kernel(n, rows, rotation_in, owner_in, fields, *rest):
    edges, slabs, (rotation_out, owner_out) = rest[:n], rest[n : 2 * n], rest[2 * n : 2 * n + 2]
    staged, block, upright, rotation, scalar_sems, sems = rest[2 * n + 2 :]
    band = lax.axis_index("lat")
    me = lax.axis_index("lon")
    depth = GROUP // fields.shape[0]

    def piece(g):
        at = pl.ds(g * depth, depth)
        return pltpu.make_async_copy(fields.at[at], block.at[at], sems.at[g])

    scalars = [
        pltpu.make_async_copy(rotation_in, rotation, scalar_sems.at[0]),
        pltpu.make_async_copy(rotation_in, rotation_out, scalar_sems.at[1]),
        pltpu.make_async_copy(owner_in, owner_out, scalar_sems.at[2]),
    ]
    for copy in scalars:
        copy.start()
    for g in range(fields.shape[0] // depth):
        piece(g).start()
    scalars[0].wait()
    turn((4 - rotation[me, band]) % 4, staged, block, upright, lambda g: piece(g).wait(), lambda g: None)
    for d in range(n):
        group = group_of(band, lax.rem(me + d, n), n)
        top, odd = first_held(group, rows), group % 2
        edges[d][...] = upright[pl.ds(top + rows * odd, HALO)]
        slabs[d][...] = upright[pl.ds(top + HALO * (1 - odd), rows)]
    scalars[1].wait()
    scalars[2].wait()


def load_kernel(n, rows, after, *refs):
    del after
    count = (len(refs) - 7) // 2
    direct, (query, key) = refs[:count], refs[count : count + 2]
    loaded, (w_query, w_key) = refs[count + 2 : 2 * count + 2], refs[2 * count + 2 : 2 * count + 4]
    query_in, key_in, sems = refs[2 * count + 4 :]
    heads, _, head_dim = w_query.shape
    pairs = list(zip(direct, loaded)) + [(query, query_in), (key, key_in)]
    copies = [pltpu.make_async_copy(*pair, sems.at[i]) for i, pair in enumerate(pairs)]
    for copy in copies:
        copy.start()
    for copy in copies:
        copy.wait()
    w_key[...] = key_in[...].T
    for h in range(heads):
        w_query[h] = query_in[:, h * head_dim : (h + 1) * head_dim]


def columns_of(segment, size):
    return pl.ds(pl.multiple_of(segment * size, size), size)


def whole_rows(n, owner, slabs, out, first):
    band = lax.axis_index("lat")
    me = lax.axis_index("lon")
    count, size = slabs[0].shape[:2]
    for d in range(n):
        segment = owner[lax.rem(me + n - d, n), band]
        out[pl.ds(first, count), columns_of(segment, size)] = slabs[d][...]


def edge_kernel(n, rows, owner, *rest):
    del rows
    whole_rows(n, owner, rest[:n], rest[n], 0)


def spread(taps, r, row):
    cols, chans = row.shape
    taps[r, :, :chans] = pltpu.roll(row, 1, 0).astype(jnp.bfloat16)
    taps[r, :, chans : 2 * chans] = row.astype(jnp.bfloat16)
    taps[r, :, 2 * chans :] = pltpu.roll(row, cols - 1, 0).astype(jnp.bfloat16)


def convolve(taps, weight, bias, first, count):
    cols, width = taps.shape[1:]
    windows = [taps[first + i : first + i + count].reshape(count * cols, width) for i in range(3)]
    depth = weight.shape[0] * width
    product = jnp.dot(
        jnp.concatenate(windows, axis=1),
        weight[...].reshape(depth, weight.shape[2]),
        preferred_element_type=jnp.float32,
    )
    return product + bias[...]


def silu(x):
    half = 0.5 * x
    return half + half * jnp.tanh(half)


def live_count(counts, row):
    inside = (row >= 0) & (row < counts.shape[0])
    return jnp.where(inside, counts[jnp.clip(row, 0, counts.shape[0] - 1)], 0)


def by_last(a, b):
    return lax.dot_general(a, b, (((1,), (1,)), ((), ())), preferred_element_type=jnp.float32)


def attend(segments, span, limits, mixed, normed, keys, values, w_query, w_out, results, here, scores, expo, turned):
    rows, chans = len(limits), mixed.shape[1]
    size = here.shape[0] // (rows * len(segments))
    heads, _, head_dim = w_query.shape
    cols = mixed.shape[0] // rows
    width = heads * size
    blocks = [(s * rows + r, s, r) for s in range(len(segments)) for r in range(*span)]
    low, high = blocks[0][0], blocks[-1][0] + 1

    def cells(s, r):
        return columns_of(segments[s] + r * (cols // size), size)

    for b, s, r in blocks:
        here[b * size : (b + 1) * size, :] = normed[cells(s, r), :]
    own = here[low * size : high * size, :]
    queries = [jnp.dot(own, w_query[h], preferred_element_type=jnp.float32) for h in range(heads)]
    queries = [query.astype(jnp.bfloat16) for query in queries]
    for b, s, r in blocks:
        part = [query[(b - low) * size : (b - low + 1) * size] for query in queries]
        scores[b] = by_last(keys[r * cols : (r + 1) * cols, :], jnp.concatenate(part, axis=0))
    key_at = lax.broadcasted_iota(jnp.int32, (cols, width), 0)
    scale = math.log2(math.e) / head_dim**0.5
    shares = {}
    for b, s, r in blocks:
        part = jnp.where(key_at < limits[r], scores[b], -jnp.inf)
        part = jnp.exp2((part - jnp.max(part, axis=0, keepdims=True)) * scale)
        shares[b] = 1.0 / jnp.sum(part, axis=0, keepdims=True)
        expo[b] = part.astype(jnp.bfloat16)
    for b, s, r in blocks:
        summed = jnp.dot(values[:, r * cols : (r + 1) * cols], expo[b], preferred_element_type=jnp.float32)
        turned[:, b * width : (b + 1) * width] = (summed * shares[b]).astype(jnp.bfloat16)
    attended = turned[:, low * width : high * width].T
    update = jnp.zeros(own.shape, jnp.float32)
    for h in range(heads):
        starts = [(b - low) * width + h * size for b, *_ in blocks]
        part = jnp.concatenate([attended[start : start + size] for start in starts], axis=0)
        weight = w_out[h * head_dim : (h + 1) * head_dim, :]
        update = update + jnp.dot(part, weight, preferred_element_type=jnp.float32)
    for b, s, r in blocks:
        cell = segments[s] * size + lax.broadcasted_iota(jnp.int32, (size, chans), 0)
        part = jnp.where(cell < limits[r], update[(b - low) * size : (b - low + 1) * size], 0.0)
        results[s][r * size : (r + 1) * size, :] = (mixed[cells(s, r), :].astype(jnp.float32) + part).astype(jnp.bfloat16)


def main_kernel(first, n, rows, owner, counts, *rest):
    slabs, sent, received = rest[:n], rest[n], rest[n + 1]
    w_conv1, b_conv1, w_conv2, b_conv2, w_key, w_value, w_query, w_out = rest[n + 2 : n + 10]
    result, mixed, normed, keys, values = rest[n + 10 : n + 15]
    grid, taps, acts, *scratch = rest[n + 15 :]
    band = lax.axis_index("lat")
    me = lax.axis_index("lon")
    group = group_of(band, me, n)
    odd = group % 2
    cols, chans = sent.shape[1:]
    cell = lax.broadcasted_iota(jnp.int32, (cols, chans), 0)
    first_row = band * (rows * n) + group * rows
    whole_rows(n, owner, slabs, grid, 2 * HALO * (1 - odd))
    grid[pl.ds(HALO + (rows - HALO) * odd, HALO)] = sent[...]
    grid[pl.ds((rows + HALO) * odd, HALO)] = received[...]
    limits = [live_count(counts, first_row - 1 + r) for r in range(rows + HALO)]

    def spread_inputs(start, stop):
        for r in range(start, stop):
            spread(taps, r, grid[r].astype(jnp.float32))

    def spread_acts(start, stop, product):
        act = silu(product)
        for r in range(start, stop):
            at = slice((r - start) * cols, (r - start + 1) * cols)
            spread(acts, r, jnp.where(cell < limits[r], act[at], 0.0))

    def mix(start, stop, product):
        for r in range(start, stop):
            here = grid[r + HALO].astype(jnp.float32) + product[(r - start) * cols : (r - start + 1) * cols]
            here = jnp.where(cell < limits[r + 1], here, 0.0)
            mixed[r * cols : (r + 1) * cols, :] = here.astype(jnp.bfloat16)
        at = slice(start * cols, stop * cols)
        flat = mixed[at, :].astype(jnp.float32)
        scaled = (flat * lax.rsqrt(jnp.mean(flat * flat, axis=1, keepdims=True) + 1e-06)).astype(jnp.bfloat16)
        normed[at, :] = scaled
        keys[at, :] = jnp.dot(scaled, w_key[...], preferred_element_type=jnp.float32).astype(jnp.bfloat16)
        values[:, at] = by_last(w_value[...], scaled).astype(jnp.bfloat16)

    total = rows + HALO
    chunks = min(CHUNKS, total // HALO)
    cuts = [-(-total * c // chunks) for c in range(chunks + 1)]
    ends = [0] + [cut + HALO for cut in cuts[1:]]
    lows = [max(cut - HALO, 0) for cut in cuts]
    firsts, seconds = [], []
    spread_inputs(ends[0], ends[1])
    for c in range(chunks):
        firsts.append(convolve(taps, w_conv1, b_conv1, cuts[c], cuts[c + 1] - cuts[c]))
        if c:
            spread_acts(cuts[c - 1], cuts[c], firsts[c - 1])
        if c + 1 < chunks:
            spread_inputs(ends[c + 1], ends[c + 2])
    for c in range(chunks):
        count = lows[c + 1] - lows[c]
        seconds.append(convolve(acts, w_conv2, b_conv2, lows[c], count) if count else None)
        if c == 0:
            spread_acts(cuts[-2], total, firsts[-1])
        elif seconds[c - 1] is not None:
            mix(lows[c - 1], lows[c], seconds[c - 1])
    mix(lows[-2], rows, seconds[-1])
    result[rows * (cols // n) :, :] = jnp.zeros((AHEAD, chans), result.dtype)
    segments = [owner[lax.rem(me + first, n), band]]
    shared = limits[1 : rows + 1], mixed, normed, keys, values, w_query, w_out
    attend(segments, (0, rows), *shared, [result], *scratch)


def rest_kernel(moves, n, rows, owner, counts, *rest):
    mixed, normed, keys, values, w_query, w_out = rest[:6]
    results, scratch = rest[6 : 6 + len(moves)], rest[6 + len(moves) :]
    band = lax.axis_index("lat")
    me = lax.axis_index("lon")
    first_row = band * (rows * n) + group_of(band, me, n) * rows
    limits = [counts[first_row + r] for r in range(rows)]
    segments = [owner[lax.rem(me + d, n), band] for d in moves]
    attend(segments, (0, rows), limits, mixed, normed, keys, values, w_query, w_out, results, *scratch)


def store_kernel(n, rows, rotation, *rest):
    slabs, (out, staged, upright, turned, sems) = rest[:n], rest[n:]
    band = lax.axis_index("lat")
    me = lax.axis_index("lon")
    depth = GROUP // out.shape[0]
    pieces = out.shape[0] // depth
    for d in range(n):
        top = group_of(band, lax.rem(me + n - d, n), n) * rows
        upright[pl.ds(top, rows)] = slabs[d][: rows * out.shape[0], :].reshape(rows, *out.shape[1:])

    def piece(g):
        at = pl.ds(g * depth, depth)
        return pltpu.make_async_copy(turned.at[at], out.at[at], sems.at[g])

    turn(rotation[me, band] % 4, staged, upright, turned, lambda g: None, lambda g: piece(g).start())
    for g in range(pieces):
        piece(g).wait()


def on_device(
    bands,
    n,
    fields,
    w_conv1,
    b_conv1,
    w_conv2,
    b_conv2,
    w_query,
    w_key,
    w_value,
    w_out,
    rotation,
    owner,
    counts,
):
    size, _, chans = fields.shape
    rows = size // n
    inner = rows - HALO
    cols = size * n
    bf16 = jnp.bfloat16
    smem = pl.BlockSpec(memory_space=pltpu.SMEM)
    vmem = pl.BlockSpec(memory_space=pltpu.VMEM)
    hbm = pl.BlockSpec(memory_space=pltpu.HBM)
    params = pltpu.CompilerParams(vmem_limit_bytes=VMEM_BYTES)
    pieces = size * size // GROUP

    def call(kernel, name, out, scalars, arrays, scratch, array_spec=vmem, scalar_spec=smem, out_spec=vmem):
        many = isinstance(out, list)
        return pl.pallas_call(
            functools.partial(kernel, n, rows),
            out_shape=out,
            in_specs=[scalar_spec] * len(scalars) + [array_spec] * len(arrays),
            out_specs=[out_spec] * len(out) if many else out_spec,
            scratch_shapes=scratch,
            compiler_params=params,
            name=name,
        )(*scalars, *arrays)

    def array(*shape):
        return jax.ShapeDtypeStruct(shape, bf16)

    order = sorted(range(1, n), key=lambda d: -min(d, n - d))

    def around_by(x, d):
        return lax.ppermute(x, "lon", [(i, (i + d) % n) for i in range(n)])

    def around(parts):
        moved = {d: around_by(parts[d], d) for d in order}
        return [parts[0]] + [moved[d] for d in range(1, n)]

    def in_hbm(x):
        return pltpu.with_memory_space_constraint(x, pltpu.HBM)

    rotation, owner = in_hbm(rotation.T), in_hbm(owner.T)
    loaded = [counts]
    loaded += [w_conv1.reshape(3, 3 * chans, chans), b_conv1.reshape(1, chans)]
    loaded += [w_conv2.reshape(3, 3 * chans, chans), b_conv2.reshape(1, chans), w_value.T, w_out]
    loaded = [in_hbm(x) for x in loaded]
    turned = [in_hbm(x) for x in (w_query, w_key.T)]
    staging = pltpu.VMEM((chans // LANES, size * (size + 8), LANES), jnp.float32)
    block = pltpu.VMEM((size, size, chans), bf16)

    slabs = [array(HALO, size, chans)] * n + [array(rows, size, chans)] * n
    scratch = [staging, block, block, pltpu.SMEM(rotation.shape, rotation.dtype)]
    scratch += [pltpu.SemaphoreType.DMA((3,)), pltpu.SemaphoreType.DMA((pieces,))]
    held = slabs + [pltpu.VMEM(x.shape, x.dtype) for x in (rotation, owner)]
    *slabs, rotation, owner = call(send_kernel, "send", held, [rotation, owner], [in_hbm(fields)], scratch, hbm, hbm)
    edges = around(slabs[:n])
    slabs = around(slabs[n:])

    snake = [a * n + shard_of(a, g, n) for a in range(bands) for g in range(n)]
    pairs = [(snake[i], snake[i + 1 if i % 2 else i - 1]) for i in range(1, bands * n - 1)]
    sent = call(edge_kernel, "edge", array(HALO, cols, chans), [owner], edges, [])
    received = lax.ppermute(sent, ("lat", "lon"), pairs)

    head_dim = w_key.shape[1]
    heads = chans // head_dim
    held = [pltpu.VMEM(x.shape, x.dtype) for x in loaded]
    held += [pltpu.VMEM((heads, chans, head_dim), bf16), pltpu.VMEM(w_key.shape, bf16)]
    scratch = [pltpu.VMEM(x.shape, bf16) for x in turned] + [pltpu.SemaphoreType.DMA((len(loaded) + 2,))]
    loaded = call(load_kernel, "load", held, [sent], loaded + turned, scratch, hbm, hbm)
    counts, *convs, w_value, w_out, w_query, w_key = loaded

    def taps(count):
        return pltpu.VMEM((count, cols, 3 * chans), bf16)

    def working(segments):
        blocks, width = segments * rows, heads * size
        return [
            pltpu.VMEM((blocks * size, chans), bf16),
            pltpu.VMEM((blocks, cols, width), jnp.float32),
            pltpu.VMEM((blocks, cols, width), bf16),
            pltpu.VMEM((head_dim, blocks * width), bf16),
        ]

    cells = rows * cols
    result = array(rows * size, chans)
    first, *others = [*order, 0]
    results = {}
    results[first], *held = call(
        functools.partial(main_kernel, first),
        "main",
        [array(rows * size + AHEAD, chans), array(cells, chans), array(cells, chans), array(cells, head_dim), array(head_dim, cells)],
        [owner, counts],
        slabs + [sent, received, *convs, w_key, w_value, w_query, w_out],
        [pltpu.VMEM((rows + 2 * HALO, cols, chans), bf16), taps(rows + 2 * HALO), taps(rows + HALO)] + working(1),
    )
    moved = {first: around_by(results[first], first)}
    rest = call(
        functools.partial(rest_kernel, others),
        "rest",
        [result] * len(others),
        [owner, counts],
        held + [w_query, w_out],
        working(len(others)),
    )
    for d, x in zip(others, rest):
        moved[d] = around_by(x, d) if d else x
    slabs = [moved[d] for d in range(n)]
    scratch = [staging, block, block, pltpu.SemaphoreType.DMA((pieces,))]
    return call(store_kernel, "store", array(*fields.shape), [rotation], slabs, scratch, out_spec=hbm)


def solution(mesh):
    in_specs = (P("lat", "lon", None), P(), P(), P(), P(), P(), P(), P(), P(), P(), P(), P())
    out_specs = P("lat", "lon", None)
    body = functools.partial(on_device, mesh.shape["lat"], mesh.shape["lon"])
    return jax.shard_map(body, mesh=mesh, in_specs=in_specs, out_specs=out_specs, check_vma=False)
```

```python
import functools
import math

import jax
import jax.numpy as jnp
from jax import lax
from jax.experimental import pallas as pl
from jax.experimental.pallas import tpu as pltpu
from jax.sharding import PartitionSpec as P

HALO = 2
LANES = 128
GROUP = 256
CHUNKS = 4
AHEAD = 16
VMEM_BYTES = 28 * 1024 * 1024


def group_of(band, shard, n):
    outer = jnp.where((shard == n - 2) == (band % 2 == 0), 0, n - 1)
    return jnp.where(shard < n - 2, shard + 1, outer)


def shard_of(band, group, n):
    if 0 < group < n - 1:
        return group - 1
    return n - 2 if (group == 0) == (band % 2 == 0) else n - 1


def first_held(group, rows):
    return group * rows - HALO * (group % 2)


def turn(quarter, staged, block, out, ready, done):
    size, _, chans = block.shape
    tiles = staged.shape[0]
    pitch = staged.shape[1] // size
    depth = GROUP // size
    pieces = size // depth

    def column(col):
        parts = [staged[t, pl.ds(col, size, stride=pitch), :] for t in range(tiles)]
        return jnp.concatenate(parts, axis=1).astype(jnp.bfloat16)

    def keep(i, row):
        for t in range(tiles):
            staged[t, pl.ds(i * pitch, size), :] = row[:, t * LANES : (t + 1) * LANES]

    @pl.when(quarter == 0)
    def _():
        for g in range(pieces):
            ready(g)
            out[g * depth : (g + 1) * depth] = block[g * depth : (g + 1) * depth]
            done(g)

    @pl.when(quarter == 1)
    def _():
        for i in range(size):
            if i % depth == 0:
                ready(i // depth)
            keep(i, block[i].astype(jnp.float32))
        for i in range(size):
            out[i] = column(size - 1 - i)
            if i % depth == depth - 1:
                done(i // depth)

    @pl.when(quarter == 2)
    def _():
        i = lax.broadcasted_iota(jnp.int32, (GROUP, GROUP), 0)
        j = lax.broadcasted_iota(jnp.int32, (GROUP, GROUP), 1)
        backwards = jnp.where(i + j == GROUP - 1, 1.0, 0.0).astype(jnp.bfloat16)
        for g in reversed(range(pieces)):
            ready(pieces - 1 - g)
            cells = block[size - (g + 1) * depth : size - g * depth].reshape(GROUP, chans)
            turned = jnp.dot(backwards, cells, preferred_element_type=jnp.float32).astype(jnp.bfloat16)
            out[g * depth : (g + 1) * depth] = turned.reshape(depth, size, chans)
            done(g)

    @pl.when(quarter == 3)
    def _():
        for i in range(size):
            if i % depth == 0:
                ready(i // depth)
            keep(size - 1 - i, block[i].astype(jnp.float32))
        for i in range(size):
            out[i] = column(i)
            if i % depth == depth - 1:
                done(i // depth)


def send_kernel(n, rows, rotation_in, owner_in, fields, *rest):
    edges, slabs, (rotation_out, owner_out) = rest[:n], rest[n : 2 * n], rest[2 * n : 2 * n + 2]
    staged, block, upright, rotation, scalar_sems, sems = rest[2 * n + 2 :]
    band = lax.axis_index("lat")
    me = lax.axis_index("lon")
    depth = GROUP // fields.shape[0]

    def piece(g):
        at = pl.ds(g * depth, depth)
        return pltpu.make_async_copy(fields.at[at], block.at[at], sems.at[g])

    scalars = [
        pltpu.make_async_copy(rotation_in, rotation, scalar_sems.at[0]),
        pltpu.make_async_copy(rotation_in, rotation_out, scalar_sems.at[1]),
        pltpu.make_async_copy(owner_in, owner_out, scalar_sems.at[2]),
    ]
    for copy in scalars:
        copy.start()
    for g in range(fields.shape[0] // depth):
        piece(g).start()
    scalars[0].wait()
    turn((4 - rotation[me, band]) % 4, staged, block, upright, lambda g: piece(g).wait(), lambda g: None)
    for d in range(n):
        group = group_of(band, lax.rem(me + d, n), n)
        top, odd = first_held(group, rows), group % 2
        edges[d][...] = upright[pl.ds(top + rows * odd, HALO)]
        slabs[d][...] = upright[pl.ds(top + HALO * (1 - odd), rows)]
    scalars[1].wait()
    scalars[2].wait()


def load_kernel(n, rows, after, *refs):
    del after
    count = (len(refs) - 7) // 2
    direct, (query, key) = refs[:count], refs[count : count + 2]
    loaded, (w_query, w_key) = refs[count + 2 : 2 * count + 2], refs[2 * count + 2 : 2 * count + 4]
    query_in, key_in, sems = refs[2 * count + 4 :]
    heads, _, head_dim = w_query.shape
    pairs = list(zip(direct, loaded)) + [(query, query_in), (key, key_in)]
    copies = [pltpu.make_async_copy(*pair, sems.at[i]) for i, pair in enumerate(pairs)]
    for copy in copies:
        copy.start()
    for copy in copies:
        copy.wait()
    w_key[...] = key_in[...].T
    for h in range(heads):
        w_query[h] = query_in[:, h * head_dim : (h + 1) * head_dim]


def columns_of(segment, size):
    return pl.ds(pl.multiple_of(segment * size, size), size)


def whole_rows(n, owner, slabs, out, first):
    band = lax.axis_index("lat")
    me = lax.axis_index("lon")
    count, size = slabs[0].shape[:2]
    for d in range(n):
        segment = owner[lax.rem(me + n - d, n), band]
        out[pl.ds(first, count), columns_of(segment, size)] = slabs[d][...]


def edge_kernel(n, rows, owner, *rest):
    del rows
    whole_rows(n, owner, rest[:n], rest[n], 0)


def spread(taps, r, row):
    cols, chans = row.shape
    taps[r, :, :chans] = pltpu.roll(row, 1, 0).astype(jnp.bfloat16)
    taps[r, :, chans : 2 * chans] = row.astype(jnp.bfloat16)
    taps[r, :, 2 * chans :] = pltpu.roll(row, cols - 1, 0).astype(jnp.bfloat16)


def convolve(taps, weight, bias, first, count):
    cols, width = taps.shape[1:]
    windows = [taps[first + i : first + i + count].reshape(count * cols, width) for i in range(3)]
    depth = weight.shape[0] * width
    product = jnp.dot(
        jnp.concatenate(windows, axis=1),
        weight[...].reshape(depth, weight.shape[2]),
        preferred_element_type=jnp.float32,
    )
    return product + bias[...]


def silu(x):
    half = 0.5 * x
    return half + half * jnp.tanh(half)


def live_count(counts, row):
    inside = (row >= 0) & (row < counts.shape[0])
    return jnp.where(inside, counts[jnp.clip(row, 0, counts.shape[0] - 1)], 0)


def by_last(a, b):
    return lax.dot_general(a, b, (((1,), (1,)), ((), ())), preferred_element_type=jnp.float32)


def attend(segments, span, limits, mixed, normed, keys, values, w_query, w_out, results, here, scores, expo, turned):
    rows, chans = len(limits), mixed.shape[1]
    size = here.shape[0] // (rows * len(segments))
    heads, _, head_dim = w_query.shape
    cols = mixed.shape[0] // rows
    width = heads * size
    blocks = [(s * rows + r, s, r) for s in range(len(segments)) for r in range(*span)]
    low, high = blocks[0][0], blocks[-1][0] + 1

    def cells(s, r):
        return columns_of(segments[s] + r * (cols // size), size)

    for b, s, r in blocks:
        here[b * size : (b + 1) * size, :] = normed[cells(s, r), :]
    own = here[low * size : high * size, :]
    queries = [jnp.dot(own, w_query[h], preferred_element_type=jnp.float32) for h in range(heads)]
    queries = [query.astype(jnp.bfloat16) for query in queries]
    for b, s, r in blocks:
        part = [query[(b - low) * size : (b - low + 1) * size] for query in queries]
        scores[b] = by_last(keys[r * cols : (r + 1) * cols, :], jnp.concatenate(part, axis=0))
    key_at = lax.broadcasted_iota(jnp.int32, (cols, width), 0)
    scale = math.log2(math.e) / head_dim**0.5
    shares = {}
    for b, s, r in blocks:
        part = jnp.where(key_at < limits[r], scores[b], -jnp.inf)
        part = jnp.exp2((part - jnp.max(part, axis=0, keepdims=True)) * scale)
        shares[b] = 1.0 / jnp.sum(part, axis=0, keepdims=True)
        expo[b] = part.astype(jnp.bfloat16)
    for b, s, r in blocks:
        summed = jnp.dot(values[:, r * cols : (r + 1) * cols], expo[b], preferred_element_type=jnp.float32)
        turned[:, b * width : (b + 1) * width] = (summed * shares[b]).astype(jnp.bfloat16)
    attended = turned[:, low * width : high * width].T
    update = jnp.zeros(own.shape, jnp.float32)
    for h in range(heads):
        starts = [(b - low) * width + h * size for b, *_ in blocks]
        part = jnp.concatenate([attended[start : start + size] for start in starts], axis=0)
        weight = w_out[h * head_dim : (h + 1) * head_dim, :]
        update = update + jnp.dot(part, weight, preferred_element_type=jnp.float32)
    for b, s, r in blocks:
        cell = segments[s] * size + lax.broadcasted_iota(jnp.int32, (size, chans), 0)
        part = jnp.where(cell < limits[r], update[(b - low) * size : (b - low + 1) * size], 0.0)
        results[s][r * size : (r + 1) * size, :] = (mixed[cells(s, r), :].astype(jnp.float32) + part).astype(jnp.bfloat16)


def main_kernel(first, n, rows, owner, counts, *rest):
    slabs, sent, received = rest[:n], rest[n], rest[n + 1]
    w_conv1, b_conv1, w_conv2, b_conv2, w_key, w_value, w_query, w_out = rest[n + 2 : n + 10]
    result, mixed, normed, keys, values = rest[n + 10 : n + 15]
    grid, taps, acts, *scratch = rest[n + 15 :]
    band = lax.axis_index("lat")
    me = lax.axis_index("lon")
    group = group_of(band, me, n)
    odd = group % 2
    cols, chans = sent.shape[1:]
    cell = lax.broadcasted_iota(jnp.int32, (cols, chans), 0)
    first_row = band * (rows * n) + group * rows
    whole_rows(n, owner, slabs, grid, 2 * HALO * (1 - odd))
    grid[pl.ds(HALO + (rows - HALO) * odd, HALO)] = sent[...]
    grid[pl.ds((rows + HALO) * odd, HALO)] = received[...]
    limits = [live_count(counts, first_row - 1 + r) for r in range(rows + HALO)]

    def spread_inputs(start, stop):
        for r in range(start, stop):
            spread(taps, r, grid[r].astype(jnp.float32))

    def spread_acts(start, stop, product):
        act = silu(product)
        for r in range(start, stop):
            at = slice((r - start) * cols, (r - start + 1) * cols)
            spread(acts, r, jnp.where(cell < limits[r], act[at], 0.0))

    def mix(start, stop, product):
        for r in range(start, stop):
            here = grid[r + HALO].astype(jnp.float32) + product[(r - start) * cols : (r - start + 1) * cols]
            here = jnp.where(cell < limits[r + 1], here, 0.0)
            mixed[r * cols : (r + 1) * cols, :] = here.astype(jnp.bfloat16)
        at = slice(start * cols, stop * cols)
        flat = mixed[at, :].astype(jnp.float32)
        scaled = (flat * lax.rsqrt(jnp.mean(flat * flat, axis=1, keepdims=True) + 1e-06)).astype(jnp.bfloat16)
        normed[at, :] = scaled
        keys[at, :] = jnp.dot(scaled, w_key[...], preferred_element_type=jnp.float32).astype(jnp.bfloat16)
        values[:, at] = by_last(w_value[...], scaled).astype(jnp.bfloat16)

    total = rows + HALO
    chunks = min(CHUNKS, total // HALO)
    cuts = [-(-total * c // chunks) for c in range(chunks + 1)]
    ends = [0] + [cut + HALO for cut in cuts[1:]]
    lows = [max(cut - HALO, 0) for cut in cuts]
    firsts, seconds = [], []
    spread_inputs(ends[0], ends[1])
    for c in range(chunks):
        firsts.append(convolve(taps, w_conv1, b_conv1, cuts[c], cuts[c + 1] - cuts[c]))
        if c:
            spread_acts(cuts[c - 1], cuts[c], firsts[c - 1])
        if c + 1 < chunks:
            spread_inputs(ends[c + 1], ends[c + 2])
    for c in range(chunks):
        count = lows[c + 1] - lows[c]
        seconds.append(convolve(acts, w_conv2, b_conv2, lows[c], count) if count else None)
        if c == 0:
            spread_acts(cuts[-2], total, firsts[-1])
        elif seconds[c - 1] is not None:
            mix(lows[c - 1], lows[c], seconds[c - 1])
    mix(lows[-2], rows, seconds[-1])
    result[rows * (cols // n) :, :] = jnp.zeros((AHEAD, chans), result.dtype)
    segments = [owner[lax.rem(me + first, n), band]]
    shared = limits[1 : rows + 1], mixed, normed, keys, values, w_query, w_out
    attend(segments, (0, rows), *shared, [result], *scratch)


def rest_kernel(moves, n, rows, owner, counts, *rest):
    mixed, normed, keys, values, w_query, w_out = rest[:6]
    results, scratch = rest[6 : 6 + len(moves)], rest[6 + len(moves) :]
    band = lax.axis_index("lat")
    me = lax.axis_index("lon")
    first_row = band * (rows * n) + group_of(band, me, n) * rows
    limits = [counts[first_row + r] for r in range(rows)]
    segments = [owner[lax.rem(me + d, n), band] for d in moves]
    attend(segments, (0, rows), limits, mixed, normed, keys, values, w_query, w_out, results, *scratch)


def store_kernel(n, rows, rotation, *rest):
    slabs, (out, staged, upright, turned, sems) = rest[:n], rest[n:]
    band = lax.axis_index("lat")
    me = lax.axis_index("lon")
    depth = GROUP // out.shape[0]
    pieces = out.shape[0] // depth
    for d in range(n):
        top = group_of(band, lax.rem(me + n - d, n), n) * rows
        upright[pl.ds(top, rows)] = slabs[d][: rows * out.shape[0], :].reshape(rows, *out.shape[1:])

    def piece(g):
        at = pl.ds(g * depth, depth)
        return pltpu.make_async_copy(turned.at[at], out.at[at], sems.at[g])

    turn(rotation[me, band] % 4, staged, upright, turned, lambda g: None, lambda g: piece(g).start())
    for g in range(pieces):
        piece(g).wait()


def on_device(
    bands,
    n,
    fields,
    w_conv1,
    b_conv1,
    w_conv2,
    b_conv2,
    w_query,
    w_key,
    w_value,
    w_out,
    rotation,
    owner,
    counts,
):
    size, _, chans = fields.shape
    rows = size // n
    inner = rows - HALO
    cols = size * n
    bf16 = jnp.bfloat16
    smem = pl.BlockSpec(memory_space=pltpu.SMEM)
    vmem = pl.BlockSpec(memory_space=pltpu.VMEM)
    hbm = pl.BlockSpec(memory_space=pltpu.HBM)
    params = pltpu.CompilerParams(vmem_limit_bytes=VMEM_BYTES)
    pieces = size * size // GROUP

    def call(kernel, name, out, scalars, arrays, scratch, array_spec=vmem, scalar_spec=smem, out_spec=vmem):
        many = isinstance(out, list)
        return pl.pallas_call(
            functools.partial(kernel, n, rows),
            out_shape=out,
            in_specs=[scalar_spec] * len(scalars) + [array_spec] * len(arrays),
            out_specs=[out_spec] * len(out) if many else out_spec,
            scratch_shapes=scratch,
            compiler_params=params,
            name=name,
        )(*scalars, *arrays)

    def array(*shape):
        return jax.ShapeDtypeStruct(shape, bf16)

    order = sorted(range(1, n), key=lambda d: -min(d, n - d))

    def around_by(x, d):
        return lax.ppermute(x, "lon", [(i, (i + d) % n) for i in range(n)])

    def around(parts):
        moved = {d: around_by(parts[d], d) for d in order}
        return [parts[0]] + [moved[d] for d in range(1, n)]

    def in_hbm(x):
        return pltpu.with_memory_space_constraint(x, pltpu.HBM)

    rotation, owner = in_hbm(rotation.T), in_hbm(owner.T)
    loaded = [counts]
    loaded += [w_conv1.reshape(3, 3 * chans, chans), b_conv1.reshape(1, chans)]
    loaded += [w_conv2.reshape(3, 3 * chans, chans), b_conv2.reshape(1, chans), w_value.T, w_out]
    loaded = [in_hbm(x) for x in loaded]
    turned = [in_hbm(x) for x in (w_query, w_key.T)]
    staging = pltpu.VMEM((chans // LANES, size * (size + 8), LANES), jnp.float32)
    block = pltpu.VMEM((size, size, chans), bf16)

    slabs = [array(HALO, size, chans)] * n + [array(rows, size, chans)] * n
    scratch = [staging, block, block, pltpu.SMEM(rotation.shape, rotation.dtype)]
    scratch += [pltpu.SemaphoreType.DMA((3,)), pltpu.SemaphoreType.DMA((pieces,))]
    held = slabs + [pltpu.VMEM(x.shape, x.dtype) for x in (rotation, owner)]
    *slabs, rotation, owner = call(send_kernel, "send", held, [rotation, owner], [in_hbm(fields)], scratch, hbm, hbm)
    edges = around(slabs[:n])
    slabs = around(slabs[n:])

    snake = [a * n + shard_of(a, g, n) for a in range(bands) for g in range(n)]
    pairs = [(snake[i], snake[i + 1 if i % 2 else i - 1]) for i in range(1, bands * n - 1)]
    sent = call(edge_kernel, "edge", array(HALO, cols, chans), [owner], edges, [])
    received = lax.ppermute(sent, ("lat", "lon"), pairs)

    head_dim = w_key.shape[1]
    heads = chans // head_dim
    held = [pltpu.VMEM(x.shape, x.dtype) for x in loaded]
    held += [pltpu.VMEM((heads, chans, head_dim), bf16), pltpu.VMEM(w_key.shape, bf16)]
    scratch = [pltpu.VMEM(x.shape, bf16) for x in turned] + [pltpu.SemaphoreType.DMA((len(loaded) + 2,))]
    loaded = call(load_kernel, "load", held, [sent], loaded + turned, scratch, hbm, hbm)
    counts, *convs, w_value, w_out, w_query, w_key = loaded

    def taps(count):
        return pltpu.VMEM((count, cols, 3 * chans), bf16)

    def working(segments):
        blocks, width = segments * rows, heads * size
        return [
            pltpu.VMEM((blocks * size, chans), bf16),
            pltpu.VMEM((blocks, cols, width), jnp.float32),
            pltpu.VMEM((blocks, cols, width), bf16),
            pltpu.VMEM((head_dim, blocks * width), bf16),
        ]

    cells = rows * cols
    result = array(rows * size, chans)
    first, *others = [*order, 0]
    results = {}
    results[first], *held = call(
        functools.partial(main_kernel, first),
        "main",
        [array(rows * size + AHEAD, chans), array(cells, chans), array(cells, chans), array(cells, head_dim), array(head_dim, cells)],
        [owner, counts],
        slabs + [sent, received, *convs, w_key, w_value, w_query, w_out],
        [pltpu.VMEM((rows + 2 * HALO, cols, chans), bf16), taps(rows + 2 * HALO), taps(rows + HALO)] + working(1),
    )
    moved = {first: around_by(results[first], first)}
    rest = call(
        functools.partial(rest_kernel, others),
        "rest",
        [result] * len(others),
        [owner, counts],
        held + [w_query, w_out],
        working(len(others)),
    )
    for d, x in zip(others, rest):
        moved[d] = around_by(x, d) if d else x
    slabs = [moved[d] for d in range(n)]
    scratch = [staging, block, block, pltpu.SemaphoreType.DMA((pieces,))]
    return call(store_kernel, "store", array(*fields.shape), [rotation], slabs, scratch, out_spec=hbm)


def solution(mesh):
    in_specs = (P("lat", "lon", None), P(), P(), P(), P(), P(), P(), P(), P(), P(), P(), P())
    out_specs = P("lat", "lon", None)
    body = functools.partial(on_device, mesh.shape["lat"], mesh.shape["lon"])
    return jax.shard_map(body, mesh=mesh, in_specs=in_specs, out_specs=out_specs, check_vma=False)
```

```python
import functools
import math

import jax
import jax.numpy as jnp
from jax import lax
from jax.experimental import pallas as pl
from jax.experimental.pallas import tpu as pltpu
from jax.sharding import PartitionSpec as P

HALO = 2
LANES = 128
GROUP = 256
CHUNKS = 3
AHEAD = 16
VMEM_BYTES = 28 * 1024 * 1024


def group_of(band, shard, n):
    outer = jnp.where((shard == n - 2) == (band % 2 == 0), 0, n - 1)
    return jnp.where(shard < n - 2, shard + 1, outer)


def shard_of(band, group, n):
    if 0 < group < n - 1:
        return group - 1
    return n - 2 if (group == 0) == (band % 2 == 0) else n - 1


def first_held(group, rows):
    return group * rows - HALO * (group % 2)


def turn(quarter, staged, block, out, ready, done):
    size, _, chans = block.shape
    tiles = staged.shape[0]
    pitch = staged.shape[1] // size
    depth = GROUP // size
    pieces = size // depth

    def column(col):
        parts = [staged[t, pl.ds(col, size, stride=pitch), :] for t in range(tiles)]
        return jnp.concatenate(parts, axis=1).astype(jnp.bfloat16)

    def keep(i, row):
        for t in range(tiles):
            staged[t, pl.ds(i * pitch, size), :] = row[:, t * LANES : (t + 1) * LANES]

    @pl.when(quarter == 0)
    def _():
        for g in range(pieces):
            ready(g)
            out[g * depth : (g + 1) * depth] = block[g * depth : (g + 1) * depth]
            done(g)

    @pl.when(quarter == 1)
    def _():
        for i in range(size):
            if i % depth == 0:
                ready(i // depth)
            keep(i, block[i].astype(jnp.float32))
        for i in range(size):
            out[i] = column(size - 1 - i)
            if i % depth == depth - 1:
                done(i // depth)

    @pl.when(quarter == 2)
    def _():
        i = lax.broadcasted_iota(jnp.int32, (GROUP, GROUP), 0)
        j = lax.broadcasted_iota(jnp.int32, (GROUP, GROUP), 1)
        backwards = jnp.where(i + j == GROUP - 1, 1.0, 0.0).astype(jnp.bfloat16)
        for g in reversed(range(pieces)):
            ready(pieces - 1 - g)
            cells = block[size - (g + 1) * depth : size - g * depth].reshape(GROUP, chans)
            turned = jnp.dot(backwards, cells, preferred_element_type=jnp.float32).astype(jnp.bfloat16)
            out[g * depth : (g + 1) * depth] = turned.reshape(depth, size, chans)
            done(g)

    @pl.when(quarter == 3)
    def _():
        for i in range(size):
            if i % depth == 0:
                ready(i // depth)
            keep(size - 1 - i, block[i].astype(jnp.float32))
        for i in range(size):
            out[i] = column(i)
            if i % depth == depth - 1:
                done(i // depth)


def send_kernel(n, rows, rotation_in, owner_in, fields, *rest):
    edges, slabs, (rotation_out, owner_out) = rest[:n], rest[n : 2 * n], rest[2 * n : 2 * n + 2]
    staged, block, upright, rotation, scalar_sems, sems = rest[2 * n + 2 :]
    band = lax.axis_index("lat")
    me = lax.axis_index("lon")
    depth = GROUP // fields.shape[0]

    def piece(g):
        at = pl.ds(g * depth, depth)
        return pltpu.make_async_copy(fields.at[at], block.at[at], sems.at[g])

    scalars = [
        pltpu.make_async_copy(rotation_in, rotation, scalar_sems.at[0]),
        pltpu.make_async_copy(rotation_in, rotation_out, scalar_sems.at[1]),
        pltpu.make_async_copy(owner_in, owner_out, scalar_sems.at[2]),
    ]
    for copy in scalars:
        copy.start()
    for g in range(fields.shape[0] // depth):
        piece(g).start()
    scalars[0].wait()
    turn((4 - rotation[me, band]) % 4, staged, block, upright, lambda g: piece(g).wait(), lambda g: None)
    for d in range(n):
        group = group_of(band, lax.rem(me + d, n), n)
        top, odd = first_held(group, rows), group % 2
        edges[d][...] = upright[pl.ds(top + rows * odd, HALO)]
        slabs[d][...] = upright[pl.ds(top + HALO * (1 - odd), rows)]
    scalars[1].wait()
    scalars[2].wait()


def load_kernel(n, rows, after, *refs):
    del after
    count = (len(refs) - 7) // 2
    direct, (query, key) = refs[:count], refs[count : count + 2]
    loaded, (w_query, w_key) = refs[count + 2 : 2 * count + 2], refs[2 * count + 2 : 2 * count + 4]
    query_in, key_in, sems = refs[2 * count + 4 :]
    pairs = list(zip(direct, loaded)) + [(query, query_in), (key, key_in)]
    copies = [pltpu.make_async_copy(*pair, sems.at[i]) for i, pair in enumerate(pairs)]
    for copy in copies:
        copy.start()
    for copy in copies:
        copy.wait()
    w_key[...] = key_in[...].T
    w_query[...] = query_in[...]


def columns_of(segment, size):
    return pl.ds(pl.multiple_of(segment * size, size), size)


def whole_rows(n, owner, slabs, out, first):
    band = lax.axis_index("lat")
    me = lax.axis_index("lon")
    count, size = slabs[0].shape[:2]
    for d in range(n):
        segment = owner[lax.rem(me + n - d, n), band]
        out[pl.ds(first, count), columns_of(segment, size)] = slabs[d][...]


def edge_kernel(n, rows, owner, *rest):
    del rows
    whole_rows(n, owner, rest[:n], rest[n], 0)


def spread(taps, r, row):
    cols, chans = row.shape
    taps[r, :, :chans] = pltpu.roll(row, 1, 0).astype(jnp.bfloat16)
    taps[r, :, chans : 2 * chans] = row.astype(jnp.bfloat16)
    taps[r, :, 2 * chans :] = pltpu.roll(row, cols - 1, 0).astype(jnp.bfloat16)


def convolve(taps, weight, bias, first, count):
    cols, width = taps.shape[1:]
    windows = [taps[first + i : first + i + count].reshape(count * cols, width) for i in range(3)]
    depth = weight.shape[0] * width
    product = jnp.dot(
        jnp.concatenate(windows, axis=1),
        weight[...].reshape(depth, weight.shape[2]),
        preferred_element_type=jnp.float32,
    )
    return product + bias[...]


def silu(x):
    half = 0.5 * x
    return half + half * jnp.tanh(half)


def live_count(counts, row):
    inside = (row >= 0) & (row < counts.shape[0])
    return jnp.where(inside, counts[jnp.clip(row, 0, counts.shape[0] - 1)], 0)


def by_last(a, b):
    return lax.dot_general(a, b, (((1,), (1,)), ((), ())), preferred_element_type=jnp.float32)


def attend(segments, span, limits, mixed, normed, keys, values, w_query, w_out, results, here, scores, expo, turned):
    rows, chans = len(limits), mixed.shape[1]
    size = here.shape[0] // (rows * len(segments))
    head_dim = keys.shape[1]
    heads = chans // head_dim
    cols = mixed.shape[0] // rows
    width = heads * size
    blocks = [(s * rows + r, s, r) for s in range(len(segments)) for r in range(*span)]
    low, high = blocks[0][0], blocks[-1][0] + 1

    def cells(s, r):
        return columns_of(segments[s] + r * (cols // size), size)

    for b, s, r in blocks:
        here[b * size : (b + 1) * size, :] = normed[cells(s, r), :]
    own = here[low * size : high * size, :]
    query = jnp.dot(own, w_query[...], preferred_element_type=jnp.float32).astype(jnp.bfloat16)
    queries = [query[:, h * head_dim : (h + 1) * head_dim] for h in range(heads)]
    for b, s, r in blocks:
        part = [query[(b - low) * size : (b - low + 1) * size] for query in queries]
        scores[b] = by_last(keys[r * cols : (r + 1) * cols, :], jnp.concatenate(part, axis=0))
    key_at = lax.broadcasted_iota(jnp.int32, (cols, width), 0)
    scale = math.log2(math.e) / head_dim**0.5
    shares = {}
    for b, s, r in blocks:
        part = jnp.where(key_at < limits[r], scores[b], -jnp.inf)
        part = jnp.exp2((part - jnp.max(part, axis=0, keepdims=True)) * scale)
        shares[b] = 1.0 / jnp.sum(part, axis=0, keepdims=True)
        expo[b] = part.astype(jnp.bfloat16)
    for b, s, r in blocks:
        summed = jnp.dot(values[:, r * cols : (r + 1) * cols], expo[b], preferred_element_type=jnp.float32)
        turned[:, b * width : (b + 1) * width] = (summed * shares[b]).astype(jnp.bfloat16)
    attended = turned[:, low * width : high * width].T
    parts = []
    for h in range(heads):
        starts = [(b - low) * width + h * size for b, *_ in blocks]
        parts.append(jnp.concatenate([attended[start : start + size] for start in starts], axis=0))
    update = jnp.dot(jnp.concatenate(parts, axis=1), w_out[...], preferred_element_type=jnp.float32)
    for b, s, r in blocks:
        cell = segments[s] * size + lax.broadcasted_iota(jnp.int32, (size, chans), 0)
        part = jnp.where(cell < limits[r], update[(b - low) * size : (b - low + 1) * size], 0.0)
        results[s][r * size : (r + 1) * size, :] = (mixed[cells(s, r), :].astype(jnp.float32) + part).astype(jnp.bfloat16)


def main_kernel(first, n, rows, owner, counts, *rest):
    slabs, sent, received = rest[:n], rest[n], rest[n + 1]
    w_conv1, b_conv1, w_conv2, b_conv2, w_key, w_value, w_query, w_out = rest[n + 2 : n + 10]
    result, mixed, normed, keys, values = rest[n + 10 : n + 15]
    grid, taps, acts, *scratch = rest[n + 15 :]
    band = lax.axis_index("lat")
    me = lax.axis_index("lon")
    group = group_of(band, me, n)
    odd = group % 2
    cols, chans = sent.shape[1:]
    cell = lax.broadcasted_iota(jnp.int32, (cols, chans), 0)
    first_row = band * (rows * n) + group * rows
    whole_rows(n, owner, slabs, grid, 2 * HALO * (1 - odd))
    grid[pl.ds(HALO + (rows - HALO) * odd, HALO)] = sent[...]
    grid[pl.ds((rows + HALO) * odd, HALO)] = received[...]
    limits = [live_count(counts, first_row - 1 + r) for r in range(rows + HALO)]

    def spread_inputs(start, stop):
        for r in range(start, stop):
            spread(taps, r, grid[r].astype(jnp.float32))

    def spread_acts(start, stop, product):
        act = silu(product)
        for r in range(start, stop):
            at = slice((r - start) * cols, (r - start + 1) * cols)
            spread(acts, r, jnp.where(cell < limits[r], act[at], 0.0))

    def mix(start, stop, product):
        for r in range(start, stop):
            here = grid[r + HALO].astype(jnp.float32) + product[(r - start) * cols : (r - start + 1) * cols]
            here = jnp.where(cell < limits[r + 1], here, 0.0)
            mixed[r * cols : (r + 1) * cols, :] = here.astype(jnp.bfloat16)
        at = slice(start * cols, stop * cols)
        flat = mixed[at, :].astype(jnp.float32)
        scaled = (flat * lax.rsqrt(jnp.mean(flat * flat, axis=1, keepdims=True) + 1e-06)).astype(jnp.bfloat16)
        normed[at, :] = scaled
        keys[at, :] = jnp.dot(scaled, w_key[...], preferred_element_type=jnp.float32).astype(jnp.bfloat16)
        values[:, at] = by_last(w_value[...], scaled).astype(jnp.bfloat16)

    total = rows + HALO
    chunks = min(CHUNKS, total // HALO)
    cuts = [-(-total * c // chunks) for c in range(chunks + 1)]
    ends = [0] + [cut + HALO for cut in cuts[1:]]
    lows = [max(cut - HALO, 0) for cut in cuts]
    firsts, seconds = [], []
    spread_inputs(ends[0], ends[1])
    for c in range(chunks):
        firsts.append(convolve(taps, w_conv1, b_conv1, cuts[c], cuts[c + 1] - cuts[c]))
        if c:
            spread_acts(cuts[c - 1], cuts[c], firsts[c - 1])
        if c + 1 < chunks:
            spread_inputs(ends[c + 1], ends[c + 2])
    for c in range(chunks):
        count = lows[c + 1] - lows[c]
        seconds.append(convolve(acts, w_conv2, b_conv2, lows[c], count) if count else None)
        if c == 0:
            spread_acts(cuts[-2], total, firsts[-1])
        elif seconds[c - 1] is not None:
            mix(lows[c - 1], lows[c], seconds[c - 1])
    mix(lows[-2], rows, seconds[-1])
    result[rows * (cols // n) :, :] = jnp.zeros((AHEAD, chans), result.dtype)
    segments = [owner[lax.rem(me + first, n), band]]
    shared = limits[1 : rows + 1], mixed, normed, keys, values, w_query, w_out
    attend(segments, (0, rows), *shared, [result], *scratch)


def rest_kernel(moves, n, rows, owner, counts, *rest):
    mixed, normed, keys, values, w_query, w_out = rest[:6]
    results, scratch = rest[6 : 6 + len(moves)], rest[6 + len(moves) :]
    band = lax.axis_index("lat")
    me = lax.axis_index("lon")
    first_row = band * (rows * n) + group_of(band, me, n) * rows
    limits = [counts[first_row + r] for r in range(rows)]
    segments = [owner[lax.rem(me + d, n), band] for d in moves]
    attend(segments, (0, rows), limits, mixed, normed, keys, values, w_query, w_out, results, *scratch)


def store_kernel(n, rows, rotation, *rest):
    slabs, (out, staged, upright, turned, sems) = rest[:n], rest[n:]
    band = lax.axis_index("lat")
    me = lax.axis_index("lon")
    depth = GROUP // out.shape[0]
    pieces = out.shape[0] // depth
    for d in range(n):
        top = group_of(band, lax.rem(me + n - d, n), n) * rows
        upright[pl.ds(top, rows)] = slabs[d][: rows * out.shape[0], :].reshape(rows, *out.shape[1:])

    def piece(g):
        at = pl.ds(g * depth, depth)
        return pltpu.make_async_copy(turned.at[at], out.at[at], sems.at[g])

    turn(rotation[me, band] % 4, staged, upright, turned, lambda g: None, lambda g: piece(g).start())
    for g in range(pieces):
        piece(g).wait()


def on_device(
    bands,
    n,
    fields,
    w_conv1,
    b_conv1,
    w_conv2,
    b_conv2,
    w_query,
    w_key,
    w_value,
    w_out,
    rotation,
    owner,
    counts,
):
    size, _, chans = fields.shape
    rows = size // n
    inner = rows - HALO
    cols = size * n
    bf16 = jnp.bfloat16
    smem = pl.BlockSpec(memory_space=pltpu.SMEM)
    vmem = pl.BlockSpec(memory_space=pltpu.VMEM)
    hbm = pl.BlockSpec(memory_space=pltpu.HBM)
    params = pltpu.CompilerParams(vmem_limit_bytes=VMEM_BYTES)
    pieces = size * size // GROUP

    def call(kernel, name, out, scalars, arrays, scratch, array_spec=vmem, scalar_spec=smem, out_spec=vmem):
        many = isinstance(out, list)
        return pl.pallas_call(
            functools.partial(kernel, n, rows),
            out_shape=out,
            in_specs=[scalar_spec] * len(scalars) + [array_spec] * len(arrays),
            out_specs=[out_spec] * len(out) if many else out_spec,
            scratch_shapes=scratch,
            compiler_params=params,
            name=name,
        )(*scalars, *arrays)

    def array(*shape):
        return jax.ShapeDtypeStruct(shape, bf16)

    order = sorted(range(1, n), key=lambda d: -min(d, n - d))

    def around_by(x, d):
        return lax.ppermute(x, "lon", [(i, (i + d) % n) for i in range(n)])

    def around(parts):
        moved = {d: around_by(parts[d], d) for d in order}
        return [parts[0]] + [moved[d] for d in range(1, n)]

    def in_hbm(x):
        return pltpu.with_memory_space_constraint(x, pltpu.HBM)

    rotation, owner = in_hbm(rotation.T), in_hbm(owner.T)
    loaded = [counts]
    loaded += [w_conv1.reshape(3, 3 * chans, chans), b_conv1.reshape(1, chans)]
    loaded += [w_conv2.reshape(3, 3 * chans, chans), b_conv2.reshape(1, chans), w_value.T, w_out]
    loaded = [in_hbm(x) for x in loaded]
    turned = [in_hbm(x) for x in (w_query, w_key.T)]
    staging = pltpu.VMEM((chans // LANES, size * (size + 8), LANES), jnp.float32)
    block = pltpu.VMEM((size, size, chans), bf16)

    slabs = [array(HALO, size, chans)] * n + [array(rows, size, chans)] * n
    scratch = [staging, block, block, pltpu.SMEM(rotation.shape, rotation.dtype)]
    scratch += [pltpu.SemaphoreType.DMA((3,)), pltpu.SemaphoreType.DMA((pieces,))]
    held = slabs + [pltpu.VMEM(x.shape, x.dtype) for x in (rotation, owner)]
    *slabs, rotation, owner = call(send_kernel, "send", held, [rotation, owner], [in_hbm(fields)], scratch, hbm, hbm)
    edges = around(slabs[:n])
    slabs = around(slabs[n:])

    snake = [a * n + shard_of(a, g, n) for a in range(bands) for g in range(n)]
    pairs = [(snake[i], snake[i + 1 if i % 2 else i - 1]) for i in range(1, bands * n - 1)]
    sent = call(edge_kernel, "edge", array(HALO, cols, chans), [owner], edges, [])
    received = lax.ppermute(sent, ("lat", "lon"), pairs)

    head_dim = w_key.shape[1]
    heads = chans // head_dim
    held = [pltpu.VMEM(x.shape, x.dtype) for x in loaded]
    held += [pltpu.VMEM(w_query.shape, bf16), pltpu.VMEM(w_key.shape, bf16)]
    scratch = [pltpu.VMEM(x.shape, bf16) for x in turned] + [pltpu.SemaphoreType.DMA((len(loaded) + 2,))]
    loaded = call(load_kernel, "load", held, [sent], loaded + turned, scratch, hbm, hbm)
    counts, *convs, w_value, w_out, w_query, w_key = loaded

    def taps(count):
        return pltpu.VMEM((count, cols, 3 * chans), bf16)

    def working(segments):
        blocks, width = segments * rows, heads * size
        return [
            pltpu.VMEM((blocks * size, chans), bf16),
            pltpu.VMEM((blocks, cols, width), jnp.float32),
            pltpu.VMEM((blocks, cols, width), bf16),
            pltpu.VMEM((head_dim, blocks * width), bf16),
        ]

    cells = rows * cols
    result = array(rows * size, chans)
    first, *others = [*order, 0]
    results = {}
    results[first], *held = call(
        functools.partial(main_kernel, first),
        "main",
        [array(rows * size + AHEAD, chans), array(cells, chans), array(cells, chans), array(cells, head_dim), array(head_dim, cells)],
        [owner, counts],
        slabs + [sent, received, *convs, w_key, w_value, w_query, w_out],
        [pltpu.VMEM((rows + 2 * HALO, cols, chans), bf16), taps(rows + 2 * HALO), taps(rows + HALO)] + working(1),
    )
    moved = {first: around_by(results[first], first)}
    rest = call(
        functools.partial(rest_kernel, others),
        "rest",
        [result] * len(others),
        [owner, counts],
        held + [w_query, w_out],
        working(len(others)),
    )
    for d, x in zip(others, rest):
        moved[d] = around_by(x, d) if d else x
    slabs = [moved[d] for d in range(n)]
    scratch = [staging, block, block, pltpu.SemaphoreType.DMA((pieces,))]
    return call(store_kernel, "store", array(*fields.shape), [rotation], slabs, scratch, out_spec=hbm)


def solution(mesh):
    in_specs = (P("lat", "lon", None), P(), P(), P(), P(), P(), P(), P(), P(), P(), P(), P())
    out_specs = P("lat", "lon", None)
    body = functools.partial(on_device, mesh.shape["lat"], mesh.shape["lon"])
    return jax.shard_map(body, mesh=mesh, in_specs=in_specs, out_specs=out_specs, check_vma=False)
```

```python
import functools
import math

import jax
import jax.numpy as jnp
from jax import lax
from jax.experimental import pallas as pl
from jax.experimental.pallas import tpu as pltpu
from jax.sharding import PartitionSpec as P

HALO = 2
LANES = 128
GROUP = 256
CHUNKS = 3
AHEAD = 16
VMEM_BYTES = 28 * 1024 * 1024


def group_of(band, shard, n):
    outer = jnp.where((shard == n - 2) == (band % 2 == 0), 0, n - 1)
    return jnp.where(shard < n - 2, shard + 1, outer)


def shard_of(band, group, n):
    if 0 < group < n - 1:
        return group - 1
    return n - 2 if (group == 0) == (band % 2 == 0) else n - 1


def first_held(group, rows):
    return group * rows - HALO * (group % 2)


def turn(quarter, staged, block, out, ready, done):
    size, _, chans = block.shape
    tiles = staged.shape[0]
    pitch = staged.shape[1] // size
    depth = GROUP // size
    pieces = size // depth

    def column(col):
        parts = [staged[t, pl.ds(col, size, stride=pitch), :] for t in range(tiles)]
        return jnp.concatenate(parts, axis=1).astype(jnp.bfloat16)

    def keep(i, row):
        for t in range(tiles):
            staged[t, pl.ds(i * pitch, size), :] = row[:, t * LANES : (t + 1) * LANES]

    @pl.when(quarter == 0)
    def _():
        for g in range(pieces):
            ready(g)
            out[g * depth : (g + 1) * depth] = block[g * depth : (g + 1) * depth]
            done(g)

    @pl.when(quarter == 1)
    def _():
        for i in range(size):
            if i % depth == 0:
                ready(i // depth)
            keep(i, block[i].astype(jnp.float32))
        for i in range(size):
            out[i] = column(size - 1 - i)
            if i % depth == depth - 1:
                done(i // depth)

    @pl.when(quarter == 2)
    def _():
        i = lax.broadcasted_iota(jnp.int32, (GROUP, GROUP), 0)
        j = lax.broadcasted_iota(jnp.int32, (GROUP, GROUP), 1)
        backwards = jnp.where(i + j == GROUP - 1, 1.0, 0.0).astype(jnp.bfloat16)
        for g in reversed(range(pieces)):
            ready(pieces - 1 - g)
            cells = block[size - (g + 1) * depth : size - g * depth].reshape(GROUP, chans)
            turned = jnp.dot(backwards, cells, preferred_element_type=jnp.float32).astype(jnp.bfloat16)
            out[g * depth : (g + 1) * depth] = turned.reshape(depth, size, chans)
            done(g)

    @pl.when(quarter == 3)
    def _():
        for i in range(size):
            if i % depth == 0:
                ready(i // depth)
            keep(size - 1 - i, block[i].astype(jnp.float32))
        for i in range(size):
            out[i] = column(i)
            if i % depth == depth - 1:
                done(i // depth)


def send_kernel(n, rows, rotation_in, owner_in, fields, *rest):
    edges, slabs, (rotation_out, owner_out) = rest[:n], rest[n : 2 * n], rest[2 * n : 2 * n + 2]
    staged, block, upright, rotation, scalar_sems, sems = rest[2 * n + 2 :]
    band = lax.axis_index("lat")
    me = lax.axis_index("lon")
    depth = GROUP // fields.shape[0]

    def piece(g):
        at = pl.ds(g * depth, depth)
        return pltpu.make_async_copy(fields.at[at], block.at[at], sems.at[g])

    scalars = [
        pltpu.make_async_copy(rotation_in, rotation, scalar_sems.at[0]),
        pltpu.make_async_copy(rotation_in, rotation_out, scalar_sems.at[1]),
        pltpu.make_async_copy(owner_in, owner_out, scalar_sems.at[2]),
    ]
    for copy in scalars:
        copy.start()
    for g in range(fields.shape[0] // depth):
        piece(g).start()
    scalars[0].wait()
    turn((4 - rotation[me, band]) % 4, staged, block, upright, lambda g: piece(g).wait(), lambda g: None)
    for d in range(n):
        group = group_of(band, lax.rem(me + d, n), n)
        top, odd = first_held(group, rows), group % 2
        edges[d][...] = upright[pl.ds(top + rows * odd, HALO)]
        slabs[d][...] = upright[pl.ds(top + HALO * (1 - odd), rows)]
    scalars[1].wait()
    scalars[2].wait()


def load_kernel(n, rows, after, *refs):
    del after
    count = (len(refs) - 7) // 2
    direct, (query, key) = refs[:count], refs[count : count + 2]
    loaded, (w_query, w_key) = refs[count + 2 : 2 * count + 2], refs[2 * count + 2 : 2 * count + 4]
    query_in, key_in, sems = refs[2 * count + 4 :]
    pairs = list(zip(direct, loaded)) + [(query, query_in), (key, key_in)]
    copies = [pltpu.make_async_copy(*pair, sems.at[i]) for i, pair in enumerate(pairs)]
    for copy in copies:
        copy.start()
    for copy in copies:
        copy.wait()
    w_key[...] = key_in[...].T
    w_query[...] = query_in[...]


def columns_of(segment, size):
    return pl.ds(pl.multiple_of(segment * size, size), size)


def whole_rows(n, owner, slabs, out, first):
    band = lax.axis_index("lat")
    me = lax.axis_index("lon")
    count, size = slabs[0].shape[:2]
    for d in range(n):
        segment = owner[lax.rem(me + n - d, n), band]
        out[pl.ds(first, count), columns_of(segment, size)] = slabs[d][...]


def edge_kernel(n, rows, owner, *rest):
    del rows
    whole_rows(n, owner, rest[:n], rest[n], 0)


def spread(taps, r, row):
    cols, chans = row.shape
    taps[r, :, :chans] = pltpu.roll(row, 1, 0).astype(jnp.bfloat16)
    taps[r, :, chans : 2 * chans] = row.astype(jnp.bfloat16)
    taps[r, :, 2 * chans :] = pltpu.roll(row, cols - 1, 0).astype(jnp.bfloat16)


def convolve(taps, weight, bias, first, count):
    cols, width = taps.shape[1:]
    windows = [taps[first + i : first + i + count].reshape(count * cols, width) for i in range(3)]
    depth = weight.shape[0] * width
    product = jnp.dot(
        jnp.concatenate(windows, axis=1),
        weight[...].reshape(depth, weight.shape[2]),
        preferred_element_type=jnp.float32,
    )
    return product + bias[...]


def silu(x):
    half = 0.5 * x
    return half + half * jnp.tanh(half)


def live_count(counts, row):
    inside = (row >= 0) & (row < counts.shape[0])
    return jnp.where(inside, counts[jnp.clip(row, 0, counts.shape[0] - 1)], 0)


def by_last(a, b):
    return lax.dot_general(a, b, (((1,), (1,)), ((), ())), preferred_element_type=jnp.float32)


def attend(segments, span, limits, mixed, normed, keys, values, w_query, w_out, results, here, scores, expo, turned):
    rows, chans = len(limits), mixed.shape[1]
    size = here.shape[0] // (rows * len(segments))
    head_dim = keys.shape[1]
    heads = chans // head_dim
    cols = mixed.shape[0] // rows
    width = heads * size
    blocks = [(s * rows + r, s, r) for s in range(len(segments)) for r in range(*span)]
    low, high = blocks[0][0], blocks[-1][0] + 1

    def cells(s, r):
        return columns_of(segments[s] + r * (cols // size), size)

    for b, s, r in blocks:
        here[b * size : (b + 1) * size, :] = normed[cells(s, r), :]
    own = here[low * size : high * size, :]
    query = jnp.dot(own, w_query[...], preferred_element_type=jnp.float32).astype(jnp.bfloat16)
    queries = [query[:, h * head_dim : (h + 1) * head_dim] for h in range(heads)]
    for b, s, r in blocks:
        part = [query[(b - low) * size : (b - low + 1) * size] for query in queries]
        scores[b] = by_last(keys[r * cols : (r + 1) * cols, :], jnp.concatenate(part, axis=0))
    key_at = lax.broadcasted_iota(jnp.int32, (cols, width), 0)
    scale = math.log2(math.e) / head_dim**0.5
    shares = {}
    for b, s, r in blocks:
        part = jnp.where(key_at < limits[r], scores[b], -jnp.inf)
        part = jnp.exp2((part - jnp.max(part, axis=0, keepdims=True)) * scale)
        shares[b] = 1.0 / jnp.sum(part, axis=0, keepdims=True)
        expo[b] = part.astype(jnp.bfloat16)
    for b, s, r in blocks:
        summed = jnp.dot(values[:, r * cols : (r + 1) * cols], expo[b], preferred_element_type=jnp.float32)
        turned[:, b * width : (b + 1) * width] = (summed * shares[b]).astype(jnp.bfloat16)
    attended = turned[:, low * width : high * width].T
    parts = []
    for h in range(heads):
        starts = [(b - low) * width + h * size for b, *_ in blocks]
        parts.append(jnp.concatenate([attended[start : start + size] for start in starts], axis=0))
    update = jnp.dot(jnp.concatenate(parts, axis=1), w_out[...], preferred_element_type=jnp.float32)
    for b, s, r in blocks:
        cell = segments[s] * size + lax.broadcasted_iota(jnp.int32, (size, chans), 0)
        part = jnp.where(cell < limits[r], update[(b - low) * size : (b - low + 1) * size], 0.0)
        results[s][r * size : (r + 1) * size, :] = (mixed[cells(s, r), :].astype(jnp.float32) + part).astype(jnp.bfloat16)


def main_kernel(first, n, rows, owner, counts, *rest):
    slabs, sent, received = rest[:n], rest[n], rest[n + 1]
    w_conv1, b_conv1, w_conv2, b_conv2, w_key, w_value, w_query, w_out = rest[n + 2 : n + 10]
    result, mixed, normed, keys, values = rest[n + 10 : n + 15]
    grid, taps, acts, *scratch = rest[n + 15 :]
    band = lax.axis_index("lat")
    me = lax.axis_index("lon")
    group = group_of(band, me, n)
    odd = group % 2
    cols, chans = sent.shape[1:]
    cell = lax.broadcasted_iota(jnp.int32, (cols, chans), 0)
    first_row = band * (rows * n) + group * rows
    whole_rows(n, owner, slabs, grid, 2 * HALO * (1 - odd))
    grid[pl.ds(HALO + (rows - HALO) * odd, HALO)] = sent[...]
    grid[pl.ds((rows + HALO) * odd, HALO)] = received[...]
    limits = [live_count(counts, first_row - 1 + r) for r in range(rows + HALO)]

    def spread_inputs(start, stop):
        for r in range(start, stop):
            spread(taps, r, grid[r].astype(jnp.float32))

    def spread_acts(start, stop, product):
        act = silu(product)
        for r in range(start, stop):
            at = slice((r - start) * cols, (r - start + 1) * cols)
            spread(acts, r, jnp.where(cell < limits[r], act[at], 0.0))

    def mix(start, stop, product):
        for r in range(start, stop):
            here = grid[r + HALO].astype(jnp.float32) + product[(r - start) * cols : (r - start + 1) * cols]
            here = jnp.where(cell < limits[r + 1], here, 0.0)
            mixed[r * cols : (r + 1) * cols, :] = here.astype(jnp.bfloat16)
        at = slice(start * cols, stop * cols)
        flat = mixed[at, :].astype(jnp.float32)
        scaled = (flat * lax.rsqrt(jnp.mean(flat * flat, axis=1, keepdims=True) + 1e-06)).astype(jnp.bfloat16)
        normed[at, :] = scaled
        keys[at, :] = jnp.dot(scaled, w_key[...], preferred_element_type=jnp.float32).astype(jnp.bfloat16)
        values[:, at] = by_last(w_value[...], scaled).astype(jnp.bfloat16)

    total = rows + HALO
    chunks = min(CHUNKS, total // HALO)
    cuts = [min(-(-total // chunks) * c, total) for c in range(chunks + 1)]
    ends = [0] + [cut + HALO for cut in cuts[1:]]
    lows = [max(cut - HALO, 0) for cut in cuts]
    firsts, seconds = [], []
    spread_inputs(ends[0], ends[1])
    for c in range(chunks):
        firsts.append(convolve(taps, w_conv1, b_conv1, cuts[c], cuts[c + 1] - cuts[c]))
        if c:
            spread_acts(cuts[c - 1], cuts[c], firsts[c - 1])
        if c + 1 < chunks:
            spread_inputs(ends[c + 1], ends[c + 2])
    for c in range(chunks):
        count = lows[c + 1] - lows[c]
        seconds.append(convolve(acts, w_conv2, b_conv2, lows[c], count) if count else None)
        if c == 0:
            spread_acts(cuts[-2], total, firsts[-1])
        elif seconds[c - 1] is not None:
            mix(lows[c - 1], lows[c], seconds[c - 1])
    mix(lows[-2], rows, seconds[-1])
    result[rows * (cols // n) :, :] = jnp.zeros((AHEAD, chans), result.dtype)
    segments = [owner[lax.rem(me + first, n), band]]
    shared = limits[1 : rows + 1], mixed, normed, keys, values, w_query, w_out
    attend(segments, (0, rows), *shared, [result], *scratch)


def rest_kernel(moves, n, rows, owner, counts, *rest):
    mixed, normed, keys, values, w_query, w_out = rest[:6]
    results, scratch = rest[6 : 6 + len(moves)], rest[6 + len(moves) :]
    band = lax.axis_index("lat")
    me = lax.axis_index("lon")
    first_row = band * (rows * n) + group_of(band, me, n) * rows
    limits = [counts[first_row + r] for r in range(rows)]
    segments = [owner[lax.rem(me + d, n), band] for d in moves]
    attend(segments, (0, rows), limits, mixed, normed, keys, values, w_query, w_out, results, *scratch)


def store_kernel(n, rows, rotation, *rest):
    slabs, (out, staged, upright, turned, sems) = rest[:n], rest[n:]
    band = lax.axis_index("lat")
    me = lax.axis_index("lon")
    depth = GROUP // out.shape[0]
    pieces = out.shape[0] // depth
    for d in range(n):
        top = group_of(band, lax.rem(me + n - d, n), n) * rows
        upright[pl.ds(top, rows)] = slabs[d][: rows * out.shape[0], :].reshape(rows, *out.shape[1:])

    def piece(g):
        at = pl.ds(g * depth, depth)
        return pltpu.make_async_copy(turned.at[at], out.at[at], sems.at[g])

    turn(rotation[me, band] % 4, staged, upright, turned, lambda g: None, lambda g: piece(g).start())
    for g in range(pieces):
        piece(g).wait()


def on_device(
    bands,
    n,
    fields,
    w_conv1,
    b_conv1,
    w_conv2,
    b_conv2,
    w_query,
    w_key,
    w_value,
    w_out,
    rotation,
    owner,
    counts,
):
    size, _, chans = fields.shape
    rows = size // n
    inner = rows - HALO
    cols = size * n
    bf16 = jnp.bfloat16
    smem = pl.BlockSpec(memory_space=pltpu.SMEM)
    vmem = pl.BlockSpec(memory_space=pltpu.VMEM)
    hbm = pl.BlockSpec(memory_space=pltpu.HBM)
    params = pltpu.CompilerParams(vmem_limit_bytes=VMEM_BYTES)
    pieces = size * size // GROUP

    def call(kernel, name, out, scalars, arrays, scratch, array_spec=vmem, scalar_spec=smem, out_spec=vmem):
        many = isinstance(out, list)
        return pl.pallas_call(
            functools.partial(kernel, n, rows),
            out_shape=out,
            in_specs=[scalar_spec] * len(scalars) + [array_spec] * len(arrays),
            out_specs=[out_spec] * len(out) if many else out_spec,
            scratch_shapes=scratch,
            compiler_params=params,
            name=name,
        )(*scalars, *arrays)

    def array(*shape):
        return jax.ShapeDtypeStruct(shape, bf16)

    order = sorted(range(1, n), key=lambda d: -min(d, n - d))

    def around_by(x, d):
        return lax.ppermute(x, "lon", [(i, (i + d) % n) for i in range(n)])

    def around(parts):
        moved = {d: around_by(parts[d], d) for d in order}
        return [parts[0]] + [moved[d] for d in range(1, n)]

    def in_hbm(x):
        return pltpu.with_memory_space_constraint(x, pltpu.HBM)

    rotation, owner = in_hbm(rotation.T), in_hbm(owner.T)
    loaded = [counts]
    loaded += [w_conv1.reshape(3, 3 * chans, chans), b_conv1.reshape(1, chans)]
    loaded += [w_conv2.reshape(3, 3 * chans, chans), b_conv2.reshape(1, chans), w_value.T, w_out]
    loaded = [in_hbm(x) for x in loaded]
    turned = [in_hbm(x) for x in (w_query, w_key.T)]
    staging = pltpu.VMEM((chans // LANES, size * (size + 8), LANES), jnp.float32)
    block = pltpu.VMEM((size, size, chans), bf16)

    slabs = [array(HALO, size, chans)] * n + [array(rows, size, chans)] * n
    scratch = [staging, block, block, pltpu.SMEM(rotation.shape, rotation.dtype)]
    scratch += [pltpu.SemaphoreType.DMA((3,)), pltpu.SemaphoreType.DMA((pieces,))]
    held = slabs + [pltpu.VMEM(x.shape, x.dtype) for x in (rotation, owner)]
    *slabs, rotation, owner = call(send_kernel, "send", held, [rotation, owner], [in_hbm(fields)], scratch, hbm, hbm)
    edges = around(slabs[:n])
    slabs = around(slabs[n:])

    snake = [a * n + shard_of(a, g, n) for a in range(bands) for g in range(n)]
    pairs = [(snake[i], snake[i + 1 if i % 2 else i - 1]) for i in range(1, bands * n - 1)]
    sent = call(edge_kernel, "edge", array(HALO, cols, chans), [owner], edges, [])
    received = lax.ppermute(sent, ("lat", "lon"), pairs)

    head_dim = w_key.shape[1]
    heads = chans // head_dim
    held = [pltpu.VMEM(x.shape, x.dtype) for x in loaded]
    held += [pltpu.VMEM(w_query.shape, bf16), pltpu.VMEM(w_key.shape, bf16)]
    scratch = [pltpu.VMEM(x.shape, bf16) for x in turned] + [pltpu.SemaphoreType.DMA((len(loaded) + 2,))]
    loaded = call(load_kernel, "load", held, [sent], loaded + turned, scratch, hbm, hbm)
    counts, *convs, w_value, w_out, w_query, w_key = loaded

    def taps(count):
        return pltpu.VMEM((count, cols, 3 * chans), bf16)

    def working(segments):
        blocks, width = segments * rows, heads * size
        return [
            pltpu.VMEM((blocks * size, chans), bf16),
            pltpu.VMEM((blocks, cols, width), jnp.float32),
            pltpu.VMEM((blocks, cols, width), bf16),
            pltpu.VMEM((head_dim, blocks * width), bf16),
        ]

    cells = rows * cols
    result = array(rows * size, chans)
    first, *others = [*order, 0]
    results = {}
    results[first], *held = call(
        functools.partial(main_kernel, first),
        "main",
        [array(rows * size + AHEAD, chans), array(cells, chans), array(cells, chans), array(cells, head_dim), array(head_dim, cells)],
        [owner, counts],
        slabs + [sent, received, *convs, w_key, w_value, w_query, w_out],
        [pltpu.VMEM((rows + 2 * HALO, cols, chans), bf16), taps(rows + 2 * HALO), taps(rows + HALO)] + working(1),
    )
    moved = {first: around_by(results[first], first)}
    rest = call(
        functools.partial(rest_kernel, others),
        "rest",
        [result] * len(others),
        [owner, counts],
        held + [w_query, w_out],
        working(len(others)),
    )
    for d, x in zip(others, rest):
        moved[d] = around_by(x, d) if d else x
    slabs = [moved[d] for d in range(n)]
    scratch = [staging, block, block, pltpu.SemaphoreType.DMA((pieces,))]
    return call(store_kernel, "store", array(*fields.shape), [rotation], slabs, scratch, out_spec=hbm)


def solution(mesh):
    in_specs = (P("lat", "lon", None), P(), P(), P(), P(), P(), P(), P(), P(), P(), P(), P())
    out_specs = P("lat", "lon", None)
    body = functools.partial(on_device, mesh.shape["lat"], mesh.shape["lon"])
    return jax.shard_map(body, mesh=mesh, in_specs=in_specs, out_specs=out_specs, check_vma=False)
```

```python
import functools
import math

import jax
import jax.numpy as jnp
from jax import lax
from jax.experimental import pallas as pl
from jax.experimental.pallas import tpu as pltpu
from jax.sharding import PartitionSpec as P

HALO = 2
LANES = 128
GROUP = 256
CHUNKS = 3
AHEAD = 16
VMEM_BYTES = 28 * 1024 * 1024


def group_of(band, shard, n):
    outer = jnp.where((shard == n - 2) == (band % 2 == 0), 0, n - 1)
    return jnp.where(shard < n - 2, shard + 1, outer)


def shard_of(band, group, n):
    if 0 < group < n - 1:
        return group - 1
    return n - 2 if (group == 0) == (band % 2 == 0) else n - 1


def first_held(group, rows):
    return group * rows - HALO * (group % 2)


def turn(quarter, staged, block, out, ready, done):
    size, _, chans = block.shape
    tiles = staged.shape[0]
    pitch = staged.shape[1] // size
    depth = GROUP // size
    pieces = size // depth

    def column(col):
        parts = [staged[t, pl.ds(col, size, stride=pitch), :] for t in range(tiles)]
        return jnp.concatenate(parts, axis=1).astype(jnp.bfloat16)

    def keep(i, row):
        for t in range(tiles):
            staged[t, pl.ds(i * pitch, size), :] = row[:, t * LANES : (t + 1) * LANES]

    @pl.when(quarter == 0)
    def _():
        for g in range(pieces):
            ready(g)
            out[g * depth : (g + 1) * depth] = block[g * depth : (g + 1) * depth]
            done(g)

    @pl.when(quarter == 1)
    def _():
        for i in range(size):
            if i % depth == 0:
                ready(i // depth)
            keep(i, block[i].astype(jnp.float32))
        for i in range(size):
            out[i] = column(size - 1 - i)
            if i % depth == depth - 1:
                done(i // depth)

    @pl.when(quarter == 2)
    def _():
        i = lax.broadcasted_iota(jnp.int32, (GROUP, GROUP), 0)
        j = lax.broadcasted_iota(jnp.int32, (GROUP, GROUP), 1)
        backwards = jnp.where(i + j == GROUP - 1, 1.0, 0.0).astype(jnp.bfloat16)
        for g in reversed(range(pieces)):
            ready(pieces - 1 - g)
            cells = block[size - (g + 1) * depth : size - g * depth].reshape(GROUP, chans)
            turned = jnp.dot(backwards, cells, preferred_element_type=jnp.float32).astype(jnp.bfloat16)
            out[g * depth : (g + 1) * depth] = turned.reshape(depth, size, chans)
            done(g)

    @pl.when(quarter == 3)
    def _():
        for i in range(size):
            if i % depth == 0:
                ready(i // depth)
            keep(size - 1 - i, block[i].astype(jnp.float32))
        for i in range(size):
            out[i] = column(i)
            if i % depth == depth - 1:
                done(i // depth)


def send_kernel(n, rows, rotation_in, owner_in, fields, *rest):
    edges, slabs, (rotation_out, owner_out) = rest[:n], rest[n : 2 * n], rest[2 * n : 2 * n + 2]
    staged, block, upright, rotation, scalar_sems, sems = rest[2 * n + 2 :]
    band = lax.axis_index("lat")
    me = lax.axis_index("lon")
    depth = GROUP // fields.shape[0]

    def piece(g):
        at = pl.ds(g * depth, depth)
        return pltpu.make_async_copy(fields.at[at], block.at[at], sems.at[g])

    scalars = [
        pltpu.make_async_copy(rotation_in, rotation, scalar_sems.at[0]),
        pltpu.make_async_copy(rotation_in, rotation_out, scalar_sems.at[1]),
        pltpu.make_async_copy(owner_in, owner_out, scalar_sems.at[2]),
    ]
    for copy in scalars:
        copy.start()
    for g in range(fields.shape[0] // depth):
        piece(g).start()
    scalars[0].wait()
    turn((4 - rotation[me, band]) % 4, staged, block, upright, lambda g: piece(g).wait(), lambda g: None)
    for d in range(n):
        group = group_of(band, lax.rem(me + d, n), n)
        top, odd = first_held(group, rows), group % 2
        edges[d][...] = upright[pl.ds(top + rows * odd, HALO)]
        slabs[d][...] = upright[pl.ds(top + HALO * (1 - odd), rows)]
    scalars[1].wait()
    scalars[2].wait()


def load_kernel(n, rows, after, *refs):
    del after
    count = (len(refs) - 7) // 2
    direct, (query, key) = refs[:count], refs[count : count + 2]
    loaded, (w_query, w_key) = refs[count + 2 : 2 * count + 2], refs[2 * count + 2 : 2 * count + 4]
    query_in, key_in, sems = refs[2 * count + 4 :]
    pairs = list(zip(direct, loaded)) + [(query, query_in), (key, key_in)]
    copies = [pltpu.make_async_copy(*pair, sems.at[i]) for i, pair in enumerate(pairs)]
    for copy in copies:
        copy.start()
    for copy in copies:
        copy.wait()
    w_key[...] = key_in[...].T
    w_query[...] = query_in[...]


def columns_of(segment, size):
    return pl.ds(pl.multiple_of(segment * size, size), size)


def whole_rows(n, owner, slabs, out, first):
    band = lax.axis_index("lat")
    me = lax.axis_index("lon")
    count, size = slabs[0].shape[:2]
    for d in range(n):
        segment = owner[lax.rem(me + n - d, n), band]
        out[pl.ds(first, count), columns_of(segment, size)] = slabs[d][...]


def edge_kernel(n, rows, owner, *rest):
    del rows
    whole_rows(n, owner, rest[:n], rest[n], 0)


def spread(taps, r, row):
    cols, chans = row.shape
    taps[r, :, :chans] = pltpu.roll(row, 1, 0).astype(jnp.bfloat16)
    taps[r, :, chans : 2 * chans] = row.astype(jnp.bfloat16)
    taps[r, :, 2 * chans :] = pltpu.roll(row, cols - 1, 0).astype(jnp.bfloat16)


def convolve(taps, weight, bias, first, count):
    cols, width = taps.shape[1:]
    windows = [taps[first + i : first + i + count].reshape(count * cols, width) for i in range(3)]
    depth = weight.shape[0] * width
    product = jnp.dot(
        jnp.concatenate(windows, axis=1),
        weight[...].reshape(depth, weight.shape[2]),
        preferred_element_type=jnp.float32,
    )
    return product + bias[...]


def silu(x):
    half = 0.5 * x
    return half + half * jnp.tanh(half)


def live_count(counts, row):
    inside = (row >= 0) & (row < counts.shape[0])
    return jnp.where(inside, counts[jnp.clip(row, 0, counts.shape[0] - 1)], 0)


def by_last(a, b):
    return lax.dot_general(a, b, (((1,), (1,)), ((), ())), preferred_element_type=jnp.float32)


def attend(segments, span, limits, mixed, normed, keys, values, w_query, w_out, results, here, scores, expo, turned):
    rows, chans = len(limits), mixed.shape[1]
    size = here.shape[0] // (rows * len(segments))
    head_dim = keys.shape[1]
    heads = chans // head_dim
    cols = mixed.shape[0] // rows
    width = heads * size
    blocks = [(s * rows + r, s, r) for s in range(len(segments)) for r in range(*span)]
    low, high = blocks[0][0], blocks[-1][0] + 1

    def cells(s, r):
        return columns_of(segments[s] + r * (cols // size), size)

    for b, s, r in blocks:
        here[b * size : (b + 1) * size, :] = normed[cells(s, r), :]
    own = here[low * size : high * size, :]
    query = jnp.dot(own, w_query[...], preferred_element_type=jnp.float32).astype(jnp.bfloat16)
    queries = [query[:, h * head_dim : (h + 1) * head_dim] for h in range(heads)]
    for b, s, r in blocks:
        part = [query[(b - low) * size : (b - low + 1) * size] for query in queries]
        scores[b] = by_last(keys[r * cols : (r + 1) * cols, :], jnp.concatenate(part, axis=0))
    key_at = lax.broadcasted_iota(jnp.int32, (cols, width), 0)
    scale = math.log2(math.e) / head_dim**0.5
    shares = {}
    for b, s, r in blocks:
        part = jnp.where(key_at < limits[r], scores[b], -jnp.inf)
        part = jnp.exp2((part - jnp.max(part, axis=0, keepdims=True)) * scale)
        shares[b] = 1.0 / jnp.sum(part, axis=0, keepdims=True)
        expo[b] = part.astype(jnp.bfloat16)
    for b, s, r in blocks:
        summed = jnp.dot(values[:, r * cols : (r + 1) * cols], expo[b], preferred_element_type=jnp.float32)
        turned[:, b * width : (b + 1) * width] = (summed * shares[b]).astype(jnp.bfloat16)
    attended = turned[:, low * width : high * width].T
    parts = []
    for h in range(heads):
        starts = [(b - low) * width + h * size for b, *_ in blocks]
        parts.append(jnp.concatenate([attended[start : start + size] for start in starts], axis=0))
    update = jnp.dot(jnp.concatenate(parts, axis=1), w_out[...], preferred_element_type=jnp.float32)
    for b, s, r in blocks:
        cell = segments[s] * size + lax.broadcasted_iota(jnp.int32, (size, chans), 0)
        part = jnp.where(cell < limits[r], update[(b - low) * size : (b - low + 1) * size], 0.0)
        results[s][r * size : (r + 1) * size, :] = (mixed[cells(s, r), :].astype(jnp.float32) + part).astype(jnp.bfloat16)


def main_kernel(first, n, rows, owner, counts, *rest):
    slabs, sent, received = rest[:n], rest[n], rest[n + 1]
    w_conv1, b_conv1, w_conv2, b_conv2, w_key, w_value, w_query, w_out = rest[n + 2 : n + 10]
    result, mixed, normed, keys, values = rest[n + 10 : n + 15]
    grid, taps, acts, *scratch = rest[n + 15 :]
    band = lax.axis_index("lat")
    me = lax.axis_index("lon")
    group = group_of(band, me, n)
    odd = group % 2
    cols, chans = sent.shape[1:]
    cell = lax.broadcasted_iota(jnp.int32, (cols, chans), 0)
    first_row = band * (rows * n) + group * rows
    whole_rows(n, owner, slabs, grid, 2 * HALO * (1 - odd))
    grid[pl.ds(HALO + (rows - HALO) * odd, HALO)] = sent[...]
    grid[pl.ds((rows + HALO) * odd, HALO)] = received[...]
    limits = [live_count(counts, first_row - 1 + r) for r in range(rows + HALO)]

    def spread_inputs(start, stop):
        for r in range(start, stop):
            spread(taps, r, grid[r].astype(jnp.float32))

    def spread_acts(start, stop, product):
        act = silu(product)
        for r in range(start, stop):
            at = slice((r - start) * cols, (r - start + 1) * cols)
            spread(acts, r, jnp.where(cell < limits[r], act[at], 0.0))

    def mix(start, stop, product):
        for r in range(start, stop):
            here = grid[r + HALO].astype(jnp.float32) + product[(r - start) * cols : (r - start + 1) * cols]
            here = jnp.where(cell < limits[r + 1], here, 0.0)
            mixed[r * cols : (r + 1) * cols, :] = here.astype(jnp.bfloat16)
        at = slice(start * cols, stop * cols)
        flat = mixed[at, :].astype(jnp.float32)
        scaled = (flat * lax.rsqrt(jnp.mean(flat * flat, axis=1, keepdims=True) + 1e-06)).astype(jnp.bfloat16)
        normed[at, :] = scaled
        keys[at, :] = jnp.dot(scaled, w_key[...], preferred_element_type=jnp.float32).astype(jnp.bfloat16)
        values[:, at] = by_last(w_value[...], scaled).astype(jnp.bfloat16)

    total = rows + HALO
    chunks = min(CHUNKS, total // HALO)
    cuts = [min(-(-total // chunks) * c, total) for c in range(chunks + 1)]
    ends = [0] + [cut + HALO for cut in cuts[1:]]
    lows = [max(cut - HALO, 0) for cut in cuts]
    firsts, seconds = [], []
    spread_inputs(ends[0], ends[1])
    for c in range(chunks):
        firsts.append(convolve(taps, w_conv1, b_conv1, cuts[c], cuts[c + 1] - cuts[c]))
        if c:
            spread_acts(cuts[c - 1], cuts[c], firsts[c - 1])
        if c + 1 < chunks:
            spread_inputs(ends[c + 1], ends[c + 2])
    for c in range(chunks):
        count = lows[c + 1] - lows[c]
        seconds.append(convolve(acts, w_conv2, b_conv2, lows[c], count) if count else None)
        if c == 0:
            spread_acts(cuts[-2], total, firsts[-1])
        elif seconds[c - 1] is not None:
            mix(lows[c - 1], lows[c], seconds[c - 1])
    mix(lows[-2], rows, seconds[-1])
    result[rows * (cols // n) :, :] = jnp.zeros((AHEAD, chans), result.dtype)
    segments = [owner[lax.rem(me + first, n), band]]
    shared = limits[1 : rows + 1], mixed, normed, keys, values, w_query, w_out
    attend(segments, (0, rows), *shared, [result], *scratch)


def rest_kernel(moves, n, rows, owner, counts, *rest):
    mixed, normed, keys, values, w_query, w_out = rest[:6]
    results, scratch = rest[6 : 6 + len(moves)], rest[6 + len(moves) :]
    band = lax.axis_index("lat")
    me = lax.axis_index("lon")
    first_row = band * (rows * n) + group_of(band, me, n) * rows
    limits = [counts[first_row + r] for r in range(rows)]
    segments = [owner[lax.rem(me + d, n), band] for d in moves]
    attend(segments, (0, rows), limits, mixed, normed, keys, values, w_query, w_out, results, *scratch)


def store_kernel(n, rows, rotation, *rest):
    slabs, (out, staged, upright, turned, sems) = rest[:n], rest[n:]
    band = lax.axis_index("lat")
    me = lax.axis_index("lon")
    depth = GROUP // out.shape[0]
    pieces = out.shape[0] // depth
    for d in range(n):
        top = group_of(band, lax.rem(me + n - d, n), n) * rows
        upright[pl.ds(top, rows)] = slabs[d][: rows * out.shape[0], :].reshape(rows, *out.shape[1:])

    def piece(g):
        at = pl.ds(g * depth, depth)
        return pltpu.make_async_copy(turned.at[at], out.at[at], sems.at[g])

    turn(rotation[me, band] % 4, staged, upright, turned, lambda g: None, lambda g: piece(g).start())
    for g in range(pieces):
        piece(g).wait()


def on_device(
    bands,
    n,
    fields,
    w_conv1,
    b_conv1,
    w_conv2,
    b_conv2,
    w_query,
    w_key,
    w_value,
    w_out,
    rotation,
    owner,
    counts,
):
    size, _, chans = fields.shape
    rows = size // n
    inner = rows - HALO
    cols = size * n
    bf16 = jnp.bfloat16
    smem = pl.BlockSpec(memory_space=pltpu.SMEM)
    vmem = pl.BlockSpec(memory_space=pltpu.VMEM)
    hbm = pl.BlockSpec(memory_space=pltpu.HBM)
    params = pltpu.CompilerParams(vmem_limit_bytes=VMEM_BYTES)
    pieces = size * size // GROUP

    def call(kernel, name, out, scalars, arrays, scratch, array_spec=vmem, scalar_spec=smem, out_spec=vmem):
        many = isinstance(out, list)
        return pl.pallas_call(
            functools.partial(kernel, n, rows),
            out_shape=out,
            in_specs=[scalar_spec] * len(scalars) + [array_spec] * len(arrays),
            out_specs=[out_spec] * len(out) if many else out_spec,
            scratch_shapes=scratch,
            compiler_params=params,
            name=name,
        )(*scalars, *arrays)

    def array(*shape):
        return jax.ShapeDtypeStruct(shape, bf16)

    order = sorted(range(1, n), key=lambda d: -min(d, n - d))

    def around_by(x, d):
        return lax.ppermute(x, "lon", [(i, (i + d) % n) for i in range(n)])

    def around(parts):
        moved = {d: around_by(parts[d], d) for d in order}
        return [parts[0]] + [moved[d] for d in range(1, n)]

    def in_hbm(x):
        return pltpu.with_memory_space_constraint(x, pltpu.HBM)

    rotation, owner = in_hbm(rotation.T), in_hbm(owner.T)
    loaded = [counts]
    loaded += [w_conv1.reshape(3, 3 * chans, chans), b_conv1.reshape(1, chans)]
    loaded += [w_conv2.reshape(3, 3 * chans, chans), b_conv2.reshape(1, chans), w_value.T, w_out]
    loaded = [in_hbm(x) for x in loaded]
    turned = [in_hbm(x) for x in (w_query, w_key.T)]
    staging = pltpu.VMEM((chans // LANES, size * (size + 8), LANES), jnp.float32)
    block = pltpu.VMEM((size, size, chans), bf16)

    slabs = [array(HALO, size, chans)] * n + [array(rows, size, chans)] * n
    scratch = [staging, block, block, pltpu.SMEM(rotation.shape, rotation.dtype)]
    scratch += [pltpu.SemaphoreType.DMA((3,)), pltpu.SemaphoreType.DMA((pieces,))]
    held = slabs + [pltpu.VMEM(x.shape, x.dtype) for x in (rotation, owner)]
    *slabs, rotation, owner = call(send_kernel, "send", held, [rotation, owner], [in_hbm(fields)], scratch, hbm, hbm)
    edges = around(slabs[:n])
    slabs = around(slabs[n:])

    snake = [a * n + shard_of(a, g, n) for a in range(bands) for g in range(n)]
    pairs = [(snake[i], snake[i + 1 if i % 2 else i - 1]) for i in range(1, bands * n - 1)]
    sent = call(edge_kernel, "edge", array(HALO, cols, chans), [owner], edges, [])
    received = lax.ppermute(sent, ("lat", "lon"), pairs)

    head_dim = w_key.shape[1]
    heads = chans // head_dim
    held = [pltpu.VMEM(x.shape, x.dtype) for x in loaded]
    held += [pltpu.VMEM(w_query.shape, bf16), pltpu.VMEM(w_key.shape, bf16)]
    scratch = [pltpu.VMEM(x.shape, bf16) for x in turned] + [pltpu.SemaphoreType.DMA((len(loaded) + 2,))]
    loaded = call(load_kernel, "load", held, [sent], loaded + turned, scratch, hbm, hbm)
    counts, *convs, w_value, w_out, w_query, w_key = loaded

    def taps(count):
        return pltpu.VMEM((count, cols, 3 * chans), bf16)

    def working(segments):
        blocks, width = segments * rows, heads * size
        return [
            pltpu.VMEM((blocks * size, chans), bf16),
            pltpu.VMEM((blocks, cols, width), jnp.float32),
            pltpu.VMEM((blocks, cols, width), bf16),
            pltpu.VMEM((head_dim, blocks * width), bf16),
        ]

    cells = rows * cols
    result = array(rows * size, chans)
    first, *others = [*order, 0]
    results = {}
    results[first], *held = call(
        functools.partial(main_kernel, first),
        "main",
        [array(rows * size + AHEAD, chans), array(cells, chans), array(cells, chans), array(cells, head_dim), array(head_dim, cells)],
        [owner, counts],
        slabs + [sent, received, *convs, w_key, w_value, w_query, w_out],
        [pltpu.VMEM((rows + 2 * HALO, cols, chans), bf16), taps(rows + 2 * HALO), taps(rows + HALO)] + working(1),
    )
    moved = {first: around_by(results[first], first)}
    for name, group in (("rest", others[:-1]), ("own", others[-1:])):
        parts = call(
            functools.partial(rest_kernel, group),
            name,
            [result] * len(group),
            [owner, counts],
            held + [w_query, w_out],
            working(len(group)),
        )
        for d, x in zip(group, parts):
            moved[d] = around_by(x, d) if d else x
    slabs = [moved[d] for d in range(n)]
    scratch = [staging, block, block, pltpu.SemaphoreType.DMA((pieces,))]
    return call(store_kernel, "store", array(*fields.shape), [rotation], slabs, scratch, out_spec=hbm)


def solution(mesh):
    in_specs = (P("lat", "lon", None), P(), P(), P(), P(), P(), P(), P(), P(), P(), P(), P())
    out_specs = P("lat", "lon", None)
    body = functools.partial(on_device, mesh.shape["lat"], mesh.shape["lon"])
    return jax.shard_map(body, mesh=mesh, in_specs=in_specs, out_specs=out_specs, check_vma=False)
```

```python
import functools
import math

import jax
import jax.numpy as jnp
from jax import lax
from jax.experimental import pallas as pl
from jax.experimental.pallas import tpu as pltpu
from jax.sharding import PartitionSpec as P

HALO = 2
LANES = 128
GROUP = 256
CHUNKS = 3
AHEAD = 16
VMEM_BYTES = 28 * 1024 * 1024


def group_of(band, shard, n):
    outer = jnp.where((shard == n - 2) == (band % 2 == 0), 0, n - 1)
    return jnp.where(shard < n - 2, shard + 1, outer)


def shard_of(band, group, n):
    if 0 < group < n - 1:
        return group - 1
    return n - 2 if (group == 0) == (band % 2 == 0) else n - 1


def first_held(group, rows):
    return group * rows - HALO * (group % 2)


def turn(quarter, staged, block, out, ready, done):
    size, _, chans = block.shape
    tiles = staged.shape[0]
    pitch = staged.shape[1] // size
    depth = GROUP // size
    pieces = size // depth

    def column(col):
        parts = [staged[t, pl.ds(col, size, stride=pitch), :] for t in range(tiles)]
        return jnp.concatenate(parts, axis=1).astype(jnp.bfloat16)

    def keep(i, row):
        for t in range(tiles):
            staged[t, pl.ds(i * pitch, size), :] = row[:, t * LANES : (t + 1) * LANES]

    @pl.when(quarter == 0)
    def _():
        for g in range(pieces):
            ready(g)
            out[g * depth : (g + 1) * depth] = block[g * depth : (g + 1) * depth]
            done(g)

    @pl.when(quarter == 1)
    def _():
        for i in range(size):
            if i % depth == 0:
                ready(i // depth)
            keep(i, block[i].astype(jnp.float32))
        for i in range(size):
            out[i] = column(size - 1 - i)
            if i % depth == depth - 1:
                done(i // depth)

    @pl.when(quarter == 2)
    def _():
        i = lax.broadcasted_iota(jnp.int32, (GROUP, GROUP), 0)
        j = lax.broadcasted_iota(jnp.int32, (GROUP, GROUP), 1)
        backwards = jnp.where(i + j == GROUP - 1, 1.0, 0.0).astype(jnp.bfloat16)
        for g in reversed(range(pieces)):
            ready(pieces - 1 - g)
            cells = block[size - (g + 1) * depth : size - g * depth].reshape(GROUP, chans)
            turned = jnp.dot(backwards, cells, preferred_element_type=jnp.float32).astype(jnp.bfloat16)
            out[g * depth : (g + 1) * depth] = turned.reshape(depth, size, chans)
            done(g)

    @pl.when(quarter == 3)
    def _():
        for i in range(size):
            if i % depth == 0:
                ready(i // depth)
            keep(size - 1 - i, block[i].astype(jnp.float32))
        for i in range(size):
            out[i] = column(i)
            if i % depth == depth - 1:
                done(i // depth)


def send_kernel(n, rows, rotation_in, owner_in, fields, *rest):
    edges, slabs, (rotation_out, owner_out) = rest[:n], rest[n : 2 * n], rest[2 * n : 2 * n + 2]
    staged, block, upright, rotation, scalar_sems, sems = rest[2 * n + 2 :]
    band = lax.axis_index("lat")
    me = lax.axis_index("lon")
    depth = GROUP // fields.shape[0]

    def piece(g):
        at = pl.ds(g * depth, depth)
        return pltpu.make_async_copy(fields.at[at], block.at[at], sems.at[g])

    scalars = [
        pltpu.make_async_copy(rotation_in, rotation, scalar_sems.at[0]),
        pltpu.make_async_copy(rotation_in, rotation_out, scalar_sems.at[1]),
        pltpu.make_async_copy(owner_in, owner_out, scalar_sems.at[2]),
    ]
    for copy in scalars:
        copy.start()
    for g in range(fields.shape[0] // depth):
        piece(g).start()
    scalars[0].wait()
    turn((4 - rotation[me, band]) % 4, staged, block, upright, lambda g: piece(g).wait(), lambda g: None)
    for d in range(n):
        group = group_of(band, lax.rem(me + d, n), n)
        top, odd = first_held(group, rows), group % 2
        edges[d][...] = upright[pl.ds(top + rows * odd, HALO)]
        slabs[d][...] = upright[pl.ds(top + HALO * (1 - odd), rows)]
    scalars[1].wait()
    scalars[2].wait()


def load_kernel(n, rows, after, *refs):
    del after
    count = (len(refs) - 7) // 2
    direct, (query, key) = refs[:count], refs[count : count + 2]
    loaded, (w_query, w_key) = refs[count + 2 : 2 * count + 2], refs[2 * count + 2 : 2 * count + 4]
    query_in, key_in, sems = refs[2 * count + 4 :]
    pairs = list(zip(direct, loaded)) + [(query, query_in), (key, key_in)]
    copies = [pltpu.make_async_copy(*pair, sems.at[i]) for i, pair in enumerate(pairs)]
    for copy in copies:
        copy.start()
    for copy in copies:
        copy.wait()
    w_key[...] = key_in[...].T
    w_query[...] = query_in[...]


def columns_of(segment, size):
    return pl.ds(pl.multiple_of(segment * size, size), size)


def whole_rows(n, owner, slabs, out, first):
    band = lax.axis_index("lat")
    me = lax.axis_index("lon")
    count, size = slabs[0].shape[:2]
    for d in range(n):
        segment = owner[lax.rem(me + n - d, n), band]
        out[pl.ds(first, count), columns_of(segment, size)] = slabs[d][...]


def edge_kernel(n, rows, owner, *rest):
    del rows
    whole_rows(n, owner, rest[:n], rest[n], 0)


def spread(taps, r, row):
    cols, chans = row.shape
    taps[r, :, :chans] = pltpu.roll(row, 1, 0).astype(jnp.bfloat16)
    taps[r, :, chans : 2 * chans] = row.astype(jnp.bfloat16)
    taps[r, :, 2 * chans :] = pltpu.roll(row, cols - 1, 0).astype(jnp.bfloat16)


def convolve(taps, weight, bias, first, count):
    cols, width = taps.shape[1:]
    windows = [taps[first + i : first + i + count].reshape(count * cols, width) for i in range(3)]
    depth = weight.shape[0] * width
    product = jnp.dot(
        jnp.concatenate(windows, axis=1),
        weight[...].reshape(depth, weight.shape[2]),
        preferred_element_type=jnp.float32,
    )
    return product + bias[...]


def silu(x):
    half = 0.5 * x
    return half + half * jnp.tanh(half)


def live_count(counts, row):
    inside = (row >= 0) & (row < counts.shape[0])
    return jnp.where(inside, counts[jnp.clip(row, 0, counts.shape[0] - 1)], 0)


def by_last(a, b):
    return lax.dot_general(a, b, (((1,), (1,)), ((), ())), preferred_element_type=jnp.float32)


def attend(segments, span, limits, mixed, normed, keys, values, w_query, w_out, results, here, scores, expo, turned):
    rows, chans = len(limits), mixed.shape[1]
    size = here.shape[0] // (rows * len(segments))
    head_dim = keys.shape[1]
    heads = chans // head_dim
    cols = mixed.shape[0] // rows
    width = heads * size
    blocks = [(s * rows + r, s, r) for s in range(len(segments)) for r in range(*span)]
    low, high = blocks[0][0], blocks[-1][0] + 1

    def cells(s, r):
        return columns_of(segments[s] + r * (cols // size), size)

    for b, s, r in blocks:
        here[b * size : (b + 1) * size, :] = normed[cells(s, r), :]
    own = here[low * size : high * size, :]
    query = jnp.dot(own, w_query[...], preferred_element_type=jnp.float32).astype(jnp.bfloat16)
    queries = [query[:, h * head_dim : (h + 1) * head_dim] for h in range(heads)]
    for b, s, r in blocks:
        part = [query[(b - low) * size : (b - low + 1) * size] for query in queries]
        scores[b] = by_last(keys[r * cols : (r + 1) * cols, :], jnp.concatenate(part, axis=0))
    key_at = lax.broadcasted_iota(jnp.int32, (cols, width), 0)
    scale = math.log2(math.e) / head_dim**0.5
    shares = {}
    for b, s, r in blocks:
        part = jnp.where(key_at < limits[r], scores[b], -jnp.inf)
        part = jnp.exp2((part - jnp.max(part, axis=0, keepdims=True)) * scale)
        shares[b] = 1.0 / jnp.sum(part, axis=0, keepdims=True)
        expo[b] = part.astype(jnp.bfloat16)
    for b, s, r in blocks:
        summed = jnp.dot(values[:, r * cols : (r + 1) * cols], expo[b], preferred_element_type=jnp.float32)
        turned[:, b * width : (b + 1) * width] = (summed * shares[b]).astype(jnp.bfloat16)
    attended = turned[:, low * width : high * width].T
    parts = []
    for h in range(heads):
        starts = [(b - low) * width + h * size for b, *_ in blocks]
        parts.append(jnp.concatenate([attended[start : start + size] for start in starts], axis=0))
    update = jnp.dot(jnp.concatenate(parts, axis=1), w_out[...], preferred_element_type=jnp.float32)
    for b, s, r in blocks:
        cell = segments[s] * size + lax.broadcasted_iota(jnp.int32, (size, chans), 0)
        part = jnp.where(cell < limits[r], update[(b - low) * size : (b - low + 1) * size], 0.0)
        results[s][r * size : (r + 1) * size, :] = (mixed[cells(s, r), :].astype(jnp.float32) + part).astype(jnp.bfloat16)


def main_kernel(first, n, rows, owner, counts, *rest):
    slabs, sent, received = rest[:n], rest[n], rest[n + 1]
    w_conv1, b_conv1, w_conv2, b_conv2, w_key, w_value, w_query, w_out = rest[n + 2 : n + 10]
    result, mixed, normed, keys, values = rest[n + 10 : n + 15]
    grid, taps, acts, *scratch = rest[n + 15 :]
    band = lax.axis_index("lat")
    me = lax.axis_index("lon")
    group = group_of(band, me, n)
    odd = group % 2
    cols, chans = sent.shape[1:]
    cell = lax.broadcasted_iota(jnp.int32, (cols, chans), 0)
    first_row = band * (rows * n) + group * rows
    whole_rows(n, owner, slabs, grid, 2 * HALO * (1 - odd))
    grid[pl.ds(HALO + (rows - HALO) * odd, HALO)] = sent[...]
    grid[pl.ds((rows + HALO) * odd, HALO)] = received[...]
    limits = [live_count(counts, first_row - 1 + r) for r in range(rows + HALO)]

    def spread_inputs(start, stop):
        for r in range(start, stop):
            spread(taps, r, grid[r].astype(jnp.float32))

    def spread_acts(start, stop, product):
        act = silu(product)
        for r in range(start, stop):
            at = slice((r - start) * cols, (r - start + 1) * cols)
            spread(acts, r, jnp.where(cell < limits[r], act[at], 0.0))

    def mix(start, stop, product):
        for r in range(start, stop):
            here = grid[r + HALO].astype(jnp.float32) + product[(r - start) * cols : (r - start + 1) * cols]
            here = jnp.where(cell < limits[r + 1], here, 0.0)
            mixed[r * cols : (r + 1) * cols, :] = here.astype(jnp.bfloat16)
        at = slice(start * cols, stop * cols)
        flat = mixed[at, :].astype(jnp.float32)
        scaled = (flat * lax.rsqrt(jnp.mean(flat * flat, axis=1, keepdims=True) + 1e-06)).astype(jnp.bfloat16)
        normed[at, :] = scaled
        keys[at, :] = jnp.dot(scaled, w_key[...], preferred_element_type=jnp.float32).astype(jnp.bfloat16)
        values[:, at] = by_last(w_value[...], scaled).astype(jnp.bfloat16)

    total = rows + HALO
    chunks = min(CHUNKS, total // HALO)
    cuts = [min(-(-total // chunks) * c, total) for c in range(chunks + 1)]
    ends = [0] + [cut + HALO for cut in cuts[1:]]
    lows = [max(cut - HALO, 0) for cut in cuts]
    firsts, seconds = [], []
    spread_inputs(ends[0], ends[1])
    for c in range(chunks):
        firsts.append(convolve(taps, w_conv1, b_conv1, cuts[c], cuts[c + 1] - cuts[c]))
        if c:
            spread_acts(cuts[c - 1], cuts[c], firsts[c - 1])
        if c + 1 < chunks:
            spread_inputs(ends[c + 1], ends[c + 2])
    for c in range(chunks):
        count = lows[c + 1] - lows[c]
        seconds.append(convolve(acts, w_conv2, b_conv2, lows[c], count) if count else None)
        if c == 0:
            spread_acts(cuts[-2], total, firsts[-1])
        elif seconds[c - 1] is not None:
            mix(lows[c - 1], lows[c], seconds[c - 1])
    mix(lows[-2], rows, seconds[-1])
    result[rows * (cols // n) :, :] = jnp.zeros((AHEAD, chans), result.dtype)
    segments = [owner[lax.rem(me + first, n), band]]
    shared = limits[1 : rows + 1], mixed, normed, keys, values, w_query, w_out
    attend(segments, (0, rows), *shared, [result], *scratch)


def rest_kernel(moves, n, rows, owner, counts, *rest):
    mixed, normed, keys, values, w_query, w_out = rest[:6]
    results, scratch = rest[6 : 6 + len(moves)], rest[6 + len(moves) :]
    band = lax.axis_index("lat")
    me = lax.axis_index("lon")
    first_row = band * (rows * n) + group_of(band, me, n) * rows
    limits = [counts[first_row + r] for r in range(rows)]
    segments = [owner[lax.rem(me + d, n), band] for d in moves]
    attend(segments, (0, rows), limits, mixed, normed, keys, values, w_query, w_out, results, *scratch)


def store_kernel(n, rows, rotation, *rest):
    slabs, (out, staged, upright, turned, sems) = rest[:n], rest[n:]
    band = lax.axis_index("lat")
    me = lax.axis_index("lon")
    depth = GROUP // out.shape[0]
    pieces = out.shape[0] // depth
    for d in range(n):
        top = group_of(band, lax.rem(me + n - d, n), n) * rows
        upright[pl.ds(top, rows)] = slabs[d][: rows * out.shape[0], :].reshape(rows, *out.shape[1:])

    def piece(g):
        at = pl.ds(g * depth, depth)
        return pltpu.make_async_copy(turned.at[at], out.at[at], sems.at[g])

    turn(rotation[me, band] % 4, staged, upright, turned, lambda g: None, lambda g: piece(g).start())
    for g in range(pieces):
        piece(g).wait()


def on_device(
    bands,
    n,
    fields,
    w_conv1,
    b_conv1,
    w_conv2,
    b_conv2,
    w_query,
    w_key,
    w_value,
    w_out,
    rotation,
    owner,
    counts,
):
    size, _, chans = fields.shape
    rows = size // n
    inner = rows - HALO
    cols = size * n
    bf16 = jnp.bfloat16
    smem = pl.BlockSpec(memory_space=pltpu.SMEM)
    vmem = pl.BlockSpec(memory_space=pltpu.VMEM)
    hbm = pl.BlockSpec(memory_space=pltpu.HBM)
    params = pltpu.CompilerParams(vmem_limit_bytes=VMEM_BYTES)
    pieces = size * size // GROUP

    def call(kernel, name, out, scalars, arrays, scratch, array_spec=vmem, scalar_spec=smem, out_spec=vmem):
        many = isinstance(out, list)
        return pl.pallas_call(
            functools.partial(kernel, n, rows),
            out_shape=out,
            in_specs=[scalar_spec] * len(scalars) + [array_spec] * len(arrays),
            out_specs=[out_spec] * len(out) if many else out_spec,
            scratch_shapes=scratch,
            compiler_params=params,
            name=name,
        )(*scalars, *arrays)

    def array(*shape):
        return jax.ShapeDtypeStruct(shape, bf16)

    order = sorted(range(1, n), key=lambda d: (-min(d, n - d), -d))

    def around_by(x, d):
        return lax.ppermute(x, "lon", [(i, (i + d) % n) for i in range(n)])

    def around(parts):
        moved = {d: around_by(parts[d], d) for d in order}
        return [parts[0]] + [moved[d] for d in range(1, n)]

    def in_hbm(x):
        return pltpu.with_memory_space_constraint(x, pltpu.HBM)

    rotation, owner = in_hbm(rotation.T), in_hbm(owner.T)
    loaded = [counts]
    loaded += [w_conv1.reshape(3, 3 * chans, chans), b_conv1.reshape(1, chans)]
    loaded += [w_conv2.reshape(3, 3 * chans, chans), b_conv2.reshape(1, chans), w_value.T, w_out]
    loaded = [in_hbm(x) for x in loaded]
    turned = [in_hbm(x) for x in (w_query, w_key.T)]
    staging = pltpu.VMEM((chans // LANES, size * (size + 8), LANES), jnp.float32)
    block = pltpu.VMEM((size, size, chans), bf16)

    slabs = [array(HALO, size, chans)] * n + [array(rows, size, chans)] * n
    scratch = [staging, block, block, pltpu.SMEM(rotation.shape, rotation.dtype)]
    scratch += [pltpu.SemaphoreType.DMA((3,)), pltpu.SemaphoreType.DMA((pieces,))]
    held = slabs + [pltpu.VMEM(x.shape, x.dtype) for x in (rotation, owner)]
    *slabs, rotation, owner = call(send_kernel, "send", held, [rotation, owner], [in_hbm(fields)], scratch, hbm, hbm)
    edges = around(slabs[:n])
    slabs = around(slabs[n:])

    snake = [a * n + shard_of(a, g, n) for a in range(bands) for g in range(n)]
    pairs = [(snake[i], snake[i + 1 if i % 2 else i - 1]) for i in range(1, bands * n - 1)]
    sent = call(edge_kernel, "edge", array(HALO, cols, chans), [owner], edges, [])
    received = lax.ppermute(sent, ("lat", "lon"), pairs)

    head_dim = w_key.shape[1]
    heads = chans // head_dim
    held = [pltpu.VMEM(x.shape, x.dtype) for x in loaded]
    held += [pltpu.VMEM(w_query.shape, bf16), pltpu.VMEM(w_key.shape, bf16)]
    scratch = [pltpu.VMEM(x.shape, bf16) for x in turned] + [pltpu.SemaphoreType.DMA((len(loaded) + 2,))]
    loaded = call(load_kernel, "load", held, [sent], loaded + turned, scratch, hbm, hbm)
    counts, *convs, w_value, w_out, w_query, w_key = loaded

    def taps(count):
        return pltpu.VMEM((count, cols, 3 * chans), bf16)

    def working(segments):
        blocks, width = segments * rows, heads * size
        return [
            pltpu.VMEM((blocks * size, chans), bf16),
            pltpu.VMEM((blocks, cols, width), jnp.float32),
            pltpu.VMEM((blocks, cols, width), bf16),
            pltpu.VMEM((head_dim, blocks * width), bf16),
        ]

    cells = rows * cols
    result = array(rows * size, chans)
    first, *others = [*order, 0]
    results = {}
    results[first], *held = call(
        functools.partial(main_kernel, first),
        "main",
        [array(rows * size + AHEAD, chans), array(cells, chans), array(cells, chans), array(cells, head_dim), array(head_dim, cells)],
        [owner, counts],
        slabs + [sent, received, *convs, w_key, w_value, w_query, w_out],
        [pltpu.VMEM((rows + 2 * HALO, cols, chans), bf16), taps(rows + 2 * HALO), taps(rows + HALO)] + working(1),
    )
    moved = {first: around_by(results[first], first)}
    for name, group in (("rest", others[:-1]), ("own", others[-1:])):
        parts = call(
            functools.partial(rest_kernel, group),
            name,
            [result] * len(group),
            [owner, counts],
            held + [w_query, w_out],
            working(len(group)),
        )
        for d, x in zip(group, parts):
            moved[d] = around_by(x, d) if d else x
    slabs = [moved[d] for d in range(n)]
    scratch = [staging, block, block, pltpu.SemaphoreType.DMA((pieces,))]
    return call(store_kernel, "store", array(*fields.shape), [rotation], slabs, scratch, out_spec=hbm)


def solution(mesh):
    in_specs = (P("lat", "lon", None), P(), P(), P(), P(), P(), P(), P(), P(), P(), P(), P())
    out_specs = P("lat", "lon", None)
    body = functools.partial(on_device, mesh.shape["lat"], mesh.shape["lon"])
    return jax.shard_map(body, mesh=mesh, in_specs=in_specs, out_specs=out_specs, check_vma=False)
```
